128 devices in a mesh: series: 4 (over x), tm: 32 (over z, y, core).
Axes of the slice: x: 4, y: 4, z: 4, core: 2. Of those that a mesh axis runs over, the one named last changes fastest.
Arguments:
- raw_values: float32 [4, 4096], P('series', 'tm'), may hold values from -6 to 6
- hours: int32 [4, 4096], P('series', 'tm'), may hold values from 0 to 23
- doc_lengths: int32 [4, 7], P('series'), may hold values from 16 to 4000, as said below
- doc_scale: float32 [4, 7], P('series'), may hold values from 0.5 to 2
- dataset_ids: int32 [4, 7, 1], P('series'), may hold values from 0 to 7
- lag_offsets: int32 [84], replicated, may hold values from 1 to 384, as said below
- w_lag: bfloat16 [87, 144], replicated, may hold values from -0.625 to 0.625
- w_qkv: bfloat16 [2, 144, 432], replicated, may hold values from -0.5 to 0.5
- w_out: bfloat16 [2, 144, 144], replicated, may hold values from -1.5 to 1.5
- w_gate_up: bfloat16 [2, 144, 768], replicated, may hold values from -0.5 to 0.5
- w_down: bfloat16 [2, 384, 144], replicated, may hold values from -0.3125 to 0.3125
- gains: float32 [2, 2, 144], replicated, may hold values from 0.5 to 1.5
- cotangent: float32 [4, 4096, 144], P('series', 'tm'), may hold values from -6 to 6
Outputs:
- activations: float32 [4, 4096, 144], P('series', 'tm')
- raw_grad: float32 [4, 4096], P('series', 'tm')
- scale_mean: float32 [8], replicated
- w_lag_grad: float32 [87, 144], replicated
- w_qkv_grad: float32 [2, 144, 432], replicated
- w_out_grad: float32 [2, 144, 144], replicated
- w_gate_up_grad: float32 [2, 144, 768], replicated
- w_down_grad: float32 [2, 384, 144], replicated
- gains_grad: float32 [2, 2, 144], replicated
The draws below stay inside these ranges and needn't reach their ends.
Inputs may be any that keep to these rules, and one draw needn't show every extreme that they name: `doc_lengths`: each row holds 3 short series, then one long series, then 3 short series; short ones have 32 // 2 to 32 steps; the row sums to 4096. `lag_offsets`: distinct and rising, the last equal to 384.
All inputs are finite; a program needn't handle non-finite values.
Results may differ from the reference program's by a relative error of at most 0.025.
Values may be sent and summed in bfloat16 or wider, within the bound.
No kernel may reach another device: no remote copies, remote signals or barrier semaphores. Data moves between devices by JAX's collectives and lax.ppermute only.
A program may use at most 192 MiB of HBM per device.

```python
import math
import jax
import jax.numpy as jnp
from jax import lax

D = 144
HEADS = 9
HEAD_DIM = 16
FF = 384
LAGS = 84
LAYERS = 2
SHORT_LEN = 32
SIDE_DOCS = 3
DATASETS = 8
SHORT_DOCS = 6
DOCS = 7
GROUPS = 4
LEN = 4096
MAXLAG = 384
FEATS = 87


def draw_doc_lengths(key, part):
    key = jax.random.fold_in(key, 5)
    first_key, third_key, fourth_key = jax.random.split(key, 3)
    least = SHORT_LEN // 2
    shorts = jax.random.randint(first_key, (GROUPS, SHORT_DOCS), least, SHORT_LEN + 1)
    least_slot = jax.random.randint(third_key, (GROUPS, 1), 0, SHORT_DOCS)
    columns = jnp.arange(SHORT_DOCS)[None, :]
    shorts = jnp.where(columns == least_slot, least, shorts)
    lucky = jax.random.randint(fourth_key, (), 0, GROUPS)
    group_rows = jnp.arange(GROUPS)[:, None]
    shorts = jnp.where(group_rows == lucky, least, shorts)
    long_length = LEN - jnp.sum(shorts, axis=1, keepdims=True)
    return jnp.concatenate([shorts[:, :SIDE_DOCS], long_length, shorts[:, SIDE_DOCS:]], axis=1).astype(jnp.int32)


def draw_lag_offsets(key, part):
    key = jax.random.fold_in(key, 11)
    order = jax.random.permutation(key, MAXLAG - 1) + 1
    chosen = jnp.sort(order[:LAGS - 1])
    return jnp.concatenate([chosen, jnp.array([MAXLAG])]).astype(jnp.int32)


def touch_ends(result, key, low, largest):
    extent = result.shape
    index_at = [jax.random.randint(jax.random.fold_in(key, axis), (), 0, extent[axis]) for axis in range(len(extent))]
    result = result.at[tuple(index_at)].set(low)
    longest = extent.index(max(extent))
    index_at[longest] = (index_at[longest] + 1) % extent[longest]
    return result.at[tuple(index_at)].set(largest)


def block_scale(key, shape, cuts, low, largest):
    level, own = 1.0, jax.random.fold_in(key, 6)
    for axis_at, blocks in cuts:
        heights = jnp.exp(jax.random.uniform(jax.random.fold_in(own, axis_at), (blocks,), jnp.float32, low / len(cuts), largest / len(cuts)))
        level = level * jnp.repeat(heights, shape[axis_at] // blocks).reshape([-1 if axis == axis_at else 1 for axis in range(len(shape))])
    return level


def distinct(stream_key, rows, amount, top, lift):
    order = jax.random.permutation(jax.random.fold_in(stream_key, 1), amount)
    pull = order
    for power in range(3):
        pull = pull * pull // amount
    pull = pull * lift // amount
    chance = jax.random.randint(jax.random.fold_in(stream_key, 2), (rows, amount), 0, 4096) + pull
    fixed_rows = jax.random.permutation(jax.random.fold_in(stream_key, 3), rows)[jnp.arange(amount) % rows]
    chance = jnp.where(jnp.arange(rows)[:, None] == fixed_rows[None, :], 1 << 14, chance)
    priority = chance * amount + jnp.arange(amount)
    return lax.top_k(priority.astype(jnp.int32), top)[1].astype(jnp.int32)


def noise(rng, dims, deviation, limit, shards=(), held_as=jnp.bfloat16):
    values = jax.random.normal(rng, dims, jnp.float32) * deviation
    if len(shards) > 0:
        values = block_scale(rng, dims, shards, -0.22, 0.18) * values
    return jnp.clip(values, min=-limit, max=limit).astype(held_as)


def setup_inputs(seed: int = 0) -> dict:
    splits = jax.random.split(jax.random.key(seed), 14)
    return {
        "raw_values": noise(splits[0], (GROUPS, LEN), 1.0, 6.0, ((0, 4), (1, 32)), jnp.float32),
        "hours": touch_ends(jax.random.randint(splits[1], (GROUPS, LEN), 0, 24), jax.random.fold_in(splits[1], 1), 0, 23).astype(jnp.int32),
        "doc_lengths": draw_doc_lengths(jax.random.fold_in(splits[13], 71), 0),
        "doc_scale": jnp.clip(jnp.exp(math.log(2.0) - 1.3862944 * jax.random.uniform(splits[3], (GROUPS, DOCS), jnp.float32) ** block_scale(splits[3], (GROUPS, DOCS), ((0, 4),), -0.2, 0.2)), 0.5, 2.0),
        "dataset_ids": distinct(splits[4], GROUPS * DOCS, DATASETS, 1, 0).reshape((GROUPS, DOCS, 1)),
        "lag_offsets": draw_lag_offsets(jax.random.fold_in(splits[13], 71), 0),
        "w_lag": noise(splits[6], (FEATS, D), FEATS ** -0.5, 0.625),
        "w_qkv": noise(splits[7], (LAYERS, D, 3 * D), D ** -0.5, 0.5),
        "w_out": noise(splits[8], (LAYERS, D, D), (D // 8) ** -0.5, 1.5),
        "w_gate_up": noise(splits[9], (LAYERS, D, 2 * FF), D ** -0.5, 0.5),
        "w_down": noise(splits[10], (LAYERS, FF, D), FF ** -0.5, 0.3125),
        "gains": jnp.clip(1.0 + 0.1 * jax.random.normal(splits[11], (LAYERS, 2, D), jnp.float32), 0.5, 1.5),
        "cotangent": noise(splits[12], (GROUPS, LEN, D), 1.0, 6.0, ((0, 4), (1, 32)), jnp.float32),
    }


HIGH = lax.Precision.HIGHEST
EPSILON = 1e-06
MASKED = -1e+30

@jax.custom_vjp
def low(v):
    return lax.optimization_barrier(v.astype(jnp.bfloat16)).astype(jnp.float32)

@jax.custom_vjp
def low_back(v):
    return v

def low_keep(v):
    return (low(v), None)

def low_pass(kept, grad):
    return (grad,)

def back_keep(v):
    return (v, None)

def back_low(kept, grad):
    return (low(grad),)
low.defvjp(low_keep, low_pass)
low_back.defvjp(back_keep, back_low)

def doc_info(places, lengths, scales):
    ends = jnp.cumsum(lengths).astype(jnp.int32)
    after = places[:, None] >= ends[None, :]
    which = lax.optimization_barrier(jnp.sum(after.astype(jnp.int32), axis=1)).astype(jnp.int32)
    start = lax.optimization_barrier(jnp.sum(jnp.where(after, lengths[None, :], 0), axis=1)).astype(jnp.int32)
    labels = jnp.arange(lengths.shape[0], dtype=jnp.int32)
    picked = lax.optimization_barrier(jnp.sum(jnp.where(which[:, None] == labels[None, :], scales[None, :], jnp.float32(0.0)), axis=1))
    return (which, start, picked)

def lag_features(extended, places, local_rows, lag_offsets, hours, start, own_scale):
    index = (MAXLAG + local_rows[:, None] - lag_offsets[None, :]).astype(jnp.int32)
    lagged = jnp.take(extended, index)
    valid = places[:, None] - lag_offsets[None, :] >= start[:, None]
    values = jnp.where(valid, lagged, jnp.float32(0.0)) / own_scale[:, None]
    angle = hours.astype(jnp.float32) * (2.0 * math.pi / 24.0)
    return jnp.concatenate([values, jnp.sin(angle)[:, None], jnp.cos(angle)[:, None], jnp.log(own_scale)[:, None]], axis=1)

def rope_turn(field, places, sign):
    rows = field.shape[0]
    shaped = field.reshape(rows, HEADS, HEAD_DIM)
    half = HEAD_DIM // 2
    freqs = 10000.0 ** (-jnp.arange(half, dtype=jnp.float32) / half)
    angle = places.astype(jnp.float32)[:, None] * freqs[None, :]
    cosine = jnp.cos(angle)[:, None, :]
    sine = sign * jnp.sin(angle)[:, None, :]
    first = shaped[..., :half]
    second = shaped[..., half:]
    turned = jnp.concatenate([first * cosine - second * sine, second * cosine + first * sine], axis=-1)
    return turned.reshape(rows, HEADS * HEAD_DIM)

def normed(resid, gain):
    factor = lax.rsqrt(lax.optimization_barrier(jnp.mean(resid * resid, axis=-1, keepdims=True)) + EPSILON)
    return resid * factor * gain

def gated(gate_up):
    return jax.nn.silu(gate_up[:, :FF]) * gate_up[:, FF:]

def matmul(left, right):
    return jnp.dot(left, right, precision=HIGH, preferred_element_type=jnp.float32)

def attend_block(q_block, q_places, q_which, keys, values, places, which):
    raw = jnp.einsum('thd,jhd->htj', q_block, keys, precision=HIGH) * HEAD_DIM ** (-0.5)
    raw = low_back(raw)
    allowed = (which[None, :] == q_which[:, None]) & (places[None, :] <= q_places[:, None])
    masked = jnp.where(allowed[None], raw, MASKED)
    probs = low(jax.nn.softmax(masked, axis=-1))
    out = jnp.einsum('htj,jhd->thd', probs, values, precision=HIGH)
    return low(low_back(out))

def attention(query, key, value, places, which):
    span = query.shape[0]
    block = min(512, span)
    count = span // block
    keys = key.reshape(span, HEADS, HEAD_DIM)
    values = value.reshape(span, HEADS, HEAD_DIM)
    saved = jax.checkpoint(attend_block)
    blocks = (query.reshape(count, block, HEADS, HEAD_DIM), places.reshape(count, block), which.reshape(count, block))
    outs = lax.map(lambda part: saved(part[0], part[1], part[2], keys, values, places, which), blocks)
    return outs.reshape(span, HEADS * HEAD_DIM)

def reference(raw_values, hours, doc_lengths, doc_scale, dataset_ids, lag_offsets, w_lag, w_qkv, w_out, w_gate_up, w_down, gains, cotangent):
    span = raw_values.shape[1]
    places = jnp.arange(span, dtype=jnp.int32)
    params = (w_lag.astype(jnp.float32), w_qkv.astype(jnp.float32), w_out.astype(jnp.float32), w_gate_up.astype(jnp.float32), w_down.astype(jnp.float32), gains.astype(jnp.float32))

    def one_group(totals, group):
        raw, hour, lengths, scales, cot = group
        which, start, own_scale = doc_info(places, lengths, scales)

        def forward(raw, p_lag, p_qkv, p_out, p_gate_up, p_down, p_gains):
            extended = jnp.concatenate([jnp.zeros((MAXLAG,), jnp.float32), raw])
            feats = low(lag_features(extended, places, places, lag_offsets, hour, start, own_scale))
            resid = low_back(matmul(feats, p_lag))
            for layer in range(LAYERS):
                normal_a = low(normed(resid, p_gains[layer, 0]))
                mixed = low_back(matmul(normal_a, p_qkv[layer]))
                query = low(rope_turn(mixed[:, :D], places, 1.0))
                key = low(rope_turn(mixed[:, D:2 * D], places, 1.0))
                value = low(mixed[:, 2 * D:])
                attended = attention(query, key, value, places, which)
                resid = resid + low_back(matmul(attended, p_out[layer]))
                normal_b = low(normed(resid, p_gains[layer, 1]))
                gate_up = low_back(matmul(normal_b, p_gate_up[layer]))
                hidden = low(gated(gate_up))
                resid = resid + low_back(matmul(hidden, p_down[layer]))
            return resid
        out, back = jax.vjp(forward, raw, *params)
        grads = back(cot)
        totals = tuple((t + g for t, g in zip(totals, grads[1:])))
        return (totals, (out, grads[0]))
    start_totals = tuple((jnp.zeros(p.shape, jnp.float32) for p in params))
    totals, outs = lax.scan(one_group, start_totals, (raw_values, hours, doc_lengths, doc_scale, cotangent))
    member = (dataset_ids.reshape(-1)[:, None] == jnp.arange(DATASETS, dtype=jnp.int32)[None, :]).astype(jnp.float32)
    scale_mean = lax.optimization_barrier(jnp.sum(member * doc_scale.reshape(-1)[:, None], axis=0)) / lax.optimization_barrier(jnp.sum(member, axis=0))
    return (outs[0], outs[1], scale_mean, totals[0], totals[1], totals[2], totals[3], totals[4], totals[5])
```

```python
import math

import jax
import jax.numpy as jnp
import numpy as np
from jax import lax
from jax.experimental import pallas as pl
from jax.experimental.pallas import tpu as pltpu
from jax.sharding import PartitionSpec as P


D = 144
HEADS = 9
HEAD_DIM = 16
FF = 384
LAGS = 84
LAYERS = 2
DATASETS = 8
DOCS = 7
LEN = 4096
MAXLAG = 384
FEATS = 87
EPSILON = 1e-06
MASKED = -1e30
AUG = 192
STAT = AUG - D
LROW = D
DROW = D + 27
BLOCK = 512
BLOCKS = LEN // BLOCK
TILE = 128
TILES = LEN // TILE
STEPS = BLOCKS + 1
HALF = 64
ROWS = HEADS * HALF
LAGCOLS = 400
VMEM = 56 * 2**20

bf16 = jnp.bfloat16
f32 = jnp.float32
HIGH = lax.Precision.HIGHEST


def nn(a, b, precision=None):
    return lax.dot_general(a, b, (((1,), (0,)), ((), ())), precision=precision, preferred_element_type=f32)


def nt(a, b, precision=None):
    return lax.dot_general(a, b, (((1,), (1,)), ((), ())), precision=precision, preferred_element_type=f32)


def tn(a, b, precision=None):
    return lax.dot_general(a, b, (((0,), (0,)), ((), ())), precision=precision, preferred_element_type=f32)


def iota(shape, dim):
    return lax.broadcasted_iota(jnp.int32, shape, dim)


def eye(rows, cols, dtype):
    return (iota((rows, cols), 0) == iota((rows, cols), 1)).astype(dtype)


def column(row, size):
    keep = iota((size, size), 0) == iota((size, size), 1)
    return jnp.sum(jnp.where(keep, row, 0.0), axis=1, keepdims=True)


def geometry():
    index = lax.axis_index("tm")
    chip, core = index // 2, index % 2
    low = jnp.where(core == 0, chip, TILES - 1 - chip)
    return chip, core, low, TILES - 1 - low


def doc_start(places, len_ref):
    start = jnp.zeros_like(places)
    end = jnp.int32(0)
    for d in range(DOCS):
        end = end + len_ref[d]
        start = jnp.where(places >= end, end, start)
    return start


def doc_scale_at(places, len_ref, scale_ref):
    own = jnp.full(places.shape, scale_ref[0], f32)
    end = jnp.int32(0)
    for d in range(1, DOCS):
        end = end + len_ref[d - 1]
        own = jnp.where(places >= end, scale_ref[d], own)
    return own


def own_places(low, high):
    lane = iota((1, TILE), 1)
    return jnp.where(lane < HALF, low, high) * TILE + lane


def half_places(u, tile):
    return iota((HALF, 1), 0) + (tile * TILE + u * HALF)


def rotate(x, cosine, sine):
    cols = x.shape[1]
    parts = x.reshape(HEADS, 2, 8, cols)
    one, two = parts[:, 0], parts[:, 1]
    turned = jnp.stack([one * cosine - two * sine, two * cosine + one * sine], axis=1)
    return turned.reshape(D, cols)


def norm_factor(x):
    return lax.rsqrt(jnp.mean(x * x, axis=0, keepdims=True) + EPSILON)


def norm_back(x, gain, d_normal):
    r = norm_factor(x)
    scaled = d_normal * gain
    inner = jnp.mean(x * scaled, axis=0, keepdims=True)
    d_x = r * scaled - (r * r * r * inner) * x
    return d_x, jnp.sum(d_normal * x * r, axis=1, keepdims=True)


def head_columns(h, *firsts):
    col = iota((1, AUG), 1)
    keep = (col >= h * HEAD_DIM) & (col < (h + 1) * HEAD_DIM)
    for first in firsts:
        keep = keep | (col == first + h)
    return keep


def spread(ref, rows, *firsts):
    zero = jnp.zeros((HALF, AUG), f32)
    for h in range(HEADS):
        keep = head_columns(h, *firsts)
        for u in range(2):
            part = rows[u * HALF : (u + 1) * HALF]
            ref[u, h * HALF : (h + 1) * HALF, :] = jnp.where(keep, part, zero).astype(bf16)


def own_heads(x):
    col = iota((1, D), 1) // HEAD_DIM
    total = jnp.zeros((HALF, D), f32)
    for h in range(HEADS):
        total = jnp.where(col == h, x[h * HALF : (h + 1) * HALF, :D], total)
    return total


def three_parts(x):
    hi = x.astype(bf16)
    rest = x - hi.astype(f32)
    mid = rest.astype(bf16)
    return hi, mid, (rest - mid.astype(f32)).astype(bf16)


def put_tiles(ref, first, grads):
    at = first
    for c in range(grads.shape[1] // TILE):
        for r in range(grads.shape[0] // 16):
            ref[at] = grads[16 * r : 16 * (r + 1), c * TILE : (c + 1) * TILE].astype(bf16)
            at += 1
    return at


def qkv_block(normal, w_qkv, rope_ref, k, kaug_ref, vaug_ref, qall_ref):
    mixed = tn(w_qkv, normal)
    cosine = rope_ref[0:8, k * BLOCK : (k + 1) * BLOCK]
    sine = rope_ref[8:16, k * BLOCK : (k + 1) * BLOCK]
    qall_ref[k] = (rotate(mixed[:D], cosine, sine).astype(bf16).astype(f32) * HEAD_DIM**-0.5).astype(bf16)
    kaug_ref[k, 0:D, :] = rotate(mixed[D : 2 * D], cosine, sine).astype(bf16)
    vaug_ref[k, 0:D, :] = mixed[2 * D :].astype(bf16)
    ones = jnp.ones((STAT, BLOCK), bf16)
    kaug_ref[k, D:AUG, :] = ones
    vaug_ref[k, D:AUG, :] = ones


def own_tile(ref, low, high):
    lane = iota((1, TILE), 1)

    def at(tile):
        return ref[tile // 4, 0:D, pl.ds(pl.multiple_of((tile % 4) * TILE, TILE), TILE)].astype(f32)

    return jnp.where(lane < HALF, at(low), at(high)).astype(bf16)


def query_bias(u, tile, block, len_ref):
    places = half_places(u, tile)
    start = doc_start(places, len_ref)
    keys = iota((1, BLOCK), 1) + block * BLOCK
    return jnp.where((keys <= places) & (keys >= start), 0.0, MASKED)


def key_bias(u, tile, block, len_ref):
    keys = half_places(u, tile)
    places = iota((1, BLOCK), 1) + block * BLOCK
    start = doc_start(places, len_ref)
    return jnp.where((keys <= places) & (keys >= start), 0.0, MASKED)


def biased(scores, bias):
    return (scores.reshape(HEADS, HALF, BLOCK) + bias[None]).reshape(ROWS, BLOCK)


def attend(q_rows, kaug_ref, vaug_ref, len_ref, low, high, qbd, top_ref, acc_ref):
    spread(qbd, q_rows)
    top_ref[...] = jnp.full(top_ref.shape, MASKED, f32)
    acc_ref[...] = jnp.zeros(acc_ref.shape, f32)
    first = low // 4 + 1

    def step(s, carry):
        late = s >= first
        u = late.astype(jnp.int32)
        tile = jnp.where(late, high, low)
        block = s - jnp.where(late, first, 0)
        scores = biased(nn(qbd[u], kaug_ref[block]), query_bias(u, tile, block, len_ref))
        old = top_ref[u]
        new = jnp.maximum(old, jnp.max(scores, axis=1, keepdims=True))
        probs = jnp.exp(scores - new)
        acc_ref[u] = acc_ref[u] * jnp.exp(old - new) + nt(probs.astype(bf16), vaug_ref[block])
        top_ref[u] = new
        return carry

    lax.fori_loop(0, STEPS, step, 0)
    attended, stats = [], []
    lane = iota((1, STAT), 1)
    for u in range(2):
        acc = acc_ref[u]
        total = acc[:, D : D + 1]
        attended.append(own_heads(acc[:, :D] / total))
        parts = three_parts(-(top_ref[u] + jnp.log(total)))
        stat = jnp.zeros((HALF, STAT), f32)
        for j in range(3):
            part = parts[j].astype(f32)
            for h in range(HEADS):
                stat = jnp.where(lane == 9 * j + h, part[h * HALF : (h + 1) * HALF], stat)
        stats.append(stat)
    att_rows = jnp.concatenate(attended, axis=0).astype(bf16)
    stat_rows = jnp.concatenate(stats, axis=0).astype(bf16)
    return nt(eye(D, D, bf16), att_rows).astype(bf16), nt(eye(STAT, STAT, bf16), stat_rows).astype(bf16)


def feed_forward(resid, attended, w_out, w_gate_up, w_down, gain):
    mid = resid + tn(w_out, attended)
    normal = (mid * norm_factor(mid) * gain).astype(bf16)
    gate_up = tn(w_gate_up, normal)
    gate = gate_up[:FF]
    hidden = (gate * jax.nn.sigmoid(gate) * gate_up[FF:]).astype(bf16)
    return mid, normal, gate_up, hidden, mid + tn(w_down, hidden)


def feed_back(grad, attended, mid, normal, gate_up, hidden, w_out, w_gate_up, w_down, gain, stat, pack_ref, first):
    d_out = grad.astype(bf16)
    at = put_tiles(pack_ref, first, nt(d_out, hidden))
    d_hidden = nn(w_down, d_out)
    gate, up = gate_up[:FF], gate_up[FF:]
    sig = jax.nn.sigmoid(gate)
    d_gate = d_hidden * up * (sig * (1.0 + gate * (1.0 - sig)))
    d_up = d_hidden * (gate * sig)
    d_gate_up = jnp.concatenate([d_gate, d_up], axis=0).astype(bf16)
    at = put_tiles(pack_ref, at, nt(normal, d_gate_up))
    d_mid, d_gain = norm_back(mid, gain, nn(w_gate_up, d_gate_up))
    grad = grad + d_mid
    d_branch = grad.astype(bf16)
    at = put_tiles(pack_ref, at, nt(attended, d_branch[:TILE]))
    zeros = jnp.zeros((TILE - 64, TILE), bf16)
    tail = nt(attended, jnp.concatenate([jnp.zeros((48, TILE), bf16), d_branch[TILE:], zeros], axis=0))
    d_att = nn(w_out, d_branch).astype(bf16)
    product = d_att.astype(f32) * attended.astype(f32)
    delta = -jnp.sum(product.reshape(HEADS, HEAD_DIM, TILE), axis=1)
    delta = jnp.concatenate([delta, jnp.zeros((16 - HEADS, TILE), f32)], axis=0)
    hi, lo, _ = three_parts(delta)
    row, col = iota((STAT, 16), 0), iota((STAT, 16), 1)
    place = [((row == 27 + 9 * j + col) & (col < HEADS)).astype(bf16) for j in range(2)]
    stat = stat.astype(f32) + nn(place[0], hi) + nn(place[1], lo)
    return grad, jnp.concatenate([d_att, stat.astype(bf16)], axis=0), tail, d_gain, at


def gain_column(gains_ref, which):
    return column(gains_ref[which : which + 1, :], D)


def first_kernel(
    len_ref, scale_ref, values_ref, lag_ref, w_lag_ref, w_qkv_ref, w_out_ref, w_gate_up_ref, w_down_ref, gains_ref, rope_ref,
    next_ref, next_resid_ref, kaug_ref, vaug_ref, qall_ref, lagged_ref, feats_ref, w_dense_ref, resid_ref, normal_a_ref,
    q_ref, k_ref, v_ref, att_ref, stat_ref, mid_ref, normal_b_ref, gate_up_ref, hidden_ref,
    series, toeplitz, extra, qbd, top_ref, acc_ref,
):
    chip, core, low, high = geometry()
    places = iota((TILES, TILE), 0) * TILE + iota((TILES, TILE), 1)
    own = doc_scale_at(places, len_ref, scale_ref)
    values = values_ref[:, 0, :] / own
    angle = values_ref[:, 1, :] * (2.0 * math.pi / 24.0)
    sine, cosine, level = jnp.sin(angle), jnp.cos(angle), jnp.log(own)
    series[0:8, :] = jnp.zeros((8, TILE), f32)
    series[8 : 8 + TILES, :] = values.astype(bf16).astype(f32)
    extra[...] = jnp.zeros(extra.shape, f32)
    for r in range(TILES):
        at = slice(r * TILE, (r + 1) * TILE)
        extra[0:1, at] = sine[r : r + 1]
        extra[1:2, at] = cosine[r : r + 1]
        extra[2:3, at] = level[r : r + 1]
    toeplitz[:, 0:MAXLAG] = jnp.zeros((TILE, MAXLAG), bf16)

    def shift(m, carry):
        window = jnp.concatenate([series[pl.ds(m + 7, 1), :], series[pl.ds(m + 8, 1), :]], axis=1)
        rolled = pltpu.roll(jnp.broadcast_to(window, (TILE, 2 * TILE)), 1, 1, stride=1, stride_axis=0)
        toeplitz[:, pl.ds(pl.multiple_of((m + 3) * TILE, TILE), TILE)] = rolled[:, TILE:].astype(bf16)
        return carry

    lax.fori_loop(0, TILES, shift, 0, unroll=4)

    rows = iota((FEATS, 1), 0)
    diagonal = iota((FEATS, LAGS), 0) == iota((FEATS, LAGS), 1)
    offsets = jnp.sum(jnp.where(diagonal, lag_ref[...].astype(f32), 0.0), axis=1, keepdims=True)
    offsets = jnp.where(rows < LAGS, offsets - 1.0, (rows - LAGS + MAXLAG).astype(f32))
    chosen = (iota((FEATS, LAGCOLS), 1).astype(f32) == offsets).astype(bf16)
    w_dense = tn(w_lag_ref[...], chosen).astype(bf16)
    w_dense_ref[...] = w_dense

    gain_a, gain_b = gain_column(gains_ref, 0), gain_column(gains_ref, 1)
    w_qkv = w_qkv_ref[0]
    lag_rows = iota((TILE, 1), 0) + 1
    for k in range(BLOCKS):
        place = iota((1, BLOCK), 1) + k * BLOCK
        start = doc_start(place, len_ref)
        resid = nn(w_dense[:, MAXLAG:], extra[:, k * BLOCK : (k + 1) * BLOCK].astype(bf16))
        for b in range(3):
            at = MAXLAG + k * BLOCK - b * TILE
            lagged = toeplitz[:, at : at + BLOCK]
            if k in (0, BLOCKS - 1):
                valid = place - (lag_rows + b * TILE) >= start
                lagged = jnp.where(valid, lagged.astype(f32), 0.0).astype(bf16)
            resid = resid + nn(w_dense[:, b * TILE : (b + 1) * TILE], lagged)
        normal = (resid * norm_factor(resid) * gain_a).astype(bf16)
        qkv_block(normal, w_qkv, rope_ref, k, kaug_ref, vaug_ref, qall_ref)

    place = own_places(low, high)
    start = doc_start(place, len_ref)
    lane = iota((1, TILE), 1)

    def tile_of(ref, tile):
        return ref[:, pl.ds(pl.multiple_of(tile * TILE, TILE), TILE)].astype(f32)

    for b in range(3):
        lagged = jnp.where(lane < HALF, tile_of(toeplitz, low + 3 - b), tile_of(toeplitz, high + 3 - b))
        valid = place - (lag_rows + b * TILE) >= start
        lagged_ref[b * TILE : (b + 1) * TILE, :] = jnp.where(valid, lagged, 0.0).astype(bf16)
    lagged_ref[MAXLAG:, :] = jnp.where(lane < HALF, tile_of(extra, low), tile_of(extra, high)).astype(bf16)
    lagged = lagged_ref[...]
    feats_ref[0:FEATS, :] = nn(chosen, lagged)
    feats_ref[FEATS:, :] = jnp.zeros((96 - FEATS, TILE), f32)
    resid = nn(w_dense, lagged)
    resid_ref[...] = resid
    normal_a_ref[...] = (resid * norm_factor(resid) * gain_a).astype(bf16)
    own_rows(qall_ref, kaug_ref, vaug_ref, low, high, q_ref, k_ref, v_ref)
    attended, stat_ref[...] = attend(q_ref[...].astype(f32), kaug_ref, vaug_ref, len_ref, low, high, qbd, top_ref, acc_ref)
    att_ref[...] = attended
    mid, normal_b, gate_up, hidden, resid = feed_forward(resid, attended, w_out_ref[0], w_gate_up_ref[0], w_down_ref[0], gain_b)
    mid_ref[...], normal_b_ref[...], gate_up_ref[...], hidden_ref[...] = mid, normal_b, gate_up, hidden
    next_resid_ref[...] = resid
    next_ref[...] = (resid * norm_factor(resid) * gain_column(gains_ref, 2)).astype(bf16)


def own_rows(qall_ref, kaug_ref, vaug_ref, low, high, q_ref, k_ref, v_ref):
    unit = eye(TILE, TILE, bf16)
    for source, target, fill in ((qall_ref, q_ref, 0.0), (kaug_ref, k_ref, 1.0), (vaug_ref, v_ref, 1.0)):
        target[:, :D] = nt(unit, own_tile(source, low, high)).astype(bf16)
        target[:, D:] = jnp.full((TILE, STAT), fill, bf16)


def natural_tiles(own_refs, other_refs, put):
    chip, core, _, _ = geometry()
    mine = (iota((1, TILE), 1) < HALF) == (core == 0)
    for k in range(4):
        for j in range(4):
            source = ((chip // 4) ^ k) * 4 + ((chip % 4) ^ j)
            own, other = own_refs[k][j].astype(f32), other_refs[k][j].astype(f32)
            put(source, jnp.where(mine, own, other).astype(bf16))
            put(TILES - 1 - source, jnp.where(mine, other, own).astype(bf16))


def second_kernel(*refs):
    own_refs, other_refs = refs[0:4], refs[4:8]
    (len_ref, resid_in_ref, cot_ref, w_qkv_ref, w_out_ref, w_gate_up_ref, w_down_ref, gains_ref, rope_ref,
     act_ref, kaug_ref, vaug_ref, qall_ref, q_ref, k_ref, v_ref, grad_ref, payload_ref, rows_ref, tail_ref, pack_ref,
     normal_all, qbd, top_ref, acc_ref) = refs[8:]
    chip, core, low, high = geometry()

    def put(tile, value):
        normal_all[tile // 4, :, pl.ds(pl.multiple_of((tile % 4) * TILE, TILE), TILE)] = value

    natural_tiles(own_refs, other_refs, put)
    w_qkv = w_qkv_ref[1]
    for k in range(BLOCKS):
        qkv_block(normal_all[k], w_qkv, rope_ref, k, kaug_ref, vaug_ref, qall_ref)
    own_rows(qall_ref, kaug_ref, vaug_ref, low, high, q_ref, k_ref, v_ref)
    attended, stat = attend(q_ref[...].astype(f32), kaug_ref, vaug_ref, len_ref, low, high, qbd, top_ref, acc_ref)
    gain = gain_column(gains_ref, 3)
    w_out, w_gate_up, w_down = w_out_ref[1], w_gate_up_ref[1], w_down_ref[1]
    mid, normal_b, gate_up, hidden, out = feed_forward(resid_in_ref[...], attended, w_out, w_gate_up, w_down, gain)
    act_ref[...] = nt(eye(TILE, TILE, f32), out, HIGH)
    grad = nt(eye(D, D, f32), cot_ref[...], HIGH)
    grad, payload, tail, d_gain, _ = feed_back(
        grad, attended, mid, normal_b, gate_up, hidden, w_out, w_gate_up, w_down, gain, stat, pack_ref, 0
    )
    grad_ref[...] = grad
    payload_ref[...] = payload
    rows_ref[...] = nt(eye(TILE, TILE, bf16), payload).astype(bf16)
    tail_ref[...] = jnp.where(iota((1, TILE), 1) == 99, d_gain, tail)


def query_back_kernel(len_ref, q_ref, rows_ref, kaug_ref, vaug_ref, dq_ref, qbd, dbd, acc_ref):
    chip, core, low, high = geometry()
    rows = rows_ref[...].astype(f32)
    spread(qbd, jnp.concatenate([q_ref[:, :D].astype(f32), rows[:, D:]], axis=1), LROW, LROW + 9, LROW + 18)
    spread(dbd, rows, DROW, DROW + 9)
    acc_ref[...] = jnp.zeros(acc_ref.shape, f32)
    first = low // 4 + 1

    def step(s, carry):
        late = s >= first
        u = late.astype(jnp.int32)
        tile = jnp.where(late, high, low)
        block = s - jnp.where(late, first, 0)
        scores = biased(nn(qbd[u], kaug_ref[block]), query_bias(u, tile, block, len_ref))
        d_scores = jnp.exp(scores) * nn(dbd[u], vaug_ref[block])
        acc_ref[u] = acc_ref[u] + nt(d_scores.astype(bf16), kaug_ref[block])
        return carry

    lax.fori_loop(0, STEPS, step, 0)
    for u in range(2):
        dq_ref[u * HALF : (u + 1) * HALF, :] = own_heads(acc_ref[u]) * HEAD_DIM**-0.5


def key_back(own_refs, other_refs, len_ref, qall_ref, k_ref, v_ref, dq_ref, grad, resid, normal, w_qkv, gain, rope_ref,
             qaug, daug, kbd, vbd, dk_ref, dv_ref):
    chip, core, low, high = geometry()

    def put(tile, value):
        at = pl.ds(pl.multiple_of((tile % 4) * TILE, TILE), TILE)
        daug[tile // 4, :, at] = value
        qaug[tile // 4, D:AUG, at] = value[D:]

    natural_tiles(own_refs, other_refs, put)
    qaug[:, 0:D, :] = qall_ref[...]
    spread(kbd, k_ref[...].astype(f32), LROW, LROW + 9, LROW + 18)
    spread(vbd, v_ref[...].astype(f32), DROW, DROW + 9)
    dk_ref[...] = jnp.zeros(dk_ref.shape, f32)
    dv_ref[...] = jnp.zeros(dv_ref.shape, f32)
    first = BLOCKS - low // 4

    def step(s, carry):
        late = s >= first
        u = late.astype(jnp.int32)
        tile = jnp.where(late, high, low)
        block = tile // 4 + s - jnp.where(late, first, 0)
        probs = jnp.exp(biased(nn(kbd[u], qaug[block]), key_bias(u, tile, block, len_ref)))
        d_scores = probs * nn(vbd[u], daug[block])
        dv_ref[u] = dv_ref[u] + nt(probs.astype(bf16), daug[block])
        dk_ref[u] = dk_ref[u] + nt(d_scores.astype(bf16), qaug[block])
        return carry

    lax.fori_loop(0, STEPS, step, 0)
    unit = eye(D, D, f32)
    d_query = nt(unit, dq_ref[...], HIGH)
    d_key = nt(unit, jnp.concatenate([own_heads(dk_ref[0]), own_heads(dk_ref[1])], axis=0), HIGH)
    d_value = nt(unit, jnp.concatenate([own_heads(dv_ref[0]), own_heads(dv_ref[1])], axis=0), HIGH)
    lane = iota((1, TILE), 1)

    def rope_of(tile):
        return rope_ref[:, pl.ds(pl.multiple_of(tile * TILE, TILE), TILE)]

    rope = jnp.where(lane < HALF, rope_of(low), rope_of(high))
    cosine, sine = rope[0:8], -rope[8:16]
    d_mixed = jnp.concatenate([rotate(d_query, cosine, sine), rotate(d_key, cosine, sine), d_value], axis=0).astype(bf16)
    d_in, d_gain = norm_back(resid, gain, nn(w_qkv, d_mixed))
    head = nt(normal, d_mixed[:MAXLAG])
    tail = nt(normal, jnp.concatenate([d_mixed[MAXLAG:], jnp.zeros((TILE - 48, TILE), bf16)], axis=0))
    return grad + d_in, head, tail, d_gain


def third_kernel(*refs):
    own_refs, other_refs = refs[0:4], refs[4:8]
    (len_ref, qall_ref, k_ref, v_ref, dq_ref, grad_in_ref, resid_ref, normal_a_ref, tail_in_ref, w_qkv_ref, w_out_ref, w_gate_up_ref,
     w_down_ref, gains_ref, rope_ref, att_ref, stat_ref, mid_ref, normal_b_ref, gate_up_ref, hidden_ref,
     grad_ref, payload_ref, rows_ref, tail_ref, tail1_ref, pack_ref,
     qaug, daug, kbd, vbd, dk_ref, dv_ref) = refs[8:]
    grad, head, tail1, d_gain = key_back(
        own_refs, other_refs, len_ref, qall_ref, k_ref, v_ref, dq_ref, grad_in_ref[...], resid_ref[...], normal_a_ref[...],
        w_qkv_ref[1], gain_column(gains_ref, 2), rope_ref, qaug, daug, kbd, vbd, dk_ref, dv_ref,
    )
    at = put_tiles(pack_ref, 0, head)
    lane = iota((1, TILE), 1)
    tail1 = tail1 + tail_in_ref[...]
    tail1 = jnp.where(lane == 98, d_gain, tail1)
    grad, payload, tail, d_gain, _ = feed_back(
        grad, att_ref[...], mid_ref[...], normal_b_ref[...], gate_up_ref[...], hidden_ref[...], w_out_ref[0], w_gate_up_ref[0],
        w_down_ref[0], gain_column(gains_ref, 1), stat_ref[...], pack_ref, at,
    )
    grad_ref[...] = grad
    payload_ref[...] = payload
    rows_ref[...] = nt(eye(TILE, TILE, bf16), payload).astype(bf16)
    tail_ref[...] = tail
    tail1_ref[...] = jnp.where(lane == 97, d_gain, tail1)


def last_kernel(*refs):
    own_refs, other_refs = refs[0:4], refs[4:8]
    (len_ref, scale_ref, ids_ref, qall_ref, k_ref, v_ref, dq_ref, grad_in_ref, resid_ref, normal_a_ref, tail_in_ref, tail1_ref, pack2_ref,
     pack3_ref, w_qkv_ref, gains_ref, rope_ref, w_dense_ref, feats_ref,
     out_ref, qaug, daug, kbd, vbd, dk_ref, dv_ref, raw_ref) = refs[8:]
    chip, core, low, high = geometry()
    d_first, head, tail0, d_gain = key_back(
        own_refs, other_refs, len_ref, qall_ref, k_ref, v_ref, dq_ref, grad_in_ref[...], resid_ref[...], normal_a_ref[...],
        w_qkv_ref[0], gain_column(gains_ref, 0), rope_ref, qaug, daug, kbd, vbd, dk_ref, dv_ref,
    )
    d_first = d_first.astype(bf16)
    feats = feats_ref[...].astype(bf16)
    empty = jnp.zeros((64, TILE), bf16)
    tail0 = tail0 + tail_in_ref[...] + nt(d_first, jnp.concatenate([empty, feats[:64]], axis=0))
    tail1 = tail1_ref[...] + nt(d_first, jnp.concatenate([empty, feats[64:], empty[:32]], axis=0))
    lane, row = iota((1, TILE), 1), iota((D, 1), 0)
    tail1 = jnp.where(lane == 96, d_gain, tail1)
    sums, counts = jnp.zeros((D, 1), f32), jnp.zeros((D, 1), f32)
    owner = (lax.axis_index("tm") == 0).astype(f32)
    for d in range(DOCS):
        hit = jnp.where(row == ids_ref[d], owner, 0.0)
        sums, counts = sums + hit * scale_ref[d], counts + hit
    high_part = sums.astype(bf16).astype(f32)
    tail1 = jnp.where(lane == 100, high_part, tail1)
    tail1 = jnp.where(lane == 101, sums - high_part, tail1)
    tail1 = jnp.where(lane == 102, counts, tail1)

    place = own_places(low, high)
    start = doc_start(place, len_ref)
    own = doc_scale_at(place, len_ref, scale_ref)
    flip = (iota((TILE, TILE), 0) + iota((TILE, TILE), 1) == TILE - 1).astype(bf16)
    raw_ref[...] = jnp.zeros(raw_ref.shape, f32)
    lags = TILE - iota((TILE, 1), 0)
    for b in range(3):
        weights = nn(w_dense_ref[:, b * TILE : (b + 1) * TILE], flip).astype(bf16)
        d_lagged = tn(weights, d_first)
        valid = place - (lags + b * TILE) >= start
        d_lagged = jnp.where(valid, d_lagged, 0.0) / own
        for u in range(2):
            half = jnp.where((lane < HALF) == (u == 0), d_lagged, 0.0)
            wide = jnp.concatenate([jnp.zeros((TILE, TILE), f32), half], axis=1)
            rolled = pltpu.roll(wide, TILE, 1, stride=1, stride_axis=0)
            total = jnp.sum(rolled, axis=0, keepdims=True)
            tile = (low if u == 0 else high) - b + 8
            raw_ref[pl.ds(tile, 1), :] = raw_ref[pl.ds(tile, 1), :] + total[:, TILE:]
            raw_ref[pl.ds(tile - 1, 1), :] = raw_ref[pl.ds(tile - 1, 1), :] + total[:, :TILE]

    out_ref[:, 2] = jnp.zeros((128, 16, TILE), bf16)
    group = lax.axis_index("series") * TILES
    for r in range(TILES):
        line = jnp.broadcast_to(raw_ref[8 + r : 9 + r, :], (16, TILE))
        out_ref[group + r, 2] = jnp.where(iota((16, 1), 0) == 0, line, 0.0).astype(bf16)
    for t in range(90):
        out_ref[t // 2, t % 2] = pack2_ref[t]
    for t in range(117):
        out_ref[(t + 90) // 2, t % 2] = pack3_ref[t]
    at = 207
    for part in (head, tail0, tail1):
        for c in range(part.shape[1] // TILE):
            for r in range(9):
                out_ref[at // 2, at % 2] = part[16 * r : 16 * (r + 1), c * TILE : (c + 1) * TILE].astype(bf16)
                at += 1
    for t in range(at, 256):
        out_ref[t // 2, t % 2] = jnp.zeros((16, TILE), bf16)


def sum_kernel(in_ref, out_ref, raw_ref):
    total = jnp.zeros((3, 16, TILE), f32)
    total = lax.fori_loop(0, 16, lambda i, t: t + jnp.sum(in_ref[pl.ds(i * 8, 8)].astype(f32), axis=0), total)
    out_ref[...] = total[:2].astype(bf16)
    raw_ref[...] = total[2, 0:1]


def unpack_kernel(in_ref, lag_ref, qkv_ref, out_ref, gate_up_ref, down_ref, gains_ref, scale_ref):
    def tile(t):
        return in_ref[t // 2, t % 2]

    def columns(first, count):
        return [jnp.concatenate([tile(first + 9 * c + r) for r in range(9)], axis=0) for c in range(count)]

    layers = ((207, 234, 117), (90, 243, 0))
    unit = eye(TILE, TILE, bf16)
    tails = []
    for layer, (at_qkv, at_tail, at_rest) in enumerate(layers):
        for c, part in enumerate(columns(at_qkv, 3)):
            qkv_ref[layer, :, c * TILE : (c + 1) * TILE] = part.astype(f32)
        tail = columns(at_tail, 1)[0]
        tails.append(tail)
        qkv_ref[layer, :, MAXLAG:] = tail[:, :48].astype(f32)
        for c, part in enumerate(columns(at_rest, 3)):
            down_ref[layer, c * TILE : (c + 1) * TILE, :] = nt(unit, part)
        for c, part in enumerate(columns(at_rest + 27, 6)):
            gate_up_ref[layer, :, c * TILE : (c + 1) * TILE] = part.astype(f32)
        out_ref[layer, :, :TILE] = columns(at_rest + 81, 1)[0].astype(f32)
        out_ref[layer, :, TILE:] = tail[:, 48:64].astype(f32)
    row, lane = iota((96, TILE), 0), iota((96, TILE), 1)
    pick0 = ((lane == row + 64) & (row < 64)).astype(bf16)
    pick1 = ((lane == row) & (row >= 64) & (row < FEATS)).astype(bf16)
    lag = nt(pick0, tails[0]) + nt(pick1, tails[1])
    lag_ref[...] = lag[:FEATS]
    rest = nt((iota((8, TILE), 1) == iota((8, TILE), 0) + 96).astype(bf16), tails[1])
    gains_ref[...] = rest[:4]
    scale_ref[...] = (rest[4:5] + rest[5:6]) / rest[6:7]


def shape(*dims, dtype=f32):
    return jax.ShapeDtypeStruct(dims, dtype)


def call(kernel, smem, operands, outs, scratch):
    count = len(operands)
    specs = [pl.BlockSpec(memory_space=pltpu.SMEM if n in smem else pltpu.VMEM) for n in range(count)]
    return pl.pallas_call(
        kernel,
        out_shape=outs,
        in_specs=specs,
        out_specs=jax.tree.map(lambda _: pl.BlockSpec(memory_space=pltpu.VMEM), outs),
        scratch_shapes=scratch,
        compiler_params=pltpu.CompilerParams(vmem_limit_bytes=VMEM),
    )(*operands)


def pair_permute(x, bit):
    return lax.ppermute(x, "tm", [(i, i ^ bit) for i in range(32)])


def gather(block):
    near = jnp.stack([block] + [pair_permute(block, 2 * k) for k in range(1, 4)])
    own = [near] + [pair_permute(near, 8 * k) for k in range(1, 4)]
    return own + [pair_permute(piece, 1) for piece in own]


def to_halves(n, which):
    if n < 16:
        return 2 * n + which
    return 63 - 2 * n - which


def rope_table():
    freqs = 10000.0 ** (-np.arange(8, dtype=np.float64) / 8)
    angle = np.arange(LEN, dtype=np.float64)[None, :] * freqs[:, None]
    return np.concatenate([np.cos(angle), np.sin(angle)], axis=0).astype(np.float32)


def body(
    raw_values, hours, doc_lengths, doc_scale, dataset_ids, lag_offsets, w_lag, w_qkv, w_out, w_gate_up, w_down, gains, cotangent
):
    lengths, scales, ids = doc_lengths.reshape(DOCS), doc_scale.reshape(DOCS), dataset_ids.reshape(DOCS)
    gains4 = gains.reshape(2 * LAYERS, D)
    rope = jnp.asarray(rope_table())
    both = jnp.concatenate([raw_values, hours.astype(f32)], axis=0)
    values = lax.all_to_all(jnp.broadcast_to(both[None], (32, 2, TILE)), "tm", 0, 0)
    cot = [
        lax.ppermute(cotangent[0, w * HALF : (w + 1) * HALF], "tm", [(n, to_halves(n, w)) for n in range(32)]) for w in range(2)
    ]
    cot = jnp.concatenate(cot, axis=0)
    wide = [shape(BLOCKS, AUG, BLOCK, dtype=bf16), shape(BLOCKS, AUG, BLOCK, dtype=bf16), shape(BLOCKS, D, BLOCK, dtype=bf16)]
    rows = [shape(TILE, AUG, dtype=bf16)] * 3
    narrow, narrow_low = shape(D, TILE), shape(D, TILE, dtype=bf16)
    payload_shape = shape(AUG, TILE, dtype=bf16)
    bd = pltpu.VMEM((2, ROWS, AUG), bf16)
    acc = pltpu.VMEM((2, ROWS, AUG), f32)
    top = pltpu.VMEM((2, ROWS, 1), f32)
    aug = pltpu.VMEM((BLOCKS, AUG, BLOCK), bf16)

    (next1, resid1, kaug0, vaug0, qall0, lagged, feats, w_dense, resid0, normal_a0, q0, k0, v0, att0, stat0, mid0, normal_b0,
     gate_up0, hidden0) = call(
        first_kernel, (0, 1),
        (lengths, scales, values, lag_offsets.reshape(1, LAGS), w_lag, w_qkv, w_out, w_gate_up, w_down, gains4, rope),
        [narrow_low, narrow] + wide
        + [shape(LAGCOLS, TILE, dtype=bf16), shape(96, TILE), shape(D, LAGCOLS, dtype=bf16), narrow, narrow_low]
        + rows
        + [narrow_low, shape(STAT, TILE, dtype=bf16), narrow, narrow_low, shape(2 * FF, TILE), shape(FF, TILE, dtype=bf16)],
        [pltpu.VMEM((8 + TILES, TILE), f32), pltpu.VMEM((TILE, MAXLAG + LEN), bf16), pltpu.VMEM((16, LEN), f32), bd, top, acc],
    )

    act, kaug1, vaug1, qall1, q1, k1, v1, grad, payload, payload_rows, tail1, pack2 = call(
        second_kernel, (8,),
        (*gather(next1), lengths, resid1, cot, w_qkv, w_out, w_gate_up, w_down, gains4, rope),
        [shape(TILE, D)] + wide + rows
        + [narrow, payload_shape, shape(TILE, AUG, dtype=bf16), narrow, shape(90, 16, TILE, dtype=bf16)],
        [pltpu.VMEM((BLOCKS, D, BLOCK), bf16), bd, top, acc],
    )
    act = [
        lax.ppermute(act[w * HALF : (w + 1) * HALF], "tm", [(to_halves(n, w), n) for n in range(32)]) for w in range(2)
    ]

    def query_back(q, payload_rows, kaug, vaug):
        return call(query_back_kernel, (0,), (lengths, q, payload_rows, kaug, vaug), shape(TILE, D), [bd, bd, acc])

    pieces = gather(payload)
    dq = query_back(q1, payload_rows, kaug1, vaug1)
    grad, payload, payload_rows, tail0, tail1, pack3 = call(
        third_kernel, (8,),
        (*pieces, lengths, qall1, k1, v1, dq, grad, resid1, next1, tail1, w_qkv, w_out, w_gate_up, w_down, gains4, rope,
         att0, stat0, mid0, normal_b0, gate_up0, hidden0),
        [narrow, payload_shape, shape(TILE, AUG, dtype=bf16), narrow, narrow, shape(117, 16, TILE, dtype=bf16)],
        [aug, aug, bd, bd, acc, acc],
    )
    pieces = gather(payload)
    dq = query_back(q0, payload_rows, kaug0, vaug0)
    packed = call(
        last_kernel, (8, 9, 10),
        (*pieces, lengths, scales, ids, qall0, k0, v0, dq, grad, resid0, normal_a0, tail0, tail1, pack2, pack3, w_qkv, gains4, rope,
         w_dense, feats),
        shape(128, 3, 16, TILE, dtype=bf16),
        [aug, aug, bd, bd, acc, acc, pltpu.VMEM((8 + TILES, TILE), f32)],
    )
    parts = lax.all_to_all(packed, ("series", "tm"), 0, 0)
    share, raw_grad = call(sum_kernel, (), (parts,), [shape(2, 16, TILE, dtype=bf16), shape(1, TILE)], [])
    shares = lax.all_to_all(jnp.broadcast_to(share[None], (128, 2, 16, TILE)), ("series", "tm"), 0, 0)
    g_lag, g_qkv, g_out, g_gate_up, g_down, g_gains, scale = call(
        unpack_kernel, (), (shares,),
        [shape(FEATS, D), shape(LAYERS, D, 3 * D), shape(LAYERS, D, D), shape(LAYERS, D, 2 * FF), shape(LAYERS, FF, D),
         shape(2 * LAYERS, D), shape(1, D)],
        [],
    )
    act = jnp.concatenate(act, axis=0)
    return (
        act[None], raw_grad, scale[0, :DATASETS], g_lag, g_qkv, g_out, g_gate_up, g_down, g_gains.reshape(LAYERS, 2, D),
    )


def solution(mesh):
    placed = (
        P("series", "tm"),
        P("series", "tm"),
        P("series", None),
        P("series", None),
        P("series", None, None),
        P(),
        P(),
        P(),
        P(),
        P(),
        P(),
        P(),
        P("series", "tm", None),
    )
    return jax.shard_map(
        body,
        mesh=mesh,
        in_specs=placed,
        out_specs=(P("series", "tm", None), P("series", "tm"), P(), P(), P(), P(), P(), P(), P()),
        check_vma=False,
    )
```

```python
import math

import jax
import jax.numpy as jnp
import numpy as np
from jax import lax
from jax.experimental import pallas as pl
from jax.experimental.pallas import tpu as pltpu
from jax.sharding import PartitionSpec as P


D = 144
HEADS = 9
HEAD_DIM = 16
FF = 384
LAGS = 84
LAYERS = 2
DATASETS = 8
DOCS = 7
LEN = 4096
MAXLAG = 384
FEATS = 87
EPSILON = 1e-06
MASKED = -1e30
AUG = 192
STAT = AUG - D
LROW = D
DROW = D + 27
BLOCK = 512
BLOCKS = LEN // BLOCK
TILE = 128
TILES = LEN // TILE
STEPS = BLOCKS + 1
HALF = 64
ROWS = HEADS * HALF
LAGCOLS = 400
EARLY = 103
LATE = 24
WIDE = AUG + HALF
SAFE = 40.0
VMEM = 28 * 2**20

bf16 = jnp.bfloat16
f32 = jnp.float32
HIGH = lax.Precision.HIGHEST


def nn(a, b, precision=None):
    return lax.dot_general(a, b, (((1,), (0,)), ((), ())), precision=precision, preferred_element_type=f32)


def nt(a, b, precision=None):
    return lax.dot_general(a, b, (((1,), (1,)), ((), ())), precision=precision, preferred_element_type=f32)


def tn(a, b, precision=None):
    return lax.dot_general(a, b, (((0,), (0,)), ((), ())), precision=precision, preferred_element_type=f32)


def iota(shape, dim):
    return lax.broadcasted_iota(jnp.int32, shape, dim)


def eye(rows, cols, dtype):
    return (iota((rows, cols), 0) == iota((rows, cols), 1)).astype(dtype)


def column(row, size):
    keep = iota((size, size), 0) == iota((size, size), 1)
    return jnp.sum(jnp.where(keep, row, 0.0), axis=1, keepdims=True)


def pair_of(chip):
    return jnp.where(chip < 8, 2 * chip, TILES - 1 - 2 * chip)


def geometry():
    index = lax.axis_index("tm")
    chip, core = index // 2, index % 2
    tile = pair_of(chip)
    low = jnp.where(core == 0, tile, TILES - 1 - tile)
    return chip, core, low, TILES - 1 - low


def doc_start(places, len_ref):
    start = jnp.zeros_like(places)
    end = jnp.int32(0)
    for d in range(DOCS):
        end = end + len_ref[d]
        start = jnp.where(places >= end, end, start)
    return start


def doc_scale_at(places, len_ref, scale_ref):
    own = jnp.full(places.shape, scale_ref[0], f32)
    end = jnp.int32(0)
    for d in range(1, DOCS):
        end = end + len_ref[d - 1]
        own = jnp.where(places >= end, scale_ref[d], own)
    return own


def own_places(low, high):
    lane = iota((1, TILE), 1)
    return jnp.where(lane < HALF, low, high) * TILE + lane


def half_places(u, tile):
    return iota((HALF, 1), 0) + (tile * TILE + u * HALF)


def rotate(x, cosine, sine):
    cols = x.shape[1]
    parts = x.reshape(HEADS, 2, 8, cols)
    one, two = parts[:, 0], parts[:, 1]
    turned = jnp.stack([one * cosine - two * sine, two * cosine + one * sine], axis=1)
    return turned.reshape(D, cols)


def norm_factor(x):
    return lax.rsqrt(jnp.mean(x * x, axis=0, keepdims=True) + EPSILON)


def norm_back(x, gain, d_normal):
    r = norm_factor(x)
    scaled = d_normal * gain
    inner = jnp.mean(x * scaled, axis=0, keepdims=True)
    d_x = r * scaled - (r * r * r * inner) * x
    return d_x, jnp.sum(d_normal * x * r, axis=1, keepdims=True)


def head_columns(h, *firsts):
    col = iota((1, AUG), 1)
    keep = (col >= h * HEAD_DIM) & (col < (h + 1) * HEAD_DIM)
    for first in firsts:
        keep = keep | (col == first + h)
    return keep


def spread(ref, rows, *firsts):
    zero = jnp.zeros((HALF, AUG), f32)
    for h in range(HEADS):
        keep = head_columns(h, *firsts)
        for u in range(2):
            part = rows[u * HALF : (u + 1) * HALF]
            ref[u, h * HALF : (h + 1) * HALF, 0:AUG] = jnp.where(keep, part, zero).astype(bf16)
    if ref.shape[2] == WIDE:
        unit = eye(HALF, HALF, bf16)
        for h in range(HEADS):
            for u in range(2):
                ref[u, h * HALF : (h + 1) * HALF, AUG:WIDE] = unit


def own_heads(x):
    col = iota((1, D), 1) // HEAD_DIM
    total = jnp.zeros((HALF, D), f32)
    for h in range(HEADS):
        total = jnp.where(col == h, x[h * HALF : (h + 1) * HALF, :D], total)
    return total


def three_parts(x):
    hi = x.astype(bf16)
    rest = x - hi.astype(f32)
    mid = rest.astype(bf16)
    return hi, mid, (rest - mid.astype(f32)).astype(bf16)


class Tiles:
    def __init__(self, ref):
        self.ref, self.count = ref, 0

    def tile(self, value):
        self.ref[self.count] = value.astype(bf16)
        self.count += 1

    def __call__(self, grads):
        for c in range(grads.shape[1] // TILE):
            for r in range(grads.shape[0] // 16):
                self.tile(grads[16 * r : 16 * (r + 1), c * TILE : (c + 1) * TILE].astype(f32))


class Pairs(Tiles):
    def __init__(self, core, keep_ref, send_ref, rest_ref=None):
        self.core, self.refs, self.rest, self.count, self.even = core, (keep_ref, send_ref), rest_ref, 0, None

    def tile(self, value):
        if self.count == self.refs[0].shape[0]:
            self.rest[0] = value.astype(bf16)
        elif self.even is None:
            self.even = value
        else:
            self.refs[0][self.count] = jnp.where(self.core == 0, self.even, value).astype(bf16)
            self.refs[1][self.count] = jnp.where(self.core == 0, value, self.even).astype(bf16)
            self.even = None
            self.count += 1


def turned(w):
    return tn(w, eye(D, D, bf16)).astype(bf16)


def key_value_block(normal, w_qkv, rope_ref, k, kaug_ref, vaug_ref):
    mixed = nn(w_qkv[D:], normal)
    at = slice(k * BLOCK, (k + 1) * BLOCK)
    keys = rotate(mixed[:D], rope_ref[0:8, at], rope_ref[8:16, at])
    ones = jnp.ones((STAT, BLOCK), bf16)
    kaug_ref[k, 0:D, :] = keys.astype(bf16)
    vaug_ref[k, 0:D, :] = mixed[D:].astype(bf16)
    kaug_ref[k, D:AUG, :] = ones
    vaug_ref[k, D:AUG, :] = ones
    return head_sizes(keys)


def query_of(normal, w_qkv, cosine, sine):
    turned = rotate(nn(w_qkv[:D], normal), cosine, sine)
    return (turned.astype(bf16).astype(f32) * HEAD_DIM**-0.5).astype(bf16)


def own_rope(rope_ref, low, high):
    def at(tile):
        return rope_ref[:, pl.ds(pl.multiple_of(tile * TILE, TILE), TILE)]

    both = jnp.where(iota((1, TILE), 1) < HALF, at(low), at(high))
    return both[0:8], both[8:16]


def own_tile(ref, low, high):
    lane = iota((1, TILE), 1)

    def at(tile):
        return ref[tile // 4, 0:D, pl.ds(pl.multiple_of((tile % 4) * TILE, TILE), TILE)].astype(f32)

    return jnp.where(lane < HALF, at(low), at(high)).astype(bf16)


def query_bias(u, tile, block, len_ref):
    places = half_places(u, tile)
    start = doc_start(places, len_ref)
    keys = iota((1, BLOCK), 1) + block * BLOCK
    return jnp.where((keys <= places) & (keys >= start), 0.0, MASKED).astype(bf16)


def key_bias(u, tile, block, len_ref):
    keys = half_places(u, tile)
    places = iota((1, BLOCK), 1) + block * BLOCK
    start = doc_start(places, len_ref)
    return jnp.where((keys <= places) & (keys >= start), 0.0, MASKED).astype(bf16)


def scores_of(rows, columns, bias):
    return nn(rows, jnp.concatenate([columns, bias], axis=0))


def query_step(s, low, high):
    first = low // 4 + 1
    late = s >= first
    return late.astype(jnp.int32), jnp.where(late, high, low), s - jnp.where(late, first, 0)


def key_step(s, low, high):
    first = BLOCKS - low // 4
    late = s >= first
    tile = jnp.where(late, high, low)
    return late.astype(jnp.int32), tile, tile // 4 + s - jnp.where(late, first, 0)


def head_sizes(x):
    return jnp.max(jnp.sum((x * x).reshape(HEADS, HEAD_DIM, x.shape[1]), axis=1), axis=1, keepdims=True)


def attend(query, k_size, kaug_ref, vaug_ref, len_ref, low, high, qbd, top_ref, acc_ref, q_rows_ref):
    q_rows = nt(eye(TILE, TILE, bf16), query)
    q_rows_ref[...] = q_rows.astype(bf16)
    spread(qbd, jnp.concatenate([q_rows, jnp.zeros((TILE, STAT), f32)], axis=1))
    q_size = head_sizes(query.astype(f32))
    acc_ref[...] = jnp.zeros(acc_ref.shape, f32)
    safe = jnp.max(q_size * k_size) <= SAFE * SAFE

    @pl.when(safe)
    def _():
        top_ref[...] = jnp.zeros(top_ref.shape, f32)
        for s in range(STEPS):
            u, tile, block = query_step(s, low, high)
            scores = scores_of(qbd[u], kaug_ref[block], query_bias(u, tile, block, len_ref))
            acc_ref[u] = acc_ref[u] + nt(jnp.exp(scores).astype(bf16), vaug_ref[block])

    @pl.when(jnp.logical_not(safe))
    def _():
        top_ref[...] = jnp.full(top_ref.shape, MASKED, f32)

        def step(s, carry):
            u, tile, block = query_step(s, low, high)
            scores = scores_of(qbd[u], kaug_ref[block], query_bias(u, tile, block, len_ref))
            old = top_ref[u]
            new = jnp.maximum(old, jnp.max(scores, axis=1, keepdims=True))
            probs = jnp.exp(scores - new)
            acc_ref[u] = acc_ref[u] * jnp.exp(old - new) + nt(probs.astype(bf16), vaug_ref[block])
            top_ref[u] = new
            return carry

        lax.fori_loop(0, STEPS, step, 0)

    attended, stats = [], []
    lane = iota((1, STAT), 1)
    for u in range(2):
        acc = acc_ref[u]
        total = acc[:, D : D + 1]
        attended.append(own_heads(acc[:, :D] / total))
        parts = three_parts(-(top_ref[u] + jnp.log(total)))
        stat = jnp.zeros((HALF, STAT), f32)
        for j in range(3):
            part = parts[j].astype(f32)
            for h in range(HEADS):
                stat = jnp.where(lane == 9 * j + h, part[h * HALF : (h + 1) * HALF], stat)
        stats.append(stat)
    att_rows = jnp.concatenate(attended, axis=0).astype(bf16)
    stat_rows = jnp.concatenate(stats, axis=0).astype(bf16)
    return nt(eye(D, D, bf16), att_rows).astype(bf16), nt(eye(STAT, STAT, bf16), stat_rows).astype(bf16)


def feed_forward(resid, attended, w_out, w_gate_up, w_down, gain):
    mid = resid + nn(w_out, attended)
    normal = (mid * norm_factor(mid) * gain).astype(bf16)
    gate_up = nn(w_gate_up, normal)
    gate = gate_up[:FF]
    hidden = (gate * jax.nn.sigmoid(gate) * gate_up[FF:]).astype(bf16)
    return mid, normal, gate_up, hidden, mid + nn(w_down, hidden)


def feed_back(grad, attended, mid, gate_up, w_out, w_gate_up, w_down, gain, stat, low_refs, traffic):
    d_out_ref, d_gate_up_ref, d_branch_ref, hidden_ref, normal_ref = low_refs
    d_out = grad.astype(bf16)
    d_hidden = tn(w_down, d_out)
    gate, up = gate_up[:FF], gate_up[FF:]
    sig = jax.nn.sigmoid(gate)
    d_gate = d_hidden * up * (sig * (1.0 + gate * (1.0 - sig)))
    d_up = d_hidden * (gate * sig)
    hidden_ref[...] = (gate * sig * up).astype(bf16)
    normal_ref[...] = (mid * norm_factor(mid) * gain).astype(bf16)
    d_gate_up = jnp.concatenate([d_gate, d_up], axis=0).astype(bf16)
    d_mid, d_gain = norm_back(mid, gain, nn(w_gate_up, d_gate_up))
    grad = grad + d_mid
    d_branch = grad.astype(bf16)
    d_att = nn(w_out, d_branch).astype(bf16)
    d_out_ref[...], d_gate_up_ref[...], d_branch_ref[...] = d_out, d_gate_up, d_branch
    traffic.send(*low_refs)
    product = d_att.astype(f32) * attended.astype(f32)
    delta = -jnp.sum(product.reshape(HEADS, HEAD_DIM, TILE), axis=1)
    delta = jnp.concatenate([delta, jnp.zeros((16 - HEADS, TILE), f32)], axis=0)
    hi, lo, _ = three_parts(delta)
    row, col = iota((STAT, 16), 0), iota((STAT, 16), 1)
    place = [((row == 27 + 9 * j + col) & (col < HEADS)).astype(bf16) for j in range(2)]
    stat = stat.astype(f32) + nn(place[0], hi) + nn(place[1], lo)
    return grad, jnp.concatenate([d_att, stat.astype(bf16)], axis=0), d_gain


def feed_grads(put, hidden, d_out, normal, d_gate_up, attended, d_branch):
    put(nt(d_out, hidden))
    put(nt(normal, d_gate_up))
    put(nt(attended, d_branch[:TILE]))
    rows = [jnp.zeros((48, TILE), bf16), d_branch[TILE:], jnp.zeros((TILE - 64, TILE), bf16)]
    return nt(attended, jnp.concatenate(rows, axis=0))


def gain_column(gains_ref, which):
    return column(gains_ref[which // 2, which % 2 : which % 2 + 1, :], D)


def first_kernel(
    traffic, values_ref, len_ref, scale_ref, lag_ref, w_lag_ref, w_qkv_ref, w_out_ref, w_gate_up_ref, w_down_ref, gains_ref, rope_ref,
    copies_ref, next_ref, next_resid_ref, kaug_ref, vaug_ref, normal_all, lagged_ref, feats_ref, w_dense_ref, resid_ref, normal_a_ref,
    q_ref, att_ref, stat_ref, mid_ref, gate_up_ref,
    series, toeplitz, extra, qbd, top_ref, acc_ref,
):
    chip, core, low, high = geometry()
    traffic.ready(2)
    places = iota((TILES, TILE), 0) * TILE + iota((TILES, TILE), 1)
    own = doc_scale_at(places, len_ref, scale_ref)
    values = values_ref[:, 0, :] / own
    angle = values_ref[:, 1, :] * (2.0 * math.pi / 24.0)
    sine, cosine, level = jnp.sin(angle), jnp.cos(angle), jnp.log(own)
    series[0:8, :] = jnp.zeros((8, TILE), f32)
    series[8 : 8 + TILES, :] = values.astype(bf16).astype(f32)
    extra[...] = jnp.zeros(extra.shape, f32)
    for r in range(TILES):
        at = slice(r * TILE, (r + 1) * TILE)
        extra[0:1, at] = sine[r : r + 1]
        extra[1:2, at] = cosine[r : r + 1]
        extra[2:3, at] = level[r : r + 1]
    toeplitz[:, 0:MAXLAG] = jnp.zeros((TILE, MAXLAG), bf16)

    def shift(m, carry):
        window = jnp.concatenate([series[pl.ds(m + 7, 1), :], series[pl.ds(m + 8, 1), :]], axis=1)
        rolled = pltpu.roll(jnp.broadcast_to(window, (TILE, 2 * TILE)), 1, 1, stride=1, stride_axis=0)
        toeplitz[:, pl.ds(pl.multiple_of((m + 3) * TILE, TILE), TILE)] = rolled[:, TILE:].astype(bf16)
        return carry

    lax.fori_loop(0, TILES, shift, 0, unroll=4)

    traffic.ready()

    rows = iota((FEATS, 1), 0)
    diagonal = iota((FEATS, LAGS), 0) == iota((FEATS, LAGS), 1)
    offsets = jnp.sum(jnp.where(diagonal, lag_ref[...].astype(f32), 0.0), axis=1, keepdims=True)
    offsets = jnp.where(rows < LAGS, offsets - 1.0, (rows - LAGS + MAXLAG).astype(f32))
    chosen = (iota((FEATS, LAGCOLS), 1).astype(f32) == offsets).astype(bf16)
    w_dense = nn(w_lag_ref[...], chosen).astype(bf16)
    w_dense_ref[...] = w_dense

    gain_a, gain_b = gain_column(gains_ref, 0), gain_column(gains_ref, 1)
    w_qkv = turned(w_qkv_ref[0])
    lag_rows = iota((TILE, 1), 0) + 1
    k_size = jnp.zeros((HEADS, 1), f32)
    for k in range(BLOCKS):
        place = iota((1, BLOCK), 1) + k * BLOCK
        start = doc_start(place, len_ref)
        parts = []
        for b in range(3):
            at = MAXLAG + k * BLOCK - b * TILE
            lagged = toeplitz[:, at : at + BLOCK]
            if k in (0, BLOCKS - 1):
                valid = place - (lag_rows + b * TILE) >= start
                lagged = jnp.where(valid, lagged.astype(f32), 0.0).astype(bf16)
            parts.append(lagged)
        parts.append(extra[:, k * BLOCK : (k + 1) * BLOCK].astype(bf16))
        resid = nn(w_dense, jnp.concatenate(parts, axis=0))
        normal = (resid * norm_factor(resid) * gain_a).astype(bf16)
        normal_all[k] = normal
        k_size = jnp.maximum(k_size, key_value_block(normal, w_qkv, rope_ref, k, kaug_ref, vaug_ref))

    traffic.send(kaug_ref, vaug_ref, normal_all, w_dense_ref)

    place = own_places(low, high)
    start = doc_start(place, len_ref)
    lane = iota((1, TILE), 1)

    def tile_of(ref, tile):
        return ref[:, pl.ds(pl.multiple_of(tile * TILE, TILE), TILE)].astype(f32)

    for b in range(3):
        lagged = jnp.where(lane < HALF, tile_of(toeplitz, low + 3 - b), tile_of(toeplitz, high + 3 - b))
        valid = place - (lag_rows + b * TILE) >= start
        lagged_ref[b * TILE : (b + 1) * TILE, :] = jnp.where(valid, lagged, 0.0).astype(bf16)
    lagged_ref[MAXLAG:, :] = jnp.where(lane < HALF, tile_of(extra, low), tile_of(extra, high)).astype(bf16)
    lagged = lagged_ref[...]
    feats_ref[0:FEATS, :] = nn(chosen, lagged)
    feats_ref[FEATS:, :] = jnp.zeros((96 - FEATS, TILE), f32)
    resid = nn(w_dense, lagged)
    resid_ref[...] = resid
    normal = (resid * norm_factor(resid) * gain_a).astype(bf16)
    normal_a_ref[...] = normal
    traffic.send(lagged_ref, feats_ref, resid_ref, normal_a_ref)
    query = query_of(normal, w_qkv, *own_rope(rope_ref, low, high))
    attended, stat_ref[...] = attend(query, k_size, kaug_ref, vaug_ref, len_ref, low, high, qbd, top_ref, acc_ref, q_ref)
    att_ref[...] = attended
    traffic.send(q_ref, att_ref, stat_ref)
    mid, _, gate_up, _, resid = feed_forward(
        resid, attended, turned(w_out_ref[0]), turned(w_gate_up_ref[0]), w_down_ref[0], gain_b
    )
    mid_ref[...], gate_up_ref[...] = mid, gate_up
    traffic.send(mid_ref, gate_up_ref)
    next_resid_ref[...] = resid
    normal = (resid * norm_factor(resid) * gain_column(gains_ref, 2)).astype(bf16)
    next_ref[...] = normal
    copies_ref[...] = jnp.broadcast_to(normal[None], copies_ref.shape)


def natural_tiles(own_ref, other_ref, put):
    _, core, _, _ = geometry()
    mine = (iota((1, TILE), 1) < HALF) == (core == 0)
    for chip in range(TILES // 2):
        tile = 2 * chip if chip < 8 else TILES - 1 - 2 * chip
        own, other = own_ref[chip].astype(f32), other_ref[chip].astype(f32)
        for t, value in ((tile, jnp.where(mine, own, other)), (TILES - 1 - tile, jnp.where(mine, other, own))):
            put(t // 4, slice(t % 4 * TILE, (t % 4 + 1) * TILE), value.astype(bf16))


def second_kernel(
    traffic, own_ref, other_ref, len_ref, cot_own_ref, cot_other_ref, normal_ref, resid_in_ref, turned_qkv_ref, turned_out_ref,
    turned_gate_up_ref, w_out_ref, w_gate_up_ref, w_down_ref, gains_ref, rope_ref,
    copies_ref, act_ref, kaug_ref, vaug_ref, normal_all, q_ref, grad_ref, payload_ref, att_ref, d_gain_ref,
    d_out_ref, d_gate_up_ref, d_branch_ref, hidden_ref, normal_b_ref,
    qbd, top_ref, acc_ref,
):
    chip, core, low, high = geometry()

    def put(block, columns, value):
        normal_all[block, :, columns] = value

    natural_tiles(own_ref, other_ref, put)
    traffic.send(normal_all)
    traffic.ready()
    w_qkv = turned_qkv_ref[1]
    k_size = jnp.zeros((HEADS, 1), f32)
    for k in range(BLOCKS):
        k_size = jnp.maximum(k_size, key_value_block(normal_all[k], w_qkv, rope_ref, k, kaug_ref, vaug_ref))
    traffic.send(kaug_ref, vaug_ref)
    query = query_of(normal_ref[...], w_qkv, *own_rope(rope_ref, low, high))
    attended, stat = attend(query, k_size, kaug_ref, vaug_ref, len_ref, low, high, qbd, top_ref, acc_ref, q_ref)
    gain = gain_column(gains_ref, 3)
    w_out, w_gate_up, w_down = w_out_ref[1], w_gate_up_ref[1], w_down_ref[1]
    mid, _, gate_up, _, out = feed_forward(
        resid_in_ref[...], attended, turned_out_ref[1], turned_gate_up_ref[1], w_down, gain
    )
    act_ref[...] = out
    att_ref[...] = attended
    traffic.send(act_ref, att_ref, q_ref)
    grad = tile_halves(cot_own_ref[...].astype(f32), cot_other_ref[...].astype(f32))
    low_refs = (d_out_ref, d_gate_up_ref, d_branch_ref, hidden_ref, normal_b_ref)
    grad, payload, d_gain_ref[...] = feed_back(grad, attended, mid, gate_up, w_out, w_gate_up, w_down, gain, stat, low_refs, traffic)
    grad_ref[...] = grad
    payload_ref[...] = payload
    copies_ref[...] = jnp.broadcast_to(payload[None], copies_ref.shape)


def query_back(
    traffic, count, layer, payload_ref, q_ref, len_ref, rope_ref, kaug_ref, vaug_ref, normal_all, w_qkv_ref, dq_ref, qall_ref, kbd, vbd,
    qbd, dbd, acc_ref,
):
    chip, core, low, high = geometry()
    traffic.ready(count)
    unit = eye(TILE, TILE, bf16)
    rows = nt(unit, payload_ref[...])
    spread(qbd, jnp.concatenate([q_ref[...].astype(f32), rows[:, D:]], axis=1), LROW, LROW + 9, LROW + 18)
    spread(dbd, rows, DROW, DROW + 9)
    ones = jnp.ones((TILE, STAT), f32)
    spread(kbd, jnp.concatenate([nt(unit, own_tile(kaug_ref, low, high)), ones], axis=1), LROW, LROW + 9, LROW + 18)
    spread(vbd, jnp.concatenate([nt(unit, own_tile(vaug_ref, low, high)), ones], axis=1), DROW, DROW + 9)
    w_qkv = w_qkv_ref[layer]
    for k in range(BLOCKS):
        at = slice(k * BLOCK, (k + 1) * BLOCK)
        qall_ref[k] = query_of(normal_all[k], w_qkv, rope_ref[0:8, at], rope_ref[8:16, at])
    traffic.send(kbd, vbd, qall_ref)
    acc_ref[...] = jnp.zeros(acc_ref.shape, f32)
    for s in range(STEPS):
        u, tile, block = query_step(s, low, high)
        scores = scores_of(qbd[u], kaug_ref[block], query_bias(u, tile, block, len_ref))
        d_scores = jnp.exp(scores) * nn(dbd[u], vaug_ref[block])
        acc_ref[u] = acc_ref[u] + nt(d_scores.astype(bf16), kaug_ref[block])
    d_query = jnp.concatenate([own_heads(acc_ref[0]), own_heads(acc_ref[1])], axis=0) * HEAD_DIM**-0.5
    cosine, sine = own_rope(rope_ref, low, high)
    dq_ref[...] = rotate(nt(eye(D, D, f32), d_query, HIGH), cosine, -sine)


def key_back(traffic, own_ref, other_ref, len_ref, qall_ref, kbd, vbd, dq_ref, grad_ref, resid_ref, layer, w_qkv_ref, gains_ref, rope_ref, daug, dk_ref, dv_ref):
    chip, core, low, high = geometry()

    def put(block, columns, value):
        daug[block, :, columns] = value

    natural_tiles(own_ref, other_ref, put)
    traffic.ready()
    dk_ref[...] = jnp.zeros(dk_ref.shape, f32)
    dv_ref[...] = jnp.zeros(dv_ref.shape, f32)
    for s in range(STEPS):
        u, tile, block = key_step(s, low, high)
        queries = jnp.concatenate([qall_ref[block], daug[block, D:AUG, :]], axis=0)
        probs = jnp.exp(scores_of(kbd[u], queries, key_bias(u, tile, block, len_ref)))
        d_scores = probs * nn(vbd[u], daug[block])
        dv_ref[u] = dv_ref[u] + nt(probs.astype(bf16), daug[block])
        dk_ref[u] = dk_ref[u] + nt(d_scores.astype(bf16), queries)
    unit = eye(D, D, f32)
    d_key = nt(unit, jnp.concatenate([own_heads(dk_ref[0]), own_heads(dk_ref[1])], axis=0), HIGH)
    d_value = nt(unit, jnp.concatenate([own_heads(dv_ref[0]), own_heads(dv_ref[1])], axis=0), HIGH)
    cosine, sine = own_rope(rope_ref, low, high)
    d_mixed = jnp.concatenate([dq_ref[...], rotate(d_key, cosine, -sine), d_value], axis=0).astype(bf16)
    d_in, d_gain = norm_back(resid_ref[...], gain_column(gains_ref, 2 * layer), nn(w_qkv_ref[layer], d_mixed))
    return grad_ref[...] + d_in, d_mixed, d_gain


def projection_grads(normal, d_mixed):
    tail = nt(normal, jnp.concatenate([d_mixed[MAXLAG:], jnp.zeros((TILE - 48, TILE), bf16)], axis=0))
    return nt(normal, d_mixed[:MAXLAG]), tail


def third_kernel(
    traffic, own_ref, other_ref, len_ref, qall_ref, kbd, vbd, dq_ref, grad_in_ref, resid_ref, att_ref, stat_ref, mid_ref, gate_up_ref,
    w_qkv_ref, w_out_ref, w_gate_up_ref, w_down_ref, gains_ref, rope_ref,
    copies_ref, grad_ref, payload_ref, d_mixed_ref, d_gain_a_ref, d_gain_b_ref, d_out_ref, d_gate_up_ref, d_branch_ref, hidden_ref,
    normal_b_ref,
    daug, dk_ref, dv_ref,
):
    grad, d_mixed_ref[...], d_gain_a_ref[...] = key_back(
        traffic, own_ref, other_ref, len_ref, qall_ref, kbd, vbd, dq_ref, grad_in_ref, resid_ref, 1, w_qkv_ref, gains_ref,
        rope_ref, daug, dk_ref, dv_ref,
    )
    low_refs = (d_out_ref, d_gate_up_ref, d_branch_ref, hidden_ref, normal_b_ref)
    grad, payload, d_gain_b_ref[...] = feed_back(
        grad, att_ref[...], mid_ref[...], gate_up_ref[...], w_out_ref[0], w_gate_up_ref[0], w_down_ref[0], gain_column(gains_ref, 1),
        stat_ref[...], low_refs, traffic,
    )
    grad_ref[...] = grad
    payload_ref[...] = payload
    copies_ref[...] = jnp.broadcast_to(payload[None], copies_ref.shape)


def second_window_kernel(
    traffic, len_ref, hidden_ref, d_out_ref, normal_ref, d_gate_up_ref, att_ref, d_branch_ref, d_gain_ref, payload_ref, q_ref, rope_ref,
    kaug_ref, vaug_ref, normal_all, w_qkv_ref,
    pack_ref, tail_ref, dq_ref, qall_ref, kbd, vbd, qbd, dbd, acc_ref,
):
    traffic.ready(8)
    tail = feed_grads(
        Tiles(pack_ref), hidden_ref[...], d_out_ref[...], normal_ref[...], d_gate_up_ref[...], att_ref[...], d_branch_ref[...]
    )
    tail_ref[...] = jnp.where(iota((1, TILE), 1) == 99, d_gain_ref[...], tail)
    traffic.send(pack_ref, tail_ref)
    query_back(
        traffic, 15, 1, payload_ref, q_ref, len_ref, rope_ref, kaug_ref, vaug_ref, normal_all, w_qkv_ref, dq_ref, qall_ref, kbd, vbd, qbd,
        dbd, acc_ref,
    )


def third_window_kernel(
    traffic, len_ref, pack_in_ref, tail_in_ref, normal_a_ref, d_mixed_ref, d_gain_a_ref, hidden_ref, d_out_ref, normal_ref, d_gate_up_ref,
    att_ref, d_branch_ref, d_gain_b_ref, payload_ref, q_ref, rope_ref, kaug_ref, vaug_ref, normal_all, w_qkv_ref,
    keep_ref, send_ref, rest_ref, tail0_ref, tail1_ref, dq_ref, qall_ref, kbd, vbd, qbd, dbd, acc_ref,
):
    traffic.ready(13)
    put = Pairs(lax.axis_index("tm") % 2, keep_ref, send_ref, rest_ref)
    for t in range(pack_in_ref.shape[0]):
        put.tile(pack_in_ref[t].astype(f32))
    head, tail = projection_grads(normal_a_ref[...], d_mixed_ref[...])
    put(head)
    tail0_ref[...] = feed_grads(
        put, hidden_ref[...], d_out_ref[...], normal_ref[...], d_gate_up_ref[...], att_ref[...], d_branch_ref[...]
    )
    lane = iota((1, TILE), 1)
    tail = jnp.where(lane == 98, d_gain_a_ref[...], tail + tail_in_ref[...])
    tail1_ref[...] = jnp.where(lane == 97, d_gain_b_ref[...], tail)
    traffic.send(keep_ref, send_ref, rest_ref, tail0_ref, tail1_ref)
    query_back(
        traffic, 20, 0, payload_ref, q_ref, len_ref, rope_ref, kaug_ref, vaug_ref, normal_all, w_qkv_ref, dq_ref, qall_ref, kbd, vbd, qbd,
        dbd, acc_ref,
    )


def last_kernel(
    traffic, own_ref, other_ref, len_ref, scale_ref, ids_ref, qall_ref, kbd, vbd, dq_ref, grad_in_ref, resid_ref, normal_a_ref, tail0_ref,
    tail1_ref, rest_ref, w_dense_ref, feats_ref, w_qkv_ref, gains_ref, rope_ref,
    keep_ref, send_ref, daug, dk_ref, dv_ref, raw_ref,
):
    chip, core, low, high = geometry()
    d_first, d_mixed, d_gain = key_back(
        traffic, own_ref, other_ref, len_ref, qall_ref, kbd, vbd, dq_ref, grad_in_ref, resid_ref, 0, w_qkv_ref, gains_ref,
        rope_ref, daug, dk_ref, dv_ref,
    )
    head, tail0 = projection_grads(normal_a_ref[...], d_mixed)
    d_first = d_first.astype(bf16)
    feats = feats_ref[...].astype(bf16)
    empty = jnp.zeros((64, TILE), bf16)
    tail0 = tail0 + tail0_ref[...] + nt(d_first, jnp.concatenate([empty, feats[:64]], axis=0))
    tail1 = tail1_ref[...] + nt(d_first, jnp.concatenate([empty, feats[64:], empty[:32]], axis=0))
    lane, row = iota((1, TILE), 1), iota((D, 1), 0)
    tail1 = jnp.where(lane == 96, d_gain, tail1)
    sums, counts = jnp.zeros((D, 1), f32), jnp.zeros((D, 1), f32)
    owner = (lax.axis_index("tm") == 0).astype(f32)
    for d in range(DOCS):
        hit = jnp.where(row == ids_ref[d], owner, 0.0)
        sums, counts = sums + hit * scale_ref[d], counts + hit
    high_part = sums.astype(bf16).astype(f32)
    tail1 = jnp.where(lane == 100, high_part, tail1)
    tail1 = jnp.where(lane == 101, sums - high_part, tail1)
    tail1 = jnp.where(lane == 102, counts, tail1)

    place = own_places(low, high)
    start = doc_start(place, len_ref)
    own = doc_scale_at(place, len_ref, scale_ref)
    flip = (iota((TILE, TILE), 0) + iota((TILE, TILE), 1) == TILE - 1).astype(bf16)
    raw_ref[...] = jnp.zeros(raw_ref.shape, f32)
    lags = TILE - iota((TILE, 1), 0)
    for b in range(3):
        weights = nn(w_dense_ref[:, b * TILE : (b + 1) * TILE], flip).astype(bf16)
        d_lagged = tn(weights, d_first)
        valid = place - (lags + b * TILE) >= start
        d_lagged = jnp.where(valid, d_lagged, 0.0) / own
        for u in range(2):
            half = jnp.where((lane < HALF) == (u == 0), d_lagged, 0.0)
            wide = jnp.concatenate([jnp.zeros((TILE, TILE), f32), half], axis=1)
            rolled = pltpu.roll(wide, TILE, 1, stride=1, stride_axis=0)
            total = jnp.sum(rolled, axis=0, keepdims=True)
            for tile, part in (((low if u == 0 else high) - b + 16, total[:, TILE:]), ((low if u == 0 else high) - b + 15, total[:, :TILE])):
                at = tile % 2, pl.ds(tile // 2, 1)
                raw_ref[at] = raw_ref[at] + part

    put = Pairs(core, keep_ref, send_ref)
    put.tile(rest_ref[0].astype(f32))
    for part in (head, tail0, tail1):
        put(part)
    for k in range(2):
        put.tile(raw_ref[k, 8:24, :])


def summed(in_ref):
    count, rows, _ = in_ref.shape
    total = jnp.zeros((rows, TILE), f32)
    return lax.fori_loop(0, count // 8, lambda i, t: t + jnp.sum(in_ref[pl.ds(i * 8, 8)].astype(f32), axis=0), total)


def pair_sum_kernel(early_ref, early_in_ref, late_ref, late_in_ref, out_ref):
    zero = jnp.zeros((16, TILE), bf16)
    late = late_ref.shape[0] - 1
    series = lax.axis_index("series")
    out_ref[:, 32:40, :] = jnp.zeros((64, 8, TILE), bf16)

    def both(ref, in_ref, t):
        return ref[t].astype(f32) + in_ref[t].astype(f32)

    for t in range(128):
        value = zero
        if t < EARLY:
            value = both(early_ref, early_in_ref, t).astype(bf16)
        elif t < EARLY + late:
            value = both(late_ref, late_in_ref, t - EARLY).astype(bf16)
        out_ref[t // 2, t % 2 * 16 : t % 2 * 16 + 16, :] = value
    raw = both(late_ref, late_in_ref, late)
    for c in range(16):
        line = jnp.where(iota((8, 1), 0) == 0, raw[c : c + 1], 0.0)
        out_ref[series * 16 + c, 32:40, :] = line.astype(bf16)


def sum_kernel(in_ref, out_ref, raw_ref):
    total = summed(in_ref)
    out_ref[...] = jnp.broadcast_to(total[:32].astype(bf16)[None], out_ref.shape)
    raw_ref[...] = total[32:33]


def unpack_kernel(own_ref, other_ref, lag_ref, qkv_ref, out_ref, gate_up_ref, down_ref, gains_ref, scale_ref):
    core = lax.axis_index("tm") % 2

    def tile(t):
        at = t // 4, slice(t // 2 % 2 * 16, t // 2 % 2 * 16 + 16)
        return jnp.where(core == t % 2, own_ref[at].astype(f32), other_ref[at].astype(f32))

    def columns(first, count):
        return [jnp.concatenate([tile(first + 9 * c + r) for r in range(9)], axis=0) for c in range(count)]

    layers = ((207, 234, 117), (90, 243, 0))
    tails = []
    for layer, (at_qkv, at_tail, at_rest) in enumerate(layers):
        for c, part in enumerate(columns(at_qkv, 3)):
            qkv_ref[layer, :, c * TILE : (c + 1) * TILE] = part
        tail = columns(at_tail, 1)[0]
        tails.append(tail)
        qkv_ref[layer, :, MAXLAG:] = tail[:, :48]
        for c, part in enumerate(columns(at_rest, 3)):
            down_ref[layer, :, c * TILE : (c + 1) * TILE] = part
        for c, part in enumerate(columns(at_rest + 27, 6)):
            gate_up_ref[layer, :, c * TILE : (c + 1) * TILE] = part
        out_ref[layer, :, :TILE] = columns(at_rest + 81, 1)[0]
        out_ref[layer, :, TILE:] = tail[:, 48:64]
    lag = jnp.where(iota((1, TILE), 1) < 64, pltpu.roll(tails[0], 64, 1), tails[1])
    lag_ref[...] = lag[:, :FEATS]
    pick = (iota((8, TILE), 1) == iota((8, TILE), 0) + 96).astype(bf16)
    rest = nt(pick, tails[1].astype(bf16))
    gains_ref[0] = rest[0:2]
    gains_ref[1] = rest[2:4]
    scale_ref[...] = ((rest[4:5] + rest[5:6]) / rest[6:7])[:, :DATASETS]


def weights_kernel(traffic, cot_ref, w_qkv_ref, w_out_ref, w_gate_up_ref, low_cot_ref, qkv_ref, out_ref, gate_up_ref):
    traffic.ready()
    low_cot_ref[...] = cot_ref[...].astype(bf16)
    for source, target in ((w_qkv_ref, qkv_ref), (w_out_ref, out_ref), (w_gate_up_ref, gate_up_ref)):
        for layer in range(LAYERS):
            target[layer] = turned(source[layer])


def first_values_kernel(traffic, raw_ref, hours_ref, out_ref):
    traffic.ready()
    both = jnp.concatenate([raw_ref[...], hours_ref[...].astype(f32)], axis=0)
    out_ref[...] = jnp.broadcast_to(both[None], out_ref.shape)


def shape(*dims, dtype=f32):
    return jax.ShapeDtypeStruct(dims, dtype)


class Traffic:
    def __init__(self, loads, stores):
        self.loads, self.stores, self.waited, self.sent = loads, stores, 0, set()
        for copy in loads:
            copy.start()

    def ready(self, count=None):
        count = len(self.loads) if count is None else count
        for copy in self.loads[self.waited : count]:
            copy.wait()
        self.waited = max(self.waited, count)

    def send(self, *refs):
        for ref, copy in self.stores:
            if any(ref is r for r in refs):
                copy.start()
                self.sent.add(id(copy))

    def finish(self):
        self.ready()
        for _, copy in self.stores:
            if id(copy) not in self.sent:
                copy.start()
        for _, copy in self.stores:
            copy.wait()


def call(kernel, operands, outs, scratch=(), tables=(), weights=(), cost=None):
    several = isinstance(outs, list)
    outs = outs if several else [outs]
    fetched = (*tables, *weights)
    buffers = [pltpu.SMEM(x.shape, x.dtype) for x in tables] + [pltpu.VMEM(x.shape, x.dtype) for x in weights]
    is_far = [not isinstance(out, jax.ShapeDtypeStruct) for out in outs]
    buffers += [pltpu.VMEM(out.shape, out.dtype) for out, far in zip(outs, is_far) if far]
    count, extra, copies = len(operands), len(buffers), len(buffers)

    def wrapped(*refs):
        refs = list(refs)
        ins, sources = refs[:count], refs[count : count + len(fetched)]
        results = refs[count + len(fetched) : count + len(fetched) + len(outs)]
        rest = refs[count + len(fetched) + len(outs) :]
        if not copies:
            kernel(*ins, *results, *rest)
            return
        own, held, sems = rest[: len(scratch)], rest[len(scratch) : -1], rest[-1]
        loads = [pltpu.make_async_copy(a, b, sems.at[n]) for n, (a, b) in enumerate(zip(sources, held))]
        stores, at = [], len(fetched)
        for n, far in enumerate(is_far):
            if far:
                stores.append((held[at], pltpu.make_async_copy(held[at], results[n], sems.at[at])))
                results[n] = held[at]
                at += 1
        traffic = Traffic(loads, stores)
        kernel(traffic, *ins, *held[: len(fetched)], *results, *own)
        traffic.finish()

    vmem, hbm = pl.BlockSpec(memory_space=pltpu.VMEM), pl.BlockSpec(memory_space=pltpu.HBM)
    results = pl.pallas_call(
        wrapped,
        out_shape=outs,
        in_specs=[vmem] * count + [hbm] * len(fetched),
        out_specs=[hbm if far else vmem for far in is_far],
        scratch_shapes=[*scratch, *buffers, pltpu.SemaphoreType.DMA((copies,))] if copies else list(scratch),
        compiler_params=pltpu.CompilerParams(vmem_limit_bytes=VMEM),
        cost_estimate=cost and pl.CostEstimate(flops=cost * 10**9, bytes_accessed=10**6, transcendentals=0),
    )(*operands, *(pltpu.with_memory_space_constraint(x, pltpu.HBM) for x in fetched))
    return results if several else results[0]


def pair_permute(x, bit):
    return lax.ppermute(x, "tm", [(i, i ^ bit) for i in range(32)])


def gather(copies, beside):
    groups = [[2 * chip + core for chip in range(16)] for core in range(2)]
    own = lax.all_to_all(copies, "tm", 0, 0, axis_index_groups=groups)
    own, beside = lax.optimization_barrier((own, beside))
    return own, pair_permute(own, 1), beside


def swap(block):
    return lax.ppermute(block, "tm", [(n, n if n % 2 == 0 else 32 - n) for n in range(32)])


def tile_halves(own, other):
    lane = iota((1, TILE), 1) < HALF
    return jnp.where(lane == (lax.axis_index("tm") < 16), own, other)


def rope_table():
    freqs = 10000.0 ** (-np.arange(8, dtype=np.float64) / 8)
    angle = np.arange(LEN, dtype=np.float64)[None, :] * freqs[:, None]
    return np.concatenate([np.cos(angle), np.sin(angle)], axis=0).astype(np.float32)


def body(
    raw_values, hours, doc_lengths, doc_scale, dataset_ids, lag_offsets, w_lag, w_qkv, w_out, w_gate_up, w_down, gains, cotangent
):
    lengths, scales, ids = doc_lengths.reshape(DOCS), doc_scale.reshape(DOCS), dataset_ids.reshape(DOCS)
    def low(*dims):
        return shape(*dims, dtype=bf16)

    def far(*dims, dtype=f32):
        return pltpu.HBM(dims, dtype)

    def far_low(*dims):
        return far(*dims, dtype=bf16)

    w_lag, w_down, lags = w_lag.T, w_down.transpose(0, 2, 1), lag_offsets.reshape(1, LAGS)
    rope = jnp.asarray(rope_table())
    values = lax.all_to_all(call(first_values_kernel, (), shape(32, 2, TILE), weights=(raw_values, hours)), "tm", 0, 0)
    aug, all_d = far_low(BLOCKS, AUG, BLOCK), far_low(BLOCKS, D, BLOCK)
    mine, mine_low, ff_low, column_shape = far(D, TILE), far_low(D, TILE), far_low(FF, TILE), far(D, 1)
    payload_shape = far_low(AUG, TILE)
    low_grads = [mine_low, far_low(2 * FF, TILE), mine_low, ff_low, mine_low]
    wide_bd = pltpu.VMEM((2, ROWS, WIDE), bf16)
    acc = pltpu.VMEM((2, ROWS, AUG), f32)
    top = pltpu.VMEM((2, ROWS, 1), f32)
    aug_scratch = pltpu.VMEM((BLOCKS, AUG, BLOCK), bf16)

    (copies, next1, resid1, kaug0, vaug0, normal_all0, lagged, feats, w_dense, resid0, normal_a0, q0, att0, stat0, mid0, gate_up0) = call(
        first_kernel,
        (values,),
        [low(16, D, TILE), mine_low, mine, aug, aug, all_d, far_low(LAGCOLS, TILE), far(96, TILE), far_low(D, LAGCOLS), mine, mine_low,
         far_low(TILE, D), mine_low, far_low(STAT, TILE), mine, far(2 * FF, TILE)],
        [pltpu.VMEM((8 + TILES, TILE), f32), pltpu.VMEM((TILE, MAXLAG + LEN), bf16), pltpu.VMEM((16, LEN), f32), wide_bd, top, acc],
        tables=(lengths, scales), weights=(lags, w_lag, w_qkv, w_out, w_gate_up, w_down, gains, rope),
    )

    low_cot, *turned_weights = call(
        weights_kernel, (), [mine_low, far_low(LAYERS, 3 * D, D), far_low(LAYERS, D, D), far_low(LAYERS, 2 * FF, D)],
        weights=(cotangent[0].T, w_qkv, w_out, w_gate_up),
    )
    own, other, cot = gather(copies, swap(low_cot))
    copies, act, kaug1, vaug1, normal_all1, q1, grad, payload, att1, d_gain_b1, *low1 = call(
        second_kernel,
        (own, other),
        [low(16, AUG, TILE), mine, aug, aug, all_d, far_low(TILE, D), mine, payload_shape, mine_low, column_shape, *low_grads],
        [wide_bd, top, acc],
        tables=(lengths,),
        weights=(cot, pair_permute(cot, 1), next1, resid1, *turned_weights, w_out, w_gate_up, w_down, gains, rope),
    )

    bd = pltpu.VMEM((2, ROWS, AUG), bf16)
    side_shapes = [mine, all_d, far_low(2, ROWS, WIDE), far_low(2, ROWS, AUG)]
    d_out, d_gate_up, d_branch, hidden, normal_b = low1
    pack, tail, dq, qall, kbd, vbd = call(
        second_window_kernel, (), [far_low(90, 16, TILE), mine, *side_shapes], [wide_bd, bd, acc],
        tables=(lengths,),
        weights=(hidden, d_out, normal_b, d_gate_up, att1, d_branch, d_gain_b1, payload, q1, rope, kaug1, vaug1, normal_all1,
                 turned_weights[0]), cost=8,
    )
    own, other, dq = gather(copies, dq)
    copies, grad, payload, d_mixed, d_gain_a1, d_gain_b0, *low0 = call(
        third_kernel,
        (own, other),
        [low(16, AUG, TILE), mine, payload_shape, far_low(3 * D, TILE), column_shape, column_shape, *low_grads],
        [aug_scratch, acc, acc],
        tables=(lengths,),
        weights=(qall, kbd, vbd, dq, grad, resid1, att0, stat0, mid0, gate_up0, w_qkv, w_out, w_gate_up, w_down, gains, rope),
    )
    d_out, d_gate_up, d_branch, hidden, normal_b = low0
    early, early_out, rest, tail0, tail1, dq, qall, kbd, vbd = call(
        third_window_kernel, (),
        [far_low(EARLY, 16, TILE), far_low(EARLY, 16, TILE), far_low(1, 16, TILE), mine, mine, *side_shapes], [wide_bd, bd, acc],
        tables=(lengths,),
        weights=(pack, tail, next1, d_mixed, d_gain_a1, hidden, d_out, normal_b, d_gate_up, att0, d_branch, d_gain_b0, payload, q0, rope,
                 kaug0, vaug0, normal_all0, turned_weights[0]), cost=8,
    )
    own, other, (dq, early_in) = gather(copies, (dq, pair_permute(early_out, 1)))
    late, late_out = call(
        last_kernel,
        (own, other),
        [low(LATE, 16, TILE)] * 2,
        [aug_scratch, acc, acc, pltpu.VMEM((2, 24, TILE), f32)],
        tables=(lengths, scales, ids),
        weights=(qall, kbd, vbd, dq, grad, resid0, normal_a0, tail0, tail1, rest, w_dense, feats, w_qkv, gains, rope),
    )
    packed = call(pair_sum_kernel, (early, early_in, late, pair_permute(late_out, 1)), low(64, 40, TILE))
    same_core = [[2 * chip + core for chip in range(64)] for core in range(2)]
    parts = lax.all_to_all(packed, ("series", "tm"), 0, 0, axis_index_groups=same_core)
    share, raw_grad = call(sum_kernel, (parts,), [low(64, 32, TILE), shape(1, TILE)])
    share, act = lax.optimization_barrier((share, act))
    own = lax.all_to_all(share, ("series", "tm"), 0, 0, axis_index_groups=same_core)
    own, act = lax.optimization_barrier((own, swap(tile_halves(act, pair_permute(act, 1)))))
    g_lag, g_qkv, g_out, g_gate_up, g_down, g_gains, scale = call(
        unpack_kernel,
        (own, pair_permute(own, 1)),
        [shape(D, FEATS), shape(LAYERS, D, 3 * D), shape(LAYERS, D, D), shape(LAYERS, D, 2 * FF), shape(LAYERS, D, FF),
         shape(LAYERS, 2, D), shape(1, DATASETS)],
    )
    return (
        act.T[None], raw_grad, scale.reshape(DATASETS), g_lag.T, g_qkv, g_out, g_gate_up, g_down.transpose(0, 2, 1), g_gains,
    )


def solution(mesh):
    placed = (
        P("series", "tm"),
        P("series", "tm"),
        P("series", None),
        P("series", None),
        P("series", None, None),
        P(),
        P(),
        P(),
        P(),
        P(),
        P(),
        P(),
        P("series", "tm", None),
    )
    return jax.shard_map(
        body,
        mesh=mesh,
        in_specs=placed,
        out_specs=(P("series", "tm", None), P("series", "tm"), P(), P(), P(), P(), P(), P(), P()),
        check_vma=False,
    )
```

```python
import math

import jax
import jax.numpy as jnp
import numpy as np
from jax import lax
from jax.experimental import pallas as pl
from jax.experimental.pallas import tpu as pltpu
from jax.sharding import PartitionSpec as P


D = 144
HEADS = 9
HEAD_DIM = 16
FF = 384
LAGS = 84
LAYERS = 2
DATASETS = 8
DOCS = 7
LEN = 4096
MAXLAG = 384
FEATS = 87
EPSILON = 1e-06
MASKED = -1e30
AUG = 192
STAT = AUG - D
LROW = D
DROW = D + 27
BLOCK = 512
BLOCKS = LEN // BLOCK
TILE = 128
TILES = LEN // TILE
STEPS = BLOCKS + 1
UNROLL = 3
HALF = 64
ROWS = HEADS * HALF
LAGCOLS = 400
EARLY = 103
LATE = 24
WIDE = AUG + HALF
SAFE = 40.0
VMEM = 28 * 2**20

bf16 = jnp.bfloat16
f32 = jnp.float32
HIGH = lax.Precision.HIGHEST


def nn(a, b, precision=None):
    return lax.dot_general(a, b, (((1,), (0,)), ((), ())), precision=precision, preferred_element_type=f32)


def nt(a, b, precision=None):
    return lax.dot_general(a, b, (((1,), (1,)), ((), ())), precision=precision, preferred_element_type=f32)


def tn(a, b, precision=None):
    return lax.dot_general(a, b, (((0,), (0,)), ((), ())), precision=precision, preferred_element_type=f32)


def iota(shape, dim):
    return lax.broadcasted_iota(jnp.int32, shape, dim)


def eye(rows, cols, dtype):
    return (iota((rows, cols), 0) == iota((rows, cols), 1)).astype(dtype)


def column(row, size):
    keep = iota((size, size), 0) == iota((size, size), 1)
    return jnp.sum(jnp.where(keep, row, 0.0), axis=1, keepdims=True)


def pair_of(chip):
    return jnp.where(chip < 8, 2 * chip, TILES - 1 - 2 * chip)


def geometry():
    index = lax.axis_index("tm")
    chip, core = index // 2, index % 2
    tile = pair_of(chip)
    low = jnp.where(core == 0, tile, TILES - 1 - tile)
    return chip, core, low, TILES - 1 - low


def doc_start(places, len_ref):
    start = jnp.zeros_like(places)
    end = jnp.int32(0)
    for d in range(DOCS):
        end = end + len_ref[d]
        start = jnp.where(places >= end, end, start)
    return start


def doc_scale_at(places, len_ref, scale_ref):
    own = jnp.full(places.shape, scale_ref[0], f32)
    end = jnp.int32(0)
    for d in range(1, DOCS):
        end = end + len_ref[d - 1]
        own = jnp.where(places >= end, scale_ref[d], own)
    return own


def own_places(low, high):
    lane = iota((1, TILE), 1)
    return jnp.where(lane < HALF, low, high) * TILE + lane


def half_places(u, tile):
    return iota((HALF, 1), 0) + (tile * TILE + u * HALF)


def rotate(x, cosine, sine):
    cols = x.shape[1]
    parts = x.reshape(HEADS, 2, 8, cols)
    one, two = parts[:, 0], parts[:, 1]
    turned = jnp.stack([one * cosine - two * sine, two * cosine + one * sine], axis=1)
    return turned.reshape(D, cols)


def norm_factor(x):
    return lax.rsqrt(jnp.mean(x * x, axis=0, keepdims=True) + EPSILON)


def norm_back(x, gain, d_normal):
    r = norm_factor(x)
    scaled = d_normal * gain
    inner = jnp.mean(x * scaled, axis=0, keepdims=True)
    d_x = r * scaled - (r * r * r * inner) * x
    return d_x, jnp.sum(d_normal * x * r, axis=1, keepdims=True)


def head_columns(h, *firsts):
    col = iota((1, AUG), 1)
    keep = (col >= h * HEAD_DIM) & (col < (h + 1) * HEAD_DIM)
    for first in firsts:
        keep = keep | (col == first + h)
    return keep


def spread(ref, rows, *firsts):
    zero = jnp.zeros((HALF, AUG), f32)
    for h in range(HEADS):
        keep = head_columns(h, *firsts)
        for u in range(2):
            part = rows[u * HALF : (u + 1) * HALF]
            ref[u, h * HALF : (h + 1) * HALF, 0:AUG] = jnp.where(keep, part, zero).astype(bf16)
    if ref.shape[2] == WIDE:
        unit = eye(HALF, HALF, bf16)
        for h in range(HEADS):
            for u in range(2):
                ref[u, h * HALF : (h + 1) * HALF, AUG:WIDE] = unit


def own_heads(x):
    col = iota((1, D), 1) // HEAD_DIM
    total = jnp.zeros((HALF, D), f32)
    for h in range(HEADS):
        total = jnp.where(col == h, x[h * HALF : (h + 1) * HALF, :D], total)
    return total


def three_parts(x):
    hi = x.astype(bf16)
    rest = x - hi.astype(f32)
    mid = rest.astype(bf16)
    return hi, mid, (rest - mid.astype(f32)).astype(bf16)


class Tiles:
    def __init__(self, ref):
        self.ref, self.count = ref, 0

    def tile(self, value):
        self.ref[self.count] = value.astype(bf16)
        self.count += 1

    def __call__(self, grads):
        for c in range(grads.shape[1] // TILE):
            for r in range(grads.shape[0] // 16):
                self.tile(grads[16 * r : 16 * (r + 1), c * TILE : (c + 1) * TILE].astype(f32))


class Pairs(Tiles):
    def __init__(self, core, keep_ref, send_ref, rest_ref=None):
        self.core, self.refs, self.rest, self.count, self.even = core, (keep_ref, send_ref), rest_ref, 0, None

    def tile(self, value):
        if self.count == self.refs[0].shape[0]:
            self.rest[0] = value.astype(bf16)
        elif self.even is None:
            self.even = value
        else:
            self.refs[0][self.count] = jnp.where(self.core == 0, self.even, value).astype(bf16)
            self.refs[1][self.count] = jnp.where(self.core == 0, value, self.even).astype(bf16)
            self.even = None
            self.count += 1


def turned(w):
    return tn(w, eye(D, D, bf16)).astype(bf16)


def key_value_block(normal, w_qkv, rope_ref, k, kaug_ref, vaug_ref):
    mixed = nn(w_qkv[D:], normal)
    at = slice(k * BLOCK, (k + 1) * BLOCK)
    keys = rotate(mixed[:D], rope_ref[0:8, at], rope_ref[8:16, at])
    ones = jnp.ones((STAT, BLOCK), bf16)
    kaug_ref[k, 0:D, :] = keys.astype(bf16)
    vaug_ref[k, 0:D, :] = mixed[D:].astype(bf16)
    kaug_ref[k, D:AUG, :] = ones
    vaug_ref[k, D:AUG, :] = ones
    return head_sizes(keys)


def query_of(normal, w_qkv, cosine, sine):
    turned = rotate(nn(w_qkv[:D], normal), cosine, sine)
    return (turned.astype(bf16).astype(f32) * HEAD_DIM**-0.5).astype(bf16)


def own_rope(rope_ref, low, high):
    def at(tile):
        return rope_ref[:, pl.ds(pl.multiple_of(tile * TILE, TILE), TILE)]

    both = jnp.where(iota((1, TILE), 1) < HALF, at(low), at(high))
    return both[0:8], both[8:16]


def own_tile(ref, low, high):
    lane = iota((1, TILE), 1)

    def at(tile):
        return ref[tile // 4, 0:D, pl.ds(pl.multiple_of((tile % 4) * TILE, TILE), TILE)].astype(f32)

    return jnp.where(lane < HALF, at(low), at(high)).astype(bf16)


def query_bias(u, tile, block, len_ref):
    places = half_places(u, tile)
    start = doc_start(places, len_ref)
    keys = iota((1, BLOCK), 1) + block * BLOCK
    return jnp.where((keys <= places) & (keys >= start), 0.0, MASKED).astype(bf16)


def key_bias(u, tile, block, len_ref):
    keys = half_places(u, tile)
    places = iota((1, BLOCK), 1) + block * BLOCK
    start = doc_start(places, len_ref)
    return jnp.where((keys <= places) & (keys >= start), 0.0, MASKED).astype(bf16)


def scores_of(rows, columns, bias):
    return nn(rows, jnp.concatenate([columns, bias], axis=0))


def run_steps(step):
    def several(i, carry):
        for j in range(UNROLL):
            step(i * UNROLL + j)
        return carry

    lax.fori_loop(0, STEPS // UNROLL, several, 0)


def query_step(s, low, high):
    first = low // 4 + 1
    late = s >= first
    return late.astype(jnp.int32), jnp.where(late, high, low), s - jnp.where(late, first, 0)


def key_step(s, low, high):
    first = BLOCKS - low // 4
    late = s >= first
    tile = jnp.where(late, high, low)
    return late.astype(jnp.int32), tile, tile // 4 + s - jnp.where(late, first, 0)


def head_sizes(x):
    return jnp.max(jnp.sum((x * x).reshape(HEADS, HEAD_DIM, x.shape[1]), axis=1), axis=1, keepdims=True)


def attend(query, k_size, kaug_ref, vaug_ref, len_ref, low, high, qbd, top_ref, acc_ref, q_rows_ref):
    q_rows = nt(eye(TILE, TILE, bf16), query)
    q_rows_ref[...] = q_rows.astype(bf16)
    spread(qbd, jnp.concatenate([q_rows, jnp.zeros((TILE, STAT), f32)], axis=1))
    q_size = head_sizes(query.astype(f32))
    acc_ref[...] = jnp.zeros(acc_ref.shape, f32)
    safe = jnp.max(q_size * k_size) <= SAFE * SAFE

    @pl.when(safe)
    def _():
        top_ref[...] = jnp.zeros(top_ref.shape, f32)

        def step(s):
            u, tile, block = query_step(s, low, high)
            scores = scores_of(qbd[u], kaug_ref[block], query_bias(u, tile, block, len_ref))
            acc_ref[u] = acc_ref[u] + nt(jnp.exp(scores).astype(bf16), vaug_ref[block])

        run_steps(step)

    @pl.when(jnp.logical_not(safe))
    def _():
        top_ref[...] = jnp.full(top_ref.shape, MASKED, f32)

        def step(s, carry):
            u, tile, block = query_step(s, low, high)
            scores = scores_of(qbd[u], kaug_ref[block], query_bias(u, tile, block, len_ref))
            old = top_ref[u]
            new = jnp.maximum(old, jnp.max(scores, axis=1, keepdims=True))
            probs = jnp.exp(scores - new)
            acc_ref[u] = acc_ref[u] * jnp.exp(old - new) + nt(probs.astype(bf16), vaug_ref[block])
            top_ref[u] = new
            return carry

        lax.fori_loop(0, STEPS, step, 0)

    attended, stats = [], []
    lane = iota((1, STAT), 1)
    for u in range(2):
        acc = acc_ref[u]
        total = acc[:, D : D + 1]
        attended.append(own_heads(acc[:, :D] / total))
        parts = three_parts(-(top_ref[u] + jnp.log(total)))
        stat = jnp.zeros((HALF, STAT), f32)
        for j in range(3):
            part = parts[j].astype(f32)
            for h in range(HEADS):
                stat = jnp.where(lane == 9 * j + h, part[h * HALF : (h + 1) * HALF], stat)
        stats.append(stat)
    att_rows = jnp.concatenate(attended, axis=0).astype(bf16)
    stat_rows = jnp.concatenate(stats, axis=0).astype(bf16)
    return nt(eye(D, D, bf16), att_rows).astype(bf16), nt(eye(STAT, STAT, bf16), stat_rows).astype(bf16)


def feed_forward(resid, attended, w_out, w_gate_up, w_down, gain):
    mid = resid + nn(w_out, attended)
    normal = (mid * norm_factor(mid) * gain).astype(bf16)
    gate_up = nn(w_gate_up, normal)
    gate = gate_up[:FF]
    hidden = (gate * jax.nn.sigmoid(gate) * gate_up[FF:]).astype(bf16)
    return mid, normal, gate_up, hidden, mid + nn(w_down, hidden)


def feed_back(grad, attended, mid, gate_up, w_out, w_gate_up, w_down, gain, stat, low_refs, traffic):
    d_out_ref, d_gate_up_ref, d_branch_ref, hidden_ref, normal_ref = low_refs
    d_out = grad.astype(bf16)
    d_hidden = tn(w_down, d_out)
    gate, up = gate_up[:FF], gate_up[FF:]
    sig = jax.nn.sigmoid(gate)
    d_gate = d_hidden * up * (sig * (1.0 + gate * (1.0 - sig)))
    d_up = d_hidden * (gate * sig)
    hidden_ref[...] = (gate * sig * up).astype(bf16)
    normal_ref[...] = (mid * norm_factor(mid) * gain).astype(bf16)
    d_gate_up = jnp.concatenate([d_gate, d_up], axis=0).astype(bf16)
    d_mid, d_gain = norm_back(mid, gain, nn(w_gate_up, d_gate_up))
    grad = grad + d_mid
    d_branch = grad.astype(bf16)
    d_att = nn(w_out, d_branch).astype(bf16)
    d_out_ref[...], d_gate_up_ref[...], d_branch_ref[...] = d_out, d_gate_up, d_branch
    traffic.send(*low_refs)
    product = d_att.astype(f32) * attended.astype(f32)
    delta = -jnp.sum(product.reshape(HEADS, HEAD_DIM, TILE), axis=1)
    delta = jnp.concatenate([delta, jnp.zeros((16 - HEADS, TILE), f32)], axis=0)
    hi, lo, _ = three_parts(delta)
    row, col = iota((STAT, 16), 0), iota((STAT, 16), 1)
    place = [((row == 27 + 9 * j + col) & (col < HEADS)).astype(bf16) for j in range(2)]
    stat = stat.astype(f32) + nn(place[0], hi) + nn(place[1], lo)
    return grad, jnp.concatenate([d_att, stat.astype(bf16)], axis=0), d_gain


def feed_grads(put, hidden, d_out, normal, d_gate_up, attended, d_branch):
    put(nt(d_out, hidden))
    put(nt(normal, d_gate_up))
    put(nt(attended, d_branch[:TILE]))
    rows = [jnp.zeros((48, TILE), bf16), d_branch[TILE:], jnp.zeros((TILE - 64, TILE), bf16)]
    return nt(attended, jnp.concatenate(rows, axis=0))


def gain_column(gains_ref, which):
    return column(gains_ref[which // 2, which % 2 : which % 2 + 1, :], D)


def first_kernel(
    traffic, values_ref, len_ref, scale_ref, lag_ref, w_lag_ref, w_qkv_ref, w_out_ref, w_gate_up_ref, w_down_ref, gains_ref, rope_ref,
    copies_ref, next_ref, next_resid_ref, kaug_ref, vaug_ref, normal_all, lagged_ref, feats_ref, w_dense_ref, resid_ref, normal_a_ref,
    q_ref, att_ref, stat_ref, mid_ref, gate_up_ref,
    series, toeplitz, extra, qbd, top_ref, acc_ref,
):
    chip, core, low, high = geometry()
    traffic.ready(2)
    places = iota((TILES, TILE), 0) * TILE + iota((TILES, TILE), 1)
    own = doc_scale_at(places, len_ref, scale_ref)
    values = values_ref[:, 0, :] / own
    angle = values_ref[:, 1, :] * (2.0 * math.pi / 24.0)
    sine, cosine, level = jnp.sin(angle), jnp.cos(angle), jnp.log(own)
    series[0:8, :] = jnp.zeros((8, TILE), f32)
    series[8 : 8 + TILES, :] = values.astype(bf16).astype(f32)
    extra[...] = jnp.zeros(extra.shape, f32)
    for r in range(TILES):
        at = slice(r * TILE, (r + 1) * TILE)
        extra[0:1, at] = sine[r : r + 1]
        extra[1:2, at] = cosine[r : r + 1]
        extra[2:3, at] = level[r : r + 1]
    toeplitz[:, 0:MAXLAG] = jnp.zeros((TILE, MAXLAG), bf16)

    def shift(m, carry):
        window = jnp.concatenate([series[pl.ds(m + 7, 1), :], series[pl.ds(m + 8, 1), :]], axis=1)
        rolled = pltpu.roll(jnp.broadcast_to(window, (TILE, 2 * TILE)), 1, 1, stride=1, stride_axis=0)
        toeplitz[:, pl.ds(pl.multiple_of((m + 3) * TILE, TILE), TILE)] = rolled[:, TILE:].astype(bf16)
        return carry

    lax.fori_loop(0, TILES, shift, 0, unroll=4)

    traffic.ready()

    rows = iota((FEATS, 1), 0)
    diagonal = iota((FEATS, LAGS), 0) == iota((FEATS, LAGS), 1)
    offsets = jnp.sum(jnp.where(diagonal, lag_ref[...].astype(f32), 0.0), axis=1, keepdims=True)
    offsets = jnp.where(rows < LAGS, offsets - 1.0, (rows - LAGS + MAXLAG).astype(f32))
    chosen = (iota((FEATS, LAGCOLS), 1).astype(f32) == offsets).astype(bf16)
    w_dense = nn(w_lag_ref[...], chosen).astype(bf16)
    w_dense_ref[...] = w_dense

    gain_a, gain_b = gain_column(gains_ref, 0), gain_column(gains_ref, 1)
    w_qkv = turned(w_qkv_ref[0])
    lag_rows = iota((TILE, 1), 0) + 1
    k_size = jnp.zeros((HEADS, 1), f32)
    for k in range(BLOCKS):
        place = iota((1, BLOCK), 1) + k * BLOCK
        start = doc_start(place, len_ref)
        parts = []
        for b in range(3):
            at = MAXLAG + k * BLOCK - b * TILE
            lagged = toeplitz[:, at : at + BLOCK]
            if k in (0, BLOCKS - 1):
                valid = place - (lag_rows + b * TILE) >= start
                lagged = jnp.where(valid, lagged.astype(f32), 0.0).astype(bf16)
            parts.append(lagged)
        parts.append(extra[:, k * BLOCK : (k + 1) * BLOCK].astype(bf16))
        resid = nn(w_dense, jnp.concatenate(parts, axis=0))
        normal = (resid * norm_factor(resid) * gain_a).astype(bf16)
        normal_all[k] = normal
        k_size = jnp.maximum(k_size, key_value_block(normal, w_qkv, rope_ref, k, kaug_ref, vaug_ref))

    traffic.send(kaug_ref, vaug_ref, normal_all, w_dense_ref)

    place = own_places(low, high)
    start = doc_start(place, len_ref)
    lane = iota((1, TILE), 1)

    def tile_of(ref, tile):
        return ref[:, pl.ds(pl.multiple_of(tile * TILE, TILE), TILE)].astype(f32)

    for b in range(3):
        lagged = jnp.where(lane < HALF, tile_of(toeplitz, low + 3 - b), tile_of(toeplitz, high + 3 - b))
        valid = place - (lag_rows + b * TILE) >= start
        lagged_ref[b * TILE : (b + 1) * TILE, :] = jnp.where(valid, lagged, 0.0).astype(bf16)
    lagged_ref[MAXLAG:, :] = jnp.where(lane < HALF, tile_of(extra, low), tile_of(extra, high)).astype(bf16)
    lagged = lagged_ref[...]
    feats_ref[0:FEATS, :] = nn(chosen, lagged)
    feats_ref[FEATS:, :] = jnp.zeros((96 - FEATS, TILE), f32)
    resid = nn(w_dense, lagged)
    resid_ref[...] = resid
    normal = (resid * norm_factor(resid) * gain_a).astype(bf16)
    normal_a_ref[...] = normal
    traffic.send(lagged_ref, feats_ref, resid_ref, normal_a_ref)
    query = query_of(normal, w_qkv, *own_rope(rope_ref, low, high))
    attended, stat_ref[...] = attend(query, k_size, kaug_ref, vaug_ref, len_ref, low, high, qbd, top_ref, acc_ref, q_ref)
    att_ref[...] = attended
    traffic.send(q_ref, att_ref, stat_ref)
    mid, _, gate_up, _, resid = feed_forward(
        resid, attended, turned(w_out_ref[0]), turned(w_gate_up_ref[0]), w_down_ref[0], gain_b
    )
    mid_ref[...], gate_up_ref[...] = mid, gate_up
    traffic.send(mid_ref, gate_up_ref)
    next_resid_ref[...] = resid
    normal = (resid * norm_factor(resid) * gain_column(gains_ref, 2)).astype(bf16)
    next_ref[...] = normal
    copies_ref[...] = jnp.broadcast_to(normal[None], copies_ref.shape)


def natural_tiles(own_ref, other_ref, put):
    _, core, _, _ = geometry()
    mine = (iota((1, TILE), 1) < HALF) == (core == 0)
    for chip in range(TILES // 2):
        tile = 2 * chip if chip < 8 else TILES - 1 - 2 * chip
        own, other = own_ref[chip].astype(f32), other_ref[chip].astype(f32)
        for t, value in ((tile, jnp.where(mine, own, other)), (TILES - 1 - tile, jnp.where(mine, other, own))):
            put(t // 4, slice(t % 4 * TILE, (t % 4 + 1) * TILE), value.astype(bf16))


def second_kernel(
    traffic, own_ref, other_ref, len_ref, cot_own_ref, cot_other_ref, normal_ref, resid_in_ref, turned_qkv_ref, turned_out_ref,
    turned_gate_up_ref, w_out_ref, w_gate_up_ref, w_down_ref, gains_ref, rope_ref,
    copies_ref, act_ref, kaug_ref, vaug_ref, normal_all, q_ref, grad_ref, payload_ref, att_ref, d_gain_ref,
    d_out_ref, d_gate_up_ref, d_branch_ref, hidden_ref, normal_b_ref,
    qbd, top_ref, acc_ref,
):
    chip, core, low, high = geometry()

    def put(block, columns, value):
        normal_all[block, :, columns] = value

    natural_tiles(own_ref, other_ref, put)
    traffic.send(normal_all)
    traffic.ready()
    w_qkv = turned_qkv_ref[1]
    k_size = jnp.zeros((HEADS, 1), f32)
    for k in range(BLOCKS):
        k_size = jnp.maximum(k_size, key_value_block(normal_all[k], w_qkv, rope_ref, k, kaug_ref, vaug_ref))
    traffic.send(kaug_ref, vaug_ref)
    query = query_of(normal_ref[...], w_qkv, *own_rope(rope_ref, low, high))
    attended, stat = attend(query, k_size, kaug_ref, vaug_ref, len_ref, low, high, qbd, top_ref, acc_ref, q_ref)
    gain = gain_column(gains_ref, 3)
    w_out, w_gate_up, w_down = w_out_ref[1], w_gate_up_ref[1], w_down_ref[1]
    mid, _, gate_up, _, out = feed_forward(
        resid_in_ref[...], attended, turned_out_ref[1], turned_gate_up_ref[1], w_down, gain
    )
    act_ref[...] = out
    att_ref[...] = attended
    traffic.send(act_ref, att_ref, q_ref)
    grad = tile_halves(cot_own_ref[...].astype(f32), cot_other_ref[...].astype(f32))
    low_refs = (d_out_ref, d_gate_up_ref, d_branch_ref, hidden_ref, normal_b_ref)
    grad, payload, d_gain_ref[...] = feed_back(grad, attended, mid, gate_up, w_out, w_gate_up, w_down, gain, stat, low_refs, traffic)
    grad_ref[...] = grad
    payload_ref[...] = payload
    copies_ref[...] = jnp.broadcast_to(payload[None], copies_ref.shape)


def query_back(
    traffic, count, layer, payload_ref, q_ref, len_ref, rope_ref, kaug_ref, vaug_ref, normal_all, w_qkv_ref, dq_ref, qall_ref, kbd, vbd,
    qbd, dbd, acc_ref,
):
    chip, core, low, high = geometry()
    traffic.ready(count)
    unit = eye(TILE, TILE, bf16)
    rows = nt(unit, payload_ref[...])
    spread(qbd, jnp.concatenate([q_ref[...].astype(f32), rows[:, D:]], axis=1), LROW, LROW + 9, LROW + 18)
    spread(dbd, rows, DROW, DROW + 9)
    ones = jnp.ones((TILE, STAT), f32)
    spread(kbd, jnp.concatenate([nt(unit, own_tile(kaug_ref, low, high)), ones], axis=1), LROW, LROW + 9, LROW + 18)
    spread(vbd, jnp.concatenate([nt(unit, own_tile(vaug_ref, low, high)), ones], axis=1), DROW, DROW + 9)
    w_qkv = w_qkv_ref[layer]
    for k in range(BLOCKS):
        at = slice(k * BLOCK, (k + 1) * BLOCK)
        qall_ref[k] = query_of(normal_all[k], w_qkv, rope_ref[0:8, at], rope_ref[8:16, at])
    traffic.send(kbd, vbd, qall_ref)
    acc_ref[...] = jnp.zeros(acc_ref.shape, f32)

    def step(s):
        u, tile, block = query_step(s, low, high)
        scores = scores_of(qbd[u], kaug_ref[block], query_bias(u, tile, block, len_ref))
        d_scores = jnp.exp(scores) * nn(dbd[u], vaug_ref[block])
        acc_ref[u] = acc_ref[u] + nt(d_scores.astype(bf16), kaug_ref[block])

    run_steps(step)
    d_query = jnp.concatenate([own_heads(acc_ref[0]), own_heads(acc_ref[1])], axis=0) * HEAD_DIM**-0.5
    cosine, sine = own_rope(rope_ref, low, high)
    dq_ref[...] = rotate(nt(eye(D, D, f32), d_query, HIGH), cosine, -sine)


def key_back(traffic, own_ref, other_ref, len_ref, qall_ref, kbd, vbd, dq_ref, grad_ref, resid_ref, layer, w_qkv_ref, gains_ref, rope_ref, daug, dk_ref, dv_ref):
    chip, core, low, high = geometry()

    def put(block, columns, value):
        daug[block, :, columns] = value

    natural_tiles(own_ref, other_ref, put)
    traffic.ready()
    dk_ref[...] = jnp.zeros(dk_ref.shape, f32)
    dv_ref[...] = jnp.zeros(dv_ref.shape, f32)

    def step(s):
        u, tile, block = key_step(s, low, high)
        queries = jnp.concatenate([qall_ref[block], daug[block, D:AUG, :]], axis=0)
        probs = jnp.exp(scores_of(kbd[u], queries, key_bias(u, tile, block, len_ref)))
        d_scores = probs * nn(vbd[u], daug[block])
        dv_ref[u] = dv_ref[u] + nt(probs.astype(bf16), daug[block])
        dk_ref[u] = dk_ref[u] + nt(d_scores.astype(bf16), queries)

    run_steps(step)
    unit = eye(D, D, f32)
    d_key = nt(unit, jnp.concatenate([own_heads(dk_ref[0]), own_heads(dk_ref[1])], axis=0), HIGH)
    d_value = nt(unit, jnp.concatenate([own_heads(dv_ref[0]), own_heads(dv_ref[1])], axis=0), HIGH)
    cosine, sine = own_rope(rope_ref, low, high)
    d_mixed = jnp.concatenate([dq_ref[...], rotate(d_key, cosine, -sine), d_value], axis=0).astype(bf16)
    d_in, d_gain = norm_back(resid_ref[...], gain_column(gains_ref, 2 * layer), nn(w_qkv_ref[layer], d_mixed))
    return grad_ref[...] + d_in, d_mixed, d_gain


def projection_grads(normal, d_mixed):
    tail = nt(normal, jnp.concatenate([d_mixed[MAXLAG:], jnp.zeros((TILE - 48, TILE), bf16)], axis=0))
    return nt(normal, d_mixed[:MAXLAG]), tail


def third_kernel(
    traffic, own_ref, other_ref, len_ref, qall_ref, kbd, vbd, dq_ref, grad_in_ref, resid_ref, att_ref, stat_ref, mid_ref, gate_up_ref,
    w_qkv_ref, w_out_ref, w_gate_up_ref, w_down_ref, gains_ref, rope_ref,
    copies_ref, grad_ref, payload_ref, d_mixed_ref, d_gain_a_ref, d_gain_b_ref, d_out_ref, d_gate_up_ref, d_branch_ref, hidden_ref,
    normal_b_ref,
    daug, dk_ref, dv_ref,
):
    grad, d_mixed_ref[...], d_gain_a_ref[...] = key_back(
        traffic, own_ref, other_ref, len_ref, qall_ref, kbd, vbd, dq_ref, grad_in_ref, resid_ref, 1, w_qkv_ref, gains_ref,
        rope_ref, daug, dk_ref, dv_ref,
    )
    low_refs = (d_out_ref, d_gate_up_ref, d_branch_ref, hidden_ref, normal_b_ref)
    grad, payload, d_gain_b_ref[...] = feed_back(
        grad, att_ref[...], mid_ref[...], gate_up_ref[...], w_out_ref[0], w_gate_up_ref[0], w_down_ref[0], gain_column(gains_ref, 1),
        stat_ref[...], low_refs, traffic,
    )
    grad_ref[...] = grad
    payload_ref[...] = payload
    copies_ref[...] = jnp.broadcast_to(payload[None], copies_ref.shape)


def second_window_kernel(
    traffic, len_ref, hidden_ref, d_out_ref, normal_ref, d_gate_up_ref, att_ref, d_branch_ref, d_gain_ref, payload_ref, q_ref, rope_ref,
    kaug_ref, vaug_ref, normal_all, w_qkv_ref,
    pack_ref, tail_ref, dq_ref, qall_ref, kbd, vbd, qbd, dbd, acc_ref,
):
    traffic.ready(8)
    tail = feed_grads(
        Tiles(pack_ref), hidden_ref[...], d_out_ref[...], normal_ref[...], d_gate_up_ref[...], att_ref[...], d_branch_ref[...]
    )
    tail_ref[...] = jnp.where(iota((1, TILE), 1) == 99, d_gain_ref[...], tail)
    traffic.send(pack_ref, tail_ref)
    query_back(
        traffic, 15, 1, payload_ref, q_ref, len_ref, rope_ref, kaug_ref, vaug_ref, normal_all, w_qkv_ref, dq_ref, qall_ref, kbd, vbd, qbd,
        dbd, acc_ref,
    )


def third_window_kernel(
    traffic, len_ref, pack_in_ref, tail_in_ref, normal_a_ref, d_mixed_ref, d_gain_a_ref, hidden_ref, d_out_ref, normal_ref, d_gate_up_ref,
    att_ref, d_branch_ref, d_gain_b_ref, payload_ref, q_ref, rope_ref, kaug_ref, vaug_ref, normal_all, w_qkv_ref,
    keep_ref, send_ref, rest_ref, tail0_ref, tail1_ref, dq_ref, qall_ref, kbd, vbd, qbd, dbd, acc_ref,
):
    traffic.ready(13)
    put = Pairs(lax.axis_index("tm") % 2, keep_ref, send_ref, rest_ref)
    for t in range(pack_in_ref.shape[0]):
        put.tile(pack_in_ref[t].astype(f32))
    head, tail = projection_grads(normal_a_ref[...], d_mixed_ref[...])
    put(head)
    tail0_ref[...] = feed_grads(
        put, hidden_ref[...], d_out_ref[...], normal_ref[...], d_gate_up_ref[...], att_ref[...], d_branch_ref[...]
    )
    lane = iota((1, TILE), 1)
    tail = jnp.where(lane == 98, d_gain_a_ref[...], tail + tail_in_ref[...])
    tail1_ref[...] = jnp.where(lane == 97, d_gain_b_ref[...], tail)
    traffic.send(keep_ref, send_ref, rest_ref, tail0_ref, tail1_ref)
    query_back(
        traffic, 20, 0, payload_ref, q_ref, len_ref, rope_ref, kaug_ref, vaug_ref, normal_all, w_qkv_ref, dq_ref, qall_ref, kbd, vbd, qbd,
        dbd, acc_ref,
    )


def last_kernel(
    traffic, own_ref, other_ref, len_ref, scale_ref, ids_ref, qall_ref, kbd, vbd, dq_ref, grad_in_ref, resid_ref, normal_a_ref, tail0_ref,
    tail1_ref, rest_ref, w_dense_ref, feats_ref, w_qkv_ref, gains_ref, rope_ref,
    keep_ref, send_ref, daug, dk_ref, dv_ref, raw_ref,
):
    chip, core, low, high = geometry()
    d_first, d_mixed, d_gain = key_back(
        traffic, own_ref, other_ref, len_ref, qall_ref, kbd, vbd, dq_ref, grad_in_ref, resid_ref, 0, w_qkv_ref, gains_ref,
        rope_ref, daug, dk_ref, dv_ref,
    )
    head, tail0 = projection_grads(normal_a_ref[...], d_mixed)
    d_first = d_first.astype(bf16)
    feats = feats_ref[...].astype(bf16)
    empty = jnp.zeros((64, TILE), bf16)
    tail0 = tail0 + tail0_ref[...] + nt(d_first, jnp.concatenate([empty, feats[:64]], axis=0))
    tail1 = tail1_ref[...] + nt(d_first, jnp.concatenate([empty, feats[64:], empty[:32]], axis=0))
    lane, row = iota((1, TILE), 1), iota((D, 1), 0)
    tail1 = jnp.where(lane == 96, d_gain, tail1)
    sums, counts = jnp.zeros((D, 1), f32), jnp.zeros((D, 1), f32)
    owner = (lax.axis_index("tm") == 0).astype(f32)
    for d in range(DOCS):
        hit = jnp.where(row == ids_ref[d], owner, 0.0)
        sums, counts = sums + hit * scale_ref[d], counts + hit
    high_part = sums.astype(bf16).astype(f32)
    tail1 = jnp.where(lane == 100, high_part, tail1)
    tail1 = jnp.where(lane == 101, sums - high_part, tail1)
    tail1 = jnp.where(lane == 102, counts, tail1)

    place = own_places(low, high)
    start = doc_start(place, len_ref)
    own = doc_scale_at(place, len_ref, scale_ref)
    flip = (iota((TILE, TILE), 0) + iota((TILE, TILE), 1) == TILE - 1).astype(bf16)
    raw_ref[...] = jnp.zeros(raw_ref.shape, f32)
    lags = TILE - iota((TILE, 1), 0)
    for b in range(3):
        weights = nn(w_dense_ref[:, b * TILE : (b + 1) * TILE], flip).astype(bf16)
        d_lagged = tn(weights, d_first)
        valid = place - (lags + b * TILE) >= start
        d_lagged = jnp.where(valid, d_lagged, 0.0) / own
        for u in range(2):
            half = jnp.where((lane < HALF) == (u == 0), d_lagged, 0.0)
            wide = jnp.concatenate([jnp.zeros((TILE, TILE), f32), half], axis=1)
            rolled = pltpu.roll(wide, TILE, 1, stride=1, stride_axis=0)
            total = jnp.sum(rolled, axis=0, keepdims=True)
            for tile, part in (((low if u == 0 else high) - b + 16, total[:, TILE:]), ((low if u == 0 else high) - b + 15, total[:, :TILE])):
                at = tile % 2, pl.ds(tile // 2, 1)
                raw_ref[at] = raw_ref[at] + part

    put = Pairs(core, keep_ref, send_ref)
    put.tile(rest_ref[0].astype(f32))
    for part in (head, tail0, tail1):
        put(part)
    for k in range(2):
        put.tile(raw_ref[k, 8:24, :])


def summed(in_ref):
    count, rows, _ = in_ref.shape
    total = jnp.zeros((rows, TILE), f32)
    return lax.fori_loop(0, count // 8, lambda i, t: t + jnp.sum(in_ref[pl.ds(i * 8, 8)].astype(f32), axis=0), total)


def pair_sum_kernel(early_ref, early_in_ref, late_ref, late_in_ref, out_ref):
    zero = jnp.zeros((16, TILE), bf16)
    late = late_ref.shape[0] - 1
    series = lax.axis_index("series")
    out_ref[:, 32:40, :] = jnp.zeros((64, 8, TILE), bf16)

    def both(ref, in_ref, t):
        return ref[t].astype(f32) + in_ref[t].astype(f32)

    for t in range(128):
        value = zero
        if t < EARLY:
            value = both(early_ref, early_in_ref, t).astype(bf16)
        elif t < EARLY + late:
            value = both(late_ref, late_in_ref, t - EARLY).astype(bf16)
        out_ref[t // 2, t % 2 * 16 : t % 2 * 16 + 16, :] = value
    raw = both(late_ref, late_in_ref, late)
    for c in range(16):
        line = jnp.where(iota((8, 1), 0) == 0, raw[c : c + 1], 0.0)
        out_ref[series * 16 + c, 32:40, :] = line.astype(bf16)


def sum_kernel(in_ref, out_ref, raw_ref):
    total = summed(in_ref)
    out_ref[...] = jnp.broadcast_to(total[:32].astype(bf16)[None], out_ref.shape)
    raw_ref[...] = total[32:33]


def unpack_kernel(own_ref, other_ref, lag_ref, qkv_ref, out_ref, gate_up_ref, down_ref, gains_ref, scale_ref):
    core = lax.axis_index("tm") % 2

    def tile(t):
        at = t // 4, slice(t // 2 % 2 * 16, t // 2 % 2 * 16 + 16)
        return jnp.where(core == t % 2, own_ref[at].astype(f32), other_ref[at].astype(f32))

    def columns(first, count):
        return [jnp.concatenate([tile(first + 9 * c + r) for r in range(9)], axis=0) for c in range(count)]

    layers = ((207, 234, 117), (90, 243, 0))
    tails = []
    for layer, (at_qkv, at_tail, at_rest) in enumerate(layers):
        for c, part in enumerate(columns(at_qkv, 3)):
            qkv_ref[layer, :, c * TILE : (c + 1) * TILE] = part
        tail = columns(at_tail, 1)[0]
        tails.append(tail)
        qkv_ref[layer, :, MAXLAG:] = tail[:, :48]
        for c, part in enumerate(columns(at_rest, 3)):
            down_ref[layer, :, c * TILE : (c + 1) * TILE] = part
        for c, part in enumerate(columns(at_rest + 27, 6)):
            gate_up_ref[layer, :, c * TILE : (c + 1) * TILE] = part
        out_ref[layer, :, :TILE] = columns(at_rest + 81, 1)[0]
        out_ref[layer, :, TILE:] = tail[:, 48:64]
    lag = jnp.where(iota((1, TILE), 1) < 64, pltpu.roll(tails[0], 64, 1), tails[1])
    lag_ref[...] = lag[:, :FEATS]
    pick = (iota((8, TILE), 1) == iota((8, TILE), 0) + 96).astype(bf16)
    rest = nt(pick, tails[1].astype(bf16))
    gains_ref[0] = rest[0:2]
    gains_ref[1] = rest[2:4]
    scale_ref[...] = ((rest[4:5] + rest[5:6]) / rest[6:7])[:, :DATASETS]


def weights_kernel(traffic, cot_ref, w_qkv_ref, w_out_ref, w_gate_up_ref, low_cot_ref, qkv_ref, out_ref, gate_up_ref):
    traffic.ready()
    low_cot_ref[...] = cot_ref[...].astype(bf16)
    for source, target in ((w_qkv_ref, qkv_ref), (w_out_ref, out_ref), (w_gate_up_ref, gate_up_ref)):
        for layer in range(LAYERS):
            target[layer] = turned(source[layer])


def first_values_kernel(traffic, raw_ref, hours_ref, out_ref):
    traffic.ready()
    both = jnp.concatenate([raw_ref[...], hours_ref[...].astype(f32)], axis=0)
    out_ref[...] = jnp.broadcast_to(both[None], out_ref.shape)


def shape(*dims, dtype=f32):
    return jax.ShapeDtypeStruct(dims, dtype)


class Traffic:
    def __init__(self, loads, stores):
        self.loads, self.stores, self.waited, self.sent = loads, stores, 0, set()
        for copy in loads:
            copy.start()

    def ready(self, count=None):
        count = len(self.loads) if count is None else count
        for copy in self.loads[self.waited : count]:
            copy.wait()
        self.waited = max(self.waited, count)

    def send(self, *refs):
        for ref, copy in self.stores:
            if any(ref is r for r in refs):
                copy.start()
                self.sent.add(id(copy))

    def finish(self):
        self.ready()
        for _, copy in self.stores:
            if id(copy) not in self.sent:
                copy.start()
        for _, copy in self.stores:
            copy.wait()


def call(kernel, operands, outs, scratch=(), tables=(), weights=(), cost=None):
    several = isinstance(outs, list)
    outs = outs if several else [outs]
    fetched = (*tables, *weights)
    buffers = [pltpu.SMEM(x.shape, x.dtype) for x in tables] + [pltpu.VMEM(x.shape, x.dtype) for x in weights]
    is_far = [not isinstance(out, jax.ShapeDtypeStruct) for out in outs]
    buffers += [pltpu.VMEM(out.shape, out.dtype) for out, far in zip(outs, is_far) if far]
    count, extra, copies = len(operands), len(buffers), len(buffers)

    def wrapped(*refs):
        refs = list(refs)
        ins, sources = refs[:count], refs[count : count + len(fetched)]
        results = refs[count + len(fetched) : count + len(fetched) + len(outs)]
        rest = refs[count + len(fetched) + len(outs) :]
        if not copies:
            kernel(*ins, *results, *rest)
            return
        own, held, sems = rest[: len(scratch)], rest[len(scratch) : -1], rest[-1]
        loads = [pltpu.make_async_copy(a, b, sems.at[n]) for n, (a, b) in enumerate(zip(sources, held))]
        stores, at = [], len(fetched)
        for n, far in enumerate(is_far):
            if far:
                stores.append((held[at], pltpu.make_async_copy(held[at], results[n], sems.at[at])))
                results[n] = held[at]
                at += 1
        traffic = Traffic(loads, stores)
        kernel(traffic, *ins, *held[: len(fetched)], *results, *own)
        traffic.finish()

    vmem, hbm = pl.BlockSpec(memory_space=pltpu.VMEM), pl.BlockSpec(memory_space=pltpu.HBM)
    results = pl.pallas_call(
        wrapped,
        out_shape=outs,
        in_specs=[vmem] * count + [hbm] * len(fetched),
        out_specs=[hbm if far else vmem for far in is_far],
        scratch_shapes=[*scratch, *buffers, pltpu.SemaphoreType.DMA((copies,))] if copies else list(scratch),
        compiler_params=pltpu.CompilerParams(vmem_limit_bytes=VMEM),
        cost_estimate=cost and pl.CostEstimate(flops=cost * 10**9, bytes_accessed=10**6, transcendentals=0),
    )(*operands, *(pltpu.with_memory_space_constraint(x, pltpu.HBM) for x in fetched))
    return results if several else results[0]


def pair_permute(x, bit):
    return lax.ppermute(x, "tm", [(i, i ^ bit) for i in range(32)])


def gather(copies, beside):
    groups = [[2 * chip + core for chip in range(16)] for core in range(2)]
    own = lax.all_to_all(copies, "tm", 0, 0, axis_index_groups=groups)
    own, beside = lax.optimization_barrier((own, beside))
    return own, pair_permute(own, 1), beside


def swap(block):
    return lax.ppermute(block, "tm", [(n, n if n % 2 == 0 else 32 - n) for n in range(32)])


def tile_halves(own, other):
    lane = iota((1, TILE), 1) < HALF
    return jnp.where(lane == (lax.axis_index("tm") < 16), own, other)


def rope_table():
    freqs = 10000.0 ** (-np.arange(8, dtype=np.float64) / 8)
    angle = np.arange(LEN, dtype=np.float64)[None, :] * freqs[:, None]
    return np.concatenate([np.cos(angle), np.sin(angle)], axis=0).astype(np.float32)


def body(
    raw_values, hours, doc_lengths, doc_scale, dataset_ids, lag_offsets, w_lag, w_qkv, w_out, w_gate_up, w_down, gains, cotangent
):
    lengths, scales, ids = doc_lengths.reshape(DOCS), doc_scale.reshape(DOCS), dataset_ids.reshape(DOCS)
    def low(*dims):
        return shape(*dims, dtype=bf16)

    def far(*dims, dtype=f32):
        return pltpu.HBM(dims, dtype)

    def far_low(*dims):
        return far(*dims, dtype=bf16)

    w_lag, w_down, lags = w_lag.T, w_down.transpose(0, 2, 1), lag_offsets.reshape(1, LAGS)
    rope = jnp.asarray(rope_table())
    values = lax.all_to_all(call(first_values_kernel, (), shape(32, 2, TILE), weights=(raw_values, hours)), "tm", 0, 0)
    aug, all_d = far_low(BLOCKS, AUG, BLOCK), far_low(BLOCKS, D, BLOCK)
    mine, mine_low, ff_low, column_shape = far(D, TILE), far_low(D, TILE), far_low(FF, TILE), far(D, 1)
    payload_shape = far_low(AUG, TILE)
    low_grads = [mine_low, far_low(2 * FF, TILE), mine_low, ff_low, mine_low]
    wide_bd = pltpu.VMEM((2, ROWS, WIDE), bf16)
    acc = pltpu.VMEM((2, ROWS, AUG), f32)
    top = pltpu.VMEM((2, ROWS, 1), f32)
    aug_scratch = pltpu.VMEM((BLOCKS, AUG, BLOCK), bf16)

    (copies, next1, resid1, kaug0, vaug0, normal_all0, lagged, feats, w_dense, resid0, normal_a0, q0, att0, stat0, mid0, gate_up0) = call(
        first_kernel,
        (values,),
        [low(16, D, TILE), mine_low, mine, aug, aug, all_d, far_low(LAGCOLS, TILE), far(96, TILE), far_low(D, LAGCOLS), mine, mine_low,
         far_low(TILE, D), mine_low, far_low(STAT, TILE), mine, far(2 * FF, TILE)],
        [pltpu.VMEM((8 + TILES, TILE), f32), pltpu.VMEM((TILE, MAXLAG + LEN), bf16), pltpu.VMEM((16, LEN), f32), wide_bd, top, acc],
        tables=(lengths, scales), weights=(lags, w_lag, w_qkv, w_out, w_gate_up, w_down, gains, rope),
    )

    low_cot, *turned_weights = call(
        weights_kernel, (), [mine_low, far_low(LAYERS, 3 * D, D), far_low(LAYERS, D, D), far_low(LAYERS, 2 * FF, D)],
        weights=(cotangent[0].T, w_qkv, w_out, w_gate_up),
    )
    own, other, cot = gather(copies, swap(low_cot))
    copies, act, kaug1, vaug1, normal_all1, q1, grad, payload, att1, d_gain_b1, *low1 = call(
        second_kernel,
        (own, other),
        [low(16, AUG, TILE), mine, aug, aug, all_d, far_low(TILE, D), mine, payload_shape, mine_low, column_shape, *low_grads],
        [wide_bd, top, acc],
        tables=(lengths,),
        weights=(cot, pair_permute(cot, 1), next1, resid1, *turned_weights, w_out, w_gate_up, w_down, gains, rope),
    )

    bd = pltpu.VMEM((2, ROWS, AUG), bf16)
    side_shapes = [mine, all_d, far_low(2, ROWS, WIDE), far_low(2, ROWS, AUG)]
    d_out, d_gate_up, d_branch, hidden, normal_b = low1
    pack, tail, dq, qall, kbd, vbd = call(
        second_window_kernel, (), [far_low(90, 16, TILE), mine, *side_shapes], [wide_bd, bd, acc],
        tables=(lengths,),
        weights=(hidden, d_out, normal_b, d_gate_up, att1, d_branch, d_gain_b1, payload, q1, rope, kaug1, vaug1, normal_all1,
                 turned_weights[0]), cost=8,
    )
    own, other, dq = gather(copies, dq)
    copies, grad, payload, d_mixed, d_gain_a1, d_gain_b0, *low0 = call(
        third_kernel,
        (own, other),
        [low(16, AUG, TILE), mine, payload_shape, far_low(3 * D, TILE), column_shape, column_shape, *low_grads],
        [aug_scratch, acc, acc],
        tables=(lengths,),
        weights=(qall, kbd, vbd, dq, grad, resid1, att0, stat0, mid0, gate_up0, w_qkv, w_out, w_gate_up, w_down, gains, rope),
    )
    d_out, d_gate_up, d_branch, hidden, normal_b = low0
    early, early_out, rest, tail0, tail1, dq, qall, kbd, vbd = call(
        third_window_kernel, (),
        [far_low(EARLY, 16, TILE), far_low(EARLY, 16, TILE), far_low(1, 16, TILE), mine, mine, *side_shapes], [wide_bd, bd, acc],
        tables=(lengths,),
        weights=(pack, tail, next1, d_mixed, d_gain_a1, hidden, d_out, normal_b, d_gate_up, att0, d_branch, d_gain_b0, payload, q0, rope,
                 kaug0, vaug0, normal_all0, turned_weights[0]), cost=8,
    )
    own, other, (dq, early_in) = gather(copies, (dq, pair_permute(early_out, 1)))
    late, late_out = call(
        last_kernel,
        (own, other),
        [low(LATE, 16, TILE)] * 2,
        [aug_scratch, acc, acc, pltpu.VMEM((2, 24, TILE), f32)],
        tables=(lengths, scales, ids),
        weights=(qall, kbd, vbd, dq, grad, resid0, normal_a0, tail0, tail1, rest, w_dense, feats, w_qkv, gains, rope),
    )
    packed = call(pair_sum_kernel, (early, early_in, late, pair_permute(late_out, 1)), low(64, 40, TILE))
    same_core = [[2 * chip + core for chip in range(64)] for core in range(2)]
    parts = lax.all_to_all(packed, ("series", "tm"), 0, 0, axis_index_groups=same_core)
    share, raw_grad = call(sum_kernel, (parts,), [low(64, 32, TILE), shape(1, TILE)])
    share, act = lax.optimization_barrier((share, act))
    own = lax.all_to_all(share, ("series", "tm"), 0, 0, axis_index_groups=same_core)
    own, act = lax.optimization_barrier((own, swap(tile_halves(act, pair_permute(act, 1)))))
    g_lag, g_qkv, g_out, g_gate_up, g_down, g_gains, scale = call(
        unpack_kernel,
        (own, pair_permute(own, 1)),
        [shape(D, FEATS), shape(LAYERS, D, 3 * D), shape(LAYERS, D, D), shape(LAYERS, D, 2 * FF), shape(LAYERS, D, FF),
         shape(LAYERS, 2, D), shape(1, DATASETS)],
    )
    return (
        act.T[None], raw_grad, scale.reshape(DATASETS), g_lag.T, g_qkv, g_out, g_gate_up, g_down.transpose(0, 2, 1), g_gains,
    )


def solution(mesh):
    placed = (
        P("series", "tm"),
        P("series", "tm"),
        P("series", None),
        P("series", None),
        P("series", None, None),
        P(),
        P(),
        P(),
        P(),
        P(),
        P(),
        P(),
        P("series", "tm", None),
    )
    return jax.shard_map(
        body,
        mesh=mesh,
        in_specs=placed,
        out_specs=(P("series", "tm", None), P("series", "tm"), P(), P(), P(), P(), P(), P(), P()),
        check_vma=False,
    )
```

```python
import math

import jax
import jax.numpy as jnp
import numpy as np
from jax import lax
from jax.experimental import pallas as pl
from jax.experimental.pallas import tpu as pltpu
from jax.sharding import PartitionSpec as P


D = 144
HEADS = 9
HEAD_DIM = 16
FF = 384
LAGS = 84
LAYERS = 2
DATASETS = 8
DOCS = 7
LEN = 4096
MAXLAG = 384
FEATS = 87
EPSILON = 1e-06
MASKED = -1e30
AUG = 176
STAT = AUG - D
LROW = D
DROW = D + 18
BLOCK = 512
BLOCKS = LEN // BLOCK
TILE = 128
TILES = LEN // TILE
STEPS = BLOCKS + 1
UNROLL = 3
HALF = 64
ROWS = HEADS * HALF
LAGCOLS = 400
EARLY = 103
LATE = 24
WIDE = AUG + HALF
SAFE = 40.0
VMEM = 28 * 2**20

bf16 = jnp.bfloat16
f32 = jnp.float32
HIGH = lax.Precision.HIGHEST


def nn(a, b, precision=None):
    return lax.dot_general(a, b, (((1,), (0,)), ((), ())), precision=precision, preferred_element_type=f32)


def nt(a, b, precision=None):
    return lax.dot_general(a, b, (((1,), (1,)), ((), ())), precision=precision, preferred_element_type=f32)


def tn(a, b, precision=None):
    return lax.dot_general(a, b, (((0,), (0,)), ((), ())), precision=precision, preferred_element_type=f32)


def iota(shape, dim):
    return lax.broadcasted_iota(jnp.int32, shape, dim)


def eye(rows, cols, dtype):
    return (iota((rows, cols), 0) == iota((rows, cols), 1)).astype(dtype)


def column(row, size):
    keep = iota((size, size), 0) == iota((size, size), 1)
    return jnp.sum(jnp.where(keep, row, 0.0), axis=1, keepdims=True)


def pair_of(chip):
    return jnp.where(chip < 8, 2 * chip, TILES - 1 - 2 * chip)


def geometry():
    index = lax.axis_index("tm")
    chip, core = index // 2, index % 2
    tile = pair_of(chip)
    low = jnp.where(core == 0, tile, TILES - 1 - tile)
    return chip, core, low, TILES - 1 - low


def doc_start(places, len_ref):
    start = jnp.zeros_like(places)
    end = jnp.int32(0)
    for d in range(DOCS):
        end = end + len_ref[d]
        start = jnp.where(places >= end, end, start)
    return start


def doc_scale_at(places, len_ref, scale_ref):
    own = jnp.full(places.shape, scale_ref[0], f32)
    end = jnp.int32(0)
    for d in range(1, DOCS):
        end = end + len_ref[d - 1]
        own = jnp.where(places >= end, scale_ref[d], own)
    return own


def own_places(low, high):
    lane = iota((1, TILE), 1)
    return jnp.where(lane < HALF, low, high) * TILE + lane


def half_places(u, tile):
    return iota((HALF, 1), 0) + (tile * TILE + u * HALF)


def rotate(x, cosine, sine):
    cols = x.shape[1]
    parts = x.reshape(HEADS, 2, 8, cols)
    one, two = parts[:, 0], parts[:, 1]
    turned = jnp.stack([one * cosine - two * sine, two * cosine + one * sine], axis=1)
    return turned.reshape(D, cols)


def norm_factor(x):
    return lax.rsqrt(jnp.mean(x * x, axis=0, keepdims=True) + EPSILON)


def norm_back(x, gain, d_normal):
    r = norm_factor(x)
    scaled = d_normal * gain
    inner = jnp.mean(x * scaled, axis=0, keepdims=True)
    d_x = r * scaled - (r * r * r * inner) * x
    return d_x, jnp.sum(d_normal * x * r, axis=1, keepdims=True)


def head_columns(h, *firsts):
    col = iota((1, AUG), 1)
    keep = (col >= h * HEAD_DIM) & (col < (h + 1) * HEAD_DIM)
    for first in firsts:
        keep = keep | (col == first + h)
    return keep


def spread(ref, rows, *firsts):
    zero = jnp.zeros((HALF, AUG), f32)
    for h in range(HEADS):
        keep = head_columns(h, *firsts)
        for u in range(2):
            part = rows[u * HALF : (u + 1) * HALF]
            ref[u, h * HALF : (h + 1) * HALF, 0:AUG] = jnp.where(keep, part, zero).astype(bf16)
    if ref.shape[2] == WIDE:
        unit = eye(HALF, HALF, bf16)
        for h in range(HEADS):
            for u in range(2):
                ref[u, h * HALF : (h + 1) * HALF, AUG:WIDE] = unit


def own_heads(x):
    col = iota((1, D), 1) // HEAD_DIM
    total = jnp.zeros((HALF, D), f32)
    for h in range(HEADS):
        total = jnp.where(col == h, x[h * HALF : (h + 1) * HALF, :D], total)
    return total


def two_parts(x):
    hi = x.astype(bf16)
    return hi, (x - hi.astype(f32)).astype(bf16)


class Tiles:
    def __init__(self, ref):
        self.ref, self.count = ref, 0

    def tile(self, value):
        self.ref[self.count] = value.astype(bf16)
        self.count += 1

    def __call__(self, grads):
        for c in range(grads.shape[1] // TILE):
            for r in range(grads.shape[0] // 16):
                self.tile(grads[16 * r : 16 * (r + 1), c * TILE : (c + 1) * TILE].astype(f32))


class Pairs(Tiles):
    def __init__(self, core, keep_ref, send_ref, rest_ref=None):
        self.core, self.refs, self.rest, self.count, self.even = core, (keep_ref, send_ref), rest_ref, 0, None

    def tile(self, value):
        if self.count == self.refs[0].shape[0]:
            self.rest[0] = value.astype(bf16)
        elif self.even is None:
            self.even = value
        else:
            self.refs[0][self.count] = jnp.where(self.core == 0, self.even, value).astype(bf16)
            self.refs[1][self.count] = jnp.where(self.core == 0, value, self.even).astype(bf16)
            self.even = None
            self.count += 1


def turned(w):
    return tn(w, eye(D, D, bf16)).astype(bf16)


def with_ones(x):
    return jnp.concatenate([x, jnp.ones((STAT, x.shape[1]), bf16)], axis=0)


def key_value_block(normal, w_qkv, rope_ref, k, keys_ref, values_ref):
    mixed = nn(w_qkv[D:], normal)
    at = slice(k * BLOCK, (k + 1) * BLOCK)
    keys = rotate(mixed[:D], rope_ref[0:8, at], rope_ref[8:16, at])
    keys_ref[k] = keys.astype(bf16)
    values_ref[k] = mixed[D:].astype(bf16)
    return head_sizes(keys)


def query_of(normal, w_qkv, cosine, sine):
    turned = rotate(nn(w_qkv[:D], normal), cosine, sine)
    return (turned.astype(bf16).astype(f32) * HEAD_DIM**-0.5).astype(bf16)


def own_rope(rope_ref, low, high):
    def at(tile):
        return rope_ref[:, pl.ds(pl.multiple_of(tile * TILE, TILE), TILE)]

    both = jnp.where(iota((1, TILE), 1) < HALF, at(low), at(high))
    return both[0:8], both[8:16]


def own_tile(ref, low, high):
    lane = iota((1, TILE), 1)

    def at(tile):
        return ref[tile // 4, :, pl.ds(pl.multiple_of((tile % 4) * TILE, TILE), TILE)].astype(f32)

    return jnp.where(lane < HALF, at(low), at(high)).astype(bf16)


def query_bias(u, tile, block, len_ref):
    places = half_places(u, tile)
    start = doc_start(places, len_ref)
    keys = iota((1, BLOCK), 1) + block * BLOCK
    return jnp.where((keys <= places) & (keys >= start), 0.0, MASKED).astype(bf16)


def key_bias(u, tile, block, len_ref):
    keys = half_places(u, tile)
    places = iota((1, BLOCK), 1) + block * BLOCK
    start = doc_start(places, len_ref)
    return jnp.where((keys <= places) & (keys >= start), 0.0, MASKED).astype(bf16)


def scores_of(rows, columns, bias):
    return nn(rows, jnp.concatenate([columns, bias], axis=0))


def run_steps(step):
    def several(i, carry):
        for j in range(UNROLL):
            step(i * UNROLL + j)
        return carry

    lax.fori_loop(0, STEPS // UNROLL, several, 0)


def query_step(s, low, high):
    first = low // 4 + 1
    late = s >= first
    return late.astype(jnp.int32), jnp.where(late, high, low), s - jnp.where(late, first, 0)


def key_step(s, low, high):
    first = BLOCKS - low // 4
    late = s >= first
    tile = jnp.where(late, high, low)
    return late.astype(jnp.int32), tile, tile // 4 + s - jnp.where(late, first, 0)


def head_sizes(x):
    return jnp.max(jnp.sum((x * x).reshape(HEADS, HEAD_DIM, x.shape[1]), axis=1), axis=1, keepdims=True)


def attend(query, k_size, keys_ref, values_ref, len_ref, low, high, qbd, top_ref, acc_ref, q_rows_ref):
    q_rows = nt(eye(TILE, TILE, bf16), query)
    q_rows_ref[...] = q_rows.astype(bf16)
    spread(qbd, jnp.concatenate([q_rows, jnp.zeros((TILE, STAT), f32)], axis=1))
    q_size = head_sizes(query.astype(f32))
    acc_ref[...] = jnp.zeros(acc_ref.shape, f32)
    safe = jnp.max(q_size * k_size) <= SAFE * SAFE

    @pl.when(safe)
    def _():
        top_ref[...] = jnp.zeros(top_ref.shape, f32)

        def step(s):
            u, tile, block = query_step(s, low, high)
            scores = scores_of(qbd[u], with_ones(keys_ref[block]), query_bias(u, tile, block, len_ref))
            acc_ref[u] = acc_ref[u] + nt(jnp.exp(scores).astype(bf16), with_ones(values_ref[block]))

        run_steps(step)

    @pl.when(jnp.logical_not(safe))
    def _():
        top_ref[...] = jnp.full(top_ref.shape, MASKED, f32)

        def step(s, carry):
            u, tile, block = query_step(s, low, high)
            scores = scores_of(qbd[u], with_ones(keys_ref[block]), query_bias(u, tile, block, len_ref))
            old = top_ref[u]
            new = jnp.maximum(old, jnp.max(scores, axis=1, keepdims=True))
            probs = jnp.exp(scores - new)
            acc_ref[u] = acc_ref[u] * jnp.exp(old - new) + nt(probs.astype(bf16), with_ones(values_ref[block]))
            top_ref[u] = new
            return carry

        lax.fori_loop(0, STEPS, step, 0)

    attended, stats = [], []
    lane = iota((1, STAT), 1)
    for u in range(2):
        acc = acc_ref[u]
        total = acc[:, D : D + 1]
        attended.append(own_heads(acc[:, :D] / total))
        parts = two_parts(-(top_ref[u] + jnp.log(total)))
        stat = jnp.zeros((HALF, STAT), f32)
        for j in range(2):
            part = parts[j].astype(f32)
            for h in range(HEADS):
                stat = jnp.where(lane == 9 * j + h, part[h * HALF : (h + 1) * HALF], stat)
        stats.append(stat)
    att_rows = jnp.concatenate(attended, axis=0).astype(bf16)
    stat_rows = jnp.concatenate(stats, axis=0).astype(bf16)
    return nt(eye(D, D, bf16), att_rows).astype(bf16), nt(eye(STAT, STAT, bf16), stat_rows).astype(bf16)


def feed_forward(resid, attended, w_out, w_gate_up, w_down, gain):
    mid = resid + nn(w_out, attended)
    normal = (mid * norm_factor(mid) * gain).astype(bf16)
    gate_up = nn(w_gate_up, normal)
    gate = gate_up[:FF]
    hidden = (gate * jax.nn.sigmoid(gate) * gate_up[FF:]).astype(bf16)
    return mid, normal, gate_up, hidden, mid + nn(w_down, hidden)


def feed_back(grad, attended, mid, gate_up, w_out, w_gate_up, w_down, gain, stat, low_refs, traffic):
    d_out_ref, d_gate_up_ref, d_branch_ref, hidden_ref, normal_ref = low_refs
    d_out = grad.astype(bf16)
    d_hidden = tn(w_down, d_out)
    gate, up = gate_up[:FF], gate_up[FF:]
    sig = jax.nn.sigmoid(gate)
    d_gate = d_hidden * up * (sig * (1.0 + gate * (1.0 - sig)))
    d_up = d_hidden * (gate * sig)
    hidden_ref[...] = (gate * sig * up).astype(bf16)
    normal_ref[...] = (mid * norm_factor(mid) * gain).astype(bf16)
    d_gate_up = jnp.concatenate([d_gate, d_up], axis=0).astype(bf16)
    d_mid, d_gain = norm_back(mid, gain, nn(w_gate_up, d_gate_up))
    grad = grad + d_mid
    d_branch = grad.astype(bf16)
    d_att = nn(w_out, d_branch).astype(bf16)
    d_out_ref[...], d_gate_up_ref[...], d_branch_ref[...] = d_out, d_gate_up, d_branch
    traffic.send(*low_refs)
    product = d_att.astype(f32) * attended.astype(f32)
    delta = -jnp.sum(product.reshape(HEADS, HEAD_DIM, TILE), axis=1)
    delta = jnp.concatenate([delta, jnp.zeros((16 - HEADS, TILE), f32)], axis=0)
    row, col = iota((STAT, 16), 0), iota((STAT, 16), 1)
    stat = stat.astype(f32) + nn(((row == DROW - D + col) & (col < HEADS)).astype(bf16), delta.astype(bf16))
    return grad, jnp.concatenate([d_att, stat.astype(bf16)], axis=0), d_gain


def feed_grads(put, hidden, d_out, normal, d_gate_up, attended, d_branch):
    put(nt(d_out, hidden))
    put(nt(normal, d_gate_up))
    put(nt(attended, d_branch[:TILE]))
    rows = [jnp.zeros((48, TILE), bf16), d_branch[TILE:], jnp.zeros((TILE - 64, TILE), bf16)]
    return nt(attended, jnp.concatenate(rows, axis=0))


def gain_column(gains_ref, which):
    return column(gains_ref[which // 2, which % 2 : which % 2 + 1, :], D)


def first_kernel(
    traffic, raw_hours_ref, len_ref, scale_ref, lag_ref, w_lag_ref, gains_ref, w_qkv_ref, rope_ref, w_out_ref, w_gate_up_ref, w_down_ref,
    copies_ref, next_ref, next_resid_ref, keys_ref, values_ref, normal_all, lagged_ref, feats_ref, w_dense_ref, resid_ref, normal_a_ref,
    q_ref, att_ref, stat_ref, mid_ref, gate_up_ref, own_rope_ref,
    series, toeplitz, extra, qbd, top_ref, acc_ref,
):
    chip, core, low, high = geometry()
    traffic.ready(2)
    places = iota((TILES, TILE), 0) * TILE + iota((TILES, TILE), 1)
    own = doc_scale_at(places, len_ref, scale_ref)
    values = raw_hours_ref[:, 0, :] / own
    angle = raw_hours_ref[:, 1, :] * (2.0 * math.pi / 24.0)
    sine, cosine, level = jnp.sin(angle), jnp.cos(angle), jnp.log(own)
    series[0:8, :] = jnp.zeros((8, TILE), f32)
    series[8 : 8 + TILES, :] = values.astype(bf16).astype(f32)
    extra[...] = jnp.zeros(extra.shape, f32)
    for r in range(TILES):
        at = slice(r * TILE, (r + 1) * TILE)
        extra[0:1, at] = sine[r : r + 1]
        extra[1:2, at] = cosine[r : r + 1]
        extra[2:3, at] = level[r : r + 1]
    toeplitz[:, 0:MAXLAG] = jnp.zeros((TILE, MAXLAG), bf16)

    def shift(m, carry):
        window = jnp.concatenate([series[pl.ds(m + 7, 1), :], series[pl.ds(m + 8, 1), :]], axis=1)
        rolled = pltpu.roll(jnp.broadcast_to(window, (TILE, 2 * TILE)), 1, 1, stride=1, stride_axis=0)
        toeplitz[:, pl.ds(pl.multiple_of((m + 3) * TILE, TILE), TILE)] = rolled[:, TILE:].astype(bf16)
        return carry

    lax.fori_loop(0, TILES, shift, 0, unroll=4)

    traffic.ready(7)

    rows = iota((FEATS, 1), 0)
    diagonal = iota((FEATS, LAGS), 0) == iota((FEATS, LAGS), 1)
    offsets = jnp.sum(jnp.where(diagonal, lag_ref[...].astype(f32), 0.0), axis=1, keepdims=True)
    offsets = jnp.where(rows < LAGS, offsets - 1.0, (rows - LAGS + MAXLAG).astype(f32))
    chosen = (iota((FEATS, LAGCOLS), 1).astype(f32) == offsets).astype(bf16)
    w_dense = nn(w_lag_ref[...], chosen).astype(bf16)
    w_dense_ref[...] = w_dense

    gain_a, gain_b = gain_column(gains_ref, 0), gain_column(gains_ref, 1)
    w_qkv = turned(w_qkv_ref[...])
    lag_rows = iota((TILE, 1), 0) + 1
    k_size = jnp.zeros((HEADS, 1), f32)
    for k in range(BLOCKS):
        place = iota((1, BLOCK), 1) + k * BLOCK
        start = doc_start(place, len_ref)
        parts = []
        for b in range(3):
            at = MAXLAG + k * BLOCK - b * TILE
            lagged = toeplitz[:, at : at + BLOCK]
            if k in (0, BLOCKS - 1):
                valid = place - (lag_rows + b * TILE) >= start
                lagged = jnp.where(valid, lagged.astype(f32), 0.0).astype(bf16)
            parts.append(lagged)
        parts.append(extra[:, k * BLOCK : (k + 1) * BLOCK].astype(bf16))
        resid = nn(w_dense, jnp.concatenate(parts, axis=0))
        normal = (resid * norm_factor(resid) * gain_a).astype(bf16)
        normal_all[k] = normal
        k_size = jnp.maximum(k_size, key_value_block(normal, w_qkv, rope_ref, k, keys_ref, values_ref))

    cosine, sine = own_rope(rope_ref, low, high)
    own_rope_ref[0:8], own_rope_ref[8:16] = cosine, sine
    traffic.send(keys_ref, values_ref, normal_all, w_dense_ref, own_rope_ref)

    place = own_places(low, high)
    start = doc_start(place, len_ref)
    lane = iota((1, TILE), 1)

    def tile_of(ref, tile):
        return ref[:, pl.ds(pl.multiple_of(tile * TILE, TILE), TILE)].astype(f32)

    for b in range(3):
        lagged = jnp.where(lane < HALF, tile_of(toeplitz, low + 3 - b), tile_of(toeplitz, high + 3 - b))
        valid = place - (lag_rows + b * TILE) >= start
        lagged_ref[b * TILE : (b + 1) * TILE, :] = jnp.where(valid, lagged, 0.0).astype(bf16)
    lagged_ref[MAXLAG:, :] = jnp.where(lane < HALF, tile_of(extra, low), tile_of(extra, high)).astype(bf16)
    lagged = lagged_ref[...]
    feats_ref[0:FEATS, :] = nn(chosen, lagged)
    feats_ref[FEATS:, :] = jnp.zeros((96 - FEATS, TILE), f32)
    resid = nn(w_dense, lagged)
    resid_ref[...] = resid
    normal = (resid * norm_factor(resid) * gain_a).astype(bf16)
    normal_a_ref[...] = normal
    traffic.send(lagged_ref, feats_ref, resid_ref, normal_a_ref)
    query = query_of(normal, w_qkv, cosine, sine)
    attended, stat_ref[...] = attend(query, k_size, keys_ref, values_ref, len_ref, low, high, qbd, top_ref, acc_ref, q_ref)
    att_ref[...] = attended
    traffic.send(q_ref, att_ref, stat_ref)
    traffic.ready()
    mid, _, gate_up, _, resid = feed_forward(
        resid, attended, turned(w_out_ref[...]), turned(w_gate_up_ref[...]), w_down_ref[...], gain_b
    )
    mid_ref[...], gate_up_ref[...] = mid, gate_up
    traffic.send(mid_ref, gate_up_ref)
    next_resid_ref[...] = resid
    normal = (resid * norm_factor(resid) * gain_column(gains_ref, 2)).astype(bf16)
    next_ref[...] = normal
    copies_ref[...] = jnp.broadcast_to(normal[None], copies_ref.shape)


def natural_tiles(own_ref, other_ref, put):
    _, core, _, _ = geometry()
    mine = (iota((1, TILE), 1) < HALF) == (core == 0)
    for chip in range(TILES // 2):
        tile = 2 * chip if chip < 8 else TILES - 1 - 2 * chip
        own, other = own_ref[chip].astype(f32), other_ref[chip].astype(f32)
        for t, value in ((tile, jnp.where(mine, own, other)), (TILES - 1 - tile, jnp.where(mine, other, own))):
            put(t // 4, slice(t % 4 * TILE, (t % 4 + 1) * TILE), value.astype(bf16))


def second_kernel(
    traffic, own_ref, other_ref, len_ref, turned_qkv_ref, rope_ref, normal_ref, own_rope_ref, cot_own_ref, cot_other_ref, resid_in_ref,
    turned_out_ref, turned_gate_up_ref, w_out_ref, w_gate_up_ref, w_down_ref, gains_ref,
    copies_ref, payload_ref, act_ref, keys_ref, values_ref, normal_all, q_ref, grad_ref, att_ref, d_gain_ref,
    d_out_ref, d_gate_up_ref, d_branch_ref, hidden_ref, normal_b_ref,
    qbd, top_ref, acc_ref,
):
    chip, core, low, high = geometry()

    def put(block, columns, value):
        normal_all[block, :, columns] = value

    natural_tiles(own_ref, other_ref, put)
    traffic.send(normal_all)
    traffic.ready(5)
    w_qkv = turned_qkv_ref[...]
    k_size = jnp.zeros((HEADS, 1), f32)
    for k in range(BLOCKS):
        k_size = jnp.maximum(k_size, key_value_block(normal_all[k], w_qkv, rope_ref, k, keys_ref, values_ref))
    traffic.send(keys_ref, values_ref)
    query = query_of(normal_ref[...], w_qkv, own_rope_ref[0:8], own_rope_ref[8:16])
    attended, stat = attend(query, k_size, keys_ref, values_ref, len_ref, low, high, qbd, top_ref, acc_ref, q_ref)
    traffic.ready()
    gain = gain_column(gains_ref, 3)
    w_out, w_gate_up, w_down = w_out_ref[...], w_gate_up_ref[...], w_down_ref[...]
    mid, _, gate_up, _, out = feed_forward(
        resid_in_ref[...], attended, turned_out_ref[...], turned_gate_up_ref[...], w_down, gain
    )
    act_ref[...] = out
    att_ref[...] = attended
    traffic.send(act_ref, att_ref, q_ref)
    grad = tile_halves(cot_own_ref[...].astype(f32), cot_other_ref[...].astype(f32))
    low_refs = (d_out_ref, d_gate_up_ref, d_branch_ref, hidden_ref, normal_b_ref)
    grad, payload, d_gain_ref[...] = feed_back(grad, attended, mid, gate_up, w_out, w_gate_up, w_down, gain, stat, low_refs, traffic)
    grad_ref[...] = grad
    payload_ref[...] = payload
    copies_ref[...] = jnp.broadcast_to(payload[None], copies_ref.shape)


def query_back(
    traffic, count, payload_ref, q_ref, len_ref, own_rope_ref, rope_ref, keys_ref, values_ref, normal_all, w_qkv_ref, dq_ref, qall_ref,
    k_rows_ref, v_rows_ref, qbd, dbd, acc_ref,
):
    chip, core, low, high = geometry()
    traffic.ready(count)
    unit = eye(TILE, TILE, bf16)
    rows = nt(unit, payload_ref[...])
    spread(qbd, jnp.concatenate([q_ref[...].astype(f32), rows[:, D:]], axis=1), LROW, LROW + 9)
    spread(dbd, rows, DROW)
    k_rows_ref[...] = nt(unit, own_tile(keys_ref, low, high)).astype(bf16)
    v_rows_ref[...] = nt(unit, own_tile(values_ref, low, high)).astype(bf16)
    w_qkv = w_qkv_ref[...]
    for k in range(BLOCKS):
        at = slice(k * BLOCK, (k + 1) * BLOCK)
        qall_ref[k] = query_of(normal_all[k], w_qkv, rope_ref[0:8, at], rope_ref[8:16, at])
    traffic.send(k_rows_ref, v_rows_ref, qall_ref)
    acc_ref[...] = jnp.zeros(acc_ref.shape, f32)

    def step(s):
        u, tile, block = query_step(s, low, high)
        scores = scores_of(qbd[u], with_ones(keys_ref[block]), query_bias(u, tile, block, len_ref))
        d_scores = jnp.exp(scores) * nn(dbd[u], with_ones(values_ref[block]))
        acc_ref[u] = acc_ref[u] + nt(d_scores.astype(bf16), keys_ref[block])

    run_steps(step)
    d_query = jnp.concatenate([own_heads(acc_ref[0]), own_heads(acc_ref[1])], axis=0) * HEAD_DIM**-0.5
    dq_ref[...] = rotate(turned_rows(d_query), own_rope_ref[0:8], -own_rope_ref[8:16])


def turned_rows(x):
    hi, lo = two_parts(x)
    unit = eye(D, D, bf16)
    return nt(unit, hi) + nt(unit, lo)


def key_back(traffic, count, own_ref, other_ref, len_ref, qall_ref, k_rows_ref, v_rows_ref, dq_ref, grad_ref, resid_ref, w_qkv_ref, gain,
             own_rope_ref, daug, kbd, vbd, dk_ref, dv_ref):
    chip, core, low, high = geometry()

    def put(block, columns, value):
        daug[block, :, columns] = value

    natural_tiles(own_ref, other_ref, put)
    traffic.ready(count)
    ones = jnp.ones((TILE, STAT), f32)
    spread(kbd, jnp.concatenate([k_rows_ref[...].astype(f32), ones], axis=1), LROW, LROW + 9)
    spread(vbd, jnp.concatenate([v_rows_ref[...].astype(f32), ones], axis=1), DROW)
    dk_ref[...] = jnp.zeros(dk_ref.shape, f32)
    dv_ref[...] = jnp.zeros(dv_ref.shape, f32)

    def step(s):
        u, tile, block = key_step(s, low, high)
        queries = jnp.concatenate([qall_ref[block], daug[block, D:AUG, :]], axis=0)
        probs = jnp.exp(scores_of(kbd[u], queries, key_bias(u, tile, block, len_ref)))
        d_scores = probs * nn(vbd[u], daug[block])
        dv_ref[u] = dv_ref[u] + nt(probs.astype(bf16), daug[block])
        dk_ref[u] = dk_ref[u] + nt(d_scores.astype(bf16), qall_ref[block])

    run_steps(step)
    traffic.ready()
    d_key = turned_rows(jnp.concatenate([own_heads(dk_ref[0]), own_heads(dk_ref[1])], axis=0))
    d_value = nt(eye(D, D, bf16), jnp.concatenate([own_heads(dv_ref[0]), own_heads(dv_ref[1])], axis=0).astype(bf16))
    d_key = rotate(d_key, own_rope_ref[0:8], -own_rope_ref[8:16])
    d_mixed = jnp.concatenate([dq_ref[...], d_key, d_value], axis=0).astype(bf16)
    d_in, d_gain = norm_back(resid_ref[...], gain(), nn(w_qkv_ref[...], d_mixed))
    return grad_ref[...] + d_in, d_mixed, d_gain


def projection_grads(normal, d_mixed):
    tail = nt(normal, jnp.concatenate([d_mixed[MAXLAG:], jnp.zeros((TILE - 48, TILE), bf16)], axis=0))
    return nt(normal, d_mixed[:MAXLAG]), tail


def third_kernel(
    traffic, own_ref, other_ref, len_ref, qall_ref, k_rows_ref, v_rows_ref, dq_ref, grad_in_ref, resid_ref, att_ref, stat_ref, mid_ref,
    gate_up_ref, own_rope_ref, w_qkv_ref, w_out_ref, w_gate_up_ref, w_down_ref, gains_ref,
    copies_ref, payload_ref, grad_ref, d_mixed_ref, d_gain_a_ref, d_gain_b_ref, d_out_ref, d_gate_up_ref, d_branch_ref, hidden_ref,
    normal_b_ref,
    daug, kbd, vbd, dk_ref, dv_ref,
):
    grad, d_mixed_ref[...], d_gain_a_ref[...] = key_back(
        traffic, 4, own_ref, other_ref, len_ref, qall_ref, k_rows_ref, v_rows_ref, dq_ref, grad_in_ref, resid_ref, w_qkv_ref,
        lambda: gain_column(gains_ref, 2), own_rope_ref, daug, kbd, vbd, dk_ref, dv_ref,
    )
    low_refs = (d_out_ref, d_gate_up_ref, d_branch_ref, hidden_ref, normal_b_ref)
    grad, payload, d_gain_b_ref[...] = feed_back(
        grad, att_ref[...], mid_ref[...], gate_up_ref[...], w_out_ref[...], w_gate_up_ref[...], w_down_ref[...], gain_column(gains_ref, 1),
        stat_ref[...], low_refs, traffic,
    )
    grad_ref[...] = grad
    payload_ref[...] = payload
    copies_ref[...] = jnp.broadcast_to(payload[None], copies_ref.shape)


def second_window_kernel(
    traffic, len_ref, hidden_ref, d_out_ref, normal_ref, d_gate_up_ref, att_ref, d_branch_ref, d_gain_ref, payload_ref, q_ref,
    own_rope_ref, rope_ref, keys_ref, values_ref, normal_all, w_qkv_ref,
    pack_ref, tail_ref, dq_ref, qall_ref, k_rows_ref, v_rows_ref, qbd, dbd, acc_ref,
):
    traffic.ready(8)
    tail = feed_grads(
        Tiles(pack_ref), hidden_ref[...], d_out_ref[...], normal_ref[...], d_gate_up_ref[...], att_ref[...], d_branch_ref[...]
    )
    tail_ref[...] = jnp.where(iota((1, TILE), 1) == 99, d_gain_ref[...], tail)
    traffic.send(pack_ref, tail_ref)
    query_back(
        traffic, 16, payload_ref, q_ref, len_ref, own_rope_ref, rope_ref, keys_ref, values_ref, normal_all, w_qkv_ref, dq_ref, qall_ref,
        k_rows_ref, v_rows_ref, qbd, dbd, acc_ref,
    )


def third_window_kernel(
    traffic, len_ref, pack_in_ref, tail_in_ref, normal_a_ref, d_mixed_ref, d_gain_a_ref, hidden_ref, d_out_ref, normal_ref, d_gate_up_ref,
    att_ref, d_branch_ref, d_gain_b_ref, payload_ref, q_ref, own_rope_ref, rope_ref, keys_ref, values_ref, normal_all,
    w_qkv_ref,
    keep_ref, send_ref, rest_ref, tail0_ref, tail1_ref, dq_ref, qall_ref, k_rows_ref, v_rows_ref, qbd, dbd, acc_ref,
):
    traffic.ready(13)
    put = Pairs(lax.axis_index("tm") % 2, keep_ref, send_ref, rest_ref)
    for t in range(pack_in_ref.shape[0]):
        put.tile(pack_in_ref[t].astype(f32))
    head, tail = projection_grads(normal_a_ref[...], d_mixed_ref[...])
    put(head)
    tail0_ref[...] = feed_grads(
        put, hidden_ref[...], d_out_ref[...], normal_ref[...], d_gate_up_ref[...], att_ref[...], d_branch_ref[...]
    )
    lane = iota((1, TILE), 1)
    tail = jnp.where(lane == 98, d_gain_a_ref[...], tail + tail_in_ref[...])
    tail1_ref[...] = jnp.where(lane == 97, d_gain_b_ref[...], tail)
    traffic.send(keep_ref, send_ref, rest_ref, tail0_ref, tail1_ref)
    query_back(
        traffic, 21, payload_ref, q_ref, len_ref, own_rope_ref, rope_ref, keys_ref, values_ref, normal_all, w_qkv_ref, dq_ref, qall_ref,
        k_rows_ref, v_rows_ref, qbd, dbd, acc_ref,
    )


def last_kernel(
    traffic, own_ref, other_ref, len_ref, scale_ref, ids_ref, qall_ref, k_rows_ref, v_rows_ref, dq_ref, grad_in_ref, resid_ref,
    normal_a_ref, tail0_ref, tail1_ref, rest_ref, w_dense_ref, feats_ref, own_rope_ref, w_qkv_ref, gains_ref,
    keep_ref, send_ref, daug, kbd, vbd, dk_ref, dv_ref, raw_ref,
):
    chip, core, low, high = geometry()
    d_first, d_mixed, d_gain = key_back(
        traffic, 6, own_ref, other_ref, len_ref, qall_ref, k_rows_ref, v_rows_ref, dq_ref, grad_in_ref, resid_ref, w_qkv_ref,
        lambda: gain_column(gains_ref, 0), own_rope_ref, daug, kbd, vbd, dk_ref, dv_ref,
    )
    head, tail0 = projection_grads(normal_a_ref[...], d_mixed)
    d_first = d_first.astype(bf16)
    feats = feats_ref[...].astype(bf16)
    empty = jnp.zeros((64, TILE), bf16)
    tail0 = tail0 + tail0_ref[...] + nt(d_first, jnp.concatenate([empty, feats[:64]], axis=0))
    tail1 = tail1_ref[...] + nt(d_first, jnp.concatenate([empty, feats[64:], empty[:32]], axis=0))
    lane, row = iota((1, TILE), 1), iota((D, 1), 0)
    tail1 = jnp.where(lane == 96, d_gain, tail1)
    sums, counts = jnp.zeros((D, 1), f32), jnp.zeros((D, 1), f32)
    owner = (lax.axis_index("tm") == 0).astype(f32)
    for d in range(DOCS):
        hit = jnp.where(row == ids_ref[d], owner, 0.0)
        sums, counts = sums + hit * scale_ref[d], counts + hit
    high_part = sums.astype(bf16).astype(f32)
    tail1 = jnp.where(lane == 100, high_part, tail1)
    tail1 = jnp.where(lane == 101, sums - high_part, tail1)
    tail1 = jnp.where(lane == 102, counts, tail1)

    place = own_places(low, high)
    start = doc_start(place, len_ref)
    own = doc_scale_at(place, len_ref, scale_ref)
    flip = (iota((TILE, TILE), 0) + iota((TILE, TILE), 1) == TILE - 1).astype(bf16)
    raw_ref[...] = jnp.zeros(raw_ref.shape, f32)
    lags = TILE - iota((TILE, 1), 0)
    for b in range(3):
        weights = nn(w_dense_ref[:, b * TILE : (b + 1) * TILE], flip).astype(bf16)
        d_lagged = tn(weights, d_first)
        valid = place - (lags + b * TILE) >= start
        d_lagged = jnp.where(valid, d_lagged, 0.0) / own
        for u in range(2):
            half = jnp.where((lane < HALF) == (u == 0), d_lagged, 0.0)
            wide = jnp.concatenate([jnp.zeros((TILE, TILE), f32), half], axis=1)
            rolled = pltpu.roll(wide, TILE, 1, stride=1, stride_axis=0)
            total = jnp.sum(rolled, axis=0, keepdims=True)
            for tile, part in (((low if u == 0 else high) - b + 16, total[:, TILE:]), ((low if u == 0 else high) - b + 15, total[:, :TILE])):
                at = tile % 2, pl.ds(tile // 2, 1)
                raw_ref[at] = raw_ref[at] + part

    put = Pairs(core, keep_ref, send_ref)
    put.tile(rest_ref[0].astype(f32))
    for part in (head, tail0, tail1):
        put(part)
    for k in range(2):
        put.tile(raw_ref[k, 8:24, :])


def summed(in_ref):
    count, rows, _ = in_ref.shape
    total = jnp.zeros((rows, TILE), f32)
    return lax.fori_loop(0, count // 8, lambda i, t: t + jnp.sum(in_ref[pl.ds(i * 8, 8)].astype(f32), axis=0), total)


def pair_sum_kernel(early_ref, early_in_ref, late_ref, late_in_ref, out_ref):
    zero = jnp.zeros((16, TILE), bf16)
    late = late_ref.shape[0] - 1
    series = lax.axis_index("series")
    out_ref[:, 32:40, :] = jnp.zeros((64, 8, TILE), bf16)

    def both(ref, in_ref, t):
        return ref[t].astype(f32) + in_ref[t].astype(f32)

    for t in range(128):
        value = zero
        if t < EARLY:
            value = both(early_ref, early_in_ref, t).astype(bf16)
        elif t < EARLY + late:
            value = both(late_ref, late_in_ref, t - EARLY).astype(bf16)
        out_ref[t // 2, t % 2 * 16 : t % 2 * 16 + 16, :] = value
    raw = both(late_ref, late_in_ref, late)
    for c in range(16):
        line = jnp.where(iota((8, 1), 0) == 0, raw[c : c + 1], 0.0)
        out_ref[series * 16 + c, 32:40, :] = line.astype(bf16)


def sum_kernel(in_ref, out_ref, raw_ref):
    total = summed(in_ref)
    out_ref[...] = jnp.broadcast_to(total[:32].astype(bf16)[None], out_ref.shape)
    raw_ref[...] = total[32:33]


def unpack_kernel(own_ref, other_ref, act_in_ref, act_ref, lag_ref, qkv_ref, out_ref, gate_up_ref, down_ref, gains_ref, scale_ref):
    core = lax.axis_index("tm") % 2
    act_ref[...] = act_in_ref[...]

    def tile(t):
        at = t // 4, slice(t // 2 % 2 * 16, t // 2 % 2 * 16 + 16)
        return jnp.where(core == t % 2, own_ref[at].astype(f32), other_ref[at].astype(f32))

    def columns(first, count):
        return [jnp.concatenate([tile(first + 9 * c + r) for r in range(9)], axis=0) for c in range(count)]

    layers = ((207, 234, 117), (90, 243, 0))
    tails = []
    for layer, (at_qkv, at_tail, at_rest) in enumerate(layers):
        for c, part in enumerate(columns(at_qkv, 3)):
            qkv_ref[layer, :, c * TILE : (c + 1) * TILE] = part
        tail = columns(at_tail, 1)[0]
        tails.append(tail)
        qkv_ref[layer, :, MAXLAG:] = tail[:, :48]
        for c, part in enumerate(columns(at_rest, 3)):
            down_ref[layer, :, c * TILE : (c + 1) * TILE] = part
        for c, part in enumerate(columns(at_rest + 27, 6)):
            gate_up_ref[layer, :, c * TILE : (c + 1) * TILE] = part
        out_ref[layer, :, :TILE] = columns(at_rest + 81, 1)[0]
        out_ref[layer, :, TILE:] = tail[:, 48:64]
    lag = jnp.where(iota((1, TILE), 1) < 64, pltpu.roll(tails[0], 64, 1), tails[1])
    lag_ref[...] = lag[:, :FEATS]
    pick = (iota((8, TILE), 1) == iota((8, TILE), 0) + 96).astype(bf16)
    rest = nt(pick, tails[1].astype(bf16))
    gains_ref[0] = rest[0:2]
    gains_ref[1] = rest[2:4]
    scale_ref[...] = ((rest[4:5] + rest[5:6]) / rest[6:7])[:, :DATASETS]


def weights_kernel(traffic, cot_ref, w_qkv_ref, w_out_ref, w_gate_up_ref, low_cot_ref, qkv_ref, out_ref, gate_up_ref, first_qkv_ref):
    traffic.ready(1)
    low_cot_ref[...] = cot_ref[...].astype(bf16)
    traffic.send(low_cot_ref)
    traffic.ready()
    qkv_ref[...] = turned(w_qkv_ref[1])
    first_qkv_ref[...] = turned(w_qkv_ref[0])
    out_ref[...] = turned(w_out_ref[...])
    gate_up_ref[...] = turned(w_gate_up_ref[...])


def first_values_kernel(traffic, raw_ref, hours_ref, out_ref):
    traffic.ready()
    both = jnp.concatenate([raw_ref[...], hours_ref[...].astype(f32)], axis=0)
    out_ref[...] = jnp.broadcast_to(both[None], out_ref.shape)


def shape(*dims, dtype=f32):
    return jax.ShapeDtypeStruct(dims, dtype)


class Traffic:
    def __init__(self, loads, stores):
        self.loads, self.stores, self.waited, self.sent = loads, stores, 0, set()
        for copy in loads:
            copy.start()

    def ready(self, count=None):
        count = len(self.loads) if count is None else count
        for copy in self.loads[self.waited : count]:
            copy.wait()
        self.waited = max(self.waited, count)

    def send(self, *refs):
        for ref, copy in self.stores:
            if any(ref is r for r in refs):
                copy.start()
                self.sent.add(id(copy))

    def finish(self):
        self.ready()
        for _, copy in self.stores:
            if id(copy) not in self.sent:
                copy.start()
        for _, copy in self.stores:
            copy.wait()


def call(kernel, operands, outs, scratch=(), tables=(), weights=(), cost=None):
    several = isinstance(outs, list)
    outs = outs if several else [outs]
    layers = [None] * len(tables) + [x[1] if isinstance(x, tuple) else None for x in weights]
    fetched = (*tables, *(x[0] if isinstance(x, tuple) else x for x in weights))
    shapes = [x.shape if layer is None else x.shape[1:] for x, layer in zip(fetched, layers)]
    buffers = [(pltpu.SMEM if n < len(tables) else pltpu.VMEM)(shapes[n], x.dtype) for n, x in enumerate(fetched)]
    is_far = [not isinstance(out, jax.ShapeDtypeStruct) for out in outs]
    buffers += [pltpu.VMEM(out.shape, out.dtype) for out, far in zip(outs, is_far) if far]
    count, extra, copies = len(operands), len(buffers), len(buffers)

    def wrapped(*refs):
        refs = list(refs)
        ins, sources = refs[:count], refs[count : count + len(fetched)]
        results = refs[count + len(fetched) : count + len(fetched) + len(outs)]
        rest = refs[count + len(fetched) + len(outs) :]
        if not copies:
            kernel(*ins, *results, *rest)
            return
        own, held, sems = rest[: len(scratch)], rest[len(scratch) : -1], rest[-1]
        sources = [a if layer is None else a.at[layer] for a, layer in zip(sources, layers)]
        loads = [pltpu.make_async_copy(a, b, sems.at[n]) for n, (a, b) in enumerate(zip(sources, held))]
        stores, at = [], len(fetched)
        for n, far in enumerate(is_far):
            if far:
                stores.append((held[at], pltpu.make_async_copy(held[at], results[n], sems.at[at])))
                results[n] = held[at]
                at += 1
        traffic = Traffic(loads, stores)
        kernel(traffic, *ins, *held[: len(fetched)], *results, *own)
        traffic.finish()

    vmem, hbm = pl.BlockSpec(memory_space=pltpu.VMEM), pl.BlockSpec(memory_space=pltpu.HBM)
    results = pl.pallas_call(
        wrapped,
        out_shape=outs,
        in_specs=[vmem] * count + [hbm] * len(fetched),
        out_specs=[hbm if far else vmem for far in is_far],
        scratch_shapes=[*scratch, *buffers, pltpu.SemaphoreType.DMA((copies,))] if copies else list(scratch),
        compiler_params=pltpu.CompilerParams(vmem_limit_bytes=VMEM),
        cost_estimate=cost and pl.CostEstimate(flops=cost * 10**9, bytes_accessed=10**6, transcendentals=0),
    )(*operands, *(pltpu.with_memory_space_constraint(x, pltpu.HBM) for x in fetched))
    return results if several else results[0]


def pair_permute(x, bit):
    return lax.ppermute(x, "tm", [(i, i ^ bit) for i in range(32)])


def gather(copies, beside):
    groups = [[2 * chip + core for chip in range(16)] for core in range(2)]
    own = lax.all_to_all(copies, "tm", 0, 0, axis_index_groups=groups)
    own, beside = lax.optimization_barrier((own, beside))
    return own, pair_permute(own, 1), beside


def swap(block):
    return lax.ppermute(block, "tm", [(n, n if n % 2 == 0 else 32 - n) for n in range(32)])


def tile_halves(own, other):
    lane = iota((1, TILE), 1) < HALF
    return jnp.where(lane == (lax.axis_index("tm") < 16), own, other)


def rope_table():
    freqs = 10000.0 ** (-np.arange(8, dtype=np.float64) / 8)
    angle = np.arange(LEN, dtype=np.float64)[None, :] * freqs[:, None]
    return np.concatenate([np.cos(angle), np.sin(angle)], axis=0).astype(np.float32)


def body(
    raw_values, hours, doc_lengths, doc_scale, dataset_ids, lag_offsets, w_lag, w_qkv, w_out, w_gate_up, w_down, gains, cotangent
):
    lengths, scales, ids = doc_lengths.reshape(DOCS), doc_scale.reshape(DOCS), dataset_ids.reshape(DOCS)
    def low(*dims):
        return shape(*dims, dtype=bf16)

    def far(*dims, dtype=f32):
        return pltpu.HBM(dims, dtype)

    def far_low(*dims):
        return far(*dims, dtype=bf16)

    w_lag, w_down, lags = w_lag.T, w_down.transpose(0, 2, 1), lag_offsets.reshape(1, LAGS)
    rope = jnp.asarray(rope_table())
    values = lax.all_to_all(call(first_values_kernel, (), shape(32, 2, TILE), weights=(raw_values, hours)), "tm", 0, 0)
    all_d = far_low(BLOCKS, D, BLOCK)
    mine, mine_low, ff_low, column_shape = far(D, TILE), far_low(D, TILE), far_low(FF, TILE), far(D, 1)
    payload_shapes = [far_low(16, AUG, TILE), far_low(AUG, TILE)]
    low_grads = [mine_low, far_low(2 * FF, TILE), mine_low, ff_low, mine_low]
    bd, wide_bd = pltpu.VMEM((2, ROWS, AUG), bf16), pltpu.VMEM((2, ROWS, WIDE), bf16)
    acc, acc_d = pltpu.VMEM((2, ROWS, AUG), f32), pltpu.VMEM((2, ROWS, D), f32)
    top = pltpu.VMEM((2, ROWS, 1), f32)
    back_scratch = [pltpu.VMEM((BLOCKS, AUG, BLOCK), bf16), wide_bd, bd, acc_d, acc]

    (copies, next1, resid1, keys0, values0, normal_all0, lagged, feats, w_dense, resid0, normal_a0, q0, att0, stat0, mid0, gate_up0,
     own_rope) = call(
        first_kernel,
        (values,),
        [far_low(16, D, TILE), mine_low, mine, all_d, all_d, all_d, far_low(LAGCOLS, TILE), far(96, TILE), far_low(D, LAGCOLS), mine,
         mine_low, far_low(TILE, D), mine_low, far_low(STAT, TILE), mine, far(2 * FF, TILE), far(16, TILE)],
        [pltpu.VMEM((8 + TILES, TILE), f32), pltpu.VMEM((TILE, MAXLAG + LEN), bf16), pltpu.VMEM((16, LEN), f32), wide_bd, top, acc],
        tables=(lengths, scales), weights=(lags, w_lag, gains, (w_qkv, 0), rope, (w_out, 0), (w_gate_up, 0), (w_down, 0)),
    )

    low_cot, turned_qkv, turned_out, turned_gate_up, turned_qkv0 = call(
        weights_kernel, (), [mine_low, far_low(3 * D, D), far_low(D, D), far_low(2 * FF, D), far_low(3 * D, D)],
        weights=(cotangent[0].T, w_qkv, (w_out, 1), (w_gate_up, 1)),
    )
    own, other, cot = gather(copies, swap(low_cot))
    copies, payload, act, keys1, values1, normal_all1, q1, grad, att1, d_gain_b1, *low1 = call(
        second_kernel,
        (own, other),
        [*payload_shapes, mine, all_d, all_d, all_d, far_low(TILE, D), mine, mine_low, column_shape, *low_grads],
        [wide_bd, top, acc],
        tables=(lengths,),
        weights=(turned_qkv, rope, next1, own_rope, cot, pair_permute(cot, 1), resid1, turned_out, turned_gate_up, (w_out, 1),
                 (w_gate_up, 1), (w_down, 1), gains),
    )

    rows_low = far_low(TILE, D)
    side_shapes = [mine, all_d, rows_low, rows_low]
    d_out, d_gate_up, d_branch, hidden, normal_b = low1
    pack, tail, dq, qall, k_rows, v_rows = call(
        second_window_kernel, (), [far_low(90, 16, TILE), mine, *side_shapes], [wide_bd, bd, acc_d],
        tables=(lengths,),
        weights=(hidden, d_out, normal_b, d_gate_up, att1, d_branch, d_gain_b1, payload, q1, own_rope, rope, keys1, values1, normal_all1,
                 turned_qkv), cost=8,
    )
    own, other, dq = gather(copies, dq)
    copies, payload, grad, d_mixed, d_gain_a1, d_gain_b0, *low0 = call(
        third_kernel,
        (own, other),
        [*payload_shapes, mine, far_low(3 * D, TILE), column_shape, column_shape, *low_grads],
        back_scratch,
        tables=(lengths,),
        weights=(qall, k_rows, v_rows, dq, grad, resid1, att0, stat0, mid0, gate_up0, own_rope, (w_qkv, 1), (w_out, 0), (w_gate_up, 0),
                 (w_down, 0), gains),
    )
    d_out, d_gate_up, d_branch, hidden, normal_b = low0
    early, early_out, rest, tail0, tail1, dq, qall, k_rows, v_rows = call(
        third_window_kernel, (),
        [far_low(EARLY, 16, TILE), far_low(EARLY, 16, TILE), far_low(1, 16, TILE), mine, mine, *side_shapes], [wide_bd, bd, acc_d],
        tables=(lengths,),
        weights=(pack, tail, next1, d_mixed, d_gain_a1, hidden, d_out, normal_b, d_gate_up, att0, d_branch, d_gain_b0, payload, q0,
                 own_rope, rope, keys0, values0, normal_all0, turned_qkv0), cost=8,
    )
    own, other, (dq, early_in) = gather(copies, (dq, pair_permute(early_out, 1)))
    late, late_out = call(
        last_kernel,
        (own, other),
        [low(LATE, 16, TILE)] * 2,
        [*back_scratch, pltpu.VMEM((2, 24, TILE), f32)],
        tables=(lengths, scales, ids),
        weights=(qall, k_rows, v_rows, dq, grad, resid0, normal_a0, tail0, tail1, rest, w_dense, feats, own_rope, (w_qkv, 0), gains),
    )
    packed = call(pair_sum_kernel, (early, early_in, late, pair_permute(late_out, 1)), low(64, 40, TILE))
    same_core = [[2 * chip + core for chip in range(64)] for core in range(2)]
    parts = lax.all_to_all(packed, ("series", "tm"), 0, 0, axis_index_groups=same_core)
    share, raw_grad = call(sum_kernel, (parts,), [low(64, 32, TILE), shape(1, TILE)])
    share, act = lax.optimization_barrier((share, act))
    own = lax.all_to_all(share, ("series", "tm"), 0, 0, axis_index_groups=same_core)
    own, act = lax.optimization_barrier((own, swap(tile_halves(act, pair_permute(act, 1)))))
    act, g_lag, g_qkv, g_out, g_gate_up, g_down, g_gains, scale = call(
        unpack_kernel,
        (own, pair_permute(own, 1), act),
        [shape(D, TILE), shape(D, FEATS), shape(LAYERS, D, 3 * D), shape(LAYERS, D, D), shape(LAYERS, D, 2 * FF), shape(LAYERS, D, FF),
         shape(LAYERS, 2, D), shape(1, DATASETS)],
    )
    return (
        act.T[None], raw_grad, scale.reshape(DATASETS), g_lag.T, g_qkv, g_out, g_gate_up, g_down.transpose(0, 2, 1), g_gains,
    )


def solution(mesh):
    placed = (
        P("series", "tm"),
        P("series", "tm"),
        P("series", None),
        P("series", None),
        P("series", None, None),
        P(),
        P(),
        P(),
        P(),
        P(),
        P(),
        P(),
        P("series", "tm", None),
    )
    return jax.shard_map(
        body,
        mesh=mesh,
        in_specs=placed,
        out_specs=(P("series", "tm", None), P("series", "tm"), P(), P(), P(), P(), P(), P(), P()),
        check_vma=False,
    )
```

```python
import math

import jax
import jax.numpy as jnp
import numpy as np
from jax import lax
from jax.experimental import pallas as pl
from jax.experimental.pallas import tpu as pltpu
from jax.sharding import PartitionSpec as P


D = 144
HEADS = 9
HEAD_DIM = 16
FF = 384
LAGS = 84
LAYERS = 2
DATASETS = 8
DOCS = 7
LEN = 4096
MAXLAG = 384
FEATS = 87
EPSILON = 1e-06
MASKED = -1e30
AUG = 176
STAT = AUG - D
LROW = D
DROW = D + 18
BLOCK = 512
BLOCKS = LEN // BLOCK
TILE = 128
TILES = LEN // TILE
STEPS = BLOCKS + 1
SHIFTED = 8
UNROLL = 4
HALF = 64
ROWS = HEADS * HALF
LAGCOLS = 400
EARLY = 103
LATE = 24
WIDE = AUG + HALF
SAFE = 40.0
VMEM = 28 * 2**20

bf16 = jnp.bfloat16
f32 = jnp.float32
HIGH = lax.Precision.HIGHEST


def nn(a, b, precision=None):
    return lax.dot_general(a, b, (((1,), (0,)), ((), ())), precision=precision, preferred_element_type=f32)


def nt(a, b, precision=None):
    return lax.dot_general(a, b, (((1,), (1,)), ((), ())), precision=precision, preferred_element_type=f32)


def tn(a, b, precision=None):
    return lax.dot_general(a, b, (((0,), (0,)), ((), ())), precision=precision, preferred_element_type=f32)


def iota(shape, dim):
    return lax.broadcasted_iota(jnp.int32, shape, dim)


def eye(rows, cols, dtype):
    return (iota((rows, cols), 0) == iota((rows, cols), 1)).astype(dtype)


def column(row, size):
    keep = iota((size, size), 0) == iota((size, size), 1)
    return jnp.sum(jnp.where(keep, row, 0.0), axis=1, keepdims=True)


def pair_of(chip):
    return jnp.where(chip < 8, 2 * chip, TILES - 1 - 2 * chip)


def geometry():
    index = lax.axis_index("tm")
    chip, core = index // 2, index % 2
    tile = pair_of(chip)
    low = jnp.where(core == 0, tile, TILES - 1 - tile)
    return chip, core, low, TILES - 1 - low


def doc_start(places, len_ref):
    start = jnp.zeros_like(places)
    end = jnp.int32(0)
    for d in range(DOCS):
        end = end + len_ref[d]
        start = jnp.where(places >= end, end, start)
    return start


def doc_scale_at(places, len_ref, scale_ref):
    own = jnp.full(places.shape, scale_ref[0], f32)
    end = jnp.int32(0)
    for d in range(1, DOCS):
        end = end + len_ref[d - 1]
        own = jnp.where(places >= end, scale_ref[d], own)
    return own


def own_places(low, high):
    lane = iota((1, TILE), 1)
    return jnp.where(lane < HALF, low, high) * TILE + lane


def half_places(u, tile):
    return iota((HALF, 1), 0) + (tile * TILE + u * HALF)


def rotate(x, cosine, sine):
    cols = x.shape[1]
    parts = x.reshape(HEADS, 2, 8, cols)
    one, two = parts[:, 0], parts[:, 1]
    turned = jnp.stack([one * cosine - two * sine, two * cosine + one * sine], axis=1)
    return turned.reshape(D, cols)


def norm_factor(x):
    return lax.rsqrt(jnp.mean(x * x, axis=0, keepdims=True) + EPSILON)


def norm_back(x, gain, d_normal):
    r = norm_factor(x)
    scaled = d_normal * gain
    inner = jnp.mean(x * scaled, axis=0, keepdims=True)
    d_x = r * scaled - (r * r * r * inner) * x
    return d_x, jnp.sum(d_normal * x * r, axis=1, keepdims=True)


def head_columns(h, *firsts):
    col = iota((1, AUG), 1)
    keep = (col >= h * HEAD_DIM) & (col < (h + 1) * HEAD_DIM)
    for first in firsts:
        keep = keep | (col == first + h)
    return keep


def spread(ref, rows, *firsts):
    zero = jnp.zeros((HALF, AUG), f32)
    for h in range(HEADS):
        keep = head_columns(h, *firsts)
        for u in range(2):
            part = rows[u * HALF : (u + 1) * HALF]
            ref[u, h * HALF : (h + 1) * HALF, 0:AUG] = jnp.where(keep, part, zero).astype(bf16)
    if ref.shape[2] == WIDE:
        unit = eye(HALF, HALF, bf16)
        for h in range(HEADS):
            for u in range(2):
                ref[u, h * HALF : (h + 1) * HALF, AUG:WIDE] = unit


def own_heads(x):
    col = iota((1, D), 1) // HEAD_DIM
    total = jnp.zeros((HALF, D), f32)
    for h in range(HEADS):
        total = jnp.where(col == h, x[h * HALF : (h + 1) * HALF, :D], total)
    return total


def two_parts(x):
    hi = x.astype(bf16)
    return hi, (x - hi.astype(f32)).astype(bf16)


class Tiles:
    def __init__(self, ref):
        self.ref, self.count = ref, 0

    def tile(self, value):
        self.ref[self.count] = value.astype(bf16)
        self.count += 1

    def __call__(self, grads):
        for c in range(grads.shape[1] // TILE):
            for r in range(grads.shape[0] // 16):
                self.tile(grads[16 * r : 16 * (r + 1), c * TILE : (c + 1) * TILE].astype(f32))


class Pairs(Tiles):
    def __init__(self, core, keep_ref, send_ref, rest_ref=None):
        self.core, self.refs, self.rest, self.count, self.even = core, (keep_ref, send_ref), rest_ref, 0, None

    def tile(self, value):
        if self.count == self.refs[0].shape[0]:
            self.rest[0] = value.astype(bf16)
        elif self.even is None:
            self.even = value
        else:
            self.refs[0][self.count] = jnp.where(self.core == 0, self.even, value).astype(bf16)
            self.refs[1][self.count] = jnp.where(self.core == 0, value, self.even).astype(bf16)
            self.even = None
            self.count += 1


def turned(w):
    return tn(w, eye(D, D, bf16)).astype(bf16)


def with_ones(x):
    return jnp.concatenate([x, jnp.ones((STAT, x.shape[1]), bf16)], axis=0)


def key_value_block(normal, w_qkv, rope_ref, k, keys_ref, values_ref):
    mixed = nn(w_qkv[D:], normal)
    at = slice(k * BLOCK, (k + 1) * BLOCK)
    keys = rotate(mixed[:D], rope_ref[0:8, at], rope_ref[8:16, at])
    keys_ref[k] = keys.astype(bf16)
    values_ref[k] = mixed[D:].astype(bf16)
    return head_sizes(keys)


def query_of(normal, w_qkv, cosine, sine):
    turned = rotate(nn(w_qkv[:D], normal), cosine, sine)
    return (turned.astype(bf16).astype(f32) * HEAD_DIM**-0.5).astype(bf16)


def own_rope(rope_ref, low, high):
    def at(tile):
        return rope_ref[:, pl.ds(pl.multiple_of(tile * TILE, TILE), TILE)]

    both = jnp.where(iota((1, TILE), 1) < HALF, at(low), at(high))
    return both[0:8], both[8:16]


def own_tile(ref, low, high):
    lane = iota((1, TILE), 1)

    def at(tile):
        return ref[tile // 4, :, pl.ds(pl.multiple_of((tile % 4) * TILE, TILE), TILE)].astype(f32)

    return jnp.where(lane < HALF, at(low), at(high)).astype(bf16)


def query_bias(u, tile, block, columns, len_ref):
    places = half_places(u, tile)
    start = doc_start(places, len_ref)
    keys = iota((1, columns.stop - columns.start), 1) + (block * BLOCK + columns.start)
    return jnp.where((keys <= places) & (keys >= start), 0.0, MASKED).astype(bf16)


def key_bias(u, tile, block, columns, len_ref):
    keys = half_places(u, tile)
    places = iota((1, columns.stop - columns.start), 1) + (block * BLOCK + columns.start)
    start = doc_start(places, len_ref)
    return jnp.where((keys <= places) & (keys >= start), 0.0, MASKED).astype(bf16)


def scores_of(rows, columns, bias):
    return nn(rows, jnp.concatenate([columns, bias], axis=0))


def run_steps(of_step, low, high, step):
    def several(i, carry):
        for j in range(UNROLL):
            step(*of_step(i * UNROLL + j, low, high), slice(0, BLOCK))
        return carry

    lax.fori_loop(0, (STEPS - 1) // UNROLL, several, 0)


def query_step(s, low, high):
    first = low // 4 + (low % 4 >= 2).astype(jnp.int32)
    late = s >= first
    return late.astype(jnp.int32), jnp.where(late, high, low), s - jnp.where(late, first, 0)


def query_last(low, high):
    late = low % 4 >= 2
    tile = jnp.where(late, high, low)
    return late.astype(jnp.int32), tile, tile // 4, slice(0, BLOCK // 2)


def key_step(s, low, high):
    late_short = (low % 4 < 2).astype(jnp.int32)
    first = low // 4 + 1 - late_short
    late = s >= BLOCKS - first
    block = jnp.where(late, high // 4 + late_short + s - (BLOCKS - first), first + s)
    return late.astype(jnp.int32), jnp.where(late, high, low), block


def key_last(low, high):
    late = low % 4 < 2
    tile = jnp.where(late, high, low)
    return late.astype(jnp.int32), tile, tile // 4, slice(BLOCK // 2, BLOCK)


def head_sizes(x):
    return jnp.sum((x * x).reshape(HEADS, HEAD_DIM, x.shape[1]), axis=1)


def attend(query, k_size, keys_ref, values_ref, len_ref, low, high, qbd, top_ref, acc_ref, q_rows_ref):
    q_rows = nt(eye(TILE, TILE, bf16), query)
    q_rows_ref[...] = q_rows.astype(bf16)
    spread(qbd, jnp.concatenate([q_rows, jnp.zeros((TILE, STAT), f32)], axis=1))
    q_size = jnp.max(head_sizes(query.astype(f32)), axis=1, keepdims=True)
    k_size = jnp.max(k_size, axis=1, keepdims=True)
    acc_ref[...] = jnp.zeros(acc_ref.shape, f32)
    safe = jnp.max(q_size * k_size) <= SAFE * SAFE

    @pl.when(safe)
    def _():
        top_ref[...] = jnp.zeros(top_ref.shape, f32)

        def step(u, tile, block, at):
            scores = scores_of(qbd[u], with_ones(keys_ref[block, :, at]), query_bias(u, tile, block, at, len_ref))
            acc_ref[u] = acc_ref[u] + nt(jnp.exp(scores).astype(bf16), with_ones(values_ref[block, :, at]))

        run_steps(query_step, low, high, step)
        step(*query_last(low, high))

    @pl.when(jnp.logical_not(safe))
    def _():
        top_ref[...] = jnp.full(top_ref.shape, MASKED, f32)

        def step(u, tile, block, at):
            scores = scores_of(qbd[u], with_ones(keys_ref[block, :, at]), query_bias(u, tile, block, at, len_ref))
            old = top_ref[u]
            new = jnp.maximum(old, jnp.max(scores, axis=1, keepdims=True))
            probs = jnp.exp(scores - new)
            acc_ref[u] = acc_ref[u] * jnp.exp(old - new) + nt(probs.astype(bf16), with_ones(values_ref[block, :, at]))
            top_ref[u] = new

        def whole(s, carry):
            step(*query_step(s, low, high), slice(0, BLOCK))
            return carry

        lax.fori_loop(0, STEPS - 1, whole, 0)
        step(*query_last(low, high))

    attended, stats = [], []
    lane = iota((1, STAT), 1)
    for u in range(2):
        acc = acc_ref[u]
        total = acc[:, D : D + 1]
        attended.append(own_heads(acc[:, :D] / total))
        parts = two_parts(-(top_ref[u] + jnp.log(total)))
        stat = jnp.zeros((HALF, STAT), f32)
        for j in range(2):
            part = parts[j].astype(f32)
            for h in range(HEADS):
                stat = jnp.where(lane == 9 * j + h, part[h * HALF : (h + 1) * HALF], stat)
        stats.append(stat)
    att_rows = jnp.concatenate(attended, axis=0).astype(bf16)
    stat_rows = jnp.concatenate(stats, axis=0).astype(bf16)
    return nt(eye(D, D, bf16), att_rows).astype(bf16), nt(eye(STAT, STAT, bf16), stat_rows).astype(bf16)


def feed_forward(resid, attended, w_out, w_gate_up, w_down, gain):
    mid = resid + nn(w_out, attended)
    normal = (mid * norm_factor(mid) * gain).astype(bf16)
    gate_up = nn(w_gate_up, normal)
    gate = gate_up[:FF]
    hidden = (gate * jax.nn.sigmoid(gate) * gate_up[FF:]).astype(bf16)
    return mid, normal, gate_up, hidden, mid + nn(w_down, hidden)


def feed_back(grad, attended, mid, gate_up, w_out, w_gate_up, w_down, gain, stat, low_refs, traffic):
    d_out_ref, d_gate_up_ref, d_branch_ref, hidden_ref, normal_ref = low_refs
    d_out = grad.astype(bf16)
    d_hidden = tn(w_down, d_out)
    gate, up = gate_up[:FF], gate_up[FF:]
    sig = jax.nn.sigmoid(gate)
    d_gate = d_hidden * up * (sig * (1.0 + gate * (1.0 - sig)))
    d_up = d_hidden * (gate * sig)
    hidden_ref[...] = (gate * sig * up).astype(bf16)
    normal_ref[...] = (mid * norm_factor(mid) * gain).astype(bf16)
    d_gate_up = jnp.concatenate([d_gate, d_up], axis=0).astype(bf16)
    d_mid, d_gain = norm_back(mid, gain, nn(w_gate_up, d_gate_up))
    grad = grad + d_mid
    d_branch = grad.astype(bf16)
    d_att = nn(w_out, d_branch).astype(bf16)
    d_out_ref[...], d_gate_up_ref[...], d_branch_ref[...] = d_out, d_gate_up, d_branch
    traffic.send(*low_refs)
    product = d_att.astype(f32) * attended.astype(f32)
    delta = -jnp.sum(product.reshape(HEADS, HEAD_DIM, TILE), axis=1)
    delta = jnp.concatenate([delta, jnp.zeros((16 - HEADS, TILE), f32)], axis=0)
    row, col = iota((STAT, 16), 0), iota((STAT, 16), 1)
    stat = stat.astype(f32) + nn(((row == DROW - D + col) & (col < HEADS)).astype(bf16), delta.astype(bf16))
    return grad, jnp.concatenate([d_att, stat.astype(bf16)], axis=0), d_gain


def feed_grads(put, hidden, d_out, normal, d_gate_up, attended, d_branch):
    put(nt(d_out, hidden))
    put(nt(normal, d_gate_up))
    put(nt(attended, d_branch[:TILE]))
    rows = [jnp.zeros((48, TILE), bf16), d_branch[TILE:], jnp.zeros((TILE - 64, TILE), bf16)]
    return nt(attended, jnp.concatenate(rows, axis=0))


def gain_column(gains_ref, which):
    return column(gains_ref[which // 2, which % 2 : which % 2 + 1, :], D)


def first_kernel(
    traffic, features_ref, len_ref, w_dense_ref, gains_ref, w_qkv_ref, rope_ref, chosen_ref, w_out_ref, w_gate_up_ref,
    w_down_ref,
    copies_ref, next_ref, next_resid_ref, keys_ref, values_ref, normal_all, feats_ref, resid_ref, normal_a_ref,
    q_ref, att_ref, stat_ref, mid_ref, gate_up_ref, own_rope_ref,
    series, toeplitz, lagged_ref, qbd, top_ref, acc_ref,
):
    chip, core, low, high = geometry()
    series[0:8, :] = jnp.zeros((8, TILE), f32)
    series[8 : 8 + TILES, :] = features_ref[:, 0, :].astype(bf16).astype(f32)
    toeplitz[:, 0:MAXLAG] = jnp.zeros((TILE, MAXLAG), bf16)

    def shift(m, carry):
        rows = [series[pl.ds(m * SHIFTED + 7 + n, 1), :] for n in range(SHIFTED + 1)]
        window = jnp.broadcast_to(jnp.concatenate(rows, axis=1), (TILE, (SHIFTED + 1) * TILE))
        rolled = pltpu.roll(window, 1, 1, stride=1, stride_axis=0)
        at = pl.multiple_of(m * SHIFTED * TILE + MAXLAG, TILE)
        toeplitz[:, pl.ds(at, SHIFTED * TILE)] = rolled[:, TILE:].astype(bf16)
        return carry

    lax.fori_loop(0, TILES // SHIFTED, shift, 0)

    def others(tiles):
        rows = jnp.concatenate([features_ref[t] for t in tiles], axis=1)
        return jnp.concatenate([rows, jnp.zeros_like(rows)], axis=0).astype(bf16)

    traffic.ready(5)
    w_dense = w_dense_ref[...]
    gain_a, gain_b = gain_column(gains_ref, 0), gain_column(gains_ref, 1)
    w_qkv = w_qkv_ref[...]
    lag_rows = iota((TILE, 1), 0) + 1
    k_size = jnp.zeros((HEADS, BLOCK), f32)
    for k in range(BLOCKS):
        place = iota((1, BLOCK), 1) + k * BLOCK
        start = doc_start(place, len_ref)
        parts = []
        for b in range(3):
            at = MAXLAG + k * BLOCK - b * TILE
            lagged = toeplitz[:, at : at + BLOCK]
            if k in (0, BLOCKS - 1):
                valid = place - (lag_rows + b * TILE) >= start
                lagged = jnp.where(valid, lagged.astype(f32), 0.0).astype(bf16)
            parts.append(lagged)
        parts.append(others(range(4 * k, 4 * k + 4)))
        resid = nn(w_dense, jnp.concatenate(parts, axis=0))
        normal = (resid * norm_factor(resid) * gain_a).astype(bf16)
        normal_all[k] = normal
        k_size = jnp.maximum(k_size, key_value_block(normal, w_qkv, rope_ref, k, keys_ref, values_ref))

    cosine, sine = own_rope(rope_ref, low, high)
    own_rope_ref[0:8], own_rope_ref[8:16] = cosine, sine
    traffic.send(keys_ref, values_ref, normal_all, own_rope_ref)

    place = own_places(low, high)
    start = doc_start(place, len_ref)
    lane = iota((1, TILE), 1)

    def tile_of(ref, tile):
        return ref[:, pl.ds(pl.multiple_of(tile * TILE, TILE), TILE)].astype(f32)

    for b in range(3):
        lagged = jnp.where(lane < HALF, tile_of(toeplitz, low + 3 - b), tile_of(toeplitz, high + 3 - b))
        valid = place - (lag_rows + b * TILE) >= start
        lagged_ref[b * TILE : (b + 1) * TILE, :] = jnp.where(valid, lagged, 0.0).astype(bf16)
    lagged_ref[MAXLAG:, :] = jnp.where(lane < HALF, others([low]).astype(f32), others([high]).astype(f32)).astype(bf16)
    lagged = lagged_ref[...]
    resid = nn(w_dense, lagged)
    resid_ref[...] = resid
    normal = (resid * norm_factor(resid) * gain_a).astype(bf16)
    normal_a_ref[...] = normal
    traffic.send(resid_ref, normal_a_ref)
    query = query_of(normal, w_qkv, cosine, sine)
    attended, stat_ref[...] = attend(query, k_size, keys_ref, values_ref, len_ref, low, high, qbd, top_ref, acc_ref, q_ref)
    att_ref[...] = attended
    traffic.send(q_ref, att_ref, stat_ref)
    traffic.ready()
    feats_ref[...] = nn(chosen_ref[...], lagged).astype(bf16)
    mid, _, gate_up, _, resid = feed_forward(resid, attended, w_out_ref[...], w_gate_up_ref[...], w_down_ref[...], gain_b)
    mid_ref[...], gate_up_ref[...] = mid, gate_up
    traffic.send(mid_ref, gate_up_ref, feats_ref)
    next_resid_ref[...] = resid
    normal = (resid * norm_factor(resid) * gain_column(gains_ref, 2)).astype(bf16)
    next_ref[...] = normal
    copies_ref[...] = jnp.broadcast_to(normal[None], copies_ref.shape)


def natural_tiles(own_ref, other_ref, put):
    _, core, _, _ = geometry()
    mine = (iota((1, TILE), 1) < HALF) == (core == 0)
    for chip in range(TILES // 2):
        tile = 2 * chip if chip < 8 else TILES - 1 - 2 * chip
        first, second = jnp.where(core == 0, chip, 15 - chip), jnp.where(core == 0, 15 - chip, chip)
        own, other = own_ref[first].astype(f32), other_ref[second].astype(f32)
        for t, value in ((tile, jnp.where(mine, own, other)), (TILES - 1 - tile, jnp.where(mine, other, own))):
            put(t // 4, slice(t % 4 * TILE, (t % 4 + 1) * TILE), value.astype(bf16))


def second_kernel(
    traffic, own_ref, other_ref, cot_own_ref, cot_other_ref, len_ref, turned_qkv_ref, rope_ref, normal_ref, own_rope_ref, resid_in_ref,
    turned_out_ref, turned_gate_up_ref, w_out_ref, w_gate_up_ref, w_down_ref, gains_ref,
    copies_ref, payload_ref, act_ref, keys_ref, values_ref, normal_all, q_ref, grad_ref, att_ref, d_gain_ref,
    d_out_ref, d_gate_up_ref, d_branch_ref, hidden_ref, normal_b_ref,
    qbd, top_ref, acc_ref,
):
    chip, core, low, high = geometry()

    def put(block, columns, value):
        normal_all[block, :, columns] = value

    natural_tiles(own_ref, other_ref, put)
    traffic.send(normal_all)
    traffic.ready(5)
    w_qkv = turned_qkv_ref[...]
    k_size = jnp.zeros((HEADS, BLOCK), f32)
    for k in range(BLOCKS):
        k_size = jnp.maximum(k_size, key_value_block(normal_all[k], w_qkv, rope_ref, k, keys_ref, values_ref))
    traffic.send(keys_ref, values_ref)
    query = query_of(normal_ref[...], w_qkv, own_rope_ref[0:8], own_rope_ref[8:16])
    attended, stat = attend(query, k_size, keys_ref, values_ref, len_ref, low, high, qbd, top_ref, acc_ref, q_ref)
    traffic.ready()
    gain = gain_column(gains_ref, 3)
    w_out, w_gate_up, w_down = w_out_ref[...], w_gate_up_ref[...], w_down_ref[...]
    mid, _, gate_up, _, out = feed_forward(
        resid_in_ref[...], attended, turned_out_ref[...], turned_gate_up_ref[...], w_down, gain
    )
    act_ref[...] = out
    att_ref[...] = attended
    traffic.send(act_ref, att_ref, q_ref)
    grad = tile_halves(cot_own_ref[...].astype(f32), cot_other_ref[...].astype(f32))
    low_refs = (d_out_ref, d_gate_up_ref, d_branch_ref, hidden_ref, normal_b_ref)
    grad, payload, d_gain_ref[...] = feed_back(grad, attended, mid, gate_up, w_out, w_gate_up, w_down, gain, stat, low_refs, traffic)
    grad_ref[...] = grad
    payload_ref[...] = payload
    copies_ref[...] = jnp.broadcast_to(payload[None], copies_ref.shape)


def query_back(
    traffic, count, payload_ref, q_ref, len_ref, own_rope_ref, rope_ref, keys_ref, values_ref, normal_all, w_qkv_ref, dq_ref, qall_ref,
    k_rows_ref, v_rows_ref, qbd, dbd, acc_ref,
):
    chip, core, low, high = geometry()
    traffic.ready(count)
    unit = eye(TILE, TILE, bf16)
    rows = nt(unit, payload_ref[...])
    spread(qbd, jnp.concatenate([q_ref[...].astype(f32), rows[:, D:]], axis=1), LROW, LROW + 9)
    spread(dbd, rows, DROW)
    k_rows_ref[...] = nt(unit, own_tile(keys_ref, low, high)).astype(bf16)
    v_rows_ref[...] = nt(unit, own_tile(values_ref, low, high)).astype(bf16)
    w_qkv = w_qkv_ref[...]
    for k in range(BLOCKS):
        at = slice(k * BLOCK, (k + 1) * BLOCK)
        qall_ref[k] = query_of(normal_all[k], w_qkv, rope_ref[0:8, at], rope_ref[8:16, at])
    traffic.send(k_rows_ref, v_rows_ref, qall_ref)
    acc_ref[...] = jnp.zeros(acc_ref.shape, f32)

    def step(u, tile, block, at):
        scores = scores_of(qbd[u], with_ones(keys_ref[block, :, at]), query_bias(u, tile, block, at, len_ref))
        d_scores = jnp.exp(scores) * nn(dbd[u], with_ones(values_ref[block, :, at]))
        acc_ref[u] = acc_ref[u] + nt(d_scores.astype(bf16), keys_ref[block, :, at])

    run_steps(query_step, low, high, step)
    step(*query_last(low, high))
    d_query = jnp.concatenate([own_heads(acc_ref[0]), own_heads(acc_ref[1])], axis=0) * HEAD_DIM**-0.5
    dq_ref[...] = rotate(turned_rows(d_query), own_rope_ref[0:8], -own_rope_ref[8:16])


def turned_rows(x):
    hi, lo = two_parts(x)
    unit = eye(D, D, bf16)
    return nt(unit, hi) + nt(unit, lo)


def key_back(traffic, count, own_ref, other_ref, len_ref, qall_ref, k_rows_ref, v_rows_ref, dq_ref, grad_ref, resid_ref, w_qkv_ref, gain,
             own_rope_ref, daug, kbd, vbd, dk_ref, dv_ref):
    chip, core, low, high = geometry()

    def put(block, columns, value):
        daug[block, :, columns] = value

    natural_tiles(own_ref, other_ref, put)
    traffic.ready(count)
    ones = jnp.ones((TILE, STAT), f32)
    spread(kbd, jnp.concatenate([k_rows_ref[...].astype(f32), ones], axis=1), LROW, LROW + 9)
    spread(vbd, jnp.concatenate([v_rows_ref[...].astype(f32), ones], axis=1), DROW)
    dk_ref[...] = jnp.zeros(dk_ref.shape, f32)
    dv_ref[...] = jnp.zeros(dv_ref.shape, f32)

    def step(u, tile, block, at):
        queries = jnp.concatenate([qall_ref[block, :, at], daug[block, D:AUG, at]], axis=0)
        probs = jnp.exp(scores_of(kbd[u], queries, key_bias(u, tile, block, at, len_ref)))
        d_scores = probs * nn(vbd[u], daug[block, :, at])
        dv_ref[u] = dv_ref[u] + nt(probs.astype(bf16), daug[block, :, at])
        dk_ref[u] = dk_ref[u] + nt(d_scores.astype(bf16), qall_ref[block, :, at])

    run_steps(key_step, low, high, step)
    step(*key_last(low, high))
    traffic.ready()
    d_key = turned_rows(jnp.concatenate([own_heads(dk_ref[0]), own_heads(dk_ref[1])], axis=0))
    d_value = nt(eye(D, D, bf16), jnp.concatenate([own_heads(dv_ref[0]), own_heads(dv_ref[1])], axis=0).astype(bf16))
    d_key = rotate(d_key, own_rope_ref[0:8], -own_rope_ref[8:16])
    d_mixed = jnp.concatenate([dq_ref[...], d_key, d_value], axis=0).astype(bf16)
    d_in, d_gain = norm_back(resid_ref[...], gain(), nn(w_qkv_ref[...], d_mixed))
    return grad_ref[...] + d_in, d_mixed, d_gain


def projection_grads(normal, d_mixed):
    tail = nt(normal, jnp.concatenate([d_mixed[MAXLAG:], jnp.zeros((TILE - 48, TILE), bf16)], axis=0))
    return nt(normal, d_mixed[:MAXLAG]), tail


def third_kernel(
    traffic, own_ref, other_ref, len_ref, qall_ref, k_rows_ref, v_rows_ref, dq_ref, grad_in_ref, resid_ref, att_ref, stat_ref, mid_ref,
    gate_up_ref, own_rope_ref, w_qkv_ref, w_out_ref, w_gate_up_ref, w_down_ref, gains_ref,
    copies_ref, payload_ref, grad_ref, d_mixed_ref, d_gain_a_ref, d_gain_b_ref, d_out_ref, d_gate_up_ref, d_branch_ref, hidden_ref,
    normal_b_ref,
    daug, kbd, vbd, dk_ref, dv_ref,
):
    grad, d_mixed_ref[...], d_gain_a_ref[...] = key_back(
        traffic, 4, own_ref, other_ref, len_ref, qall_ref, k_rows_ref, v_rows_ref, dq_ref, grad_in_ref, resid_ref, w_qkv_ref,
        lambda: gain_column(gains_ref, 2), own_rope_ref, daug, kbd, vbd, dk_ref, dv_ref,
    )
    low_refs = (d_out_ref, d_gate_up_ref, d_branch_ref, hidden_ref, normal_b_ref)
    grad, payload, d_gain_b_ref[...] = feed_back(
        grad, att_ref[...], mid_ref[...], gate_up_ref[...], w_out_ref[...], w_gate_up_ref[...], w_down_ref[...], gain_column(gains_ref, 1),
        stat_ref[...], low_refs, traffic,
    )
    grad_ref[...] = grad
    payload_ref[...] = payload
    copies_ref[...] = jnp.broadcast_to(payload[None], copies_ref.shape)


def second_window_kernel(
    traffic, len_ref, hidden_ref, d_out_ref, normal_ref, d_gate_up_ref, att_ref, d_branch_ref, d_gain_ref, payload_ref, q_ref,
    own_rope_ref, rope_ref, keys_ref, values_ref, normal_all, w_qkv_ref,
    pack_ref, tail_ref, dq_ref, qall_ref, k_rows_ref, v_rows_ref, qbd, dbd, acc_ref,
):
    traffic.ready(8)
    tail = feed_grads(
        Tiles(pack_ref), hidden_ref[...], d_out_ref[...], normal_ref[...], d_gate_up_ref[...], att_ref[...], d_branch_ref[...]
    )
    tail_ref[...] = jnp.where(iota((1, TILE), 1) == 99, d_gain_ref[...], tail)
    traffic.send(pack_ref, tail_ref)
    query_back(
        traffic, 16, payload_ref, q_ref, len_ref, own_rope_ref, rope_ref, keys_ref, values_ref, normal_all, w_qkv_ref, dq_ref, qall_ref,
        k_rows_ref, v_rows_ref, qbd, dbd, acc_ref,
    )


def third_window_kernel(
    traffic, len_ref, pack_in_ref, tail_in_ref, normal_a_ref, d_mixed_ref, d_gain_a_ref, hidden_ref, d_out_ref, normal_ref, d_gate_up_ref,
    att_ref, d_branch_ref, d_gain_b_ref, payload_ref, q_ref, own_rope_ref, rope_ref, keys_ref, values_ref, normal_all,
    w_qkv_ref,
    keep_ref, send_ref, rest_ref, tail0_ref, tail1_ref, dq_ref, qall_ref, k_rows_ref, v_rows_ref, qbd, dbd, acc_ref,
):
    traffic.ready(13)
    put = Pairs(lax.axis_index("tm") % 2, keep_ref, send_ref, rest_ref)
    for t in range(pack_in_ref.shape[0]):
        put.tile(pack_in_ref[t].astype(f32))
    head, tail = projection_grads(normal_a_ref[...], d_mixed_ref[...])
    put(head)
    tail0_ref[...] = feed_grads(
        put, hidden_ref[...], d_out_ref[...], normal_ref[...], d_gate_up_ref[...], att_ref[...], d_branch_ref[...]
    )
    lane = iota((1, TILE), 1)
    tail = jnp.where(lane == 98, d_gain_a_ref[...], tail + tail_in_ref[...])
    tail1_ref[...] = jnp.where(lane == 97, d_gain_b_ref[...], tail)
    traffic.send(keep_ref, send_ref, rest_ref, tail0_ref, tail1_ref)
    query_back(
        traffic, 21, payload_ref, q_ref, len_ref, own_rope_ref, rope_ref, keys_ref, values_ref, normal_all, w_qkv_ref, dq_ref, qall_ref,
        k_rows_ref, v_rows_ref, qbd, dbd, acc_ref,
    )


def last_kernel(
    traffic, own_ref, other_ref, len_ref, scale_ref, ids_ref, qall_ref, k_rows_ref, v_rows_ref, dq_ref, grad_in_ref, resid_ref,
    normal_a_ref, tail0_ref, tail1_ref, rest_ref, w_dense_ref, feats_ref, own_rope_ref, w_qkv_ref, gains_ref,
    keep_ref, send_ref, daug, kbd, vbd, dk_ref, dv_ref, raw_ref,
):
    chip, core, low, high = geometry()
    d_first, d_mixed, d_gain = key_back(
        traffic, 6, own_ref, other_ref, len_ref, qall_ref, k_rows_ref, v_rows_ref, dq_ref, grad_in_ref, resid_ref, w_qkv_ref,
        lambda: gain_column(gains_ref, 0), own_rope_ref, daug, kbd, vbd, dk_ref, dv_ref,
    )
    head, tail0 = projection_grads(normal_a_ref[...], d_mixed)
    d_first = d_first.astype(bf16)
    feats = feats_ref[...]
    empty = jnp.zeros((64, TILE), bf16)
    tail0 = tail0 + tail0_ref[...] + nt(d_first, jnp.concatenate([empty, feats[:64]], axis=0))
    tail1 = tail1_ref[...] + nt(d_first, jnp.concatenate([empty, feats[64:], empty[:32]], axis=0))
    lane, row = iota((1, TILE), 1), iota((D, 1), 0)
    tail1 = jnp.where(lane == 96, d_gain, tail1)
    sums, counts = jnp.zeros((D, 1), f32), jnp.zeros((D, 1), f32)
    owner = (lax.axis_index("tm") == 0).astype(f32)
    for d in range(DOCS):
        hit = jnp.where(row == ids_ref[d], owner, 0.0)
        sums, counts = sums + hit * scale_ref[d], counts + hit
    high_part = sums.astype(bf16).astype(f32)
    tail1 = jnp.where(lane == 100, high_part, tail1)
    tail1 = jnp.where(lane == 101, sums - high_part, tail1)
    tail1 = jnp.where(lane == 102, counts, tail1)

    place = own_places(low, high)
    start = doc_start(place, len_ref)
    own = doc_scale_at(place, len_ref, scale_ref)
    flip = (iota((TILE, TILE), 0) + iota((TILE, TILE), 1) == TILE - 1).astype(bf16)
    raw_ref[...] = jnp.zeros(raw_ref.shape, f32)
    lags = TILE - iota((TILE, 1), 0)
    for b in range(3):
        weights = nn(w_dense_ref[:, b * TILE : (b + 1) * TILE], flip).astype(bf16)
        d_lagged = tn(weights, d_first)
        valid = place - (lags + b * TILE) >= start
        d_lagged = jnp.where(valid, d_lagged, 0.0) / own
        for u in range(2):
            half = jnp.where((lane < HALF) == (u == 0), d_lagged, 0.0)
            wide = jnp.concatenate([jnp.zeros((TILE, TILE), f32), half], axis=1)
            rolled = pltpu.roll(wide, TILE, 1, stride=1, stride_axis=0)
            total = jnp.sum(rolled, axis=0, keepdims=True)
            for tile, part in (((low if u == 0 else high) - b + 16, total[:, TILE:]), ((low if u == 0 else high) - b + 15, total[:, :TILE])):
                at = tile % 2, pl.ds(tile // 2, 1)
                raw_ref[at] = raw_ref[at] + part

    put = Pairs(core, keep_ref, send_ref)
    put.tile(rest_ref[0].astype(f32))
    for part in (head, tail0, tail1):
        put(part)
    for k in range(2):
        put.tile(raw_ref[k, 8:24, :])


def summed(in_ref):
    count, rows, _ = in_ref.shape
    total = jnp.zeros((rows, TILE), f32)
    return lax.fori_loop(0, count // 8, lambda i, t: t + jnp.sum(in_ref[pl.ds(i * 8, 8)].astype(f32), axis=0), total)


def pair_sum_kernel(early_ref, early_in_ref, late_ref, late_in_ref, out_ref):
    zero = jnp.zeros((16, TILE), bf16)
    late = late_ref.shape[0] - 1
    series, core = lax.axis_index("series"), lax.axis_index("tm") % 2
    out_ref[:, 32:40, :] = jnp.zeros((64, 8, TILE), bf16)

    def both(ref, in_ref, t):
        return ref[t].astype(f32) + in_ref[t].astype(f32)

    for t in range(128):
        value = zero
        if t < EARLY:
            value = both(early_ref, early_in_ref, t).astype(bf16)
        elif t < EARLY + late:
            value = both(late_ref, late_in_ref, t - EARLY).astype(bf16)
        out_ref[jnp.where(core == 0, t // 2, 63 - t // 2), t % 2 * 16 : t % 2 * 16 + 16, :] = value
    raw = both(late_ref, late_in_ref, late)
    for c in range(16):
        line = jnp.where(iota((8, 1), 0) == 0, raw[c : c + 1], 0.0)
        chip = series * 16 + c
        out_ref[jnp.where(core == 0, chip, 63 - chip), 32:40, :] = line.astype(bf16)


def sum_kernel(in_ref, out_ref, raw_ref):
    total = summed(in_ref)
    out_ref[...] = jnp.broadcast_to(total[:32].astype(bf16)[None], out_ref.shape)
    raw_ref[...] = total[32:33]


def unpack_kernel(own_ref, other_ref, act_in_ref, act_ref, lag_ref, qkv_ref, out_ref, gate_up_ref, down_ref, gains_ref, scale_ref):
    core = lax.axis_index("tm") % 2
    act_ref[...] = act_in_ref[...]

    def tile(t):
        rows = slice(t // 2 % 2 * 16, t // 2 % 2 * 16 + 16)
        first, second = jnp.where(core == 0, t // 4, 63 - t // 4), jnp.where(core == 0, 63 - t // 4, t // 4)
        return jnp.where(core == t % 2, own_ref[first, rows].astype(f32), other_ref[second, rows].astype(f32))

    def columns(first, count):
        return [jnp.concatenate([tile(first + 9 * c + r) for r in range(9)], axis=0) for c in range(count)]

    layers = ((207, 234, 117), (90, 243, 0))
    tails = []
    for layer, (at_qkv, at_tail, at_rest) in enumerate(layers):
        for c, part in enumerate(columns(at_qkv, 3)):
            qkv_ref[layer, :, c * TILE : (c + 1) * TILE] = part
        tail = columns(at_tail, 1)[0]
        tails.append(tail)
        qkv_ref[layer, :, MAXLAG:] = tail[:, :48]
        for c, part in enumerate(columns(at_rest, 3)):
            down_ref[layer, :, c * TILE : (c + 1) * TILE] = part
        for c, part in enumerate(columns(at_rest + 27, 6)):
            gate_up_ref[layer, :, c * TILE : (c + 1) * TILE] = part
        out_ref[layer, :, :TILE] = columns(at_rest + 81, 1)[0]
        out_ref[layer, :, TILE:] = tail[:, 48:64]
    lag = jnp.where(iota((1, TILE), 1) < 64, pltpu.roll(tails[0], 64, 1), tails[1])
    lag_ref[...] = lag[:, :FEATS]
    pick = (iota((8, TILE), 1) == iota((8, TILE), 0) + 96).astype(bf16)
    rest = nt(pick, tails[1].astype(bf16))
    gains_ref[0] = rest[0:2]
    gains_ref[1] = rest[2:4]
    scale_ref[...] = ((rest[4:5] + rest[5:6]) / rest[6:7])[:, :DATASETS]


def weights_kernel(
    traffic, lag_ref, w_lag_ref, w_qkv_ref, w_out_ref, w_gate_up_ref, cot_ref,
    dense_ref, qkv0_ref, out0_ref, gate_up0_ref, qkv1_ref, out1_ref, gate_up1_ref, chosen_ref, low_cot_ref,
):
    traffic.ready()
    rows = iota((FEATS, 1), 0)
    diagonal = iota((FEATS, LAGS), 0) == iota((FEATS, LAGS), 1)
    offsets = jnp.sum(jnp.where(diagonal, lag_ref[...].astype(f32), 0.0), axis=1, keepdims=True)
    offsets = jnp.where(rows < LAGS, offsets - 1.0, (rows - LAGS + MAXLAG + 1).astype(f32))
    chosen = (iota((FEATS, LAGCOLS), 1).astype(f32) == offsets).astype(bf16)
    chosen_ref[0:FEATS, :] = chosen
    chosen_ref[FEATS:, :] = jnp.zeros((96 - FEATS, LAGCOLS), bf16)
    dense_ref[...] = nn(w_lag_ref[...], chosen).astype(bf16)
    qkv0_ref[...] = turned(w_qkv_ref[0])
    out0_ref[...] = turned(w_out_ref[0])
    gate_up0_ref[...] = turned(w_gate_up_ref[0])
    qkv1_ref[...] = turned(w_qkv_ref[1])
    out1_ref[...] = turned(w_out_ref[1])
    gate_up1_ref[...] = turned(w_gate_up_ref[1])
    low_cot_ref[...] = cot_ref[...].astype(bf16)


def first_values_kernel(traffic, len_ref, scale_ref, raw_ref, hours_ref, out_ref):
    traffic.ready()
    places = lax.axis_index("tm") * TILE + iota((1, TILE), 1)
    own = doc_scale_at(places, len_ref, scale_ref)
    angle = hours_ref[...].astype(f32) * (2.0 * math.pi / 24.0)
    rows = [raw_ref[...] / own, jnp.sin(angle), jnp.cos(angle), jnp.log(own), jnp.zeros((4, TILE), f32)]
    out_ref[...] = jnp.broadcast_to(jnp.concatenate(rows, axis=0)[None], out_ref.shape)


def shape(*dims, dtype=f32):
    return jax.ShapeDtypeStruct(dims, dtype)


class Traffic:
    def __init__(self, loads, stores):
        self.loads, self.stores, self.waited, self.sent = loads, stores, 0, set()
        for copy in loads:
            copy.start()

    def ready(self, count=None):
        count = len(self.loads) if count is None else count
        for copy in self.loads[self.waited : count]:
            copy.wait()
        self.waited = max(self.waited, count)

    def send(self, *refs):
        for ref, copy in self.stores:
            if any(ref is r for r in refs):
                copy.start()
                self.sent.add(id(copy))

    def finish(self):
        self.ready()
        for _, copy in self.stores:
            if id(copy) not in self.sent:
                copy.start()
        for _, copy in self.stores:
            copy.wait()


def call(kernel, operands, outs, scratch=(), tables=(), weights=(), cost=None):
    several = isinstance(outs, list)
    outs = outs if several else [outs]
    layers = [None] * len(tables) + [x[1] if isinstance(x, tuple) else None for x in weights]
    fetched = (*tables, *(x[0] if isinstance(x, tuple) else x for x in weights))
    shapes = [x.shape if layer is None else x.shape[1:] for x, layer in zip(fetched, layers)]
    buffers = [(pltpu.SMEM if n < len(tables) else pltpu.VMEM)(shapes[n], x.dtype) for n, x in enumerate(fetched)]
    is_far = [not isinstance(out, jax.ShapeDtypeStruct) for out in outs]
    buffers += [pltpu.VMEM(out.shape, out.dtype) for out, far in zip(outs, is_far) if far]
    count, extra, copies = len(operands), len(buffers), len(buffers)

    def wrapped(*refs):
        refs = list(refs)
        ins, sources = refs[:count], refs[count : count + len(fetched)]
        results = refs[count + len(fetched) : count + len(fetched) + len(outs)]
        rest = refs[count + len(fetched) + len(outs) :]
        if not copies:
            kernel(*ins, *results, *rest)
            return
        own, held, sems = rest[: len(scratch)], rest[len(scratch) : -1], rest[-1]
        sources = [a if layer is None else a.at[layer] for a, layer in zip(sources, layers)]
        loads = [pltpu.make_async_copy(a, b, sems.at[n]) for n, (a, b) in enumerate(zip(sources, held))]
        stores, at = [], len(fetched)
        for n, far in enumerate(is_far):
            if far:
                stores.append((held[at], pltpu.make_async_copy(held[at], results[n], sems.at[at])))
                results[n] = held[at]
                at += 1
        traffic = Traffic(loads, stores)
        kernel(traffic, *ins, *held[: len(fetched)], *results, *own)
        traffic.finish()

    vmem, hbm = pl.BlockSpec(memory_space=pltpu.VMEM), pl.BlockSpec(memory_space=pltpu.HBM)
    results = pl.pallas_call(
        wrapped,
        out_shape=outs,
        in_specs=[vmem] * count + [hbm] * len(fetched),
        out_specs=[hbm if far else vmem for far in is_far],
        scratch_shapes=[*scratch, *buffers, pltpu.SemaphoreType.DMA((copies,))] if copies else list(scratch),
        compiler_params=pltpu.CompilerParams(vmem_limit_bytes=VMEM),
        cost_estimate=cost and pl.CostEstimate(flops=cost * 10**9, bytes_accessed=10**6, transcendentals=0),
    )(*operands, *(pltpu.with_memory_space_constraint(x, pltpu.HBM) for x in fetched))
    return results if several else results[0]


def pair_permute(x, bit):
    return lax.ppermute(x, "tm", [(i, i ^ bit) for i in range(32)])


def gather(copies, beside):
    groups = [[2 * chip for chip in range(16)], [31 - 2 * chip for chip in range(16)]]
    own = lax.all_to_all(copies, "tm", 0, 0, axis_index_groups=groups)
    own, beside = lax.optimization_barrier((own, beside))
    return own, pair_permute(own, 1), beside


def swap(block):
    return lax.ppermute(block, "tm", [(n, n if n % 2 == 0 else 32 - n) for n in range(32)])


def tile_halves(own, other):
    lane = iota((1, TILE), 1) < HALF
    return jnp.where(lane == (lax.axis_index("tm") < 16), own, other)


def rope_table():
    freqs = 10000.0 ** (-np.arange(8, dtype=np.float64) / 8)
    angle = np.arange(LEN, dtype=np.float64)[None, :] * freqs[:, None]
    return np.concatenate([np.cos(angle), np.sin(angle)], axis=0).astype(np.float32)


def body(
    raw_values, hours, doc_lengths, doc_scale, dataset_ids, lag_offsets, w_lag, w_qkv, w_out, w_gate_up, w_down, gains, cotangent
):
    lengths, scales, ids = doc_lengths.reshape(DOCS), doc_scale.reshape(DOCS), dataset_ids.reshape(DOCS)
    def low(*dims):
        return shape(*dims, dtype=bf16)

    def far(*dims, dtype=f32):
        return pltpu.HBM(dims, dtype)

    def far_low(*dims):
        return far(*dims, dtype=bf16)

    w_lag, w_down, lags = w_lag.T, w_down.transpose(0, 2, 1), lag_offsets.reshape(1, LAGS)
    rope = jnp.asarray(rope_table())
    values = lax.all_to_all(call(first_values_kernel, (), shape(32, 8, TILE), tables=(lengths, scales), weights=(raw_values, hours)), "tm", 0, 0)
    turned_shapes = [far_low(3 * D, D), far_low(D, D), far_low(2 * FF, D)]
    w_dense, *turned_weights, chosen, low_cot = call(
        weights_kernel, (), [far_low(D, LAGCOLS), *turned_shapes, *turned_shapes, far_low(96, LAGCOLS), far_low(D, TILE)],
        weights=(lags, w_lag, w_qkv, w_out, w_gate_up, cotangent[0].T), cost=3,
    )
    turned0, turned1 = turned_weights[:3], turned_weights[3:]
    values, w_dense = lax.optimization_barrier((values, w_dense))
    all_d = far_low(BLOCKS, D, BLOCK)
    mine, mine_low, ff_low, column_shape = far(D, TILE), far_low(D, TILE), far_low(FF, TILE), far(D, 1)
    payload_shapes = [far_low(16, AUG, TILE), far_low(AUG, TILE)]
    low_grads = [mine_low, far_low(2 * FF, TILE), mine_low, ff_low, mine_low]
    bd, wide_bd = pltpu.VMEM((2, ROWS, AUG), bf16), pltpu.VMEM((2, ROWS, WIDE), bf16)
    acc, acc_d = pltpu.VMEM((2, ROWS, AUG), f32), pltpu.VMEM((2, ROWS, D), f32)
    top = pltpu.VMEM((2, ROWS, 1), f32)
    back_scratch = [pltpu.VMEM((BLOCKS, AUG, BLOCK), bf16), wide_bd, bd, acc_d, acc]

    (copies, next1, resid1, keys0, values0, normal_all0, feats, resid0, normal_a0, q0, att0, stat0, mid0, gate_up0, own_rope) = call(
        first_kernel,
        (values,),
        [far_low(16, D, TILE), mine_low, mine, all_d, all_d, all_d, far_low(96, TILE), mine, mine_low, far_low(TILE, D), mine_low,
         far_low(STAT, TILE), mine, far(2 * FF, TILE), far(16, TILE)],
        [pltpu.VMEM((8 + TILES, TILE), f32), pltpu.VMEM((TILE, MAXLAG + LEN), bf16),
         pltpu.VMEM((LAGCOLS, TILE), bf16), wide_bd, top, acc],
        tables=(lengths,), weights=(w_dense, gains, turned0[0], rope, chosen, *turned0[1:], (w_down, 0)),
    )

    own, other, cot = gather(copies, swap(low_cot))
    copies, payload, act, keys1, values1, normal_all1, q1, grad, att1, d_gain_b1, *low1 = call(
        second_kernel,
        (own, other, cot, pair_permute(cot, 1)),
        [*payload_shapes, mine, all_d, all_d, all_d, far_low(TILE, D), mine, mine_low, column_shape, *low_grads],
        [wide_bd, top, acc],
        tables=(lengths,),
        weights=(turned1[0], rope, next1, own_rope, resid1, *turned1[1:], (w_out, 1), (w_gate_up, 1), (w_down, 1), gains),
    )

    rows_low = far_low(TILE, D)
    side_shapes = [mine, all_d, rows_low, rows_low]
    d_out, d_gate_up, d_branch, hidden, normal_b = low1
    pack, tail, dq, qall, k_rows, v_rows = call(
        second_window_kernel, (), [far_low(90, 16, TILE), mine, *side_shapes], [wide_bd, bd, acc_d],
        tables=(lengths,),
        weights=(hidden, d_out, normal_b, d_gate_up, att1, d_branch, d_gain_b1, payload, q1, own_rope, rope, keys1, values1, normal_all1,
                 turned1[0]), cost=8,
    )
    own, other, dq = gather(copies, dq)
    copies, payload, grad, d_mixed, d_gain_a1, d_gain_b0, *low0 = call(
        third_kernel,
        (own, other),
        [*payload_shapes, mine, far_low(3 * D, TILE), column_shape, column_shape, *low_grads],
        back_scratch,
        tables=(lengths,),
        weights=(qall, k_rows, v_rows, dq, grad, resid1, att0, stat0, mid0, gate_up0, own_rope, (w_qkv, 1), (w_out, 0), (w_gate_up, 0),
                 (w_down, 0), gains),
    )
    d_out, d_gate_up, d_branch, hidden, normal_b = low0
    early, early_out, rest, tail0, tail1, dq, qall, k_rows, v_rows = call(
        third_window_kernel, (),
        [far_low(EARLY, 16, TILE), far_low(EARLY, 16, TILE), far_low(1, 16, TILE), mine, mine, *side_shapes], [wide_bd, bd, acc_d],
        tables=(lengths,),
        weights=(pack, tail, next1, d_mixed, d_gain_a1, hidden, d_out, normal_b, d_gate_up, att0, d_branch, d_gain_b0, payload, q0,
                 own_rope, rope, keys0, values0, normal_all0, turned0[0]), cost=8,
    )
    own, other, (dq, early_out) = gather(copies, (dq, early_out))
    early_in = pair_permute(early_out, 1)
    late, late_out = call(
        last_kernel,
        (own, other),
        [low(LATE, 16, TILE)] * 2,
        [*back_scratch, pltpu.VMEM((2, 24, TILE), f32)],
        tables=(lengths, scales, ids),
        weights=(qall, k_rows, v_rows, dq, grad, resid0, normal_a0, tail0, tail1, rest, w_dense, feats, own_rope, (w_qkv, 0), gains),
    )
    packed = call(pair_sum_kernel, (early, early_in, late, pair_permute(late_out, 1)), low(64, 40, TILE))
    same_core = [[2 * chip for chip in range(64)], [127 - 2 * chip for chip in range(64)]]
    parts = lax.all_to_all(packed, ("series", "tm"), 0, 0, axis_index_groups=same_core)
    share, raw_grad = call(sum_kernel, (parts,), [low(64, 32, TILE), shape(1, TILE)])
    share, act = lax.optimization_barrier((share, act))
    own = lax.all_to_all(share, ("series", "tm"), 0, 0, axis_index_groups=same_core)
    own, act = lax.optimization_barrier((own, swap(tile_halves(act, pair_permute(act, 1)))))
    act, g_lag, g_qkv, g_out, g_gate_up, g_down, g_gains, scale = call(
        unpack_kernel,
        (own, pair_permute(own, 1), act),
        [shape(D, TILE), shape(D, FEATS), shape(LAYERS, D, 3 * D), shape(LAYERS, D, D), shape(LAYERS, D, 2 * FF), shape(LAYERS, D, FF),
         shape(LAYERS, 2, D), shape(1, DATASETS)],
    )
    return (
        act.T[None], raw_grad, scale.reshape(DATASETS), g_lag.T, g_qkv, g_out, g_gate_up, g_down.transpose(0, 2, 1), g_gains,
    )


def solution(mesh):
    placed = (
        P("series", "tm"),
        P("series", "tm"),
        P("series", None),
        P("series", None),
        P("series", None, None),
        P(),
        P(),
        P(),
        P(),
        P(),
        P(),
        P(),
        P("series", "tm", None),
    )
    return jax.shard_map(
        body,
        mesh=mesh,
        in_specs=placed,
        out_specs=(P("series", "tm", None), P("series", "tm"), P(), P(), P(), P(), P(), P(), P()),
        check_vma=False,
    )
```

```python
import math

import jax
import jax.numpy as jnp
import numpy as np
from jax import lax
from jax.experimental import pallas as pl
from jax.experimental.pallas import tpu as pltpu
from jax.sharding import PartitionSpec as P


D = 144
HEADS = 9
HEAD_DIM = 16
FF = 384
LAGS = 84
LAYERS = 2
DATASETS = 8
DOCS = 7
LEN = 4096
MAXLAG = 384
FEATS = 87
EPSILON = 1e-06
MASKED = -1e30
AUG = 176
STAT = AUG - D
LROW = D
DROW = D + 18
BLOCK = 512
BLOCKS = LEN // BLOCK
TILE = 128
TILES = LEN // TILE
STEPS = BLOCKS + 1
SHIFTED = 8
HALF = 64
ROWS = HEADS * HALF
LAGCOLS = 400
EARLY = 103
LATE = 24
WIDE = AUG + HALF
SAFE = 40.0
VMEM = 28 * 2**20

bf16 = jnp.bfloat16
f32 = jnp.float32
HIGH = lax.Precision.HIGHEST


def nn(a, b, precision=None):
    return lax.dot_general(a, b, (((1,), (0,)), ((), ())), precision=precision, preferred_element_type=f32)


def nt(a, b, precision=None):
    return lax.dot_general(a, b, (((1,), (1,)), ((), ())), precision=precision, preferred_element_type=f32)


def tn(a, b, precision=None):
    return lax.dot_general(a, b, (((0,), (0,)), ((), ())), precision=precision, preferred_element_type=f32)


def iota(shape, dim):
    return lax.broadcasted_iota(jnp.int32, shape, dim)


def eye(rows, cols, dtype):
    return (iota((rows, cols), 0) == iota((rows, cols), 1)).astype(dtype)


def column(row, size):
    keep = iota((size, size), 0) == iota((size, size), 1)
    return jnp.sum(jnp.where(keep, row, 0.0), axis=1, keepdims=True)


def pair_of(chip):
    return jnp.where(chip < 8, 2 * chip, TILES - 1 - 2 * chip)


def geometry():
    index = lax.axis_index("tm")
    chip, core = index // 2, index % 2
    tile = pair_of(chip)
    low = jnp.where(core == 0, tile, TILES - 1 - tile)
    return chip, core, low, TILES - 1 - low


def doc_start(places, len_ref):
    start = jnp.zeros_like(places)
    end = jnp.int32(0)
    for d in range(DOCS):
        end = end + len_ref[d]
        start = jnp.where(places >= end, end, start)
    return start


def doc_scale_at(places, len_ref, scale_ref):
    own = jnp.full(places.shape, scale_ref[0], f32)
    end = jnp.int32(0)
    for d in range(1, DOCS):
        end = end + len_ref[d - 1]
        own = jnp.where(places >= end, scale_ref[d], own)
    return own


def own_places(low, high):
    lane = iota((1, TILE), 1)
    return jnp.where(lane < HALF, low, high) * TILE + lane


def half_places(u, tile):
    return iota((HALF, 1), 0) + (tile * TILE + u * HALF)


def rotate(x, cosine, sine):
    cols = x.shape[1]
    parts = x.reshape(HEADS, 2, 8, cols)
    one, two = parts[:, 0], parts[:, 1]
    turned = jnp.stack([one * cosine - two * sine, two * cosine + one * sine], axis=1)
    return turned.reshape(D, cols)


def norm_factor(x):
    return lax.rsqrt(jnp.mean(x * x, axis=0, keepdims=True) + EPSILON)


def norm_back(x, gain, d_normal):
    r = norm_factor(x)
    scaled = d_normal * gain
    inner = jnp.mean(x * scaled, axis=0, keepdims=True)
    d_x = r * scaled - (r * r * r * inner) * x
    return d_x, jnp.sum(d_normal * x * r, axis=1, keepdims=True)


def head_columns(h, *firsts):
    col = iota((1, AUG), 1)
    keep = (col >= h * HEAD_DIM) & (col < (h + 1) * HEAD_DIM)
    for first in firsts:
        keep = keep | (col == first + h)
    return keep


def spread(ref, rows, *firsts):
    zero = jnp.zeros((HALF, AUG), f32)
    for h in range(HEADS):
        keep = head_columns(h, *firsts)
        for u in range(2):
            part = rows[u * HALF : (u + 1) * HALF]
            ref[u, h * HALF : (h + 1) * HALF, 0:AUG] = jnp.where(keep, part, zero).astype(bf16)
    if ref.shape[2] == WIDE:
        unit = eye(HALF, HALF, bf16)
        for h in range(HEADS):
            for u in range(2):
                ref[u, h * HALF : (h + 1) * HALF, AUG:WIDE] = unit


def own_heads(x):
    col = iota((1, D), 1) // HEAD_DIM
    total = jnp.zeros((HALF, D), f32)
    for h in range(HEADS):
        total = jnp.where(col == h, x[h * HALF : (h + 1) * HALF, :D], total)
    return total


def two_parts(x):
    hi = x.astype(bf16)
    return hi, (x - hi.astype(f32)).astype(bf16)


class Tiles:
    def __init__(self, ref):
        self.ref, self.count = ref, 0

    def tile(self, value):
        self.ref[self.count] = value.astype(bf16)
        self.count += 1

    def __call__(self, grads):
        for c in range(grads.shape[1] // TILE):
            for r in range(grads.shape[0] // 16):
                self.tile(grads[16 * r : 16 * (r + 1), c * TILE : (c + 1) * TILE].astype(f32))


class Pairs(Tiles):
    def __init__(self, core, keep_ref, send_ref, rest_ref=None):
        self.core, self.refs, self.rest, self.count, self.even = core, (keep_ref, send_ref), rest_ref, 0, None

    def tile(self, value):
        if self.count == self.refs[0].shape[0]:
            self.rest[0] = value.astype(bf16)
        elif self.even is None:
            self.even = value
        else:
            self.refs[0][self.count] = jnp.where(self.core == 0, self.even, value).astype(bf16)
            self.refs[1][self.count] = jnp.where(self.core == 0, value, self.even).astype(bf16)
            self.even = None
            self.count += 1


def turned(w):
    return tn(w, eye(D, D, bf16)).astype(bf16)


def with_ones(x):
    return jnp.concatenate([x, jnp.ones((STAT, x.shape[1]), bf16)], axis=0)


def key_value_block(normal, w_qkv, rope_ref, k, keys_ref, values_ref):
    mixed = nn(w_qkv[D:], normal)
    at = slice(k * BLOCK, (k + 1) * BLOCK)
    keys = rotate(mixed[:D], rope_ref[0:8, at], rope_ref[8:16, at])
    keys_ref[k] = keys.astype(bf16)
    values_ref[k] = mixed[D:].astype(bf16)
    return head_sizes(keys)


def query_of(normal, w_qkv, cosine, sine):
    turned = rotate(nn(w_qkv[:D], normal), cosine, sine)
    return (turned.astype(bf16).astype(f32) * HEAD_DIM**-0.5).astype(bf16)


def own_rope(rope_ref, low, high):
    def at(tile):
        return rope_ref[:, pl.ds(pl.multiple_of(tile * TILE, TILE), TILE)]

    both = jnp.where(iota((1, TILE), 1) < HALF, at(low), at(high))
    return both[0:8], both[8:16]


def own_tile(ref, low, high):
    lane = iota((1, TILE), 1)

    def at(tile):
        return ref[tile // 4, :, pl.ds(pl.multiple_of((tile % 4) * TILE, TILE), TILE)].astype(f32)

    return jnp.where(lane < HALF, at(low), at(high)).astype(bf16)


def query_bias(u, tile, block, columns, len_ref):
    places = half_places(u, tile)
    start = doc_start(places, len_ref)
    keys = iota((1, columns.stop - columns.start), 1) + (block * BLOCK + columns.start)
    return jnp.where((keys <= places) & (keys >= start), 0.0, MASKED).astype(bf16)


def key_bias(u, tile, block, columns, len_ref):
    keys = half_places(u, tile)
    places = iota((1, columns.stop - columns.start), 1) + (block * BLOCK + columns.start)
    start = doc_start(places, len_ref)
    return jnp.where((keys <= places) & (keys >= start), 0.0, MASKED).astype(bf16)


def scores_of(rows, columns, bias):
    return nn(rows, jnp.concatenate([columns, bias], axis=0))


def run_steps(of_step, low, high, step, unroll=4):
    def several(i, carry):
        for j in range(unroll):
            step(*of_step(i * unroll + j, low, high), slice(0, BLOCK))
        return carry

    lax.fori_loop(0, (STEPS - 1) // unroll, several, 0)


def query_step(s, low, high):
    first = low // 4 + (low % 4 >= 2).astype(jnp.int32)
    late = s >= first
    return late.astype(jnp.int32), jnp.where(late, high, low), s - jnp.where(late, first, 0)


def query_last(low, high):
    late = low % 4 >= 2
    tile = jnp.where(late, high, low)
    return late.astype(jnp.int32), tile, tile // 4, slice(0, BLOCK // 2)


def key_step(s, low, high):
    late_short = (low % 4 < 2).astype(jnp.int32)
    first = low // 4 + 1 - late_short
    late = s >= BLOCKS - first
    block = jnp.where(late, high // 4 + late_short + s - (BLOCKS - first), first + s)
    return late.astype(jnp.int32), jnp.where(late, high, low), block


def key_last(low, high):
    late = low % 4 < 2
    tile = jnp.where(late, high, low)
    return late.astype(jnp.int32), tile, tile // 4, slice(BLOCK // 2, BLOCK)


def head_sizes(x):
    return jnp.sum((x * x).reshape(HEADS, HEAD_DIM, x.shape[1]), axis=1)


def attend(query, k_size, keys_ref, values_ref, len_ref, low, high, qbd, top_ref, acc_ref, q_rows_ref):
    q_rows = nt(eye(TILE, TILE, bf16), query)
    q_rows_ref[...] = q_rows.astype(bf16)
    spread(qbd, jnp.concatenate([q_rows, jnp.zeros((TILE, STAT), f32)], axis=1))
    q_size = jnp.max(head_sizes(query.astype(f32)), axis=1, keepdims=True)
    k_size = jnp.max(k_size, axis=1, keepdims=True)
    acc_ref[...] = jnp.zeros(acc_ref.shape, f32)
    safe = jnp.max(q_size * k_size) <= SAFE * SAFE

    @pl.when(safe)
    def _():
        top_ref[...] = jnp.zeros(top_ref.shape, f32)

        def step(u, tile, block, at):
            scores = scores_of(qbd[u], with_ones(keys_ref[block, :, at]), query_bias(u, tile, block, at, len_ref))
            acc_ref[u] = acc_ref[u] + nt(jnp.exp(scores).astype(bf16), with_ones(values_ref[block, :, at]))

        run_steps(query_step, low, high, step)
        step(*query_last(low, high))

    @pl.when(jnp.logical_not(safe))
    def _():
        top_ref[...] = jnp.full(top_ref.shape, MASKED, f32)

        def step(s, carry):
            h, s = s % HEADS, s // HEADS
            first = low // 4 + 1
            late = s >= first
            u, tile, block = late.astype(jnp.int32), jnp.where(late, high, low), s - jnp.where(late, first, 0)
            rows = pl.ds(pl.multiple_of(h * HALF, HALF), HALF)
            bias = query_bias(u, tile, block, slice(0, BLOCK), len_ref)
            scores = scores_of(qbd[u, rows], with_ones(keys_ref[block]), bias)
            old = top_ref[u, rows]
            new = jnp.maximum(old, jnp.max(scores, axis=1, keepdims=True))
            probs = jnp.exp(scores - new)
            acc_ref[u, rows] = acc_ref[u, rows] * jnp.exp(old - new) + nt(probs.astype(bf16), with_ones(values_ref[block]))
            top_ref[u, rows] = new
            return carry

        lax.fori_loop(0, STEPS * HEADS, step, 0)

    attended, stats = [], []
    lane = iota((1, STAT), 1)
    for u in range(2):
        acc = acc_ref[u]
        total = acc[:, D : D + 1]
        attended.append(own_heads(acc[:, :D] / total))
        parts = two_parts(-(top_ref[u] + jnp.log(total)))
        stat = jnp.zeros((HALF, STAT), f32)
        for j in range(2):
            part = parts[j].astype(f32)
            for h in range(HEADS):
                stat = jnp.where(lane == 9 * j + h, part[h * HALF : (h + 1) * HALF], stat)
        stats.append(stat)
    att_rows = jnp.concatenate(attended, axis=0).astype(bf16)
    stat_rows = jnp.concatenate(stats, axis=0).astype(bf16)
    return nt(eye(D, D, bf16), att_rows).astype(bf16), nt(eye(STAT, STAT, bf16), stat_rows).astype(bf16)


def feed_forward(resid, attended, w_out, w_gate_up, w_down, gain):
    mid = resid + nn(w_out, attended)
    normal = (mid * norm_factor(mid) * gain).astype(bf16)
    gate_up = nn(w_gate_up, normal)
    gate = gate_up[:FF]
    hidden = (gate * jax.nn.sigmoid(gate) * gate_up[FF:]).astype(bf16)
    return mid, normal, gate_up, hidden, mid + nn(w_down, hidden)


def feed_back(grad, attended, mid, gate_up, w_out, w_gate_up, w_down, gain, stat, low_refs, traffic):
    d_out_ref, d_gate_up_ref, d_branch_ref, hidden_ref, normal_ref = low_refs
    d_out = grad.astype(bf16)
    d_hidden = tn(w_down, d_out)
    gate, up = gate_up[:FF], gate_up[FF:]
    sig = jax.nn.sigmoid(gate)
    d_gate = d_hidden * up * (sig * (1.0 + gate * (1.0 - sig)))
    d_up = d_hidden * (gate * sig)
    hidden_ref[...] = (gate * sig * up).astype(bf16)
    normal_ref[...] = (mid * norm_factor(mid) * gain).astype(bf16)
    d_gate_up = jnp.concatenate([d_gate, d_up], axis=0).astype(bf16)
    d_mid, d_gain = norm_back(mid, gain, nn(w_gate_up, d_gate_up))
    grad = grad + d_mid
    d_branch = grad.astype(bf16)
    d_att = nn(w_out, d_branch).astype(bf16)
    d_out_ref[...], d_gate_up_ref[...], d_branch_ref[...] = d_out, d_gate_up, d_branch
    traffic.send(*low_refs)
    product = d_att.astype(f32) * attended.astype(f32)
    delta = -jnp.sum(product.reshape(HEADS, HEAD_DIM, TILE), axis=1)
    delta = jnp.concatenate([delta, jnp.zeros((16 - HEADS, TILE), f32)], axis=0)
    row, col = iota((STAT, 16), 0), iota((STAT, 16), 1)
    stat = stat.astype(f32) + nn(((row == DROW - D + col) & (col < HEADS)).astype(bf16), delta.astype(bf16))
    return grad, jnp.concatenate([d_att, stat.astype(bf16)], axis=0), d_gain


def feed_grads(put, hidden, d_out, normal, d_gate_up, attended, d_branch):
    put(nt(d_out, hidden))
    put(nt(normal, d_gate_up))
    put(nt(attended, d_branch[:TILE]))
    rows = [jnp.zeros((48, TILE), bf16), d_branch[TILE:], jnp.zeros((TILE - 64, TILE), bf16)]
    return nt(attended, jnp.concatenate(rows, axis=0))


def gain_column(gains_ref, which):
    return column(gains_ref[which // 2, which % 2 : which % 2 + 1, :], D)


def first_kernel(
    traffic, features_ref, len_ref, w_dense_ref, gains_ref, w_qkv_ref, rope_ref, chosen_ref, w_out_ref, w_gate_up_ref,
    w_down_ref,
    copies_ref, next_ref, next_resid_ref, keys_ref, values_ref, normal_all, feats_ref, resid_ref, normal_a_ref,
    q_ref, att_ref, stat_ref, mid_ref, gate_up_ref, own_rope_ref,
    series, toeplitz, lagged_ref, qbd, top_ref, acc_ref,
):
    chip, core, low, high = geometry()
    series[0:8, :] = jnp.zeros((8, TILE), f32)
    series[8 : 8 + TILES, :] = features_ref[:, 0, :].astype(bf16).astype(f32)
    toeplitz[:, 0:MAXLAG] = jnp.zeros((TILE, MAXLAG), bf16)

    def shift(m, carry):
        rows = [series[pl.ds(m * SHIFTED + 7 + n, 1), :] for n in range(SHIFTED + 1)]
        window = jnp.broadcast_to(jnp.concatenate(rows, axis=1), (TILE, (SHIFTED + 1) * TILE))
        rolled = pltpu.roll(window, 1, 1, stride=1, stride_axis=0)
        at = pl.multiple_of(m * SHIFTED * TILE + MAXLAG, TILE)
        toeplitz[:, pl.ds(at, SHIFTED * TILE)] = rolled[:, TILE:].astype(bf16)
        return carry

    lax.fori_loop(0, TILES // SHIFTED, shift, 0)

    def others(tiles):
        rows = jnp.concatenate([features_ref[t] for t in tiles], axis=1)
        return jnp.concatenate([rows, jnp.zeros_like(rows)], axis=0).astype(bf16)

    traffic.ready(5)
    w_dense = w_dense_ref[...]
    gain_a, gain_b = gain_column(gains_ref, 0), gain_column(gains_ref, 1)
    w_qkv = w_qkv_ref[...]
    lag_rows = iota((TILE, 1), 0) + 1
    k_size = jnp.zeros((HEADS, BLOCK), f32)
    for k in range(BLOCKS):
        place = iota((1, BLOCK), 1) + k * BLOCK
        start = doc_start(place, len_ref)
        parts = []
        for b in range(3):
            at = MAXLAG + k * BLOCK - b * TILE
            lagged = toeplitz[:, at : at + BLOCK]
            if k in (0, BLOCKS - 1):
                valid = place - (lag_rows + b * TILE) >= start
                lagged = jnp.where(valid, lagged.astype(f32), 0.0).astype(bf16)
            parts.append(lagged)
        parts.append(others(range(4 * k, 4 * k + 4)))
        resid = nn(w_dense, jnp.concatenate(parts, axis=0))
        normal = (resid * norm_factor(resid) * gain_a).astype(bf16)
        normal_all[k] = normal
        k_size = jnp.maximum(k_size, key_value_block(normal, w_qkv, rope_ref, k, keys_ref, values_ref))

    cosine, sine = own_rope(rope_ref, low, high)
    own_rope_ref[0:8], own_rope_ref[8:16] = cosine, sine
    traffic.send(keys_ref, values_ref, normal_all, own_rope_ref)

    place = own_places(low, high)
    start = doc_start(place, len_ref)
    lane = iota((1, TILE), 1)

    def tile_of(ref, tile):
        return ref[:, pl.ds(pl.multiple_of(tile * TILE, TILE), TILE)].astype(f32)

    for b in range(3):
        lagged = jnp.where(lane < HALF, tile_of(toeplitz, low + 3 - b), tile_of(toeplitz, high + 3 - b))
        valid = place - (lag_rows + b * TILE) >= start
        lagged_ref[b * TILE : (b + 1) * TILE, :] = jnp.where(valid, lagged, 0.0).astype(bf16)
    lagged_ref[MAXLAG:, :] = jnp.where(lane < HALF, others([low]).astype(f32), others([high]).astype(f32)).astype(bf16)
    lagged = lagged_ref[...]
    resid = nn(w_dense, lagged)
    resid_ref[...] = resid
    normal = (resid * norm_factor(resid) * gain_a).astype(bf16)
    normal_a_ref[...] = normal
    traffic.send(resid_ref, normal_a_ref)
    query = query_of(normal, w_qkv, cosine, sine)
    attended, stat_ref[...] = attend(query, k_size, keys_ref, values_ref, len_ref, low, high, qbd, top_ref, acc_ref, q_ref)
    att_ref[...] = attended
    traffic.send(q_ref, att_ref, stat_ref)
    traffic.ready()
    feats_ref[...] = nn(chosen_ref[...], lagged).astype(bf16)
    mid, _, gate_up, _, resid = feed_forward(resid, attended, w_out_ref[...], w_gate_up_ref[...], w_down_ref[...], gain_b)
    mid_ref[...], gate_up_ref[...] = mid, gate_up
    traffic.send(mid_ref, gate_up_ref, feats_ref)
    next_resid_ref[...] = resid
    normal = (resid * norm_factor(resid) * gain_column(gains_ref, 2)).astype(bf16)
    next_ref[...] = normal
    copies_ref[...] = jnp.broadcast_to(normal[None], copies_ref.shape)


def natural_tiles(own_ref, other_ref, put):
    _, core, _, _ = geometry()
    mine = (iota((1, TILE), 1) < HALF) == (core == 0)
    for chip in range(TILES // 2):
        tile = 2 * chip if chip < 8 else TILES - 1 - 2 * chip
        first, second = jnp.where(core == 0, chip, 15 - chip), jnp.where(core == 0, 15 - chip, chip)
        own, other = own_ref[first].astype(f32), other_ref[second].astype(f32)
        for t, value in ((tile, jnp.where(mine, own, other)), (TILES - 1 - tile, jnp.where(mine, other, own))):
            put(t // 4, slice(t % 4 * TILE, (t % 4 + 1) * TILE), value.astype(bf16))


def second_kernel(
    traffic, own_ref, other_ref, cot_own_ref, cot_other_ref, len_ref, turned_qkv_ref, rope_ref, normal_ref, own_rope_ref, resid_in_ref,
    turned_out_ref, turned_gate_up_ref, w_out_ref, w_gate_up_ref, w_down_ref, gains_ref,
    copies_ref, payload_ref, act_ref, keys_ref, values_ref, normal_all, q_ref, grad_ref, att_ref, d_gain_ref,
    d_out_ref, d_gate_up_ref, d_branch_ref, hidden_ref, normal_b_ref,
    qbd, top_ref, acc_ref,
):
    chip, core, low, high = geometry()

    def put(block, columns, value):
        normal_all[block, :, columns] = value

    natural_tiles(own_ref, other_ref, put)
    traffic.send(normal_all)
    traffic.ready(5)
    w_qkv = turned_qkv_ref[...]
    k_size = jnp.zeros((HEADS, BLOCK), f32)
    for k in range(BLOCKS):
        k_size = jnp.maximum(k_size, key_value_block(normal_all[k], w_qkv, rope_ref, k, keys_ref, values_ref))
    traffic.send(keys_ref, values_ref)
    query = query_of(normal_ref[...], w_qkv, own_rope_ref[0:8], own_rope_ref[8:16])
    attended, stat = attend(query, k_size, keys_ref, values_ref, len_ref, low, high, qbd, top_ref, acc_ref, q_ref)
    traffic.ready()
    gain = gain_column(gains_ref, 3)
    w_out, w_gate_up, w_down = w_out_ref[...], w_gate_up_ref[...], w_down_ref[...]
    mid, _, gate_up, _, out = feed_forward(
        resid_in_ref[...], attended, turned_out_ref[...], turned_gate_up_ref[...], w_down, gain
    )
    act_ref[...] = out
    att_ref[...] = attended
    traffic.send(act_ref, att_ref, q_ref)
    grad = tile_halves(cot_own_ref[...].astype(f32), cot_other_ref[...].astype(f32))
    low_refs = (d_out_ref, d_gate_up_ref, d_branch_ref, hidden_ref, normal_b_ref)
    grad, payload, d_gain_ref[...] = feed_back(grad, attended, mid, gate_up, w_out, w_gate_up, w_down, gain, stat, low_refs, traffic)
    grad_ref[...] = grad
    payload_ref[...] = payload
    copies_ref[...] = jnp.broadcast_to(payload[None], copies_ref.shape)


def query_back(
    traffic, count, payload_ref, q_ref, len_ref, own_rope_ref, rope_ref, keys_ref, values_ref, normal_all, w_qkv_ref, dq_ref, qall_ref,
    k_rows_ref, v_rows_ref, qbd, dbd, acc_ref,
):
    chip, core, low, high = geometry()
    traffic.ready(count)
    unit = eye(TILE, TILE, bf16)
    rows = nt(unit, payload_ref[...])
    spread(qbd, jnp.concatenate([q_ref[...].astype(f32), rows[:, D:]], axis=1), LROW, LROW + 9)
    spread(dbd, rows, DROW)
    k_rows_ref[...] = nt(unit, own_tile(keys_ref, low, high)).astype(bf16)
    v_rows_ref[...] = nt(unit, own_tile(values_ref, low, high)).astype(bf16)
    w_qkv = w_qkv_ref[...]

    def queries(k, carry):
        at = pl.ds(pl.multiple_of(k * BLOCK, BLOCK), BLOCK)
        qall_ref[k] = query_of(normal_all[k], w_qkv, rope_ref[0:8, at], rope_ref[8:16, at])
        return carry

    lax.fori_loop(0, BLOCKS, queries, 0, unroll=2)
    traffic.send(k_rows_ref, v_rows_ref, qall_ref)
    acc_ref[...] = jnp.zeros(acc_ref.shape, f32)

    def step(u, tile, block, at):
        scores = scores_of(qbd[u], with_ones(keys_ref[block, :, at]), query_bias(u, tile, block, at, len_ref))
        d_scores = jnp.exp(scores) * nn(dbd[u], with_ones(values_ref[block, :, at]))
        acc_ref[u] = acc_ref[u] + nt(d_scores.astype(bf16), keys_ref[block, :, at])

    run_steps(query_step, low, high, step, 2)
    step(*query_last(low, high))
    d_query = jnp.concatenate([own_heads(acc_ref[0]), own_heads(acc_ref[1])], axis=0) * HEAD_DIM**-0.5
    dq_ref[...] = rotate(turned_rows(d_query), own_rope_ref[0:8], -own_rope_ref[8:16])


def turned_rows(x):
    hi, lo = two_parts(x)
    unit = eye(D, D, bf16)
    return nt(unit, hi) + nt(unit, lo)


def key_back(traffic, count, own_ref, other_ref, len_ref, qall_ref, k_rows_ref, v_rows_ref, dq_ref, grad_ref, resid_ref, w_qkv_ref, gain,
             own_rope_ref, daug, kbd, vbd, dk_ref, dv_ref):
    chip, core, low, high = geometry()

    def put(block, columns, value):
        daug[block, :, columns] = value

    natural_tiles(own_ref, other_ref, put)
    traffic.ready(count)
    ones = jnp.ones((TILE, STAT), f32)
    spread(kbd, jnp.concatenate([k_rows_ref[...].astype(f32), ones], axis=1), LROW, LROW + 9)
    spread(vbd, jnp.concatenate([v_rows_ref[...].astype(f32), ones], axis=1), DROW)
    dk_ref[...] = jnp.zeros(dk_ref.shape, f32)
    dv_ref[...] = jnp.zeros(dv_ref.shape, f32)

    def step(u, tile, block, at):
        queries = jnp.concatenate([qall_ref[block, :, at], daug[block, D:AUG, at]], axis=0)
        probs = jnp.exp(scores_of(kbd[u], queries, key_bias(u, tile, block, at, len_ref)))
        d_scores = probs * nn(vbd[u], daug[block, :, at])
        dv_ref[u] = dv_ref[u] + nt(probs.astype(bf16), daug[block, :, at])
        dk_ref[u] = dk_ref[u] + nt(d_scores.astype(bf16), qall_ref[block, :, at])

    run_steps(key_step, low, high, step)
    step(*key_last(low, high))
    traffic.ready()
    d_key = turned_rows(jnp.concatenate([own_heads(dk_ref[0]), own_heads(dk_ref[1])], axis=0))
    d_value = nt(eye(D, D, bf16), jnp.concatenate([own_heads(dv_ref[0]), own_heads(dv_ref[1])], axis=0).astype(bf16))
    d_key = rotate(d_key, own_rope_ref[0:8], -own_rope_ref[8:16])
    d_mixed = jnp.concatenate([dq_ref[...], d_key, d_value], axis=0).astype(bf16)
    d_in, d_gain = norm_back(resid_ref[...], gain(), nn(w_qkv_ref[...], d_mixed))
    return grad_ref[...] + d_in, d_mixed, d_gain


def projection_grads(normal, d_mixed):
    tail = nt(normal, jnp.concatenate([d_mixed[MAXLAG:], jnp.zeros((TILE - 48, TILE), bf16)], axis=0))
    return nt(normal, d_mixed[:MAXLAG]), tail


def third_kernel(
    traffic, own_ref, other_ref, len_ref, qall_ref, k_rows_ref, v_rows_ref, dq_ref, grad_in_ref, resid_ref, att_ref, stat_ref, mid_ref,
    gate_up_ref, own_rope_ref, w_qkv_ref, w_out_ref, w_gate_up_ref, w_down_ref, gains_ref,
    copies_ref, payload_ref, grad_ref, d_mixed_ref, d_gain_a_ref, d_gain_b_ref, d_out_ref, d_gate_up_ref, d_branch_ref, hidden_ref,
    normal_b_ref,
    daug, kbd, vbd, dk_ref, dv_ref,
):
    grad, d_mixed_ref[...], d_gain_a_ref[...] = key_back(
        traffic, 4, own_ref, other_ref, len_ref, qall_ref, k_rows_ref, v_rows_ref, dq_ref, grad_in_ref, resid_ref, w_qkv_ref,
        lambda: gain_column(gains_ref, 2), own_rope_ref, daug, kbd, vbd, dk_ref, dv_ref,
    )
    low_refs = (d_out_ref, d_gate_up_ref, d_branch_ref, hidden_ref, normal_b_ref)
    grad, payload, d_gain_b_ref[...] = feed_back(
        grad, att_ref[...], mid_ref[...], gate_up_ref[...], w_out_ref[...], w_gate_up_ref[...], w_down_ref[...], gain_column(gains_ref, 1),
        stat_ref[...], low_refs, traffic,
    )
    grad_ref[...] = grad
    payload_ref[...] = payload
    copies_ref[...] = jnp.broadcast_to(payload[None], copies_ref.shape)


def second_window_kernel(
    traffic, len_ref, hidden_ref, d_out_ref, normal_ref, d_gate_up_ref, att_ref, d_branch_ref, d_gain_ref, payload_ref, q_ref,
    own_rope_ref, rope_ref, keys_ref, values_ref, normal_all, w_qkv_ref,
    pack_ref, tail_ref, dq_ref, qall_ref, k_rows_ref, v_rows_ref, qbd, dbd, acc_ref,
):
    traffic.ready(8)
    tail = feed_grads(
        Tiles(pack_ref), hidden_ref[...], d_out_ref[...], normal_ref[...], d_gate_up_ref[...], att_ref[...], d_branch_ref[...]
    )
    tail_ref[...] = jnp.where(iota((1, TILE), 1) == 99, d_gain_ref[...], tail)
    traffic.send(pack_ref, tail_ref)
    query_back(
        traffic, 16, payload_ref, q_ref, len_ref, own_rope_ref, rope_ref, keys_ref, values_ref, normal_all, w_qkv_ref, dq_ref, qall_ref,
        k_rows_ref, v_rows_ref, qbd, dbd, acc_ref,
    )


def third_window_kernel(
    traffic, len_ref, pack_in_ref, tail_in_ref, normal_a_ref, d_mixed_ref, d_gain_a_ref, hidden_ref, d_out_ref, normal_ref, d_gate_up_ref,
    att_ref, d_branch_ref, d_gain_b_ref, payload_ref, q_ref, own_rope_ref, rope_ref, keys_ref, values_ref, normal_all,
    w_qkv_ref,
    keep_ref, send_ref, rest_ref, tail0_ref, tail1_ref, dq_ref, qall_ref, k_rows_ref, v_rows_ref, qbd, dbd, acc_ref,
):
    traffic.ready(13)
    put = Pairs(lax.axis_index("tm") % 2, keep_ref, send_ref, rest_ref)
    for t in range(pack_in_ref.shape[0]):
        put.tile(pack_in_ref[t].astype(f32))
    head, tail = projection_grads(normal_a_ref[...], d_mixed_ref[...])
    put(head)
    tail0_ref[...] = feed_grads(
        put, hidden_ref[...], d_out_ref[...], normal_ref[...], d_gate_up_ref[...], att_ref[...], d_branch_ref[...]
    )
    lane = iota((1, TILE), 1)
    tail = jnp.where(lane == 98, d_gain_a_ref[...], tail + tail_in_ref[...])
    tail1_ref[...] = jnp.where(lane == 97, d_gain_b_ref[...], tail)
    traffic.send(keep_ref, send_ref, rest_ref, tail0_ref, tail1_ref)
    query_back(
        traffic, 21, payload_ref, q_ref, len_ref, own_rope_ref, rope_ref, keys_ref, values_ref, normal_all, w_qkv_ref, dq_ref, qall_ref,
        k_rows_ref, v_rows_ref, qbd, dbd, acc_ref,
    )


def last_kernel(
    traffic, own_ref, other_ref, len_ref, scale_ref, ids_ref, qall_ref, k_rows_ref, v_rows_ref, dq_ref, grad_in_ref, resid_ref,
    normal_a_ref, tail0_ref, tail1_ref, rest_ref, w_dense_ref, feats_ref, own_rope_ref, w_qkv_ref, gains_ref,
    keep_ref, send_ref, daug, kbd, vbd, dk_ref, dv_ref, raw_ref,
):
    chip, core, low, high = geometry()
    d_first, d_mixed, d_gain = key_back(
        traffic, 6, own_ref, other_ref, len_ref, qall_ref, k_rows_ref, v_rows_ref, dq_ref, grad_in_ref, resid_ref, w_qkv_ref,
        lambda: gain_column(gains_ref, 0), own_rope_ref, daug, kbd, vbd, dk_ref, dv_ref,
    )
    head, tail0 = projection_grads(normal_a_ref[...], d_mixed)
    d_first = d_first.astype(bf16)
    feats = feats_ref[...]
    empty = jnp.zeros((64, TILE), bf16)
    tail0 = tail0 + tail0_ref[...] + nt(d_first, jnp.concatenate([empty, feats[:64]], axis=0))
    tail1 = tail1_ref[...] + nt(d_first, jnp.concatenate([empty, feats[64:], empty[:32]], axis=0))
    lane, row = iota((1, TILE), 1), iota((D, 1), 0)
    tail1 = jnp.where(lane == 96, d_gain, tail1)
    sums, counts = jnp.zeros((D, 1), f32), jnp.zeros((D, 1), f32)
    owner = (lax.axis_index("tm") == 0).astype(f32)
    for d in range(DOCS):
        hit = jnp.where(row == ids_ref[d], owner, 0.0)
        sums, counts = sums + hit * scale_ref[d], counts + hit
    high_part = sums.astype(bf16).astype(f32)
    tail1 = jnp.where(lane == 100, high_part, tail1)
    tail1 = jnp.where(lane == 101, sums - high_part, tail1)
    tail1 = jnp.where(lane == 102, counts, tail1)

    place = own_places(low, high)
    start = doc_start(place, len_ref)
    own = doc_scale_at(place, len_ref, scale_ref)
    flip = (iota((TILE, TILE), 0) + iota((TILE, TILE), 1) == TILE - 1).astype(bf16)
    raw_ref[...] = jnp.zeros(raw_ref.shape, f32)
    lags = TILE - iota((TILE, 1), 0)
    for b in range(3):
        weights = nn(w_dense_ref[:, b * TILE : (b + 1) * TILE], flip).astype(bf16)
        d_lagged = tn(weights, d_first)
        valid = place - (lags + b * TILE) >= start
        d_lagged = jnp.where(valid, d_lagged, 0.0) / own
        for u in range(2):
            half = jnp.where((lane < HALF) == (u == 0), d_lagged, 0.0)
            wide = jnp.concatenate([jnp.zeros((TILE, TILE), f32), half], axis=1)
            rolled = pltpu.roll(wide, TILE, 1, stride=1, stride_axis=0)
            total = jnp.sum(rolled, axis=0, keepdims=True)
            for tile, part in (((low if u == 0 else high) - b + 16, total[:, TILE:]), ((low if u == 0 else high) - b + 15, total[:, :TILE])):
                at = tile % 2, pl.ds(tile // 2, 1)
                raw_ref[at] = raw_ref[at] + part

    put = Pairs(core, keep_ref, send_ref)
    put.tile(rest_ref[0].astype(f32))
    for part in (head, tail0, tail1):
        put(part)
    for k in range(2):
        put.tile(raw_ref[k, 8:24, :])


def summed(in_ref):
    count, rows, _ = in_ref.shape
    total = jnp.zeros((rows, TILE), f32)
    return lax.fori_loop(0, count // 8, lambda i, t: t + jnp.sum(in_ref[pl.ds(i * 8, 8)].astype(f32), axis=0), total)


def pair_sum_kernel(early_ref, early_in_ref, late_ref, late_in_ref, out_ref):
    zero = jnp.zeros((16, TILE), bf16)
    late = late_ref.shape[0] - 1
    series, core = lax.axis_index("series"), lax.axis_index("tm") % 2
    out_ref[:, 32:40, :] = jnp.zeros((64, 8, TILE), bf16)

    def both(ref, in_ref, t):
        return ref[t].astype(f32) + in_ref[t].astype(f32)

    for t in range(128):
        value = zero
        if t < EARLY:
            value = both(early_ref, early_in_ref, t).astype(bf16)
        elif t < EARLY + late:
            value = both(late_ref, late_in_ref, t - EARLY).astype(bf16)
        out_ref[jnp.where(core == 0, t // 2, 63 - t // 2), t % 2 * 16 : t % 2 * 16 + 16, :] = value
    raw = both(late_ref, late_in_ref, late)
    for c in range(16):
        line = jnp.where(iota((8, 1), 0) == 0, raw[c : c + 1], 0.0)
        chip = series * 16 + c
        out_ref[jnp.where(core == 0, chip, 63 - chip), 32:40, :] = line.astype(bf16)


def sum_kernel(in_ref, out_ref, raw_ref):
    total = summed(in_ref)
    out_ref[...] = jnp.broadcast_to(total[:32].astype(bf16)[None], out_ref.shape)
    raw_ref[...] = total[32:33]


def unpack_kernel(own_ref, other_ref, act_in_ref, act_ref, lag_ref, qkv_ref, out_ref, gate_up_ref, down_ref, gains_ref, scale_ref):
    core = lax.axis_index("tm") % 2
    act_ref[...] = act_in_ref[...]

    def tile(t):
        rows = slice(t // 2 % 2 * 16, t // 2 % 2 * 16 + 16)
        first, second = jnp.where(core == 0, t // 4, 63 - t // 4), jnp.where(core == 0, 63 - t // 4, t // 4)
        return jnp.where(core == t % 2, own_ref[first, rows].astype(f32), other_ref[second, rows].astype(f32))

    def columns(first, count):
        return [jnp.concatenate([tile(first + 9 * c + r) for r in range(9)], axis=0) for c in range(count)]

    layers = ((207, 234, 117), (90, 243, 0))
    tails = []
    for layer, (at_qkv, at_tail, at_rest) in enumerate(layers):
        for c, part in enumerate(columns(at_qkv, 3)):
            qkv_ref[layer, :, c * TILE : (c + 1) * TILE] = part
        tail = columns(at_tail, 1)[0]
        tails.append(tail)
        qkv_ref[layer, :, MAXLAG:] = tail[:, :48]
        for c, part in enumerate(columns(at_rest, 3)):
            down_ref[layer, :, c * TILE : (c + 1) * TILE] = part
        for c, part in enumerate(columns(at_rest + 27, 6)):
            gate_up_ref[layer, :, c * TILE : (c + 1) * TILE] = part
        out_ref[layer, :, :TILE] = columns(at_rest + 81, 1)[0]
        out_ref[layer, :, TILE:] = tail[:, 48:64]
    lag = jnp.where(iota((1, TILE), 1) < 64, pltpu.roll(tails[0], 64, 1), tails[1])
    lag_ref[...] = lag[:, :FEATS]
    pick = (iota((8, TILE), 1) == iota((8, TILE), 0) + 96).astype(bf16)
    rest = nt(pick, tails[1].astype(bf16))
    gains_ref[0] = rest[0:2]
    gains_ref[1] = rest[2:4]
    scale_ref[...] = ((rest[4:5] + rest[5:6]) / rest[6:7])[:, :DATASETS]


def weights_kernel(
    traffic, lag_ref, w_lag_ref, w_qkv_ref, w_out_ref, w_gate_up_ref, cot_ref,
    dense_ref, qkv0_ref, out0_ref, gate_up0_ref, qkv1_ref, out1_ref, gate_up1_ref, chosen_ref, low_cot_ref,
):
    traffic.ready()
    rows = iota((FEATS, 1), 0)
    diagonal = iota((FEATS, LAGS), 0) == iota((FEATS, LAGS), 1)
    offsets = jnp.sum(jnp.where(diagonal, lag_ref[...].astype(f32), 0.0), axis=1, keepdims=True)
    offsets = jnp.where(rows < LAGS, offsets - 1.0, (rows - LAGS + MAXLAG + 1).astype(f32))
    chosen = (iota((FEATS, LAGCOLS), 1).astype(f32) == offsets).astype(bf16)
    chosen_ref[0:FEATS, :] = chosen
    chosen_ref[FEATS:, :] = jnp.zeros((96 - FEATS, LAGCOLS), bf16)
    dense_ref[...] = nn(w_lag_ref[...], chosen).astype(bf16)
    qkv0_ref[...] = turned(w_qkv_ref[0])
    out0_ref[...] = turned(w_out_ref[0])
    gate_up0_ref[...] = turned(w_gate_up_ref[0])
    qkv1_ref[...] = turned(w_qkv_ref[1])
    out1_ref[...] = turned(w_out_ref[1])
    gate_up1_ref[...] = turned(w_gate_up_ref[1])
    low_cot_ref[...] = cot_ref[...].astype(bf16)


def first_values_kernel(traffic, len_ref, scale_ref, raw_ref, hours_ref, out_ref):
    traffic.ready()
    places = lax.axis_index("tm") * TILE + iota((1, TILE), 1)
    own = doc_scale_at(places, len_ref, scale_ref)
    angle = hours_ref[...].astype(f32) * (2.0 * math.pi / 24.0)
    rows = [raw_ref[...] / own, jnp.sin(angle), jnp.cos(angle), jnp.log(own), jnp.zeros((4, TILE), f32)]
    out_ref[...] = jnp.broadcast_to(jnp.concatenate(rows, axis=0)[None], out_ref.shape)


def shape(*dims, dtype=f32):
    return jax.ShapeDtypeStruct(dims, dtype)


class Traffic:
    def __init__(self, loads, stores):
        self.loads, self.stores, self.waited, self.sent = loads, stores, 0, set()
        for copy in loads:
            copy.start()

    def ready(self, count=None):
        count = len(self.loads) if count is None else count
        for copy in self.loads[self.waited : count]:
            copy.wait()
        self.waited = max(self.waited, count)

    def send(self, *refs):
        for ref, copy in self.stores:
            if any(ref is r for r in refs):
                copy.start()
                self.sent.add(id(copy))

    def finish(self):
        self.ready()
        for _, copy in self.stores:
            if id(copy) not in self.sent:
                copy.start()
        for _, copy in self.stores:
            copy.wait()


def call(kernel, operands, outs, scratch=(), tables=(), weights=(), cost=None):
    several = isinstance(outs, list)
    outs = outs if several else [outs]
    layers = [None] * len(tables) + [x[1] if isinstance(x, tuple) else None for x in weights]
    fetched = (*tables, *(x[0] if isinstance(x, tuple) else x for x in weights))
    shapes = [x.shape if layer is None else x.shape[1:] for x, layer in zip(fetched, layers)]
    buffers = [(pltpu.SMEM if n < len(tables) else pltpu.VMEM)(shapes[n], x.dtype) for n, x in enumerate(fetched)]
    is_far = [not isinstance(out, jax.ShapeDtypeStruct) for out in outs]
    buffers += [pltpu.VMEM(out.shape, out.dtype) for out, far in zip(outs, is_far) if far]
    count, extra, copies = len(operands), len(buffers), len(buffers)

    def wrapped(*refs):
        refs = list(refs)
        ins, sources = refs[:count], refs[count : count + len(fetched)]
        results = refs[count + len(fetched) : count + len(fetched) + len(outs)]
        rest = refs[count + len(fetched) + len(outs) :]
        if not copies:
            kernel(*ins, *results, *rest)
            return
        own, held, sems = rest[: len(scratch)], rest[len(scratch) : -1], rest[-1]
        sources = [a if layer is None else a.at[layer] for a, layer in zip(sources, layers)]
        loads = [pltpu.make_async_copy(a, b, sems.at[n]) for n, (a, b) in enumerate(zip(sources, held))]
        stores, at = [], len(fetched)
        for n, far in enumerate(is_far):
            if far:
                stores.append((held[at], pltpu.make_async_copy(held[at], results[n], sems.at[at])))
                results[n] = held[at]
                at += 1
        traffic = Traffic(loads, stores)
        kernel(traffic, *ins, *held[: len(fetched)], *results, *own)
        traffic.finish()

    vmem, hbm = pl.BlockSpec(memory_space=pltpu.VMEM), pl.BlockSpec(memory_space=pltpu.HBM)
    results = pl.pallas_call(
        wrapped,
        out_shape=outs,
        in_specs=[vmem] * count + [hbm] * len(fetched),
        out_specs=[hbm if far else vmem for far in is_far],
        scratch_shapes=[*scratch, *buffers, pltpu.SemaphoreType.DMA((copies,))] if copies else list(scratch),
        compiler_params=pltpu.CompilerParams(vmem_limit_bytes=VMEM),
        cost_estimate=cost and pl.CostEstimate(flops=cost * 10**9, bytes_accessed=10**6, transcendentals=0),
    )(*operands, *(pltpu.with_memory_space_constraint(x, pltpu.HBM) for x in fetched))
    return results if several else results[0]


def pair_permute(x, bit):
    return lax.ppermute(x, "tm", [(i, i ^ bit) for i in range(32)])


def gather(copies, beside):
    groups = [[2 * chip for chip in range(16)], [31 - 2 * chip for chip in range(16)]]
    own = lax.all_to_all(copies, "tm", 0, 0, axis_index_groups=groups)
    own, beside = lax.optimization_barrier((own, beside))
    return own, pair_permute(own, 1), beside


def swap(block):
    return lax.ppermute(block, "tm", [(n, n if n % 2 == 0 else 32 - n) for n in range(32)])


def tile_halves(own, other):
    lane = iota((1, TILE), 1) < HALF
    return jnp.where(lane == (lax.axis_index("tm") < 16), own, other)


def rope_table():
    freqs = 10000.0 ** (-np.arange(8, dtype=np.float64) / 8)
    angle = np.arange(LEN, dtype=np.float64)[None, :] * freqs[:, None]
    return np.concatenate([np.cos(angle), np.sin(angle)], axis=0).astype(np.float32)


def body(
    raw_values, hours, doc_lengths, doc_scale, dataset_ids, lag_offsets, w_lag, w_qkv, w_out, w_gate_up, w_down, gains, cotangent
):
    lengths, scales, ids = doc_lengths.reshape(DOCS), doc_scale.reshape(DOCS), dataset_ids.reshape(DOCS)
    def low(*dims):
        return shape(*dims, dtype=bf16)

    def far(*dims, dtype=f32):
        return pltpu.HBM(dims, dtype)

    def far_low(*dims):
        return far(*dims, dtype=bf16)

    w_lag, w_down, lags = w_lag.T, w_down.transpose(0, 2, 1), lag_offsets.reshape(1, LAGS)
    rope = jnp.asarray(rope_table())
    values = lax.all_to_all(call(first_values_kernel, (), shape(32, 8, TILE), tables=(lengths, scales), weights=(raw_values, hours)), "tm", 0, 0)
    turned_shapes = [far_low(3 * D, D), far_low(D, D), far_low(2 * FF, D)]
    w_dense, *turned_weights, chosen, low_cot = call(
        weights_kernel, (), [far_low(D, LAGCOLS), *turned_shapes, *turned_shapes, far_low(96, LAGCOLS), far_low(D, TILE)],
        weights=(lags, w_lag, w_qkv, w_out, w_gate_up, cotangent[0].T), cost=3,
    )
    turned0, turned1 = turned_weights[:3], turned_weights[3:]
    values, w_dense = lax.optimization_barrier((values, w_dense))
    all_d = far_low(BLOCKS, D, BLOCK)
    mine, mine_low, ff_low, column_shape = far(D, TILE), far_low(D, TILE), far_low(FF, TILE), far(D, 1)
    payload_shapes = [far_low(16, AUG, TILE), far_low(AUG, TILE)]
    low_grads = [mine_low, far_low(2 * FF, TILE), mine_low, ff_low, mine_low]
    bd, wide_bd = pltpu.VMEM((2, ROWS, AUG), bf16), pltpu.VMEM((2, ROWS, WIDE), bf16)
    acc, acc_d = pltpu.VMEM((2, ROWS, AUG), f32), pltpu.VMEM((2, ROWS, D), f32)
    top = pltpu.VMEM((2, ROWS, 1), f32)
    back_scratch = [pltpu.VMEM((BLOCKS, AUG, BLOCK), bf16), wide_bd, bd, acc_d, acc]

    (copies, next1, resid1, keys0, values0, normal_all0, feats, resid0, normal_a0, q0, att0, stat0, mid0, gate_up0, own_rope) = call(
        first_kernel,
        (values,),
        [far_low(16, D, TILE), mine_low, mine, all_d, all_d, all_d, far_low(96, TILE), mine, mine_low, far_low(TILE, D), mine_low,
         far_low(STAT, TILE), mine, far(2 * FF, TILE), far(16, TILE)],
        [pltpu.VMEM((8 + TILES, TILE), f32), pltpu.VMEM((TILE, MAXLAG + LEN), bf16),
         pltpu.VMEM((LAGCOLS, TILE), bf16), wide_bd, top, acc],
        tables=(lengths,), weights=(w_dense, gains, turned0[0], rope, chosen, *turned0[1:], (w_down, 0)),
    )

    own, other, cot = gather(copies, swap(low_cot))
    copies, payload, act, keys1, values1, normal_all1, q1, grad, att1, d_gain_b1, *low1 = call(
        second_kernel,
        (own, other, cot, pair_permute(cot, 1)),
        [*payload_shapes, mine, all_d, all_d, all_d, far_low(TILE, D), mine, mine_low, column_shape, *low_grads],
        [wide_bd, top, acc],
        tables=(lengths,),
        weights=(turned1[0], rope, next1, own_rope, resid1, *turned1[1:], (w_out, 1), (w_gate_up, 1), (w_down, 1), gains),
    )

    rows_low = far_low(TILE, D)
    side_shapes = [mine, all_d, rows_low, rows_low]
    d_out, d_gate_up, d_branch, hidden, normal_b = low1
    pack, tail, dq, qall, k_rows, v_rows = call(
        second_window_kernel, (), [far_low(90, 16, TILE), mine, *side_shapes], [wide_bd, bd, acc_d],
        tables=(lengths,),
        weights=(hidden, d_out, normal_b, d_gate_up, att1, d_branch, d_gain_b1, payload, q1, own_rope, rope, keys1, values1, normal_all1,
                 turned1[0]), cost=8,
    )
    own, other, dq = gather(copies, dq)
    copies, payload, grad, d_mixed, d_gain_a1, d_gain_b0, *low0 = call(
        third_kernel,
        (own, other),
        [*payload_shapes, mine, far_low(3 * D, TILE), column_shape, column_shape, *low_grads],
        back_scratch,
        tables=(lengths,),
        weights=(qall, k_rows, v_rows, dq, grad, resid1, att0, stat0, mid0, gate_up0, own_rope, (w_qkv, 1), (w_out, 0), (w_gate_up, 0),
                 (w_down, 0), gains),
    )
    d_out, d_gate_up, d_branch, hidden, normal_b = low0
    early, early_out, rest, tail0, tail1, dq, qall, k_rows, v_rows = call(
        third_window_kernel, (),
        [far_low(EARLY, 16, TILE), far_low(EARLY, 16, TILE), far_low(1, 16, TILE), mine, mine, *side_shapes], [wide_bd, bd, acc_d],
        tables=(lengths,),
        weights=(pack, tail, next1, d_mixed, d_gain_a1, hidden, d_out, normal_b, d_gate_up, att0, d_branch, d_gain_b0, payload, q0,
                 own_rope, rope, keys0, values0, normal_all0, turned0[0]), cost=8,
    )
    own, other, (dq, early_out) = gather(copies, (dq, early_out))
    early_in = pair_permute(early_out, 1)
    late, late_out = call(
        last_kernel,
        (own, other),
        [low(LATE, 16, TILE)] * 2,
        [*back_scratch, pltpu.VMEM((2, 24, TILE), f32)],
        tables=(lengths, scales, ids),
        weights=(qall, k_rows, v_rows, dq, grad, resid0, normal_a0, tail0, tail1, rest, w_dense, feats, own_rope, (w_qkv, 0), gains),
    )
    packed = call(pair_sum_kernel, (early, early_in, late, pair_permute(late_out, 1)), low(64, 40, TILE))
    same_core = [[2 * chip for chip in range(64)], [127 - 2 * chip for chip in range(64)]]
    parts = lax.all_to_all(packed, ("series", "tm"), 0, 0, axis_index_groups=same_core)
    share, raw_grad = call(sum_kernel, (parts,), [low(64, 32, TILE), shape(1, TILE)])
    share, act = lax.optimization_barrier((share, act))
    own = lax.all_to_all(share, ("series", "tm"), 0, 0, axis_index_groups=same_core)
    own, act = lax.optimization_barrier((own, swap(tile_halves(act, pair_permute(act, 1)))))
    act, g_lag, g_qkv, g_out, g_gate_up, g_down, g_gains, scale = call(
        unpack_kernel,
        (own, pair_permute(own, 1), act),
        [shape(D, TILE), shape(D, FEATS), shape(LAYERS, D, 3 * D), shape(LAYERS, D, D), shape(LAYERS, D, 2 * FF), shape(LAYERS, D, FF),
         shape(LAYERS, 2, D), shape(1, DATASETS)],
    )
    return (
        act.T[None], raw_grad, scale.reshape(DATASETS), g_lag.T, g_qkv, g_out, g_gate_up, g_down.transpose(0, 2, 1), g_gains,
    )


def solution(mesh):
    placed = (
        P("series", "tm"),
        P("series", "tm"),
        P("series", None),
        P("series", None),
        P("series", None, None),
        P(),
        P(),
        P(),
        P(),
        P(),
        P(),
        P(),
        P("series", "tm", None),
    )
    return jax.shard_map(
        body,
        mesh=mesh,
        in_specs=placed,
        out_specs=(P("series", "tm", None), P("series", "tm"), P(), P(), P(), P(), P(), P(), P()),
        check_vma=False,
    )
```

```python
import math

import jax
import jax.numpy as jnp
import numpy as np
from jax import lax
from jax.experimental import pallas as pl
from jax.experimental.pallas import tpu as pltpu
from jax.sharding import PartitionSpec as P


D = 144
HEADS = 9
HEAD_DIM = 16
FF = 384
LAGS = 84
LAYERS = 2
DATASETS = 8
DOCS = 7
LEN = 4096
MAXLAG = 384
FEATS = 87
EPSILON = 1e-06
MASKED = -1e30
AUG = 176
STAT = AUG - D
LROW = D
DROW = D + 18
BLOCK = 512
BLOCKS = LEN // BLOCK
TILE = 128
TILES = LEN // TILE
STEPS = BLOCKS + 1
SHIFTED = 8
HALF = 64
ROWS = HEADS * HALF
LAGCOLS = 400
EARLY = 103
LATE = 24
WIDE = AUG + HALF
SAFE = 70.0
VMEM = 28 * 2**20

bf16 = jnp.bfloat16
f32 = jnp.float32
HIGH = lax.Precision.HIGHEST


def nn(a, b, precision=None):
    return lax.dot_general(a, b, (((1,), (0,)), ((), ())), precision=precision, preferred_element_type=f32)


def nt(a, b, precision=None):
    return lax.dot_general(a, b, (((1,), (1,)), ((), ())), precision=precision, preferred_element_type=f32)


def tn(a, b, precision=None):
    return lax.dot_general(a, b, (((0,), (0,)), ((), ())), precision=precision, preferred_element_type=f32)


def iota(shape, dim):
    return lax.broadcasted_iota(jnp.int32, shape, dim)


def eye(rows, cols, dtype):
    return (iota((rows, cols), 0) == iota((rows, cols), 1)).astype(dtype)


def column(row, size):
    keep = iota((size, size), 0) == iota((size, size), 1)
    return jnp.sum(jnp.where(keep, row, 0.0), axis=1, keepdims=True)


def pair_of(chip):
    return jnp.where(chip < 8, 2 * chip, TILES - 1 - 2 * chip)


def geometry():
    index = lax.axis_index("tm")
    chip, core = index // 2, index % 2
    tile = pair_of(chip)
    low = jnp.where(core == 0, tile, TILES - 1 - tile)
    return chip, core, low, TILES - 1 - low


def doc_start(places, len_ref):
    start = jnp.zeros_like(places)
    end = jnp.int32(0)
    for d in range(DOCS):
        end = end + len_ref[d]
        start = jnp.where(places >= end, end, start)
    return start


def doc_scale_at(places, len_ref, scale_ref):
    own = jnp.full(places.shape, scale_ref[0], f32)
    end = jnp.int32(0)
    for d in range(1, DOCS):
        end = end + len_ref[d - 1]
        own = jnp.where(places >= end, scale_ref[d], own)
    return own


def own_places(low, high):
    lane = iota((1, TILE), 1)
    return jnp.where(lane < HALF, low, high) * TILE + lane


def half_places(u, tile):
    return iota((HALF, 1), 0) + (tile * TILE + u * HALF)


def rotate(x, cosine, sine):
    cols = x.shape[1]
    parts = x.reshape(HEADS, 2, 8, cols)
    one, two = parts[:, 0], parts[:, 1]
    turned = jnp.stack([one * cosine - two * sine, two * cosine + one * sine], axis=1)
    return turned.reshape(D, cols)


def norm_factor(x):
    return lax.rsqrt(jnp.mean(x * x, axis=0, keepdims=True) + EPSILON)


def norm_back(x, gain, d_normal):
    r = norm_factor(x)
    scaled = d_normal * gain
    inner = jnp.mean(x * scaled, axis=0, keepdims=True)
    d_x = r * scaled - (r * r * r * inner) * x
    return d_x, jnp.sum(d_normal * x * r, axis=1, keepdims=True)


def head_columns(h, *firsts):
    col = iota((1, AUG), 1)
    keep = (col >= h * HEAD_DIM) & (col < (h + 1) * HEAD_DIM)
    for first in firsts:
        keep = keep | (col == first + h)
    return keep


def spread(ref, rows, *firsts):
    zero = jnp.zeros((HALF, AUG), f32)
    for h in range(HEADS):
        keep = head_columns(h, *firsts)
        for u in range(2):
            part = rows[u * HALF : (u + 1) * HALF]
            ref[u, h * HALF : (h + 1) * HALF, 0:AUG] = jnp.where(keep, part, zero).astype(bf16)
    if ref.shape[2] == WIDE:
        unit = eye(HALF, HALF, bf16)
        for h in range(HEADS):
            for u in range(2):
                ref[u, h * HALF : (h + 1) * HALF, AUG:WIDE] = unit


def own_heads(x):
    col = iota((1, D), 1) // HEAD_DIM
    total = jnp.zeros((HALF, D), f32)
    for h in range(HEADS):
        total = jnp.where(col == h, x[h * HALF : (h + 1) * HALF, :D], total)
    return total


def two_parts(x):
    hi = x.astype(bf16)
    return hi, (x - hi.astype(f32)).astype(bf16)


class Tiles:
    def __init__(self, ref):
        self.ref, self.count = ref, 0

    def tile(self, value):
        self.ref[self.count] = value.astype(bf16)
        self.count += 1

    def __call__(self, grads):
        for c in range(grads.shape[1] // TILE):
            for r in range(grads.shape[0] // 16):
                self.tile(grads[16 * r : 16 * (r + 1), c * TILE : (c + 1) * TILE].astype(f32))


class Pairs(Tiles):
    def __init__(self, core, keep_ref, send_ref, rest_ref=None):
        self.core, self.refs, self.rest, self.count, self.even = core, (keep_ref, send_ref), rest_ref, 0, None

    def tile(self, value):
        if self.count == self.refs[0].shape[0]:
            self.rest[0] = value.astype(bf16)
        elif self.even is None:
            self.even = value
        else:
            self.refs[0][self.count] = jnp.where(self.core == 0, self.even, value).astype(bf16)
            self.refs[1][self.count] = jnp.where(self.core == 0, value, self.even).astype(bf16)
            self.even = None
            self.count += 1


def turned(w):
    return tn(w, eye(D, D, bf16)).astype(bf16)


def with_ones(x):
    return jnp.concatenate([x, jnp.ones((STAT, x.shape[1]), bf16)], axis=0)


def key_value_block(normal, w_qkv, rope_ref, k, keys_ref, values_ref):
    mixed = nn(w_qkv[D:], normal)
    at = slice(k * BLOCK, (k + 1) * BLOCK)
    keys = rotate(mixed[:D], rope_ref[0:8, at], rope_ref[8:16, at])
    keys_ref[k] = keys.astype(bf16)
    values_ref[k] = mixed[D:].astype(bf16)
    return head_sizes(keys * keys)


def query_of(normal, w_qkv, cosine, sine):
    turned = rotate(nn(w_qkv[:D], normal), cosine, sine)
    return (turned.astype(bf16).astype(f32) * HEAD_DIM**-0.5).astype(bf16)


def own_rope(rope_ref, low, high):
    def at(tile):
        return rope_ref[:, pl.ds(pl.multiple_of(tile * TILE, TILE), TILE)]

    both = jnp.where(iota((1, TILE), 1) < HALF, at(low), at(high))
    return both[0:8], both[8:16]


def own_tile(ref, low, high):
    lane = iota((1, TILE), 1)

    def at(tile):
        return ref[tile // 4, :, pl.ds(pl.multiple_of((tile % 4) * TILE, TILE), TILE)].astype(f32)

    return jnp.where(lane < HALF, at(low), at(high)).astype(bf16)


def query_bias(u, tile, block, columns, len_ref):
    places = half_places(u, tile)
    start = doc_start(places, len_ref)
    keys = iota((1, columns.stop - columns.start), 1) + (block * BLOCK + columns.start)
    return jnp.where((keys <= places) & (keys >= start), 0.0, MASKED).astype(bf16)


def key_bias(u, tile, block, columns, len_ref):
    keys = half_places(u, tile)
    places = iota((1, columns.stop - columns.start), 1) + (block * BLOCK + columns.start)
    start = doc_start(places, len_ref)
    return jnp.where((keys <= places) & (keys >= start), 0.0, MASKED).astype(bf16)


def scores_of(rows, columns, bias):
    return nn(rows, jnp.concatenate([columns, bias], axis=0))


def run_steps(of_step, low, high, step, unroll=4):
    def several(i, carry):
        for j in range(unroll):
            step(*of_step(i * unroll + j, low, high), slice(0, BLOCK))
        return carry

    lax.fori_loop(0, (STEPS - 1) // unroll, several, 0)


def query_step(s, low, high):
    first = low // 4 + (low % 4 >= 2).astype(jnp.int32)
    late = s >= first
    return late.astype(jnp.int32), jnp.where(late, high, low), s - jnp.where(late, first, 0)


def query_last(low, high):
    late = low % 4 >= 2
    tile = jnp.where(late, high, low)
    return late.astype(jnp.int32), tile, tile // 4, slice(0, BLOCK // 2)


def key_step(s, low, high):
    late_short = (low % 4 < 2).astype(jnp.int32)
    first = low // 4 + 1 - late_short
    late = s >= BLOCKS - first
    block = jnp.where(late, high // 4 + late_short + s - (BLOCKS - first), first + s)
    return late.astype(jnp.int32), jnp.where(late, high, low), block


def key_last(low, high):
    late = low % 4 < 2
    tile = jnp.where(late, high, low)
    return late.astype(jnp.int32), tile, tile // 4, slice(BLOCK // 2, BLOCK)


def head_sizes(squares):
    return jnp.sum(squares.reshape(HEADS, HEAD_DIM, squares.shape[1]), axis=1)


def attend(query, k_size, keys_ref, values_ref, len_ref, low, high, qbd, top_ref, acc_ref, q_rows_ref):
    q_rows = nt(eye(TILE, TILE, bf16), query)
    q_rows_ref[...] = q_rows.astype(bf16)
    spread(qbd, jnp.concatenate([q_rows, jnp.zeros((TILE, STAT), f32)], axis=1))
    query = query.astype(f32)
    q_size = jnp.max(head_sizes(query * query), axis=1, keepdims=True)
    k_size = jnp.max(k_size, axis=1, keepdims=True)
    acc_ref[...] = jnp.zeros(acc_ref.shape, f32)
    safe = jnp.max(q_size * k_size) <= SAFE * SAFE

    @pl.when(safe)
    def _():
        top_ref[...] = jnp.zeros(top_ref.shape, f32)

        def step(u, tile, block, at):
            scores = scores_of(qbd[u], with_ones(keys_ref[block, :, at]), query_bias(u, tile, block, at, len_ref))
            acc_ref[u] = acc_ref[u] + nt(jnp.exp(scores).astype(bf16), with_ones(values_ref[block, :, at]))

        run_steps(query_step, low, high, step, 8)
        step(*query_last(low, high))

    @pl.when(jnp.logical_not(safe))
    def _():
        top_ref[...] = jnp.full(top_ref.shape, MASKED, f32)

        def step(s, carry):
            h, s = s % HEADS, s // HEADS
            first = low // 4 + 1
            late = s >= first
            u, tile, block = late.astype(jnp.int32), jnp.where(late, high, low), s - jnp.where(late, first, 0)
            rows = pl.ds(pl.multiple_of(h * HALF, HALF), HALF)
            bias = query_bias(u, tile, block, slice(0, BLOCK), len_ref)
            scores = scores_of(qbd[u, rows], with_ones(keys_ref[block]), bias)
            old = top_ref[u, rows]
            new = jnp.maximum(old, jnp.max(scores, axis=1, keepdims=True))
            probs = jnp.exp(scores - new)
            acc_ref[u, rows] = acc_ref[u, rows] * jnp.exp(old - new) + nt(probs.astype(bf16), with_ones(values_ref[block]))
            top_ref[u, rows] = new
            return carry

        lax.fori_loop(0, STEPS * HEADS, step, 0)

    attended, stats = [], []
    lane, col = iota((1, STAT), 1), iota((1, D), 1) // HEAD_DIM
    for u in range(2):
        acc, top = acc_ref[u], top_ref[u]
        total, shift = jnp.ones((HALF, STAT), f32), jnp.zeros((HALF, STAT), f32)
        for h in range(HEADS):
            rows = slice(h * HALF, (h + 1) * HALF)
            here = (lane == h) | (lane == HEADS + h)
            total = jnp.where(here, acc[rows, D : D + 1], total)
            shift = jnp.where(here, top[rows], shift)
        hi, lo = two_parts(-(shift + jnp.log(total)))
        stats.append(jnp.where(lane < HEADS, hi.astype(f32), jnp.where(lane < 2 * HEADS, lo.astype(f32), 0.0)))
        own = jnp.zeros((HALF, D), f32)
        for h in range(HEADS):
            rows = slice(h * HALF, (h + 1) * HALF)
            own = jnp.where(col == h, acc[rows, :D] / acc[rows, D : D + 1], own)
        attended.append(own)
    att_rows = jnp.concatenate(attended, axis=0).astype(bf16)
    stat_rows = jnp.concatenate(stats, axis=0).astype(bf16)
    return nt(eye(D, D, bf16), att_rows).astype(bf16), nt(eye(STAT, STAT, bf16), stat_rows).astype(bf16)


def feed_forward(resid, attended, w_out, w_gate_up, w_down, gain):
    mid = resid + nn(w_out, attended)
    normal = (mid * norm_factor(mid) * gain).astype(bf16)
    gate_up = nn(w_gate_up, normal)
    gate = gate_up[:FF]
    hidden = (gate * jax.nn.sigmoid(gate) * gate_up[FF:]).astype(bf16)
    return mid, normal, gate_up, hidden, mid + nn(w_down, hidden)


def feed_back(grad, attended, mid, gate_up, w_out, w_gate_up, w_down, gain, stat, low_refs, traffic):
    d_out_ref, d_gate_up_ref, d_branch_ref, hidden_ref, normal_ref = low_refs
    d_out = grad.astype(bf16)
    d_hidden = tn(w_down, d_out)
    gate, up = gate_up[:FF], gate_up[FF:]
    sig = jax.nn.sigmoid(gate)
    d_gate = d_hidden * up * (sig * (1.0 + gate * (1.0 - sig)))
    d_up = d_hidden * (gate * sig)
    hidden_ref[...] = (gate * sig * up).astype(bf16)
    normal_ref[...] = (mid * norm_factor(mid) * gain).astype(bf16)
    d_gate_up = jnp.concatenate([d_gate, d_up], axis=0).astype(bf16)
    d_mid, d_gain = norm_back(mid, gain, nn(w_gate_up, d_gate_up))
    grad = grad + d_mid
    d_branch = grad.astype(bf16)
    d_att = nn(w_out, d_branch).astype(bf16)
    d_out_ref[...], d_gate_up_ref[...], d_branch_ref[...] = d_out, d_gate_up, d_branch
    traffic.send(*low_refs)
    product = d_att.astype(f32) * attended.astype(f32)
    delta = -jnp.sum(product.reshape(HEADS, HEAD_DIM, TILE), axis=1)
    delta = jnp.concatenate([delta, jnp.zeros((16 - HEADS, TILE), f32)], axis=0)
    row, col = iota((STAT, 16), 0), iota((STAT, 16), 1)
    stat = stat.astype(f32) + nn(((row == DROW - D + col) & (col < HEADS)).astype(bf16), delta.astype(bf16))
    return grad, jnp.concatenate([d_att, stat.astype(bf16)], axis=0), d_gain


def feed_grads(put, hidden, d_out, normal, d_gate_up, attended, d_branch):
    put(nt(d_out, hidden))
    put(nt(normal, d_gate_up))
    put(nt(attended, d_branch[:TILE]))
    rows = [jnp.zeros((48, TILE), bf16), d_branch[TILE:], jnp.zeros((TILE - 64, TILE), bf16)]
    return nt(attended, jnp.concatenate(rows, axis=0))


def gain_column(gains_ref, which):
    return column(gains_ref[which // 2, which % 2 : which % 2 + 1, :], D)


def first_kernel(
    traffic, features_ref, len_ref, w_dense_ref, gains_ref, w_qkv_ref, rope_ref, chosen_ref, w_out_ref, w_gate_up_ref,
    w_down_ref,
    copies_ref, next_ref, next_resid_ref, keys_ref, values_ref, normal_all, feats_ref, resid_ref, normal_a_ref,
    q_ref, att_ref, stat_ref, mid_ref, gate_up_ref, own_rope_ref,
    series, toeplitz, lagged_ref, qbd, top_ref, acc_ref,
):
    chip, core, low, high = geometry()
    series[0:8, :] = jnp.zeros((8, TILE), f32)
    series[8 : 8 + TILES, :] = features_ref[:, 0, :].astype(bf16).astype(f32)
    toeplitz[:, 0:MAXLAG] = jnp.zeros((TILE, MAXLAG), bf16)

    def shift(m, carry):
        rows = [series[pl.ds(m * SHIFTED + 7 + n, 1), :] for n in range(SHIFTED + 1)]
        window = jnp.broadcast_to(jnp.concatenate(rows, axis=1), (TILE, (SHIFTED + 1) * TILE))
        rolled = pltpu.roll(window, 1, 1, stride=1, stride_axis=0)
        at = pl.multiple_of(m * SHIFTED * TILE + MAXLAG, TILE)
        toeplitz[:, pl.ds(at, SHIFTED * TILE)] = rolled[:, TILE:].astype(bf16)
        return carry

    lax.fori_loop(0, TILES // SHIFTED, shift, 0)

    def others(tiles):
        rows = jnp.concatenate([features_ref[t] for t in tiles], axis=1)
        return jnp.concatenate([rows, jnp.zeros_like(rows)], axis=0).astype(bf16)

    traffic.ready(5)
    w_dense = w_dense_ref[...]
    gain_a, gain_b = gain_column(gains_ref, 0), gain_column(gains_ref, 1)
    w_qkv = w_qkv_ref[...]
    lag_rows = iota((TILE, 1), 0) + 1
    k_size = jnp.zeros((HEADS, BLOCK), f32)
    for k in range(BLOCKS):
        place = iota((1, BLOCK), 1) + k * BLOCK
        start = doc_start(place, len_ref)
        parts = []
        for b in range(3):
            at = MAXLAG + k * BLOCK - b * TILE
            lagged = toeplitz[:, at : at + BLOCK]
            if k in (0, BLOCKS - 1):
                valid = place - (lag_rows + b * TILE) >= start
                lagged = jnp.where(valid, lagged.astype(f32), 0.0).astype(bf16)
            parts.append(lagged)
        parts.append(others(range(4 * k, 4 * k + 4)))
        resid = nn(w_dense, jnp.concatenate(parts, axis=0))
        normal = (resid * norm_factor(resid) * gain_a).astype(bf16)
        normal_all[k] = normal
        k_size = jnp.maximum(k_size, key_value_block(normal, w_qkv, rope_ref, k, keys_ref, values_ref))

    cosine, sine = own_rope(rope_ref, low, high)
    own_rope_ref[0:8], own_rope_ref[8:16] = cosine, sine
    traffic.send(keys_ref, values_ref, normal_all, own_rope_ref)

    place = own_places(low, high)
    start = doc_start(place, len_ref)
    lane = iota((1, TILE), 1)

    def tile_of(ref, tile):
        return ref[:, pl.ds(pl.multiple_of(tile * TILE, TILE), TILE)].astype(f32)

    for b in range(3):
        lagged = jnp.where(lane < HALF, tile_of(toeplitz, low + 3 - b), tile_of(toeplitz, high + 3 - b))
        valid = place - (lag_rows + b * TILE) >= start
        lagged_ref[b * TILE : (b + 1) * TILE, :] = jnp.where(valid, lagged, 0.0).astype(bf16)
    lagged_ref[MAXLAG:, :] = jnp.where(lane < HALF, others([low]).astype(f32), others([high]).astype(f32)).astype(bf16)
    lagged = lagged_ref[...]
    resid = nn(w_dense, lagged)
    resid_ref[...] = resid
    normal = (resid * norm_factor(resid) * gain_a).astype(bf16)
    normal_a_ref[...] = normal
    traffic.send(resid_ref, normal_a_ref)
    query = query_of(normal, w_qkv, cosine, sine)
    attended, stat_ref[...] = attend(query, k_size, keys_ref, values_ref, len_ref, low, high, qbd, top_ref, acc_ref, q_ref)
    att_ref[...] = attended
    traffic.send(q_ref, att_ref, stat_ref)
    traffic.ready()
    feats_ref[...] = nn(chosen_ref[...], lagged).astype(bf16)
    mid, _, gate_up, _, resid = feed_forward(resid, attended, w_out_ref[...], w_gate_up_ref[...], w_down_ref[...], gain_b)
    mid_ref[...], gate_up_ref[...] = mid, gate_up
    traffic.send(mid_ref, gate_up_ref, feats_ref)
    next_resid_ref[...] = resid
    normal = (resid * norm_factor(resid) * gain_column(gains_ref, 2)).astype(bf16)
    next_ref[...] = normal
    copies_ref[...] = jnp.broadcast_to(normal[None], copies_ref.shape)


def natural_tiles(own_ref, other_ref, put):
    _, core, _, _ = geometry()
    mine = (iota((1, TILE), 1) < HALF) == (core == 0)
    for chip in range(TILES // 2):
        tile = 2 * chip if chip < 8 else TILES - 1 - 2 * chip
        first, second = jnp.where(core == 0, chip, 15 - chip), jnp.where(core == 0, 15 - chip, chip)
        own, other = own_ref[first].astype(f32), other_ref[second].astype(f32)
        for t, value in ((tile, jnp.where(mine, own, other)), (TILES - 1 - tile, jnp.where(mine, other, own))):
            put(t // 4, slice(t % 4 * TILE, (t % 4 + 1) * TILE), value.astype(bf16))


def second_kernel(
    traffic, own_ref, other_ref, cot_own_ref, cot_other_ref, len_ref, turned_qkv_ref, rope_ref, normal_ref, own_rope_ref, resid_in_ref,
    turned_out_ref, turned_gate_up_ref, w_out_ref, w_gate_up_ref, w_down_ref, gains_ref,
    copies_ref, payload_ref, act_ref, keys_ref, values_ref, normal_all, q_ref, grad_ref, att_ref, d_gain_ref,
    d_out_ref, d_gate_up_ref, d_branch_ref, hidden_ref, normal_b_ref,
    qbd, top_ref, acc_ref,
):
    chip, core, low, high = geometry()

    def put(block, columns, value):
        normal_all[block, :, columns] = value

    natural_tiles(own_ref, other_ref, put)
    traffic.send(normal_all)
    traffic.ready(5)
    w_qkv = turned_qkv_ref[...]
    k_size = jnp.zeros((HEADS, BLOCK), f32)
    for k in range(BLOCKS):
        k_size = jnp.maximum(k_size, key_value_block(normal_all[k], w_qkv, rope_ref, k, keys_ref, values_ref))
    traffic.send(keys_ref, values_ref)
    query = query_of(normal_ref[...], w_qkv, own_rope_ref[0:8], own_rope_ref[8:16])
    attended, stat = attend(query, k_size, keys_ref, values_ref, len_ref, low, high, qbd, top_ref, acc_ref, q_ref)
    traffic.ready()
    gain = gain_column(gains_ref, 3)
    w_out, w_gate_up, w_down = w_out_ref[...], w_gate_up_ref[...], w_down_ref[...]
    mid, _, gate_up, _, out = feed_forward(
        resid_in_ref[...], attended, turned_out_ref[...], turned_gate_up_ref[...], w_down, gain
    )
    act_ref[...] = out
    att_ref[...] = attended
    traffic.send(act_ref, att_ref, q_ref)
    grad = tile_halves(cot_own_ref[...].astype(f32), cot_other_ref[...].astype(f32))
    low_refs = (d_out_ref, d_gate_up_ref, d_branch_ref, hidden_ref, normal_b_ref)
    grad, payload, d_gain_ref[...] = feed_back(grad, attended, mid, gate_up, w_out, w_gate_up, w_down, gain, stat, low_refs, traffic)
    grad_ref[...] = grad
    payload_ref[...] = payload
    copies_ref[...] = jnp.broadcast_to(payload[None], copies_ref.shape)


def query_back(
    traffic, count, payload_ref, q_ref, len_ref, own_rope_ref, rope_ref, keys_ref, values_ref, normal_all, w_qkv_ref, dq_ref, qall_ref,
    k_rows_ref, v_rows_ref, qbd, dbd, acc_ref,
):
    chip, core, low, high = geometry()
    traffic.ready(count)
    unit = eye(TILE, TILE, bf16)
    rows = nt(unit, payload_ref[...])
    spread(qbd, jnp.concatenate([q_ref[...].astype(f32), rows[:, D:]], axis=1), LROW, LROW + 9)
    spread(dbd, rows, DROW)
    k_rows_ref[...] = nt(unit, own_tile(keys_ref, low, high)).astype(bf16)
    v_rows_ref[...] = nt(unit, own_tile(values_ref, low, high)).astype(bf16)
    w_qkv = w_qkv_ref[...]

    def queries(k, carry):
        at = pl.ds(pl.multiple_of(k * BLOCK, BLOCK), BLOCK)
        qall_ref[k] = query_of(normal_all[k], w_qkv, rope_ref[0:8, at], rope_ref[8:16, at])
        return carry

    lax.fori_loop(0, BLOCKS, queries, 0, unroll=2)
    traffic.send(k_rows_ref, v_rows_ref, qall_ref)
    acc_ref[...] = jnp.zeros(acc_ref.shape, f32)

    def step(u, tile, block, at):
        scores = scores_of(qbd[u], with_ones(keys_ref[block, :, at]), query_bias(u, tile, block, at, len_ref))
        d_scores = jnp.exp(scores) * nn(dbd[u], with_ones(values_ref[block, :, at]))
        acc_ref[u] = acc_ref[u] + nt(d_scores.astype(bf16), keys_ref[block, :, at])

    run_steps(query_step, low, high, step, 2)
    step(*query_last(low, high))
    d_query = jnp.concatenate([own_heads(acc_ref[0]), own_heads(acc_ref[1])], axis=0) * HEAD_DIM**-0.5
    dq_ref[...] = rotate(turned_rows(d_query), own_rope_ref[0:8], -own_rope_ref[8:16])


def turned_rows(x):
    hi, lo = two_parts(x)
    unit = eye(D, D, bf16)
    return nt(unit, hi) + nt(unit, lo)


def key_back(traffic, count, own_ref, other_ref, len_ref, qall_ref, k_rows_ref, v_rows_ref, dq_ref, grad_ref, resid_ref, w_qkv_ref, gain,
             own_rope_ref, daug, kbd, vbd, dk_ref, dv_ref):
    chip, core, low, high = geometry()

    def put(block, columns, value):
        daug[block, :, columns] = value

    natural_tiles(own_ref, other_ref, put)
    traffic.ready(count)
    ones = jnp.ones((TILE, STAT), f32)
    spread(kbd, jnp.concatenate([k_rows_ref[...].astype(f32), ones], axis=1), LROW, LROW + 9)
    spread(vbd, jnp.concatenate([v_rows_ref[...].astype(f32), ones], axis=1), DROW)
    dk_ref[...] = jnp.zeros(dk_ref.shape, f32)
    dv_ref[...] = jnp.zeros(dv_ref.shape, f32)

    def step(u, tile, block, at):
        queries = jnp.concatenate([qall_ref[block, :, at], daug[block, D:AUG, at]], axis=0)
        probs = jnp.exp(scores_of(kbd[u], queries, key_bias(u, tile, block, at, len_ref)))
        d_scores = probs * nn(vbd[u], daug[block, :, at])
        dv_ref[u] = dv_ref[u] + nt(probs.astype(bf16), daug[block, :, at])
        dk_ref[u] = dk_ref[u] + nt(d_scores.astype(bf16), qall_ref[block, :, at])

    run_steps(key_step, low, high, step)
    step(*key_last(low, high))
    traffic.ready()
    d_key = turned_rows(jnp.concatenate([own_heads(dk_ref[0]), own_heads(dk_ref[1])], axis=0))
    d_value = nt(eye(D, D, bf16), jnp.concatenate([own_heads(dv_ref[0]), own_heads(dv_ref[1])], axis=0).astype(bf16))
    d_key = rotate(d_key, own_rope_ref[0:8], -own_rope_ref[8:16])
    d_mixed = jnp.concatenate([dq_ref[...], d_key, d_value], axis=0).astype(bf16)
    d_in, d_gain = norm_back(resid_ref[...], gain(), nn(w_qkv_ref[...], d_mixed))
    return grad_ref[...] + d_in, d_mixed, d_gain


def projection_grads(normal, d_mixed):
    tail = nt(normal, jnp.concatenate([d_mixed[MAXLAG:], jnp.zeros((TILE - 48, TILE), bf16)], axis=0))
    return nt(normal, d_mixed[:MAXLAG]), tail


def third_kernel(
    traffic, own_ref, other_ref, len_ref, qall_ref, k_rows_ref, v_rows_ref, dq_ref, grad_in_ref, resid_ref, att_ref, stat_ref, mid_ref,
    gate_up_ref, own_rope_ref, w_qkv_ref, w_out_ref, w_gate_up_ref, w_down_ref, gains_ref,
    copies_ref, payload_ref, grad_ref, d_mixed_ref, d_gain_a_ref, d_gain_b_ref, d_out_ref, d_gate_up_ref, d_branch_ref, hidden_ref,
    normal_b_ref,
    daug, kbd, vbd, dk_ref, dv_ref,
):
    grad, d_mixed_ref[...], d_gain_a_ref[...] = key_back(
        traffic, 4, own_ref, other_ref, len_ref, qall_ref, k_rows_ref, v_rows_ref, dq_ref, grad_in_ref, resid_ref, w_qkv_ref,
        lambda: gain_column(gains_ref, 2), own_rope_ref, daug, kbd, vbd, dk_ref, dv_ref,
    )
    low_refs = (d_out_ref, d_gate_up_ref, d_branch_ref, hidden_ref, normal_b_ref)
    grad, payload, d_gain_b_ref[...] = feed_back(
        grad, att_ref[...], mid_ref[...], gate_up_ref[...], w_out_ref[...], w_gate_up_ref[...], w_down_ref[...], gain_column(gains_ref, 1),
        stat_ref[...], low_refs, traffic,
    )
    grad_ref[...] = grad
    payload_ref[...] = payload
    copies_ref[...] = jnp.broadcast_to(payload[None], copies_ref.shape)


def second_window_kernel(
    traffic, len_ref, hidden_ref, d_out_ref, normal_ref, d_gate_up_ref, att_ref, d_branch_ref, d_gain_ref, payload_ref, q_ref,
    own_rope_ref, rope_ref, keys_ref, values_ref, normal_all, w_qkv_ref,
    pack_ref, tail_ref, dq_ref, qall_ref, k_rows_ref, v_rows_ref, qbd, dbd, acc_ref,
):
    traffic.ready(8)
    tail = feed_grads(
        Tiles(pack_ref), hidden_ref[...], d_out_ref[...], normal_ref[...], d_gate_up_ref[...], att_ref[...], d_branch_ref[...]
    )
    tail_ref[...] = jnp.where(iota((1, TILE), 1) == 99, d_gain_ref[...], tail)
    traffic.send(pack_ref, tail_ref)
    query_back(
        traffic, 16, payload_ref, q_ref, len_ref, own_rope_ref, rope_ref, keys_ref, values_ref, normal_all, w_qkv_ref, dq_ref, qall_ref,
        k_rows_ref, v_rows_ref, qbd, dbd, acc_ref,
    )


def third_window_kernel(
    traffic, len_ref, pack_in_ref, tail_in_ref, normal_a_ref, d_mixed_ref, d_gain_a_ref, hidden_ref, d_out_ref, normal_ref, d_gate_up_ref,
    att_ref, d_branch_ref, d_gain_b_ref, payload_ref, q_ref, own_rope_ref, rope_ref, keys_ref, values_ref, normal_all,
    w_qkv_ref,
    keep_ref, send_ref, rest_ref, tail0_ref, tail1_ref, dq_ref, qall_ref, k_rows_ref, v_rows_ref, qbd, dbd, acc_ref,
):
    traffic.ready(13)
    put = Pairs(lax.axis_index("tm") % 2, keep_ref, send_ref, rest_ref)
    for t in range(pack_in_ref.shape[0]):
        put.tile(pack_in_ref[t].astype(f32))
    head, tail = projection_grads(normal_a_ref[...], d_mixed_ref[...])
    put(head)
    tail0_ref[...] = feed_grads(
        put, hidden_ref[...], d_out_ref[...], normal_ref[...], d_gate_up_ref[...], att_ref[...], d_branch_ref[...]
    )
    lane = iota((1, TILE), 1)
    tail = jnp.where(lane == 98, d_gain_a_ref[...], tail + tail_in_ref[...])
    tail1_ref[...] = jnp.where(lane == 97, d_gain_b_ref[...], tail)
    traffic.send(keep_ref, send_ref, rest_ref, tail0_ref, tail1_ref)
    query_back(
        traffic, 21, payload_ref, q_ref, len_ref, own_rope_ref, rope_ref, keys_ref, values_ref, normal_all, w_qkv_ref, dq_ref, qall_ref,
        k_rows_ref, v_rows_ref, qbd, dbd, acc_ref,
    )


def last_kernel(
    traffic, own_ref, other_ref, len_ref, scale_ref, ids_ref, qall_ref, k_rows_ref, v_rows_ref, dq_ref, grad_in_ref, resid_ref,
    normal_a_ref, tail0_ref, tail1_ref, rest_ref, w_dense_ref, feats_ref, own_rope_ref, w_qkv_ref, gains_ref,
    keep_ref, send_ref, daug, kbd, vbd, dk_ref, dv_ref, raw_ref,
):
    chip, core, low, high = geometry()
    d_first, d_mixed, d_gain = key_back(
        traffic, 6, own_ref, other_ref, len_ref, qall_ref, k_rows_ref, v_rows_ref, dq_ref, grad_in_ref, resid_ref, w_qkv_ref,
        lambda: gain_column(gains_ref, 0), own_rope_ref, daug, kbd, vbd, dk_ref, dv_ref,
    )
    head, tail0 = projection_grads(normal_a_ref[...], d_mixed)
    d_first = d_first.astype(bf16)
    feats = feats_ref[...]
    empty = jnp.zeros((64, TILE), bf16)
    tail0 = tail0 + tail0_ref[...] + nt(d_first, jnp.concatenate([empty, feats[:64]], axis=0))
    tail1 = tail1_ref[...] + nt(d_first, jnp.concatenate([empty, feats[64:], empty[:32]], axis=0))
    lane, row = iota((1, TILE), 1), iota((D, 1), 0)
    tail1 = jnp.where(lane == 96, d_gain, tail1)
    sums, counts = jnp.zeros((D, 1), f32), jnp.zeros((D, 1), f32)
    owner = (lax.axis_index("tm") == 0).astype(f32)
    for d in range(DOCS):
        hit = jnp.where(row == ids_ref[d], owner, 0.0)
        sums, counts = sums + hit * scale_ref[d], counts + hit
    high_part = sums.astype(bf16).astype(f32)
    tail1 = jnp.where(lane == 100, high_part, tail1)
    tail1 = jnp.where(lane == 101, sums - high_part, tail1)
    tail1 = jnp.where(lane == 102, counts, tail1)

    place = own_places(low, high)
    start = doc_start(place, len_ref)
    own = doc_scale_at(place, len_ref, scale_ref)
    flip = (iota((TILE, TILE), 0) + iota((TILE, TILE), 1) == TILE - 1).astype(bf16)
    raw_ref[...] = jnp.zeros(raw_ref.shape, f32)
    lags = TILE - iota((TILE, 1), 0)
    for b in range(3):
        weights = nn(w_dense_ref[:, b * TILE : (b + 1) * TILE], flip).astype(bf16)
        d_lagged = tn(weights, d_first)
        valid = place - (lags + b * TILE) >= start
        d_lagged = jnp.where(valid, d_lagged, 0.0) / own
        for u in range(2):
            half = jnp.where((lane < HALF) == (u == 0), d_lagged, 0.0)
            wide = jnp.concatenate([jnp.zeros((TILE, TILE), f32), half], axis=1)
            rolled = pltpu.roll(wide, TILE, 1, stride=1, stride_axis=0)
            total = jnp.sum(rolled, axis=0, keepdims=True)
            for tile, part in (((low if u == 0 else high) - b + 16, total[:, TILE:]), ((low if u == 0 else high) - b + 15, total[:, :TILE])):
                at = tile % 2, pl.ds(tile // 2, 1)
                raw_ref[at] = raw_ref[at] + part

    put = Pairs(core, keep_ref, send_ref)
    put.tile(rest_ref[0].astype(f32))
    for part in (head, tail0, tail1):
        put(part)
    for k in range(2):
        put.tile(raw_ref[k, 8:24, :])


def summed(in_ref):
    count, rows, _ = in_ref.shape
    total = jnp.zeros((rows, TILE), f32)
    return lax.fori_loop(0, count // 8, lambda i, t: t + jnp.sum(in_ref[pl.ds(i * 8, 8)].astype(f32), axis=0), total)


def pair_sum_kernel(early_ref, early_in_ref, late_ref, late_in_ref, out_ref):
    zero = jnp.zeros((16, TILE), bf16)
    late = late_ref.shape[0] - 1
    series, core = lax.axis_index("series"), lax.axis_index("tm") % 2
    out_ref[:, 32:40, :] = jnp.zeros((64, 8, TILE), bf16)

    def both(ref, in_ref, t):
        return ref[t].astype(f32) + in_ref[t].astype(f32)

    for t in range(128):
        value = zero
        if t < EARLY:
            value = both(early_ref, early_in_ref, t).astype(bf16)
        elif t < EARLY + late:
            value = both(late_ref, late_in_ref, t - EARLY).astype(bf16)
        out_ref[jnp.where(core == 0, t // 2, 63 - t // 2), t % 2 * 16 : t % 2 * 16 + 16, :] = value
    raw = both(late_ref, late_in_ref, late)
    for c in range(16):
        line = jnp.where(iota((8, 1), 0) == 0, raw[c : c + 1], 0.0)
        chip = series * 16 + c
        out_ref[jnp.where(core == 0, chip, 63 - chip), 32:40, :] = line.astype(bf16)


def sum_kernel(in_ref, out_ref, raw_ref):
    total = summed(in_ref)
    out_ref[...] = jnp.broadcast_to(total[:32].astype(bf16)[None], out_ref.shape)
    raw_ref[...] = total[32:33]


def unpack_kernel(own_ref, other_ref, act_in_ref, act_ref, lag_ref, qkv_ref, out_ref, gate_up_ref, down_ref, gains_ref, scale_ref):
    core = lax.axis_index("tm") % 2
    act_ref[...] = act_in_ref[...]

    def tile(t):
        rows = slice(t // 2 % 2 * 16, t // 2 % 2 * 16 + 16)
        first, second = jnp.where(core == 0, t // 4, 63 - t // 4), jnp.where(core == 0, 63 - t // 4, t // 4)
        return jnp.where(core == t % 2, own_ref[first, rows].astype(f32), other_ref[second, rows].astype(f32))

    def columns(first, count):
        return [jnp.concatenate([tile(first + 9 * c + r) for r in range(9)], axis=0) for c in range(count)]

    layers = ((207, 234, 117), (90, 243, 0))
    tails = []
    for layer, (at_qkv, at_tail, at_rest) in enumerate(layers):
        for c, part in enumerate(columns(at_qkv, 3)):
            qkv_ref[layer, :, c * TILE : (c + 1) * TILE] = part
        tail = columns(at_tail, 1)[0]
        tails.append(tail)
        qkv_ref[layer, :, MAXLAG:] = tail[:, :48]
        for c, part in enumerate(columns(at_rest, 3)):
            down_ref[layer, :, c * TILE : (c + 1) * TILE] = part
        for c, part in enumerate(columns(at_rest + 27, 6)):
            gate_up_ref[layer, :, c * TILE : (c + 1) * TILE] = part
        out_ref[layer, :, :TILE] = columns(at_rest + 81, 1)[0]
        out_ref[layer, :, TILE:] = tail[:, 48:64]
    lag = jnp.where(iota((1, TILE), 1) < 64, pltpu.roll(tails[0], 64, 1), tails[1])
    lag_ref[...] = lag[:, :FEATS]
    pick = (iota((8, TILE), 1) == iota((8, TILE), 0) + 96).astype(bf16)
    rest = nt(pick, tails[1].astype(bf16))
    gains_ref[0] = rest[0:2]
    gains_ref[1] = rest[2:4]
    scale_ref[...] = ((rest[4:5] + rest[5:6]) / rest[6:7])[:, :DATASETS]


def weights_kernel(
    traffic, lag_ref, w_lag_ref, w_qkv_ref, w_out_ref, w_gate_up_ref, cot_ref,
    dense_ref, qkv0_ref, out0_ref, gate_up0_ref, qkv1_ref, out1_ref, gate_up1_ref, chosen_ref, low_cot_ref,
):
    traffic.ready()
    rows = iota((FEATS, 1), 0)
    diagonal = iota((FEATS, LAGS), 0) == iota((FEATS, LAGS), 1)
    offsets = jnp.sum(jnp.where(diagonal, lag_ref[...].astype(f32), 0.0), axis=1, keepdims=True)
    offsets = jnp.where(rows < LAGS, offsets - 1.0, (rows - LAGS + MAXLAG + 1).astype(f32))
    chosen = (iota((FEATS, LAGCOLS), 1).astype(f32) == offsets).astype(bf16)
    chosen_ref[0:FEATS, :] = chosen
    chosen_ref[FEATS:, :] = jnp.zeros((96 - FEATS, LAGCOLS), bf16)
    dense_ref[...] = nn(w_lag_ref[...], chosen).astype(bf16)
    qkv0_ref[...] = turned(w_qkv_ref[0])
    out0_ref[...] = turned(w_out_ref[0])
    gate_up0_ref[...] = turned(w_gate_up_ref[0])
    qkv1_ref[...] = turned(w_qkv_ref[1])
    out1_ref[...] = turned(w_out_ref[1])
    gate_up1_ref[...] = turned(w_gate_up_ref[1])
    low_cot_ref[...] = cot_ref[...].astype(bf16)


def first_values_kernel(traffic, len_ref, scale_ref, raw_ref, hours_ref, out_ref):
    traffic.ready()
    places = lax.axis_index("tm") * TILE + iota((1, TILE), 1)
    own = doc_scale_at(places, len_ref, scale_ref)
    angle = hours_ref[...].astype(f32) * (2.0 * math.pi / 24.0)
    rows = [raw_ref[...] / own, jnp.sin(angle), jnp.cos(angle), jnp.log(own), jnp.zeros((4, TILE), f32)]
    out_ref[...] = jnp.broadcast_to(jnp.concatenate(rows, axis=0)[None], out_ref.shape)


def shape(*dims, dtype=f32):
    return jax.ShapeDtypeStruct(dims, dtype)


class Traffic:
    def __init__(self, loads, stores):
        self.loads, self.stores, self.waited, self.sent = loads, stores, 0, set()
        for copy in loads:
            copy.start()

    def ready(self, count=None):
        count = len(self.loads) if count is None else count
        for copy in self.loads[self.waited : count]:
            copy.wait()
        self.waited = max(self.waited, count)

    def send(self, *refs):
        for ref, copy in self.stores:
            if any(ref is r for r in refs):
                copy.start()
                self.sent.add(id(copy))

    def finish(self):
        self.ready()
        for _, copy in self.stores:
            if id(copy) not in self.sent:
                copy.start()
        for _, copy in self.stores:
            copy.wait()


def call(kernel, operands, outs, scratch=(), tables=(), weights=(), cost=None):
    several = isinstance(outs, list)
    outs = outs if several else [outs]
    layers = [None] * len(tables) + [x[1] if isinstance(x, tuple) else None for x in weights]
    fetched = (*tables, *(x[0] if isinstance(x, tuple) else x for x in weights))
    shapes = [x.shape if layer is None else x.shape[1:] for x, layer in zip(fetched, layers)]
    buffers = [(pltpu.SMEM if n < len(tables) else pltpu.VMEM)(shapes[n], x.dtype) for n, x in enumerate(fetched)]
    is_far = [not isinstance(out, jax.ShapeDtypeStruct) for out in outs]
    buffers += [pltpu.VMEM(out.shape, out.dtype) for out, far in zip(outs, is_far) if far]
    count, extra, copies = len(operands), len(buffers), len(buffers)

    def wrapped(*refs):
        refs = list(refs)
        ins, sources = refs[:count], refs[count : count + len(fetched)]
        results = refs[count + len(fetched) : count + len(fetched) + len(outs)]
        rest = refs[count + len(fetched) + len(outs) :]
        if not copies:
            kernel(*ins, *results, *rest)
            return
        own, held, sems = rest[: len(scratch)], rest[len(scratch) : -1], rest[-1]
        sources = [a if layer is None else a.at[layer] for a, layer in zip(sources, layers)]
        loads = [pltpu.make_async_copy(a, b, sems.at[n]) for n, (a, b) in enumerate(zip(sources, held))]
        stores, at = [], len(fetched)
        for n, far in enumerate(is_far):
            if far:
                stores.append((held[at], pltpu.make_async_copy(held[at], results[n], sems.at[at])))
                results[n] = held[at]
                at += 1
        traffic = Traffic(loads, stores)
        kernel(traffic, *ins, *held[: len(fetched)], *results, *own)
        traffic.finish()

    vmem, hbm = pl.BlockSpec(memory_space=pltpu.VMEM), pl.BlockSpec(memory_space=pltpu.HBM)
    results = pl.pallas_call(
        wrapped,
        out_shape=outs,
        in_specs=[vmem] * count + [hbm] * len(fetched),
        out_specs=[hbm if far else vmem for far in is_far],
        scratch_shapes=[*scratch, *buffers, pltpu.SemaphoreType.DMA((copies,))] if copies else list(scratch),
        compiler_params=pltpu.CompilerParams(vmem_limit_bytes=VMEM),
        cost_estimate=cost and pl.CostEstimate(flops=cost * 10**9, bytes_accessed=10**6, transcendentals=0),
    )(*operands, *(pltpu.with_memory_space_constraint(x, pltpu.HBM) for x in fetched))
    return results if several else results[0]


def pair_permute(x, bit):
    return lax.ppermute(x, "tm", [(i, i ^ bit) for i in range(32)])


def gather(copies, beside):
    groups = [[2 * chip for chip in range(16)], [31 - 2 * chip for chip in range(16)]]
    own = lax.all_to_all(copies, "tm", 0, 0, axis_index_groups=groups)
    own, beside = lax.optimization_barrier((own, beside))
    return own, pair_permute(own, 1), beside


def swap(block):
    return lax.ppermute(block, "tm", [(n, n if n % 2 == 0 else 32 - n) for n in range(32)])


def tile_halves(own, other):
    lane = iota((1, TILE), 1) < HALF
    return jnp.where(lane == (lax.axis_index("tm") < 16), own, other)


def rope_table():
    freqs = 10000.0 ** (-np.arange(8, dtype=np.float64) / 8)
    angle = np.arange(LEN, dtype=np.float64)[None, :] * freqs[:, None]
    return np.concatenate([np.cos(angle), np.sin(angle)], axis=0).astype(np.float32)


def body(
    raw_values, hours, doc_lengths, doc_scale, dataset_ids, lag_offsets, w_lag, w_qkv, w_out, w_gate_up, w_down, gains, cotangent
):
    lengths, scales, ids = doc_lengths.reshape(DOCS), doc_scale.reshape(DOCS), dataset_ids.reshape(DOCS)
    def low(*dims):
        return shape(*dims, dtype=bf16)

    def far(*dims, dtype=f32):
        return pltpu.HBM(dims, dtype)

    def far_low(*dims):
        return far(*dims, dtype=bf16)

    w_lag, w_down, lags = w_lag.T, w_down.transpose(0, 2, 1), lag_offsets.reshape(1, LAGS)
    rope = jnp.asarray(rope_table())
    values = lax.all_to_all(call(first_values_kernel, (), shape(32, 8, TILE), tables=(lengths, scales), weights=(raw_values, hours)), "tm", 0, 0)
    turned_shapes = [far_low(3 * D, D), far_low(D, D), far_low(2 * FF, D)]
    w_dense, *turned_weights, chosen, low_cot = call(
        weights_kernel, (), [far_low(D, LAGCOLS), *turned_shapes, *turned_shapes, far_low(96, LAGCOLS), far_low(D, TILE)],
        weights=(lags, w_lag, w_qkv, w_out, w_gate_up, cotangent[0].T), cost=3,
    )
    turned0, turned1 = turned_weights[:3], turned_weights[3:]
    values, w_dense = lax.optimization_barrier((values, w_dense))
    all_d = far_low(BLOCKS, D, BLOCK)
    mine, mine_low, ff_low, column_shape = far(D, TILE), far_low(D, TILE), far_low(FF, TILE), far(D, 1)
    payload_shapes = [far_low(16, AUG, TILE), far_low(AUG, TILE)]
    low_grads = [mine_low, far_low(2 * FF, TILE), mine_low, ff_low, mine_low]
    bd, wide_bd = pltpu.VMEM((2, ROWS, AUG), bf16), pltpu.VMEM((2, ROWS, WIDE), bf16)
    acc, acc_d = pltpu.VMEM((2, ROWS, AUG), f32), pltpu.VMEM((2, ROWS, D), f32)
    top = pltpu.VMEM((2, ROWS, 1), f32)
    back_scratch = [pltpu.VMEM((BLOCKS, AUG, BLOCK), bf16), wide_bd, bd, acc_d, acc]

    (copies, next1, resid1, keys0, values0, normal_all0, feats, resid0, normal_a0, q0, att0, stat0, mid0, gate_up0, own_rope) = call(
        first_kernel,
        (values,),
        [far_low(16, D, TILE), mine_low, mine, all_d, all_d, all_d, far_low(96, TILE), mine, mine_low, far_low(TILE, D), mine_low,
         far_low(STAT, TILE), mine, far(2 * FF, TILE), far(16, TILE)],
        [pltpu.VMEM((8 + TILES, TILE), f32), pltpu.VMEM((TILE, MAXLAG + LEN), bf16),
         pltpu.VMEM((LAGCOLS, TILE), bf16), wide_bd, top, acc],
        tables=(lengths,), weights=(w_dense, gains, turned0[0], rope, chosen, *turned0[1:], (w_down, 0)),
    )

    own, other, cot = gather(copies, swap(low_cot))
    copies, payload, act, keys1, values1, normal_all1, q1, grad, att1, d_gain_b1, *low1 = call(
        second_kernel,
        (own, other, cot, pair_permute(cot, 1)),
        [*payload_shapes, mine, all_d, all_d, all_d, far_low(TILE, D), mine, mine_low, column_shape, *low_grads],
        [wide_bd, top, acc],
        tables=(lengths,),
        weights=(turned1[0], rope, next1, own_rope, resid1, *turned1[1:], (w_out, 1), (w_gate_up, 1), (w_down, 1), gains),
    )

    rows_low = far_low(TILE, D)
    side_shapes = [mine, all_d, rows_low, rows_low]
    d_out, d_gate_up, d_branch, hidden, normal_b = low1
    pack, tail, dq, qall, k_rows, v_rows = call(
        second_window_kernel, (), [far_low(90, 16, TILE), mine, *side_shapes], [wide_bd, bd, acc_d],
        tables=(lengths,),
        weights=(hidden, d_out, normal_b, d_gate_up, att1, d_branch, d_gain_b1, payload, q1, own_rope, rope, keys1, values1, normal_all1,
                 turned1[0]), cost=8,
    )
    own, other, dq = gather(copies, dq)
    copies, payload, grad, d_mixed, d_gain_a1, d_gain_b0, *low0 = call(
        third_kernel,
        (own, other),
        [*payload_shapes, mine, far_low(3 * D, TILE), column_shape, column_shape, *low_grads],
        back_scratch,
        tables=(lengths,),
        weights=(qall, k_rows, v_rows, dq, grad, resid1, att0, stat0, mid0, gate_up0, own_rope, (w_qkv, 1), (w_out, 0), (w_gate_up, 0),
                 (w_down, 0), gains),
    )
    d_out, d_gate_up, d_branch, hidden, normal_b = low0
    early, early_out, rest, tail0, tail1, dq, qall, k_rows, v_rows = call(
        third_window_kernel, (),
        [far_low(EARLY, 16, TILE), far_low(EARLY, 16, TILE), far_low(1, 16, TILE), mine, mine, *side_shapes], [wide_bd, bd, acc_d],
        tables=(lengths,),
        weights=(pack, tail, next1, d_mixed, d_gain_a1, hidden, d_out, normal_b, d_gate_up, att0, d_branch, d_gain_b0, payload, q0,
                 own_rope, rope, keys0, values0, normal_all0, turned0[0]), cost=8,
    )
    own, other, (dq, early_out) = gather(copies, (dq, early_out))
    early_in = pair_permute(early_out, 1)
    late, late_out = call(
        last_kernel,
        (own, other),
        [low(LATE, 16, TILE)] * 2,
        [*back_scratch, pltpu.VMEM((2, 24, TILE), f32)],
        tables=(lengths, scales, ids),
        weights=(qall, k_rows, v_rows, dq, grad, resid0, normal_a0, tail0, tail1, rest, w_dense, feats, own_rope, (w_qkv, 0), gains),
    )
    packed = call(pair_sum_kernel, (early, early_in, late, pair_permute(late_out, 1)), low(64, 40, TILE))
    same_core = [[2 * chip for chip in range(64)], [127 - 2 * chip for chip in range(64)]]
    parts = lax.all_to_all(packed, ("series", "tm"), 0, 0, axis_index_groups=same_core)
    share, raw_grad = call(sum_kernel, (parts,), [low(64, 32, TILE), shape(1, TILE)])
    share, act = lax.optimization_barrier((share, act))
    own = lax.all_to_all(share, ("series", "tm"), 0, 0, axis_index_groups=same_core)
    own, act = lax.optimization_barrier((own, swap(tile_halves(act, pair_permute(act, 1)))))
    act, g_lag, g_qkv, g_out, g_gate_up, g_down, g_gains, scale = call(
        unpack_kernel,
        (own, pair_permute(own, 1), act),
        [shape(D, TILE), shape(D, FEATS), shape(LAYERS, D, 3 * D), shape(LAYERS, D, D), shape(LAYERS, D, 2 * FF), shape(LAYERS, D, FF),
         shape(LAYERS, 2, D), shape(1, DATASETS)],
    )
    return (
        act.T[None], raw_grad, scale.reshape(DATASETS), g_lag.T, g_qkv, g_out, g_gate_up, g_down.transpose(0, 2, 1), g_gains,
    )


def solution(mesh):
    placed = (
        P("series", "tm"),
        P("series", "tm"),
        P("series", None),
        P("series", None),
        P("series", None, None),
        P(),
        P(),
        P(),
        P(),
        P(),
        P(),
        P(),
        P("series", "tm", None),
    )
    return jax.shard_map(
        body,
        mesh=mesh,
        in_specs=placed,
        out_specs=(P("series", "tm", None), P("series", "tm"), P(), P(), P(), P(), P(), P(), P()),
        check_vma=False,
    )
```

```python
import math

import jax
import jax.numpy as jnp
import numpy as np
from jax import lax
from jax.experimental import pallas as pl
from jax.experimental.pallas import tpu as pltpu
from jax.sharding import PartitionSpec as P


D = 144
HEADS = 9
HEAD_DIM = 16
FF = 384
LAGS = 84
LAYERS = 2
DATASETS = 8
DOCS = 7
LEN = 4096
MAXLAG = 384
FEATS = 87
EPSILON = 1e-06
MASKED = -1e30
AUG = 176
STAT = AUG - D
LROW = D
DROW = D + 18
BLOCK = 512
BLOCKS = LEN // BLOCK
TILE = 128
TILES = LEN // TILE
STEPS = BLOCKS + 1
SHIFTED = 8
HALF = 64
ROWS = HEADS * HALF
LAGCOLS = 400
EARLY = 103
LATE = 24
WIDE = AUG + HALF
SAFE = 70.0
VMEM = 28 * 2**20

bf16 = jnp.bfloat16
f32 = jnp.float32
HIGH = lax.Precision.HIGHEST


def nn(a, b, precision=None):
    return lax.dot_general(a, b, (((1,), (0,)), ((), ())), precision=precision, preferred_element_type=f32)


def nt(a, b, precision=None):
    return lax.dot_general(a, b, (((1,), (1,)), ((), ())), precision=precision, preferred_element_type=f32)


def tn(a, b, precision=None):
    return lax.dot_general(a, b, (((0,), (0,)), ((), ())), precision=precision, preferred_element_type=f32)


def iota(shape, dim):
    return lax.broadcasted_iota(jnp.int32, shape, dim)


def eye(rows, cols, dtype):
    return (iota((rows, cols), 0) == iota((rows, cols), 1)).astype(dtype)


def column(row, size):
    keep = iota((size, size), 0) == iota((size, size), 1)
    return jnp.sum(jnp.where(keep, row, 0.0), axis=1, keepdims=True)


def pair_of(chip):
    return jnp.where(chip < 8, 2 * chip, TILES - 1 - 2 * chip)


def geometry():
    index = lax.axis_index("tm")
    chip, core = index // 2, index % 2
    tile = pair_of(chip)
    low = jnp.where(core == 0, tile, TILES - 1 - tile)
    return chip, core, low, TILES - 1 - low


def doc_start(places, len_ref):
    start = jnp.zeros_like(places)
    end = jnp.int32(0)
    for d in range(DOCS):
        end = end + len_ref[d]
        start = jnp.where(places >= end, end, start)
    return start


def doc_scale_at(places, len_ref, scale_ref):
    own = jnp.full(places.shape, scale_ref[0], f32)
    end = jnp.int32(0)
    for d in range(1, DOCS):
        end = end + len_ref[d - 1]
        own = jnp.where(places >= end, scale_ref[d], own)
    return own


def own_places(low, high):
    lane = iota((1, TILE), 1)
    return jnp.where(lane < HALF, low, high) * TILE + lane


def half_places(u, tile):
    return iota((HALF, 1), 0) + (tile * TILE + u * HALF)


def rotate(x, cosine, sine):
    cols = x.shape[1]
    parts = x.reshape(HEADS, 2, 8, cols)
    one, two = parts[:, 0], parts[:, 1]
    turned = jnp.stack([one * cosine - two * sine, two * cosine + one * sine], axis=1)
    return turned.reshape(D, cols)


def norm_factor(x):
    return lax.rsqrt(jnp.mean(x * x, axis=0, keepdims=True) + EPSILON)


def norm_back(x, gain, d_normal):
    r = norm_factor(x)
    scaled = d_normal * gain
    inner = jnp.mean(x * scaled, axis=0, keepdims=True)
    d_x = r * scaled - (r * r * r * inner) * x
    return d_x, jnp.sum(d_normal * x * r, axis=1, keepdims=True)


def head_columns(h, *firsts):
    col = iota((1, AUG), 1)
    keep = (col >= h * HEAD_DIM) & (col < (h + 1) * HEAD_DIM)
    for first in firsts:
        keep = keep | (col == first + h)
    return keep


def spread(ref, rows, *firsts):
    zero = jnp.zeros((HALF, AUG), f32)
    for h in range(HEADS):
        keep = head_columns(h, *firsts)
        for u in range(2):
            part = rows[u * HALF : (u + 1) * HALF]
            ref[u, h * HALF : (h + 1) * HALF, 0:AUG] = jnp.where(keep, part, zero).astype(bf16)
    if ref.shape[2] == WIDE:
        unit = eye(HALF, HALF, bf16)
        for h in range(HEADS):
            for u in range(2):
                ref[u, h * HALF : (h + 1) * HALF, AUG:WIDE] = unit


def own_heads(x):
    col = iota((1, D), 1) // HEAD_DIM
    total = jnp.zeros((HALF, D), f32)
    for h in range(HEADS):
        total = jnp.where(col == h, x[h * HALF : (h + 1) * HALF, :D], total)
    return total


def two_parts(x):
    hi = x.astype(bf16)
    return hi, (x - hi.astype(f32)).astype(bf16)


class Tiles:
    def __init__(self, ref):
        self.ref, self.count = ref, 0

    def tile(self, value):
        self.ref[self.count] = value.astype(bf16)
        self.count += 1

    def __call__(self, grads):
        for c in range(grads.shape[1] // TILE):
            for r in range(grads.shape[0] // 16):
                self.tile(grads[16 * r : 16 * (r + 1), c * TILE : (c + 1) * TILE].astype(f32))


class Pairs(Tiles):
    def __init__(self, core, keep_ref, send_ref, rest_ref=None):
        self.core, self.refs, self.rest, self.count, self.even = core, (keep_ref, send_ref), rest_ref, 0, None

    def tile(self, value):
        if self.count == self.refs[0].shape[0]:
            self.rest[0] = value.astype(bf16)
        elif self.even is None:
            self.even = value
        else:
            self.refs[0][self.count] = jnp.where(self.core == 0, self.even, value).astype(bf16)
            self.refs[1][self.count] = jnp.where(self.core == 0, value, self.even).astype(bf16)
            self.even = None
            self.count += 1


def turned(w):
    return tn(w, eye(D, D, bf16)).astype(bf16)


def with_ones(x):
    return jnp.concatenate([x, jnp.ones((STAT, x.shape[1]), bf16)], axis=0)


def key_value_block(normal, w_qkv, rope_ref, k, keys_ref, values_ref):
    mixed = nn(w_qkv[D:], normal)
    at = slice(k * BLOCK, (k + 1) * BLOCK)
    keys = rotate(mixed[:D], rope_ref[0:8, at], rope_ref[8:16, at])
    keys_ref[k] = keys.astype(bf16)
    values_ref[k] = mixed[D:].astype(bf16)
    return head_sizes(keys * keys)


def query_of(normal, w_qkv, cosine, sine):
    turned = rotate(nn(w_qkv[:D], normal), cosine, sine)
    return (turned.astype(bf16).astype(f32) * HEAD_DIM**-0.5).astype(bf16)


def own_rope(rope_ref, low, high):
    def at(tile):
        return rope_ref[:, pl.ds(pl.multiple_of(tile * TILE, TILE), TILE)]

    both = jnp.where(iota((1, TILE), 1) < HALF, at(low), at(high))
    return both[0:8], both[8:16]


def own_tile(ref, low, high):
    lane = iota((1, TILE), 1)

    def at(tile):
        return ref[tile // 4, :, pl.ds(pl.multiple_of((tile % 4) * TILE, TILE), TILE)].astype(f32)

    return jnp.where(lane < HALF, at(low), at(high)).astype(bf16)


def query_bias(u, tile, block, columns, len_ref):
    places = half_places(u, tile)
    start = doc_start(places, len_ref)
    keys = iota((1, columns.stop - columns.start), 1) + (block * BLOCK + columns.start)
    return jnp.where((keys <= places) & (keys >= start), 0.0, MASKED).astype(bf16)


def key_bias(u, tile, block, columns, len_ref):
    keys = half_places(u, tile)
    places = iota((1, columns.stop - columns.start), 1) + (block * BLOCK + columns.start)
    start = doc_start(places, len_ref)
    return jnp.where((keys <= places) & (keys >= start), 0.0, MASKED).astype(bf16)


def scores_of(rows, columns, bias):
    return nn(rows, jnp.concatenate([columns, bias], axis=0))


def run_steps(of_step, low, high, step, unroll=4):
    def several(i, carry):
        for j in range(unroll):
            step(*of_step(i * unroll + j, low, high), slice(0, BLOCK))
        return carry

    lax.fori_loop(0, (STEPS - 1) // unroll, several, 0)


def query_step(s, low, high):
    first = low // 4 + (low % 4 >= 2).astype(jnp.int32)
    late = s >= first
    return late.astype(jnp.int32), jnp.where(late, high, low), s - jnp.where(late, first, 0)


def query_last(low, high):
    late = low % 4 >= 2
    tile = jnp.where(late, high, low)
    return late.astype(jnp.int32), tile, tile // 4, slice(0, BLOCK // 2)


def key_step(s, low, high):
    late_short = (low % 4 < 2).astype(jnp.int32)
    first = low // 4 + 1 - late_short
    late = s >= BLOCKS - first
    block = jnp.where(late, high // 4 + late_short + s - (BLOCKS - first), first + s)
    return late.astype(jnp.int32), jnp.where(late, high, low), block


def key_last(low, high):
    late = low % 4 < 2
    tile = jnp.where(late, high, low)
    return late.astype(jnp.int32), tile, tile // 4, slice(BLOCK // 2, BLOCK)


def head_sizes(squares):
    return jnp.sum(squares.reshape(HEADS, HEAD_DIM, squares.shape[1]), axis=1)


def attend(query, k_size, keys_ref, values_ref, len_ref, low, high, qbd, top_ref, acc_ref, q_rows_ref):
    q_rows = nt(eye(TILE, TILE, bf16), query)
    q_rows_ref[...] = q_rows.astype(bf16)
    spread(qbd, jnp.concatenate([q_rows, jnp.zeros((TILE, STAT), f32)], axis=1))
    query = query.astype(f32)
    q_size = jnp.max(head_sizes(query * query), axis=1, keepdims=True)
    k_size = jnp.max(k_size, axis=1, keepdims=True)
    acc_ref[...] = jnp.zeros(acc_ref.shape, f32)
    safe = jnp.max(q_size * k_size) <= SAFE * SAFE

    @pl.when(safe)
    def _():
        top_ref[...] = jnp.zeros(top_ref.shape, f32)

        def step(u, tile, block, at):
            scores = scores_of(qbd[u], with_ones(keys_ref[block, :, at]), query_bias(u, tile, block, at, len_ref))
            acc_ref[u] = acc_ref[u] + nt(jnp.exp(scores).astype(bf16), with_ones(values_ref[block, :, at]))

        run_steps(query_step, low, high, step, 8)
        step(*query_last(low, high))

    @pl.when(jnp.logical_not(safe))
    def _():
        top_ref[...] = jnp.full(top_ref.shape, MASKED, f32)

        def step(s, carry):
            h, s = s % HEADS, s // HEADS
            first = low // 4 + 1
            late = s >= first
            u, tile, block = late.astype(jnp.int32), jnp.where(late, high, low), s - jnp.where(late, first, 0)
            rows = pl.ds(pl.multiple_of(h * HALF, HALF), HALF)
            bias = query_bias(u, tile, block, slice(0, BLOCK), len_ref)
            scores = scores_of(qbd[u, rows], with_ones(keys_ref[block]), bias)
            old = top_ref[u, rows]
            new = jnp.maximum(old, jnp.max(scores, axis=1, keepdims=True))
            probs = jnp.exp(scores - new)
            acc_ref[u, rows] = acc_ref[u, rows] * jnp.exp(old - new) + nt(probs.astype(bf16), with_ones(values_ref[block]))
            top_ref[u, rows] = new
            return carry

        lax.fori_loop(0, STEPS * HEADS, step, 0)

    attended, stats = [], []
    lane, col = iota((1, STAT), 1), iota((1, D), 1) // HEAD_DIM
    for u in range(2):
        acc, top = acc_ref[u], top_ref[u]
        total, shift = jnp.ones((HALF, STAT), f32), jnp.zeros((HALF, STAT), f32)
        for h in range(HEADS):
            rows = slice(h * HALF, (h + 1) * HALF)
            here = (lane == h) | (lane == HEADS + h)
            total = jnp.where(here, acc[rows, D : D + 1], total)
            shift = jnp.where(here, top[rows], shift)
        hi, lo = two_parts(-(shift + jnp.log(total)))
        stats.append(jnp.where(lane < HEADS, hi.astype(f32), jnp.where(lane < 2 * HEADS, lo.astype(f32), 0.0)))
        own = jnp.zeros((HALF, D), f32)
        for h in range(HEADS):
            rows = slice(h * HALF, (h + 1) * HALF)
            own = jnp.where(col == h, acc[rows, :D] / acc[rows, D : D + 1], own)
        attended.append(own)
    att_rows = jnp.concatenate(attended, axis=0).astype(bf16)
    stat_rows = jnp.concatenate(stats, axis=0).astype(bf16)
    return nt(eye(D, D, bf16), att_rows).astype(bf16), nt(eye(STAT, STAT, bf16), stat_rows).astype(bf16)


def feed_forward(resid, attended, w_out, w_gate_up, w_down, gain):
    mid = resid + nn(w_out, attended)
    normal = (mid * norm_factor(mid) * gain).astype(bf16)
    gate_up = nn(w_gate_up, normal)
    gate = gate_up[:FF]
    hidden = (gate * jax.nn.sigmoid(gate) * gate_up[FF:]).astype(bf16)
    return mid, normal, gate_up, hidden, mid + nn(w_down, hidden)


def feed_back(grad, attended, mid, gate_up, w_out, w_gate_up, w_down, gain, stat, low_refs, traffic):
    d_out_ref, d_gate_up_ref, d_branch_ref, hidden_ref, normal_ref = low_refs
    d_out = grad.astype(bf16)
    d_hidden = tn(w_down, d_out)
    gate, up = gate_up[:FF], gate_up[FF:]
    sig = jax.nn.sigmoid(gate)
    d_gate = d_hidden * up * (sig * (1.0 + gate * (1.0 - sig)))
    d_up = d_hidden * (gate * sig)
    hidden_ref[...] = (gate * sig * up).astype(bf16)
    normal_ref[...] = (mid * norm_factor(mid) * gain).astype(bf16)
    d_gate_up = jnp.concatenate([d_gate, d_up], axis=0).astype(bf16)
    d_mid, d_gain = norm_back(mid, gain, nn(w_gate_up, d_gate_up))
    grad = grad + d_mid
    d_branch = grad.astype(bf16)
    d_att = nn(w_out, d_branch).astype(bf16)
    d_out_ref[...], d_gate_up_ref[...], d_branch_ref[...] = d_out, d_gate_up, d_branch
    traffic.send(*low_refs)
    product = d_att.astype(f32) * attended.astype(f32)
    delta = -jnp.sum(product.reshape(HEADS, HEAD_DIM, TILE), axis=1)
    delta = jnp.concatenate([delta, jnp.zeros((16 - HEADS, TILE), f32)], axis=0)
    row, col = iota((STAT, 16), 0), iota((STAT, 16), 1)
    stat = stat.astype(f32) + nn(((row == DROW - D + col) & (col < HEADS)).astype(bf16), delta.astype(bf16))
    return grad, jnp.concatenate([d_att, stat.astype(bf16)], axis=0), d_gain


def feed_grads(put, hidden, d_out, normal, d_gate_up, attended, d_branch):
    put(nt(d_out, hidden))
    put(nt(normal, d_gate_up))
    put(nt(attended, d_branch[:TILE]))
    rows = [jnp.zeros((48, TILE), bf16), d_branch[TILE:], jnp.zeros((TILE - 64, TILE), bf16)]
    return nt(attended, jnp.concatenate(rows, axis=0))


def gain_column(gains_ref, which):
    return column(gains_ref[which // 2, which % 2 : which % 2 + 1, :], D)


def first_kernel(
    traffic, features_ref, len_ref, w_dense_ref, gains_ref, w_qkv_ref, rope_ref, chosen_ref, w_out_ref, w_gate_up_ref,
    w_down_ref,
    copies_ref, next_ref, next_resid_ref, keys_ref, values_ref, normal_all, feats_ref, resid_ref, normal_a_ref,
    q_ref, att_ref, stat_ref, mid_ref, gate_up_ref, own_rope_ref,
    series, toeplitz, lagged_ref, qbd, top_ref, acc_ref,
):
    chip, core, low, high = geometry()
    series[0:8, :] = jnp.zeros((8, TILE), f32)
    series[8 : 8 + TILES, :] = features_ref[:, 0, :].astype(bf16).astype(f32)
    toeplitz[:, 0:MAXLAG] = jnp.zeros((TILE, MAXLAG), bf16)

    def shift(m, carry):
        rows = [series[pl.ds(m * SHIFTED + 7 + n, 1), :] for n in range(SHIFTED + 1)]
        window = jnp.broadcast_to(jnp.concatenate(rows, axis=1), (TILE, (SHIFTED + 1) * TILE))
        rolled = pltpu.roll(window, 1, 1, stride=1, stride_axis=0)
        at = pl.multiple_of(m * SHIFTED * TILE + MAXLAG, TILE)
        toeplitz[:, pl.ds(at, SHIFTED * TILE)] = rolled[:, TILE:].astype(bf16)
        return carry

    lax.fori_loop(0, TILES // SHIFTED, shift, 0)

    def others(tiles):
        rows = jnp.concatenate([features_ref[t] for t in tiles], axis=1)
        return jnp.concatenate([rows, jnp.zeros_like(rows)], axis=0).astype(bf16)

    traffic.ready(5)
    w_dense = w_dense_ref[...]
    gain_a, gain_b = gain_column(gains_ref, 0), gain_column(gains_ref, 1)
    w_qkv = w_qkv_ref[...]
    lag_rows = iota((TILE, 1), 0) + 1
    k_size = jnp.zeros((HEADS, BLOCK), f32)
    for k in range(BLOCKS):
        place = iota((1, BLOCK), 1) + k * BLOCK
        start = doc_start(place, len_ref)
        parts = []
        for b in range(3):
            at = MAXLAG + k * BLOCK - b * TILE
            lagged = toeplitz[:, at : at + BLOCK]
            if k in (0, BLOCKS - 1):
                valid = place - (lag_rows + b * TILE) >= start
                lagged = jnp.where(valid, lagged.astype(f32), 0.0).astype(bf16)
            parts.append(lagged)
        parts.append(others(range(4 * k, 4 * k + 4)))
        resid = nn(w_dense, jnp.concatenate(parts, axis=0))
        normal = (resid * norm_factor(resid) * gain_a).astype(bf16)
        normal_all[k] = normal
        k_size = jnp.maximum(k_size, key_value_block(normal, w_qkv, rope_ref, k, keys_ref, values_ref))

    cosine, sine = own_rope(rope_ref, low, high)
    own_rope_ref[0:8], own_rope_ref[8:16] = cosine, sine
    traffic.send(keys_ref, values_ref, normal_all, own_rope_ref)

    place = own_places(low, high)
    start = doc_start(place, len_ref)
    lane = iota((1, TILE), 1)

    def tile_of(ref, tile):
        return ref[:, pl.ds(pl.multiple_of(tile * TILE, TILE), TILE)].astype(f32)

    for b in range(3):
        lagged = jnp.where(lane < HALF, tile_of(toeplitz, low + 3 - b), tile_of(toeplitz, high + 3 - b))
        valid = place - (lag_rows + b * TILE) >= start
        lagged_ref[b * TILE : (b + 1) * TILE, :] = jnp.where(valid, lagged, 0.0).astype(bf16)
    lagged_ref[MAXLAG:, :] = jnp.where(lane < HALF, others([low]).astype(f32), others([high]).astype(f32)).astype(bf16)
    lagged = lagged_ref[...]
    resid = nn(w_dense, lagged)
    resid_ref[...] = resid
    normal = (resid * norm_factor(resid) * gain_a).astype(bf16)
    normal_a_ref[...] = normal
    traffic.send(resid_ref, normal_a_ref)
    query = query_of(normal, w_qkv, cosine, sine)
    attended, stat_ref[...] = attend(query, k_size, keys_ref, values_ref, len_ref, low, high, qbd, top_ref, acc_ref, q_ref)
    att_ref[...] = attended
    traffic.send(q_ref, att_ref, stat_ref)
    traffic.ready()
    feats_ref[...] = nn(chosen_ref[...], lagged).astype(bf16)
    mid, _, gate_up, _, resid = feed_forward(resid, attended, w_out_ref[...], w_gate_up_ref[...], w_down_ref[...], gain_b)
    mid_ref[...], gate_up_ref[...] = mid, gate_up
    traffic.send(mid_ref, gate_up_ref, feats_ref)
    next_resid_ref[...] = resid
    normal = (resid * norm_factor(resid) * gain_column(gains_ref, 2)).astype(bf16)
    next_ref[...] = normal
    copies_ref[...] = jnp.broadcast_to(normal[None], copies_ref.shape)


def natural_tiles(own_ref, other_ref, put):
    _, core, _, _ = geometry()
    mine = (iota((1, TILE), 1) < HALF) == (core == 0)
    for chip in range(TILES // 2):
        tile = 2 * chip if chip < 8 else TILES - 1 - 2 * chip
        first, second = jnp.where(core == 0, chip, 15 - chip), jnp.where(core == 0, 15 - chip, chip)
        own, other = own_ref[first].astype(f32), other_ref[second].astype(f32)
        for t, value in ((tile, jnp.where(mine, own, other)), (TILES - 1 - tile, jnp.where(mine, other, own))):
            put(t // 4, slice(t % 4 * TILE, (t % 4 + 1) * TILE), value.astype(bf16))


def second_kernel(
    traffic, own_ref, other_ref, cot_own_ref, cot_other_ref, len_ref, turned_qkv_ref, rope_ref, normal_ref, own_rope_ref, resid_in_ref,
    turned_out_ref, turned_gate_up_ref, w_out_ref, w_gate_up_ref, w_down_ref, gains_ref,
    copies_ref, payload_ref, act_ref, keys_ref, values_ref, normal_all, q_ref, grad_ref, att_ref, d_gain_ref,
    d_out_ref, d_gate_up_ref, d_branch_ref, hidden_ref, normal_b_ref,
    qbd, top_ref, acc_ref,
):
    chip, core, low, high = geometry()

    def put(block, columns, value):
        normal_all[block, :, columns] = value

    natural_tiles(own_ref, other_ref, put)
    traffic.send(normal_all)
    traffic.ready(5)
    w_qkv = turned_qkv_ref[...]
    k_size = jnp.zeros((HEADS, BLOCK), f32)
    for k in range(BLOCKS):
        k_size = jnp.maximum(k_size, key_value_block(normal_all[k], w_qkv, rope_ref, k, keys_ref, values_ref))
    traffic.send(keys_ref, values_ref)
    query = query_of(normal_ref[...], w_qkv, own_rope_ref[0:8], own_rope_ref[8:16])
    attended, stat = attend(query, k_size, keys_ref, values_ref, len_ref, low, high, qbd, top_ref, acc_ref, q_ref)
    traffic.ready()
    gain = gain_column(gains_ref, 3)
    w_out, w_gate_up, w_down = w_out_ref[...], w_gate_up_ref[...], w_down_ref[...]
    mid, _, gate_up, _, out = feed_forward(
        resid_in_ref[...], attended, turned_out_ref[...], turned_gate_up_ref[...], w_down, gain
    )
    act_ref[...] = out
    att_ref[...] = attended
    traffic.send(act_ref, att_ref, q_ref)
    grad = tile_halves(cot_own_ref[...].astype(f32), cot_other_ref[...].astype(f32))
    low_refs = (d_out_ref, d_gate_up_ref, d_branch_ref, hidden_ref, normal_b_ref)
    grad, payload, d_gain_ref[...] = feed_back(grad, attended, mid, gate_up, w_out, w_gate_up, w_down, gain, stat, low_refs, traffic)
    grad_ref[...] = grad
    payload_ref[...] = payload
    copies_ref[...] = jnp.broadcast_to(payload[None], copies_ref.shape)


def query_back(
    traffic, count, payload_ref, q_ref, len_ref, own_rope_ref, rope_ref, keys_ref, values_ref, normal_all, w_qkv_ref, dq_ref, qall_ref,
    k_rows_ref, v_rows_ref, qbd, dbd, acc_ref,
):
    chip, core, low, high = geometry()
    traffic.ready(count)
    unit = eye(TILE, TILE, bf16)
    rows = nt(unit, payload_ref[...])
    spread(qbd, jnp.concatenate([q_ref[...].astype(f32), rows[:, D:]], axis=1), LROW, LROW + 9)
    spread(dbd, rows, DROW)
    k_rows_ref[...] = nt(unit, own_tile(keys_ref, low, high)).astype(bf16)
    v_rows_ref[...] = nt(unit, own_tile(values_ref, low, high)).astype(bf16)
    w_qkv = w_qkv_ref[...]

    def queries(k, carry):
        at = pl.ds(pl.multiple_of(k * BLOCK, BLOCK), BLOCK)
        qall_ref[k] = query_of(normal_all[k], w_qkv, rope_ref[0:8, at], rope_ref[8:16, at])
        return carry

    lax.fori_loop(0, BLOCKS, queries, 0, unroll=2)
    traffic.send(k_rows_ref, v_rows_ref, qall_ref)
    acc_ref[...] = jnp.zeros(acc_ref.shape, f32)

    def step(u, tile, block, at):
        scores = scores_of(qbd[u], with_ones(keys_ref[block, :, at]), query_bias(u, tile, block, at, len_ref))
        d_scores = jnp.exp(scores) * nn(dbd[u], with_ones(values_ref[block, :, at]))
        acc_ref[u] = acc_ref[u] + nt(d_scores.astype(bf16), keys_ref[block, :, at])

    run_steps(query_step, low, high, step, 2)
    step(*query_last(low, high))
    d_query = jnp.concatenate([own_heads(acc_ref[0]), own_heads(acc_ref[1])], axis=0) * HEAD_DIM**-0.5
    dq_ref[...] = rotate(turned_rows(d_query), own_rope_ref[0:8], -own_rope_ref[8:16])


def turned_rows(x):
    hi, lo = two_parts(x)
    unit = eye(D, D, bf16)
    return nt(unit, hi) + nt(unit, lo)


def key_back(traffic, count, own_ref, other_ref, len_ref, qall_ref, k_rows_ref, v_rows_ref, dq_ref, grad_ref, resid_ref, w_qkv_ref, gain,
             own_rope_ref, daug, kbd, vbd, dk_ref, dv_ref):
    chip, core, low, high = geometry()

    def put(block, columns, value):
        daug[block, :, columns] = value

    natural_tiles(own_ref, other_ref, put)
    traffic.ready(count)
    ones = jnp.ones((TILE, STAT), f32)
    spread(kbd, jnp.concatenate([k_rows_ref[...].astype(f32), ones], axis=1), LROW, LROW + 9)
    spread(vbd, jnp.concatenate([v_rows_ref[...].astype(f32), ones], axis=1), DROW)
    dk_ref[...] = jnp.zeros(dk_ref.shape, f32)
    dv_ref[...] = jnp.zeros(dv_ref.shape, f32)

    def step(u, tile, block, at):
        queries = jnp.concatenate([qall_ref[block, :, at], daug[block, D:AUG, at]], axis=0)
        probs = jnp.exp(scores_of(kbd[u], queries, key_bias(u, tile, block, at, len_ref)))
        d_scores = probs * nn(vbd[u], daug[block, :, at])
        dv_ref[u] = dv_ref[u] + nt(probs.astype(bf16), daug[block, :, at])
        dk_ref[u] = dk_ref[u] + nt(d_scores.astype(bf16), qall_ref[block, :, at])

    run_steps(key_step, low, high, step)
    step(*key_last(low, high))
    traffic.ready()
    d_key = turned_rows(jnp.concatenate([own_heads(dk_ref[0]), own_heads(dk_ref[1])], axis=0))
    d_value = nt(eye(D, D, bf16), jnp.concatenate([own_heads(dv_ref[0]), own_heads(dv_ref[1])], axis=0).astype(bf16))
    d_key = rotate(d_key, own_rope_ref[0:8], -own_rope_ref[8:16])
    d_mixed = jnp.concatenate([dq_ref[...], d_key, d_value], axis=0).astype(bf16)
    d_in, d_gain = norm_back(resid_ref[...], gain(), nn(w_qkv_ref[...], d_mixed))
    return grad_ref[...] + d_in, d_mixed, d_gain


def projection_grads(normal, d_mixed):
    tail = nt(normal, jnp.concatenate([d_mixed[MAXLAG:], jnp.zeros((TILE - 48, TILE), bf16)], axis=0))
    return nt(normal, d_mixed[:MAXLAG]), tail


def third_kernel(
    traffic, own_ref, other_ref, len_ref, qall_ref, k_rows_ref, v_rows_ref, dq_ref, grad_in_ref, resid_ref, att_ref, stat_ref, mid_ref,
    gate_up_ref, own_rope_ref, w_qkv_ref, w_out_ref, w_gate_up_ref, w_down_ref, gains_ref,
    copies_ref, payload_ref, grad_ref, d_mixed_ref, d_gain_a_ref, d_gain_b_ref, d_out_ref, d_gate_up_ref, d_branch_ref, hidden_ref,
    normal_b_ref,
    daug, kbd, vbd, dk_ref, dv_ref,
):
    grad, d_mixed_ref[...], d_gain_a_ref[...] = key_back(
        traffic, 4, own_ref, other_ref, len_ref, qall_ref, k_rows_ref, v_rows_ref, dq_ref, grad_in_ref, resid_ref, w_qkv_ref,
        lambda: gain_column(gains_ref, 2), own_rope_ref, daug, kbd, vbd, dk_ref, dv_ref,
    )
    low_refs = (d_out_ref, d_gate_up_ref, d_branch_ref, hidden_ref, normal_b_ref)
    grad, payload, d_gain_b_ref[...] = feed_back(
        grad, att_ref[...], mid_ref[...], gate_up_ref[...], w_out_ref[...], w_gate_up_ref[...], w_down_ref[...], gain_column(gains_ref, 1),
        stat_ref[...], low_refs, traffic,
    )
    grad_ref[...] = grad
    payload_ref[...] = payload
    copies_ref[...] = jnp.broadcast_to(payload[None], copies_ref.shape)


def second_window_kernel(
    traffic, len_ref, hidden_ref, d_out_ref, normal_ref, d_gate_up_ref, att_ref, d_branch_ref, d_gain_ref, payload_ref, q_ref,
    own_rope_ref, rope_ref, keys_ref, values_ref, normal_all, w_qkv_ref,
    pack_ref, tail_ref, dq_ref, qall_ref, k_rows_ref, v_rows_ref, qbd, dbd, acc_ref,
):
    traffic.ready(8)
    tail = feed_grads(
        Tiles(pack_ref), hidden_ref[...], d_out_ref[...], normal_ref[...], d_gate_up_ref[...], att_ref[...], d_branch_ref[...]
    )
    tail_ref[...] = jnp.where(iota((1, TILE), 1) == 99, d_gain_ref[...], tail)
    traffic.send(pack_ref, tail_ref)
    query_back(
        traffic, 16, payload_ref, q_ref, len_ref, own_rope_ref, rope_ref, keys_ref, values_ref, normal_all, w_qkv_ref, dq_ref, qall_ref,
        k_rows_ref, v_rows_ref, qbd, dbd, acc_ref,
    )


def third_window_kernel(
    traffic, len_ref, pack_in_ref, tail_in_ref, normal_a_ref, d_mixed_ref, d_gain_a_ref, hidden_ref, d_out_ref, normal_ref, d_gate_up_ref,
    att_ref, d_branch_ref, d_gain_b_ref, payload_ref, q_ref, own_rope_ref, rope_ref, keys_ref, values_ref, normal_all,
    w_qkv_ref,
    keep_ref, send_ref, rest_ref, tail0_ref, tail1_ref, dq_ref, qall_ref, k_rows_ref, v_rows_ref, qbd, dbd, acc_ref,
):
    traffic.ready(13)
    put = Pairs(lax.axis_index("tm") % 2, keep_ref, send_ref, rest_ref)
    for t in range(pack_in_ref.shape[0]):
        put.tile(pack_in_ref[t].astype(f32))
    head, tail = projection_grads(normal_a_ref[...], d_mixed_ref[...])
    put(head)
    tail0_ref[...] = feed_grads(
        put, hidden_ref[...], d_out_ref[...], normal_ref[...], d_gate_up_ref[...], att_ref[...], d_branch_ref[...]
    )
    lane = iota((1, TILE), 1)
    tail = jnp.where(lane == 98, d_gain_a_ref[...], tail + tail_in_ref[...])
    tail1_ref[...] = jnp.where(lane == 97, d_gain_b_ref[...], tail)
    traffic.send(keep_ref, send_ref, rest_ref, tail0_ref, tail1_ref)
    query_back(
        traffic, 21, payload_ref, q_ref, len_ref, own_rope_ref, rope_ref, keys_ref, values_ref, normal_all, w_qkv_ref, dq_ref, qall_ref,
        k_rows_ref, v_rows_ref, qbd, dbd, acc_ref,
    )


def last_kernel(
    traffic, own_ref, other_ref, len_ref, scale_ref, ids_ref, qall_ref, k_rows_ref, v_rows_ref, dq_ref, grad_in_ref, resid_ref,
    normal_a_ref, tail0_ref, tail1_ref, rest_ref, w_dense_ref, feats_ref, own_rope_ref, w_qkv_ref, gains_ref,
    keep_ref, send_ref, daug, kbd, vbd, dk_ref, dv_ref, raw_ref,
):
    chip, core, low, high = geometry()
    d_first, d_mixed, d_gain = key_back(
        traffic, 6, own_ref, other_ref, len_ref, qall_ref, k_rows_ref, v_rows_ref, dq_ref, grad_in_ref, resid_ref, w_qkv_ref,
        lambda: gain_column(gains_ref, 0), own_rope_ref, daug, kbd, vbd, dk_ref, dv_ref,
    )
    head, tail0 = projection_grads(normal_a_ref[...], d_mixed)
    d_first = d_first.astype(bf16)
    feats = feats_ref[...]
    empty = jnp.zeros((64, TILE), bf16)
    tail0 = tail0 + tail0_ref[...] + nt(d_first, jnp.concatenate([empty, feats[:64]], axis=0))
    tail1 = tail1_ref[...] + nt(d_first, jnp.concatenate([empty, feats[64:], empty[:32]], axis=0))
    lane, row = iota((1, TILE), 1), iota((D, 1), 0)
    tail1 = jnp.where(lane == 96, d_gain, tail1)
    sums, counts = jnp.zeros((D, 1), f32), jnp.zeros((D, 1), f32)
    owner = (lax.axis_index("tm") == 0).astype(f32)
    for d in range(DOCS):
        hit = jnp.where(row == ids_ref[d], owner, 0.0)
        sums, counts = sums + hit * scale_ref[d], counts + hit
    high_part = sums.astype(bf16).astype(f32)
    tail1 = jnp.where(lane == 100, high_part, tail1)
    tail1 = jnp.where(lane == 101, sums - high_part, tail1)
    tail1 = jnp.where(lane == 102, counts, tail1)

    place = own_places(low, high)
    start = doc_start(place, len_ref)
    own = doc_scale_at(place, len_ref, scale_ref)
    flip = (iota((TILE, TILE), 0) + iota((TILE, TILE), 1) == TILE - 1).astype(bf16)
    raw_ref[...] = jnp.zeros(raw_ref.shape, f32)
    lags = TILE - iota((TILE, 1), 0)
    for b in range(3):
        weights = nn(w_dense_ref[:, b * TILE : (b + 1) * TILE], flip).astype(bf16)
        d_lagged = tn(weights, d_first)
        valid = place - (lags + b * TILE) >= start
        d_lagged = jnp.where(valid, d_lagged, 0.0) / own
        for u in range(2):
            half = jnp.where((lane < HALF) == (u == 0), d_lagged, 0.0)
            wide = jnp.concatenate([jnp.zeros((TILE, TILE), f32), half], axis=1)
            rolled = pltpu.roll(wide, TILE, 1, stride=1, stride_axis=0)
            total = jnp.sum(rolled, axis=0, keepdims=True)
            for tile, part in (((low if u == 0 else high) - b + 16, total[:, TILE:]), ((low if u == 0 else high) - b + 15, total[:, :TILE])):
                at = tile % 2, pl.ds(tile // 2, 1)
                raw_ref[at] = raw_ref[at] + part

    put = Pairs(core, keep_ref, send_ref)
    put.tile(rest_ref[0].astype(f32))
    for part in (head, tail0, tail1):
        put(part)
    for k in range(2):
        put.tile(raw_ref[k, 8:24, :])


def summed(in_ref):
    count, rows, _ = in_ref.shape
    total = jnp.zeros((rows, TILE), f32)
    return lax.fori_loop(0, count // 8, lambda i, t: t + jnp.sum(in_ref[pl.ds(i * 8, 8)].astype(f32), axis=0), total)


def pair_sum_kernel(early_ref, early_in_ref, late_ref, late_in_ref, out_ref):
    zero = jnp.zeros((16, TILE), bf16)
    late = late_ref.shape[0] - 1
    series, core = lax.axis_index("series"), lax.axis_index("tm") % 2
    out_ref[:, 32:48, :] = jnp.zeros((64, 16, TILE), bf16)

    def both(ref, in_ref, t):
        return ref[t].astype(f32) + in_ref[t].astype(f32)

    for t in range(128):
        value = zero
        if t < EARLY:
            value = both(early_ref, early_in_ref, t).astype(bf16)
        elif t < EARLY + late:
            value = both(late_ref, late_in_ref, t - EARLY).astype(bf16)
        out_ref[jnp.where(core == 0, t // 2, 63 - t // 2), t % 2 * 16 : t % 2 * 16 + 16, :] = value
    raw = both(late_ref, late_in_ref, late)
    for c in range(16):
        line = jnp.where(iota((16, 1), 0) == 0, raw[c : c + 1], 0.0)
        chip = series * 16 + c
        out_ref[jnp.where(core == 0, chip, 63 - chip), 32:48, :] = line.astype(bf16)


def sum_kernel(in_ref, out_ref, raw_ref):
    total = summed(in_ref)
    out_ref[...] = jnp.broadcast_to(total[:32].astype(bf16)[None], out_ref.shape)
    raw_ref[...] = total[32:33]


def unpack_kernel(own_ref, other_ref, act_in_ref, act_ref, lag_ref, qkv_ref, out_ref, gate_up_ref, down_ref, gains_ref, scale_ref):
    core = lax.axis_index("tm") % 2
    act_ref[...] = act_in_ref[...]

    def tile(t):
        rows = slice(t // 2 % 2 * 16, t // 2 % 2 * 16 + 16)
        first, second = jnp.where(core == 0, t // 4, 63 - t // 4), jnp.where(core == 0, 63 - t // 4, t // 4)
        return jnp.where(core == t % 2, own_ref[first, rows].astype(f32), other_ref[second, rows].astype(f32))

    def columns(first, count):
        return [jnp.concatenate([tile(first + 9 * c + r) for r in range(9)], axis=0) for c in range(count)]

    layers = ((207, 234, 117), (90, 243, 0))
    tails = []
    for layer, (at_qkv, at_tail, at_rest) in enumerate(layers):
        for c, part in enumerate(columns(at_qkv, 3)):
            qkv_ref[layer, :, c * TILE : (c + 1) * TILE] = part
        tail = columns(at_tail, 1)[0]
        tails.append(tail)
        qkv_ref[layer, :, MAXLAG:] = tail[:, :48]
        for c, part in enumerate(columns(at_rest, 3)):
            down_ref[layer, :, c * TILE : (c + 1) * TILE] = part
        for c, part in enumerate(columns(at_rest + 27, 6)):
            gate_up_ref[layer, :, c * TILE : (c + 1) * TILE] = part
        out_ref[layer, :, :TILE] = columns(at_rest + 81, 1)[0]
        out_ref[layer, :, TILE:] = tail[:, 48:64]
    lag = jnp.where(iota((1, TILE), 1) < 64, pltpu.roll(tails[0], 64, 1), tails[1])
    lag_ref[...] = lag[:, :FEATS]
    pick = (iota((8, TILE), 1) == iota((8, TILE), 0) + 96).astype(bf16)
    rest = nt(pick, tails[1].astype(bf16))
    gains_ref[0] = rest[0:2]
    gains_ref[1] = rest[2:4]
    scale_ref[...] = ((rest[4:5] + rest[5:6]) / rest[6:7])[:, :DATASETS]


def weights_kernel(
    traffic, lag_ref, w_lag_ref, w_qkv_ref, w_out_ref, w_gate_up_ref, cot_ref,
    dense_ref, qkv0_ref, out0_ref, gate_up0_ref, qkv1_ref, out1_ref, gate_up1_ref, chosen_ref, low_cot_ref,
):
    traffic.ready()
    rows = iota((FEATS, 1), 0)
    diagonal = iota((FEATS, LAGS), 0) == iota((FEATS, LAGS), 1)
    offsets = jnp.sum(jnp.where(diagonal, lag_ref[...].astype(f32), 0.0), axis=1, keepdims=True)
    offsets = jnp.where(rows < LAGS, offsets - 1.0, (rows - LAGS + MAXLAG + 1).astype(f32))
    chosen = (iota((FEATS, LAGCOLS), 1).astype(f32) == offsets).astype(bf16)
    chosen_ref[0:FEATS, :] = chosen
    chosen_ref[FEATS:, :] = jnp.zeros((96 - FEATS, LAGCOLS), bf16)
    dense_ref[...] = nn(w_lag_ref[...], chosen).astype(bf16)
    qkv0_ref[...] = turned(w_qkv_ref[0])
    out0_ref[...] = turned(w_out_ref[0])
    gate_up0_ref[...] = turned(w_gate_up_ref[0])
    qkv1_ref[...] = turned(w_qkv_ref[1])
    out1_ref[...] = turned(w_out_ref[1])
    gate_up1_ref[...] = turned(w_gate_up_ref[1])
    low_cot_ref[...] = cot_ref[...].astype(bf16)


def first_values_kernel(traffic, len_ref, scale_ref, raw_ref, hours_ref, out_ref):
    traffic.ready()
    places = lax.axis_index("tm") * TILE + iota((1, TILE), 1)
    own = doc_scale_at(places, len_ref, scale_ref)
    angle = hours_ref[...].astype(f32) * (2.0 * math.pi / 24.0)
    rows = [raw_ref[...] / own, jnp.sin(angle), jnp.cos(angle), jnp.log(own), jnp.zeros((4, TILE), f32)]
    out_ref[...] = jnp.broadcast_to(jnp.concatenate(rows, axis=0)[None], out_ref.shape)


def shape(*dims, dtype=f32):
    return jax.ShapeDtypeStruct(dims, dtype)


class Traffic:
    def __init__(self, loads, stores):
        self.loads, self.stores, self.waited, self.sent = loads, stores, 0, set()
        for copy in loads:
            copy.start()

    def ready(self, count=None):
        count = len(self.loads) if count is None else count
        for copy in self.loads[self.waited : count]:
            copy.wait()
        self.waited = max(self.waited, count)

    def send(self, *refs):
        for ref, copy in self.stores:
            if any(ref is r for r in refs):
                copy.start()
                self.sent.add(id(copy))

    def finish(self):
        self.ready()
        for _, copy in self.stores:
            if id(copy) not in self.sent:
                copy.start()
        for _, copy in self.stores:
            copy.wait()


def call(kernel, operands, outs, scratch=(), tables=(), weights=(), cost=None):
    several = isinstance(outs, list)
    outs = outs if several else [outs]
    layers = [None] * len(tables) + [x[1] if isinstance(x, tuple) else None for x in weights]
    fetched = (*tables, *(x[0] if isinstance(x, tuple) else x for x in weights))
    shapes = [x.shape if layer is None else x.shape[1:] for x, layer in zip(fetched, layers)]
    buffers = [(pltpu.SMEM if n < len(tables) else pltpu.VMEM)(shapes[n], x.dtype) for n, x in enumerate(fetched)]
    is_far = [not isinstance(out, jax.ShapeDtypeStruct) for out in outs]
    buffers += [pltpu.VMEM(out.shape, out.dtype) for out, far in zip(outs, is_far) if far]
    count, extra, copies = len(operands), len(buffers), len(buffers)

    def wrapped(*refs):
        refs = list(refs)
        ins, sources = refs[:count], refs[count : count + len(fetched)]
        results = refs[count + len(fetched) : count + len(fetched) + len(outs)]
        rest = refs[count + len(fetched) + len(outs) :]
        if not copies:
            kernel(*ins, *results, *rest)
            return
        own, held, sems = rest[: len(scratch)], rest[len(scratch) : -1], rest[-1]
        sources = [a if layer is None else a.at[layer] for a, layer in zip(sources, layers)]
        loads = [pltpu.make_async_copy(a, b, sems.at[n]) for n, (a, b) in enumerate(zip(sources, held))]
        stores, at = [], len(fetched)
        for n, far in enumerate(is_far):
            if far:
                stores.append((held[at], pltpu.make_async_copy(held[at], results[n], sems.at[at])))
                results[n] = held[at]
                at += 1
        traffic = Traffic(loads, stores)
        kernel(traffic, *ins, *held[: len(fetched)], *results, *own)
        traffic.finish()

    vmem, hbm = pl.BlockSpec(memory_space=pltpu.VMEM), pl.BlockSpec(memory_space=pltpu.HBM)
    results = pl.pallas_call(
        wrapped,
        out_shape=outs,
        in_specs=[vmem] * count + [hbm] * len(fetched),
        out_specs=[hbm if far else vmem for far in is_far],
        scratch_shapes=[*scratch, *buffers, pltpu.SemaphoreType.DMA((copies,))] if copies else list(scratch),
        compiler_params=pltpu.CompilerParams(vmem_limit_bytes=VMEM),
        cost_estimate=cost and pl.CostEstimate(flops=cost * 10**9, bytes_accessed=10**6, transcendentals=0),
    )(*operands, *(pltpu.with_memory_space_constraint(x, pltpu.HBM) for x in fetched))
    return results if several else results[0]


def pair_permute(x, bit):
    return lax.ppermute(x, "tm", [(i, i ^ bit) for i in range(32)])


def gather(copies, beside):
    groups = [[2 * chip for chip in range(16)], [31 - 2 * chip for chip in range(16)]]
    own = lax.all_to_all(copies, "tm", 0, 0, axis_index_groups=groups)
    own, beside = lax.optimization_barrier((own, beside))
    return own, pair_permute(own, 1), beside


def swap(block):
    return lax.ppermute(block, "tm", [(n, n if n % 2 == 0 else 32 - n) for n in range(32)])


def tile_halves(own, other):
    lane = iota((1, TILE), 1) < HALF
    return jnp.where(lane == (lax.axis_index("tm") < 16), own, other)


def rope_table():
    freqs = 10000.0 ** (-np.arange(8, dtype=np.float64) / 8)
    angle = np.arange(LEN, dtype=np.float64)[None, :] * freqs[:, None]
    return np.concatenate([np.cos(angle), np.sin(angle)], axis=0).astype(np.float32)


def body(
    raw_values, hours, doc_lengths, doc_scale, dataset_ids, lag_offsets, w_lag, w_qkv, w_out, w_gate_up, w_down, gains, cotangent
):
    lengths, scales, ids = doc_lengths.reshape(DOCS), doc_scale.reshape(DOCS), dataset_ids.reshape(DOCS)
    def low(*dims):
        return shape(*dims, dtype=bf16)

    def far(*dims, dtype=f32):
        return pltpu.HBM(dims, dtype)

    def far_low(*dims):
        return far(*dims, dtype=bf16)

    w_lag, w_down, lags = w_lag.T, w_down.transpose(0, 2, 1), lag_offsets.reshape(1, LAGS)
    rope = jnp.asarray(rope_table())
    values = lax.all_to_all(call(first_values_kernel, (), shape(32, 8, TILE), tables=(lengths, scales), weights=(raw_values, hours)), "tm", 0, 0)
    turned_shapes = [far_low(3 * D, D), far_low(D, D), far_low(2 * FF, D)]
    w_dense, *turned_weights, chosen, low_cot = call(
        weights_kernel, (), [far_low(D, LAGCOLS), *turned_shapes, *turned_shapes, far_low(96, LAGCOLS), far_low(D, TILE)],
        weights=(lags, w_lag, w_qkv, w_out, w_gate_up, cotangent[0].T), cost=3,
    )
    turned0, turned1 = turned_weights[:3], turned_weights[3:]
    values, w_dense = lax.optimization_barrier((values, w_dense))
    all_d = far_low(BLOCKS, D, BLOCK)
    mine, mine_low, ff_low, column_shape = far(D, TILE), far_low(D, TILE), far_low(FF, TILE), far(D, 1)
    payload_shapes = [far_low(16, AUG, TILE), far_low(AUG, TILE)]
    low_grads = [mine_low, far_low(2 * FF, TILE), mine_low, ff_low, mine_low]
    bd, wide_bd = pltpu.VMEM((2, ROWS, AUG), bf16), pltpu.VMEM((2, ROWS, WIDE), bf16)
    acc, acc_d = pltpu.VMEM((2, ROWS, AUG), f32), pltpu.VMEM((2, ROWS, D), f32)
    top = pltpu.VMEM((2, ROWS, 1), f32)
    back_scratch = [pltpu.VMEM((BLOCKS, AUG, BLOCK), bf16), wide_bd, bd, acc_d, acc]

    (copies, next1, resid1, keys0, values0, normal_all0, feats, resid0, normal_a0, q0, att0, stat0, mid0, gate_up0, own_rope) = call(
        first_kernel,
        (values,),
        [far_low(16, D, TILE), mine_low, mine, all_d, all_d, all_d, far_low(96, TILE), mine, mine_low, far_low(TILE, D), mine_low,
         far_low(STAT, TILE), mine, far(2 * FF, TILE), far(16, TILE)],
        [pltpu.VMEM((8 + TILES, TILE), f32), pltpu.VMEM((TILE, MAXLAG + LEN), bf16),
         pltpu.VMEM((LAGCOLS, TILE), bf16), wide_bd, top, acc],
        tables=(lengths,), weights=(w_dense, gains, turned0[0], rope, chosen, *turned0[1:], (w_down, 0)),
    )

    own, other, cot = gather(copies, swap(low_cot))
    copies, payload, act, keys1, values1, normal_all1, q1, grad, att1, d_gain_b1, *low1 = call(
        second_kernel,
        (own, other, cot, pair_permute(cot, 1)),
        [*payload_shapes, mine, all_d, all_d, all_d, far_low(TILE, D), mine, mine_low, column_shape, *low_grads],
        [wide_bd, top, acc],
        tables=(lengths,),
        weights=(turned1[0], rope, next1, own_rope, resid1, *turned1[1:], (w_out, 1), (w_gate_up, 1), (w_down, 1), gains),
    )

    rows_low = far_low(TILE, D)
    side_shapes = [mine, all_d, rows_low, rows_low]
    d_out, d_gate_up, d_branch, hidden, normal_b = low1
    pack, tail, dq, qall, k_rows, v_rows = call(
        second_window_kernel, (), [far_low(90, 16, TILE), mine, *side_shapes], [wide_bd, bd, acc_d],
        tables=(lengths,),
        weights=(hidden, d_out, normal_b, d_gate_up, att1, d_branch, d_gain_b1, payload, q1, own_rope, rope, keys1, values1, normal_all1,
                 turned1[0]), cost=8,
    )
    own, other, dq = gather(copies, dq)
    copies, payload, grad, d_mixed, d_gain_a1, d_gain_b0, *low0 = call(
        third_kernel,
        (own, other),
        [*payload_shapes, mine, far_low(3 * D, TILE), column_shape, column_shape, *low_grads],
        back_scratch,
        tables=(lengths,),
        weights=(qall, k_rows, v_rows, dq, grad, resid1, att0, stat0, mid0, gate_up0, own_rope, (w_qkv, 1), (w_out, 0), (w_gate_up, 0),
                 (w_down, 0), gains),
    )
    d_out, d_gate_up, d_branch, hidden, normal_b = low0
    early, early_out, rest, tail0, tail1, dq, qall, k_rows, v_rows = call(
        third_window_kernel, (),
        [far_low(EARLY, 16, TILE), far_low(EARLY, 16, TILE), far_low(1, 16, TILE), mine, mine, *side_shapes], [wide_bd, bd, acc_d],
        tables=(lengths,),
        weights=(pack, tail, next1, d_mixed, d_gain_a1, hidden, d_out, normal_b, d_gate_up, att0, d_branch, d_gain_b0, payload, q0,
                 own_rope, rope, keys0, values0, normal_all0, turned0[0]), cost=8,
    )
    own, other, (dq, early_out) = gather(copies, (dq, early_out))
    early_in = pair_permute(early_out, 1)
    late, late_out = call(
        last_kernel,
        (own, other),
        [low(LATE, 16, TILE)] * 2,
        [*back_scratch, pltpu.VMEM((2, 24, TILE), f32)],
        tables=(lengths, scales, ids),
        weights=(qall, k_rows, v_rows, dq, grad, resid0, normal_a0, tail0, tail1, rest, w_dense, feats, own_rope, (w_qkv, 0), gains),
    )
    packed = call(pair_sum_kernel, (early, early_in, late, pair_permute(late_out, 1)), low(64, 48, TILE))
    same_core = [[2 * chip for chip in range(64)], [127 - 2 * chip for chip in range(64)]]
    parts = lax.all_to_all(packed, ("series", "tm"), 0, 0, axis_index_groups=same_core)
    share, raw_grad = call(sum_kernel, (parts,), [low(64, 32, TILE), shape(1, TILE)])
    share, act = lax.optimization_barrier((share, act))
    own = lax.all_to_all(share, ("series", "tm"), 0, 0, axis_index_groups=same_core)
    own, act = lax.optimization_barrier((own, swap(tile_halves(act, pair_permute(act, 1)))))
    act, g_lag, g_qkv, g_out, g_gate_up, g_down, g_gains, scale = call(
        unpack_kernel,
        (own, pair_permute(own, 1), act),
        [shape(D, TILE), shape(D, FEATS), shape(LAYERS, D, 3 * D), shape(LAYERS, D, D), shape(LAYERS, D, 2 * FF), shape(LAYERS, D, FF),
         shape(LAYERS, 2, D), shape(1, DATASETS)],
    )
    return (
        act.T[None], raw_grad, scale.reshape(DATASETS), g_lag.T, g_qkv, g_out, g_gate_up, g_down.transpose(0, 2, 1), g_gains,
    )


def solution(mesh):
    placed = (
        P("series", "tm"),
        P("series", "tm"),
        P("series", None),
        P("series", None),
        P("series", None, None),
        P(),
        P(),
        P(),
        P(),
        P(),
        P(),
        P(),
        P("series", "tm", None),
    )
    return jax.shard_map(
        body,
        mesh=mesh,
        in_specs=placed,
        out_specs=(P("series", "tm", None), P("series", "tm"), P(), P(), P(), P(), P(), P(), P()),
        check_vma=False,
    )
```

```python
import math

import jax
import jax.numpy as jnp
import numpy as np
from jax import lax
from jax.experimental import pallas as pl
from jax.experimental.pallas import tpu as pltpu
from jax.sharding import PartitionSpec as P


D = 144
HEADS = 9
HEAD_DIM = 16
FF = 384
LAGS = 84
LAYERS = 2
DATASETS = 8
DOCS = 7
LEN = 4096
MAXLAG = 384
FEATS = 87
EPSILON = 1e-06
MASKED = -1e30
AUG = 176
STAT = AUG - D
LROW = D
DROW = D + 18
BLOCK = 512
BLOCKS = LEN // BLOCK
TILE = 128
TILES = LEN // TILE
STEPS = BLOCKS + 1
SHIFTED = 8
HALF = 64
ROWS = HEADS * HALF
LAGCOLS = 400
EARLY = 103
LATE = 24
WIDE = AUG + HALF
SAFE = 70.0
VMEM = 28 * 2**20

bf16 = jnp.bfloat16
f32 = jnp.float32
HIGH = lax.Precision.HIGHEST


def nn(a, b, precision=None):
    return lax.dot_general(a, b, (((1,), (0,)), ((), ())), precision=precision, preferred_element_type=f32)


def nt(a, b, precision=None):
    return lax.dot_general(a, b, (((1,), (1,)), ((), ())), precision=precision, preferred_element_type=f32)


def tn(a, b, precision=None):
    return lax.dot_general(a, b, (((0,), (0,)), ((), ())), precision=precision, preferred_element_type=f32)


def iota(shape, dim):
    return lax.broadcasted_iota(jnp.int32, shape, dim)


def eye(rows, cols, dtype):
    return (iota((rows, cols), 0) == iota((rows, cols), 1)).astype(dtype)


def column(row, size):
    keep = iota((size, size), 0) == iota((size, size), 1)
    return jnp.sum(jnp.where(keep, row, 0.0), axis=1, keepdims=True)


def pair_of(chip):
    return jnp.where(chip < 8, 2 * chip, TILES - 1 - 2 * chip)


def geometry():
    index = lax.axis_index("tm")
    chip, core = index // 2, index % 2
    tile = pair_of(chip)
    low = jnp.where(core == 0, tile, TILES - 1 - tile)
    return chip, core, low, TILES - 1 - low


def doc_start(places, len_ref):
    start = jnp.zeros_like(places)
    end = jnp.int32(0)
    for d in range(DOCS):
        end = end + len_ref[d]
        start = jnp.where(places >= end, end, start)
    return start


def doc_scale_at(places, len_ref, scale_ref):
    own = jnp.full(places.shape, scale_ref[0], f32)
    end = jnp.int32(0)
    for d in range(1, DOCS):
        end = end + len_ref[d - 1]
        own = jnp.where(places >= end, scale_ref[d], own)
    return own


def own_places(low, high):
    lane = iota((1, TILE), 1)
    return jnp.where(lane < HALF, low, high) * TILE + lane


def half_places(u, tile):
    return iota((HALF, 1), 0) + (tile * TILE + u * HALF)


def rotate(x, cosine, sine):
    cols = x.shape[1]
    parts = x.reshape(HEADS, 2, 8, cols)
    one, two = parts[:, 0], parts[:, 1]
    turned = jnp.stack([one * cosine - two * sine, two * cosine + one * sine], axis=1)
    return turned.reshape(D, cols)


def norm_factor(x):
    return lax.rsqrt(jnp.mean(x * x, axis=0, keepdims=True) + EPSILON)


def norm_back(x, gain, d_normal):
    r = norm_factor(x)
    scaled = d_normal * gain
    inner = jnp.mean(x * scaled, axis=0, keepdims=True)
    d_x = r * scaled - (r * r * r * inner) * x
    return d_x, jnp.sum(d_normal * x * r, axis=1, keepdims=True)


def head_columns(h, *firsts):
    col = iota((1, AUG), 1)
    keep = (col >= h * HEAD_DIM) & (col < (h + 1) * HEAD_DIM)
    for first in firsts:
        keep = keep | (col == first + h)
    return keep


def spread(ref, rows, *firsts):
    zero = jnp.zeros((HALF, AUG), f32)
    for h in range(HEADS):
        keep = head_columns(h, *firsts)
        for u in range(2):
            part = rows[u * HALF : (u + 1) * HALF]
            ref[u, h * HALF : (h + 1) * HALF, 0:AUG] = jnp.where(keep, part, zero).astype(bf16)
    if ref.shape[2] == WIDE:
        unit = eye(HALF, HALF, bf16)
        for h in range(HEADS):
            for u in range(2):
                ref[u, h * HALF : (h + 1) * HALF, AUG:WIDE] = unit


def own_heads(x):
    col = iota((1, D), 1) // HEAD_DIM
    total = jnp.zeros((HALF, D), f32)
    for h in range(HEADS):
        total = jnp.where(col == h, x[h * HALF : (h + 1) * HALF, :D], total)
    return total


def two_parts(x):
    hi = x.astype(bf16)
    return hi, (x - hi.astype(f32)).astype(bf16)


class Tiles:
    def __init__(self, ref):
        self.ref, self.count = ref, 0

    def tile(self, value):
        self.ref[self.count] = value.astype(bf16)
        self.count += 1

    def __call__(self, grads):
        for c in range(grads.shape[1] // TILE):
            for r in range(grads.shape[0] // 16):
                self.tile(grads[16 * r : 16 * (r + 1), c * TILE : (c + 1) * TILE].astype(f32))


class Pairs(Tiles):
    def __init__(self, core, keep_ref, send_ref, rest_ref=None):
        self.core, self.refs, self.rest, self.count, self.even = core, (keep_ref, send_ref), rest_ref, 0, None

    def tile(self, value):
        if self.count == self.refs[0].shape[0]:
            self.rest[0] = value.astype(bf16)
        elif self.even is None:
            self.even = value
        else:
            self.refs[0][self.count] = jnp.where(self.core == 0, self.even, value).astype(bf16)
            self.refs[1][self.count] = jnp.where(self.core == 0, value, self.even).astype(bf16)
            self.even = None
            self.count += 1


def turned(w):
    return tn(w, eye(D, D, bf16)).astype(bf16)


def with_ones(x):
    return jnp.concatenate([x, jnp.ones((STAT, x.shape[1]), bf16)], axis=0)


def key_value_block(normal, w_qkv, rope_ref, k, keys_ref, values_ref):
    mixed = nn(w_qkv[D:], normal)
    at = slice(k * BLOCK, (k + 1) * BLOCK)
    keys = rotate(mixed[:D], rope_ref[0:8, at], rope_ref[8:16, at])
    keys_ref[k] = keys.astype(bf16)
    values_ref[k] = mixed[D:].astype(bf16)
    return head_sizes(keys * keys)


def query_of(normal, w_qkv, cosine, sine):
    turned = rotate(nn(w_qkv[:D], normal), cosine, sine)
    return (turned.astype(bf16).astype(f32) * HEAD_DIM**-0.5).astype(bf16)


def own_rope(rope_ref, low, high):
    def at(tile):
        return rope_ref[:, pl.ds(pl.multiple_of(tile * TILE, TILE), TILE)]

    both = jnp.where(iota((1, TILE), 1) < HALF, at(low), at(high))
    return both[0:8], both[8:16]


def own_tile(ref, low, high):
    lane = iota((1, TILE), 1)

    def at(tile):
        return ref[tile // 4, :, pl.ds(pl.multiple_of((tile % 4) * TILE, TILE), TILE)].astype(f32)

    return jnp.where(lane < HALF, at(low), at(high)).astype(bf16)


def query_bias(u, tile, block, columns, len_ref):
    places = half_places(u, tile)
    start = doc_start(places, len_ref)
    keys = iota((1, columns.stop - columns.start), 1) + (block * BLOCK + columns.start)
    return jnp.where((keys <= places) & (keys >= start), 0.0, MASKED).astype(bf16)


def key_bias(u, tile, block, columns, len_ref):
    keys = half_places(u, tile)
    places = iota((1, columns.stop - columns.start), 1) + (block * BLOCK + columns.start)
    start = doc_start(places, len_ref)
    return jnp.where((keys <= places) & (keys >= start), 0.0, MASKED).astype(bf16)


def scores_of(rows, columns, bias):
    return nn(rows, jnp.concatenate([columns, bias], axis=0))


def run_steps(of_step, low, high, step, unroll=4):
    def several(i, carry):
        for j in range(unroll):
            step(*of_step(i * unroll + j, low, high), slice(0, BLOCK))
        return carry

    lax.fori_loop(0, (STEPS - 1) // unroll, several, 0)


def query_step(s, low, high):
    first = low // 4 + (low % 4 >= 2).astype(jnp.int32)
    late = s >= first
    return late.astype(jnp.int32), jnp.where(late, high, low), s - jnp.where(late, first, 0)


def query_last(low, high):
    late = low % 4 >= 2
    tile = jnp.where(late, high, low)
    return late.astype(jnp.int32), tile, tile // 4, slice(0, BLOCK // 2)


def key_step(s, low, high):
    late_short = (low % 4 < 2).astype(jnp.int32)
    first = low // 4 + 1 - late_short
    late = s >= BLOCKS - first
    block = jnp.where(late, high // 4 + late_short + s - (BLOCKS - first), first + s)
    return late.astype(jnp.int32), jnp.where(late, high, low), block


def key_last(low, high):
    late = low % 4 < 2
    tile = jnp.where(late, high, low)
    return late.astype(jnp.int32), tile, tile // 4, slice(BLOCK // 2, BLOCK)


def head_sizes(squares):
    return jnp.sum(squares.reshape(HEADS, HEAD_DIM, squares.shape[1]), axis=1)


def attend(query, k_size, keys_ref, values_ref, len_ref, low, high, qbd, top_ref, acc_ref, q_rows_ref):
    q_rows = nt(eye(TILE, TILE, bf16), query)
    q_rows_ref[...] = q_rows.astype(bf16)
    spread(qbd, jnp.concatenate([q_rows, jnp.zeros((TILE, STAT), f32)], axis=1))
    query = query.astype(f32)
    q_size = jnp.max(head_sizes(query * query), axis=1, keepdims=True)
    k_size = jnp.max(k_size, axis=1, keepdims=True)
    acc_ref[...] = jnp.zeros(acc_ref.shape, f32)
    safe = jnp.max(q_size * k_size) <= SAFE * SAFE

    @pl.when(safe)
    def _():
        top_ref[...] = jnp.zeros(top_ref.shape, f32)

        def step(u, tile, block, at):
            scores = scores_of(qbd[u], with_ones(keys_ref[block, :, at]), query_bias(u, tile, block, at, len_ref))
            acc_ref[u] = acc_ref[u] + nt(jnp.exp(scores).astype(bf16), with_ones(values_ref[block, :, at]))

        run_steps(query_step, low, high, step, 8)
        step(*query_last(low, high))

    @pl.when(jnp.logical_not(safe))
    def _():
        top_ref[...] = jnp.full(top_ref.shape, MASKED, f32)

        def step(s, carry):
            h, s = s % HEADS, s // HEADS
            first = low // 4 + 1
            late = s >= first
            u, tile, block = late.astype(jnp.int32), jnp.where(late, high, low), s - jnp.where(late, first, 0)
            rows = pl.ds(pl.multiple_of(h * HALF, HALF), HALF)
            bias = query_bias(u, tile, block, slice(0, BLOCK), len_ref)
            scores = scores_of(qbd[u, rows], with_ones(keys_ref[block]), bias)
            old = top_ref[u, rows]
            new = jnp.maximum(old, jnp.max(scores, axis=1, keepdims=True))
            probs = jnp.exp(scores - new)
            acc_ref[u, rows] = acc_ref[u, rows] * jnp.exp(old - new) + nt(probs.astype(bf16), with_ones(values_ref[block]))
            top_ref[u, rows] = new
            return carry

        lax.fori_loop(0, STEPS * HEADS, step, 0)

    attended, stats = [], []
    lane, col = iota((1, STAT), 1), iota((1, D), 1) // HEAD_DIM
    for u in range(2):
        acc, top = acc_ref[u], top_ref[u]
        total, shift = jnp.ones((HALF, STAT), f32), jnp.zeros((HALF, STAT), f32)
        for h in range(HEADS):
            rows = slice(h * HALF, (h + 1) * HALF)
            here = (lane == h) | (lane == HEADS + h)
            total = jnp.where(here, acc[rows, D : D + 1], total)
            shift = jnp.where(here, top[rows], shift)
        hi, lo = two_parts(-(shift + jnp.log(total)))
        stats.append(jnp.where(lane < HEADS, hi.astype(f32), jnp.where(lane < 2 * HEADS, lo.astype(f32), 0.0)))
        own = jnp.zeros((HALF, D), f32)
        for h in range(HEADS):
            rows = slice(h * HALF, (h + 1) * HALF)
            own = jnp.where(col == h, acc[rows, :D] / acc[rows, D : D + 1], own)
        attended.append(own)
    att_rows = jnp.concatenate(attended, axis=0).astype(bf16)
    stat_rows = jnp.concatenate(stats, axis=0).astype(bf16)
    return nt(eye(D, D, bf16), att_rows).astype(bf16), nt(eye(STAT, STAT, bf16), stat_rows).astype(bf16)


def feed_forward(resid, attended, w_out, w_gate_up, w_down, gain):
    mid = resid + nn(w_out, attended)
    normal = (mid * norm_factor(mid) * gain).astype(bf16)
    gate_up = nn(w_gate_up, normal)
    gate = gate_up[:FF]
    hidden = (gate * jax.nn.sigmoid(gate) * gate_up[FF:]).astype(bf16)
    return mid, normal, gate_up, hidden, mid + nn(w_down, hidden)


def feed_back(grad, attended, mid, gate_up, w_out, w_gate_up, w_down, gain, stat, low_refs, traffic):
    d_out_ref, d_gate_up_ref, d_branch_ref, hidden_ref, normal_ref = low_refs
    d_out = grad.astype(bf16)
    d_hidden = tn(w_down, d_out)
    gate, up = gate_up[:FF], gate_up[FF:]
    sig = jax.nn.sigmoid(gate)
    d_gate = d_hidden * up * (sig * (1.0 + gate * (1.0 - sig)))
    d_up = d_hidden * (gate * sig)
    hidden_ref[...] = (gate * sig * up).astype(bf16)
    normal_ref[...] = (mid * norm_factor(mid) * gain).astype(bf16)
    d_gate_up = jnp.concatenate([d_gate, d_up], axis=0).astype(bf16)
    d_mid, d_gain = norm_back(mid, gain, nn(w_gate_up, d_gate_up))
    grad = grad + d_mid
    d_branch = grad.astype(bf16)
    d_att = nn(w_out, d_branch).astype(bf16)
    d_out_ref[...], d_gate_up_ref[...], d_branch_ref[...] = d_out, d_gate_up, d_branch
    traffic.send(*low_refs)
    product = d_att.astype(f32) * attended.astype(f32)
    delta = -jnp.sum(product.reshape(HEADS, HEAD_DIM, TILE), axis=1)
    delta = jnp.concatenate([delta, jnp.zeros((16 - HEADS, TILE), f32)], axis=0)
    row, col = iota((STAT, 16), 0), iota((STAT, 16), 1)
    stat = stat.astype(f32) + nn(((row == DROW - D + col) & (col < HEADS)).astype(bf16), delta.astype(bf16))
    return grad, jnp.concatenate([d_att, stat.astype(bf16)], axis=0), d_gain


def feed_grads(put, hidden, d_out, normal, d_gate_up, attended, d_branch):
    put(nt(d_out, hidden))
    put(nt(normal, d_gate_up))
    put(nt(attended, d_branch[:TILE]))
    rows = [jnp.zeros((48, TILE), bf16), d_branch[TILE:], jnp.zeros((TILE - 64, TILE), bf16)]
    return nt(attended, jnp.concatenate(rows, axis=0))


def gain_column(gains_ref, which):
    return column(gains_ref[which // 2, which % 2 : which % 2 + 1, :], D)


def first_kernel(
    traffic, features_ref, len_ref, w_dense_ref, gains_ref, w_qkv_ref, rope_ref, chosen_ref, w_out_ref, w_gate_up_ref,
    w_down_ref,
    copies_ref, next_ref, next_resid_ref, keys_ref, values_ref, normal_all, feats_ref, resid_ref, normal_a_ref,
    q_ref, att_ref, stat_ref, mid_ref, gate_up_ref, own_rope_ref,
    series, toeplitz, lagged_ref, qbd, top_ref, acc_ref,
):
    chip, core, low, high = geometry()
    series[0:8, :] = jnp.zeros((8, TILE), f32)
    series[8 : 8 + TILES, :] = features_ref[:, 0, :].astype(bf16).astype(f32)
    toeplitz[:, 0:MAXLAG] = jnp.zeros((TILE, MAXLAG), bf16)

    def shift(m, carry):
        rows = [series[pl.ds(m * SHIFTED + 7 + n, 1), :] for n in range(SHIFTED + 1)]
        window = jnp.broadcast_to(jnp.concatenate(rows, axis=1), (TILE, (SHIFTED + 1) * TILE))
        rolled = pltpu.roll(window, 1, 1, stride=1, stride_axis=0)
        at = pl.multiple_of(m * SHIFTED * TILE + MAXLAG, TILE)
        toeplitz[:, pl.ds(at, SHIFTED * TILE)] = rolled[:, TILE:].astype(bf16)
        return carry

    lax.fori_loop(0, TILES // SHIFTED, shift, 0)

    def others(tiles):
        rows = jnp.concatenate([features_ref[t] for t in tiles], axis=1)
        return jnp.concatenate([rows, jnp.zeros_like(rows)], axis=0).astype(bf16)

    traffic.ready(5)
    w_dense = w_dense_ref[...]
    gain_a, gain_b = gain_column(gains_ref, 0), gain_column(gains_ref, 1)
    w_qkv = w_qkv_ref[...]
    lag_rows = iota((TILE, 1), 0) + 1
    k_size = jnp.zeros((HEADS, BLOCK), f32)
    for k in range(BLOCKS):
        place = iota((1, BLOCK), 1) + k * BLOCK
        start = doc_start(place, len_ref)
        parts = []
        for b in range(3):
            at = MAXLAG + k * BLOCK - b * TILE
            lagged = toeplitz[:, at : at + BLOCK]
            if k in (0, BLOCKS - 1):
                valid = place - (lag_rows + b * TILE) >= start
                lagged = jnp.where(valid, lagged.astype(f32), 0.0).astype(bf16)
            parts.append(lagged)
        parts.append(others(range(4 * k, 4 * k + 4)))
        resid = nn(w_dense, jnp.concatenate(parts, axis=0))
        normal = (resid * norm_factor(resid) * gain_a).astype(bf16)
        normal_all[k] = normal
        k_size = jnp.maximum(k_size, key_value_block(normal, w_qkv, rope_ref, k, keys_ref, values_ref))

    cosine, sine = own_rope(rope_ref, low, high)
    own_rope_ref[0:8], own_rope_ref[8:16] = cosine, sine
    traffic.send(keys_ref, values_ref, normal_all, own_rope_ref)

    place = own_places(low, high)
    start = doc_start(place, len_ref)
    lane = iota((1, TILE), 1)

    def tile_of(ref, tile):
        return ref[:, pl.ds(pl.multiple_of(tile * TILE, TILE), TILE)].astype(f32)

    for b in range(3):
        lagged = jnp.where(lane < HALF, tile_of(toeplitz, low + 3 - b), tile_of(toeplitz, high + 3 - b))
        valid = place - (lag_rows + b * TILE) >= start
        lagged_ref[b * TILE : (b + 1) * TILE, :] = jnp.where(valid, lagged, 0.0).astype(bf16)
    lagged_ref[MAXLAG:, :] = jnp.where(lane < HALF, others([low]).astype(f32), others([high]).astype(f32)).astype(bf16)
    lagged = lagged_ref[...]
    resid = nn(w_dense, lagged)
    resid_ref[...] = resid
    normal = (resid * norm_factor(resid) * gain_a).astype(bf16)
    normal_a_ref[...] = normal
    traffic.send(resid_ref, normal_a_ref)
    query = query_of(normal, w_qkv, cosine, sine)
    attended, stat_ref[...] = attend(query, k_size, keys_ref, values_ref, len_ref, low, high, qbd, top_ref, acc_ref, q_ref)
    att_ref[...] = attended
    traffic.send(q_ref, att_ref, stat_ref)
    traffic.ready()
    feats_ref[...] = nn(chosen_ref[...], lagged).astype(bf16)
    mid, _, gate_up, _, resid = feed_forward(resid, attended, w_out_ref[...], w_gate_up_ref[...], w_down_ref[...], gain_b)
    mid_ref[...], gate_up_ref[...] = mid, gate_up
    traffic.send(mid_ref, gate_up_ref, feats_ref)
    next_resid_ref[...] = resid
    normal = (resid * norm_factor(resid) * gain_column(gains_ref, 2)).astype(bf16)
    next_ref[...] = normal
    copies_ref[...] = jnp.broadcast_to(normal[None], copies_ref.shape)


def natural_tiles(own_ref, other_ref, put):
    _, core, _, _ = geometry()
    mine = (iota((1, TILE), 1) < HALF) == (core == 0)
    for chip in range(TILES // 2):
        tile = 2 * chip if chip < 8 else TILES - 1 - 2 * chip
        first, second = jnp.where(core == 0, chip, 15 - chip), jnp.where(core == 0, 15 - chip, chip)
        own, other = own_ref[first].astype(f32), other_ref[second].astype(f32)
        for t, value in ((tile, jnp.where(mine, own, other)), (TILES - 1 - tile, jnp.where(mine, other, own))):
            put(t // 4, slice(t % 4 * TILE, (t % 4 + 1) * TILE), value.astype(bf16))


def second_kernel(
    traffic, own_ref, other_ref, cot_own_ref, cot_other_ref, len_ref, turned_qkv_ref, rope_ref, normal_ref, own_rope_ref, resid_in_ref,
    turned_out_ref, turned_gate_up_ref, w_out_ref, w_gate_up_ref, w_down_ref, gains_ref,
    copies_ref, payload_ref, act_ref, keys_ref, values_ref, normal_all, q_ref, grad_ref, att_ref, d_gain_ref,
    d_out_ref, d_gate_up_ref, d_branch_ref, hidden_ref, normal_b_ref,
    qbd, top_ref, acc_ref,
):
    chip, core, low, high = geometry()

    def put(block, columns, value):
        normal_all[block, :, columns] = value

    natural_tiles(own_ref, other_ref, put)
    traffic.send(normal_all)
    traffic.ready(5)
    w_qkv = turned_qkv_ref[...]
    k_size = jnp.zeros((HEADS, BLOCK), f32)
    for k in range(BLOCKS):
        k_size = jnp.maximum(k_size, key_value_block(normal_all[k], w_qkv, rope_ref, k, keys_ref, values_ref))
    traffic.send(keys_ref, values_ref)
    query = query_of(normal_ref[...], w_qkv, own_rope_ref[0:8], own_rope_ref[8:16])
    attended, stat = attend(query, k_size, keys_ref, values_ref, len_ref, low, high, qbd, top_ref, acc_ref, q_ref)
    traffic.ready()
    gain = gain_column(gains_ref, 3)
    w_out, w_gate_up, w_down = w_out_ref[...], w_gate_up_ref[...], w_down_ref[...]
    mid, _, gate_up, _, out = feed_forward(
        resid_in_ref[...], attended, turned_out_ref[...], turned_gate_up_ref[...], w_down, gain
    )
    act_ref[...] = out
    att_ref[...] = attended
    traffic.send(act_ref, att_ref, q_ref)
    grad = tile_halves(cot_own_ref[...].astype(f32), cot_other_ref[...].astype(f32))
    low_refs = (d_out_ref, d_gate_up_ref, d_branch_ref, hidden_ref, normal_b_ref)
    grad, payload, d_gain_ref[...] = feed_back(grad, attended, mid, gate_up, w_out, w_gate_up, w_down, gain, stat, low_refs, traffic)
    grad_ref[...] = grad
    payload_ref[...] = payload
    copies_ref[...] = jnp.broadcast_to(payload[None], copies_ref.shape)


def query_back(
    traffic, count, payload_ref, q_ref, len_ref, own_rope_ref, rope_ref, keys_ref, values_ref, normal_all, w_qkv_ref, dq_ref, qall_ref,
    k_rows_ref, v_rows_ref, qbd, dbd, acc_ref,
):
    chip, core, low, high = geometry()
    traffic.ready(count)
    unit = eye(TILE, TILE, bf16)
    rows = nt(unit, payload_ref[...])
    spread(qbd, jnp.concatenate([q_ref[...].astype(f32), rows[:, D:]], axis=1), LROW, LROW + 9)
    spread(dbd, rows, DROW)
    k_rows_ref[...] = nt(unit, own_tile(keys_ref, low, high)).astype(bf16)
    v_rows_ref[...] = nt(unit, own_tile(values_ref, low, high)).astype(bf16)
    w_qkv = w_qkv_ref[...]

    def queries(k, carry):
        at = pl.ds(pl.multiple_of(k * BLOCK, BLOCK), BLOCK)
        qall_ref[k] = query_of(normal_all[k], w_qkv, rope_ref[0:8, at], rope_ref[8:16, at])
        return carry

    lax.fori_loop(0, BLOCKS, queries, 0, unroll=2)
    traffic.send(k_rows_ref, v_rows_ref, qall_ref)
    acc_ref[...] = jnp.zeros(acc_ref.shape, f32)

    def step(u, tile, block, at):
        scores = scores_of(qbd[u], with_ones(keys_ref[block, :, at]), query_bias(u, tile, block, at, len_ref))
        d_scores = jnp.exp(scores) * nn(dbd[u], with_ones(values_ref[block, :, at]))
        acc_ref[u] = acc_ref[u] + nt(d_scores.astype(bf16), keys_ref[block, :, at])

    run_steps(query_step, low, high, step, 2)
    step(*query_last(low, high))
    d_query = jnp.concatenate([own_heads(acc_ref[0]), own_heads(acc_ref[1])], axis=0) * HEAD_DIM**-0.5
    dq_ref[...] = rotate(turned_rows(d_query), own_rope_ref[0:8], -own_rope_ref[8:16])


def turned_rows(x):
    hi, lo = two_parts(x)
    unit = eye(D, D, bf16)
    return nt(unit, hi) + nt(unit, lo)


def key_back(traffic, count, unroll, own_ref, other_ref, len_ref, qall_ref, k_rows_ref, v_rows_ref, dq_ref, grad_ref, resid_ref, w_qkv_ref, gain,
             own_rope_ref, daug, kbd, vbd, dk_ref, dv_ref):
    chip, core, low, high = geometry()

    def put(block, columns, value):
        daug[block, :, columns] = value

    natural_tiles(own_ref, other_ref, put)
    traffic.ready(count)
    ones = jnp.ones((TILE, STAT), f32)
    spread(kbd, jnp.concatenate([k_rows_ref[...].astype(f32), ones], axis=1), LROW, LROW + 9)
    spread(vbd, jnp.concatenate([v_rows_ref[...].astype(f32), ones], axis=1), DROW)
    dk_ref[...] = jnp.zeros(dk_ref.shape, f32)
    dv_ref[...] = jnp.zeros(dv_ref.shape, f32)

    def step(u, tile, block, at):
        queries = jnp.concatenate([qall_ref[block, :, at], daug[block, D:AUG, at]], axis=0)
        probs = jnp.exp(scores_of(kbd[u], queries, key_bias(u, tile, block, at, len_ref)))
        d_scores = probs * nn(vbd[u], daug[block, :, at])
        dv_ref[u] = dv_ref[u] + nt(probs.astype(bf16), daug[block, :, at])
        dk_ref[u] = dk_ref[u] + nt(d_scores.astype(bf16), qall_ref[block, :, at])

    run_steps(key_step, low, high, step, unroll)
    step(*key_last(low, high))
    traffic.ready()
    d_key = turned_rows(jnp.concatenate([own_heads(dk_ref[0]), own_heads(dk_ref[1])], axis=0))
    d_value = nt(eye(D, D, bf16), jnp.concatenate([own_heads(dv_ref[0]), own_heads(dv_ref[1])], axis=0).astype(bf16))
    d_key = rotate(d_key, own_rope_ref[0:8], -own_rope_ref[8:16])
    d_mixed = jnp.concatenate([dq_ref[...], d_key, d_value], axis=0).astype(bf16)
    d_in, d_gain = norm_back(resid_ref[...], gain(), nn(w_qkv_ref[...], d_mixed))
    return grad_ref[...] + d_in, d_mixed, d_gain


def projection_grads(normal, d_mixed):
    tail = nt(normal, jnp.concatenate([d_mixed[MAXLAG:], jnp.zeros((TILE - 48, TILE), bf16)], axis=0))
    return nt(normal, d_mixed[:MAXLAG]), tail


def third_kernel(
    traffic, own_ref, other_ref, len_ref, qall_ref, k_rows_ref, v_rows_ref, dq_ref, grad_in_ref, resid_ref, att_ref, stat_ref, mid_ref,
    gate_up_ref, own_rope_ref, w_qkv_ref, w_out_ref, w_gate_up_ref, w_down_ref, gains_ref,
    copies_ref, payload_ref, grad_ref, d_mixed_ref, d_gain_a_ref, d_gain_b_ref, d_out_ref, d_gate_up_ref, d_branch_ref, hidden_ref,
    normal_b_ref,
    daug, kbd, vbd, dk_ref, dv_ref,
):
    grad, d_mixed_ref[...], d_gain_a_ref[...] = key_back(
        traffic, 4, 8, own_ref, other_ref, len_ref, qall_ref, k_rows_ref, v_rows_ref, dq_ref, grad_in_ref, resid_ref, w_qkv_ref,
        lambda: gain_column(gains_ref, 2), own_rope_ref, daug, kbd, vbd, dk_ref, dv_ref,
    )
    low_refs = (d_out_ref, d_gate_up_ref, d_branch_ref, hidden_ref, normal_b_ref)
    grad, payload, d_gain_b_ref[...] = feed_back(
        grad, att_ref[...], mid_ref[...], gate_up_ref[...], w_out_ref[...], w_gate_up_ref[...], w_down_ref[...], gain_column(gains_ref, 1),
        stat_ref[...], low_refs, traffic,
    )
    grad_ref[...] = grad
    payload_ref[...] = payload
    copies_ref[...] = jnp.broadcast_to(payload[None], copies_ref.shape)


def second_window_kernel(
    traffic, len_ref, hidden_ref, d_out_ref, normal_ref, d_gate_up_ref, att_ref, d_branch_ref, d_gain_ref, payload_ref, q_ref,
    own_rope_ref, rope_ref, keys_ref, values_ref, normal_all, w_qkv_ref,
    pack_ref, tail_ref, dq_ref, qall_ref, k_rows_ref, v_rows_ref, qbd, dbd, acc_ref,
):
    traffic.ready(8)
    tail = feed_grads(
        Tiles(pack_ref), hidden_ref[...], d_out_ref[...], normal_ref[...], d_gate_up_ref[...], att_ref[...], d_branch_ref[...]
    )
    tail_ref[...] = jnp.where(iota((1, TILE), 1) == 99, d_gain_ref[...], tail)
    traffic.send(pack_ref, tail_ref)
    query_back(
        traffic, 16, payload_ref, q_ref, len_ref, own_rope_ref, rope_ref, keys_ref, values_ref, normal_all, w_qkv_ref, dq_ref, qall_ref,
        k_rows_ref, v_rows_ref, qbd, dbd, acc_ref,
    )


def third_window_kernel(
    traffic, len_ref, pack_in_ref, tail_in_ref, normal_a_ref, d_mixed_ref, d_gain_a_ref, hidden_ref, d_out_ref, normal_ref, d_gate_up_ref,
    att_ref, d_branch_ref, d_gain_b_ref, payload_ref, q_ref, own_rope_ref, rope_ref, keys_ref, values_ref, normal_all,
    w_qkv_ref,
    keep_ref, send_ref, rest_ref, tail0_ref, tail1_ref, dq_ref, qall_ref, k_rows_ref, v_rows_ref, qbd, dbd, acc_ref,
):
    traffic.ready(13)
    put = Pairs(lax.axis_index("tm") % 2, keep_ref, send_ref, rest_ref)
    for t in range(pack_in_ref.shape[0]):
        put.tile(pack_in_ref[t].astype(f32))
    head, tail = projection_grads(normal_a_ref[...], d_mixed_ref[...])
    put(head)
    tail0_ref[...] = feed_grads(
        put, hidden_ref[...], d_out_ref[...], normal_ref[...], d_gate_up_ref[...], att_ref[...], d_branch_ref[...]
    )
    lane = iota((1, TILE), 1)
    tail = jnp.where(lane == 98, d_gain_a_ref[...], tail + tail_in_ref[...])
    tail1_ref[...] = jnp.where(lane == 97, d_gain_b_ref[...], tail)
    traffic.send(keep_ref, send_ref, rest_ref, tail0_ref, tail1_ref)
    query_back(
        traffic, 21, payload_ref, q_ref, len_ref, own_rope_ref, rope_ref, keys_ref, values_ref, normal_all, w_qkv_ref, dq_ref, qall_ref,
        k_rows_ref, v_rows_ref, qbd, dbd, acc_ref,
    )


def last_kernel(
    traffic, own_ref, other_ref, len_ref, scale_ref, ids_ref, qall_ref, k_rows_ref, v_rows_ref, dq_ref, grad_in_ref, resid_ref,
    normal_a_ref, tail0_ref, tail1_ref, rest_ref, w_dense_ref, feats_ref, own_rope_ref, w_qkv_ref, gains_ref,
    keep_ref, send_ref, daug, kbd, vbd, dk_ref, dv_ref, raw_ref,
):
    chip, core, low, high = geometry()
    d_first, d_mixed, d_gain = key_back(
        traffic, 6, 4, own_ref, other_ref, len_ref, qall_ref, k_rows_ref, v_rows_ref, dq_ref, grad_in_ref, resid_ref, w_qkv_ref,
        lambda: gain_column(gains_ref, 0), own_rope_ref, daug, kbd, vbd, dk_ref, dv_ref,
    )
    head, tail0 = projection_grads(normal_a_ref[...], d_mixed)
    d_first = d_first.astype(bf16)
    feats = feats_ref[...]
    empty = jnp.zeros((64, TILE), bf16)
    tail0 = tail0 + tail0_ref[...] + nt(d_first, jnp.concatenate([empty, feats[:64]], axis=0))
    tail1 = tail1_ref[...] + nt(d_first, jnp.concatenate([empty, feats[64:], empty[:32]], axis=0))
    lane, row = iota((1, TILE), 1), iota((D, 1), 0)
    tail1 = jnp.where(lane == 96, d_gain, tail1)
    sums, counts = jnp.zeros((D, 1), f32), jnp.zeros((D, 1), f32)
    owner = (lax.axis_index("tm") == 0).astype(f32)
    for d in range(DOCS):
        hit = jnp.where(row == ids_ref[d], owner, 0.0)
        sums, counts = sums + hit * scale_ref[d], counts + hit
    high_part = sums.astype(bf16).astype(f32)
    tail1 = jnp.where(lane == 100, high_part, tail1)
    tail1 = jnp.where(lane == 101, sums - high_part, tail1)
    tail1 = jnp.where(lane == 102, counts, tail1)

    place = own_places(low, high)
    start = doc_start(place, len_ref)
    own = doc_scale_at(place, len_ref, scale_ref)
    flip = (iota((TILE, TILE), 0) + iota((TILE, TILE), 1) == TILE - 1).astype(bf16)
    raw_ref[...] = jnp.zeros(raw_ref.shape, f32)
    lags = TILE - iota((TILE, 1), 0)
    for b in range(3):
        weights = nn(w_dense_ref[:, b * TILE : (b + 1) * TILE], flip).astype(bf16)
        d_lagged = tn(weights, d_first)
        valid = place - (lags + b * TILE) >= start
        d_lagged = jnp.where(valid, d_lagged, 0.0) / own
        for u in range(2):
            half = jnp.where((lane < HALF) == (u == 0), d_lagged, 0.0)
            wide = jnp.concatenate([jnp.zeros((TILE, TILE), f32), half], axis=1)
            rolled = pltpu.roll(wide, TILE, 1, stride=1, stride_axis=0)
            total = jnp.sum(rolled, axis=0, keepdims=True)
            for tile, part in (((low if u == 0 else high) - b + 16, total[:, TILE:]), ((low if u == 0 else high) - b + 15, total[:, :TILE])):
                at = tile % 2, pl.ds(tile // 2, 1)
                raw_ref[at] = raw_ref[at] + part

    put = Pairs(core, keep_ref, send_ref)
    put.tile(rest_ref[0].astype(f32))
    for part in (head, tail0, tail1):
        put(part)
    for k in range(2):
        put.tile(raw_ref[k, 8:24, :])


def summed(in_ref):
    count, rows, _ = in_ref.shape
    total = jnp.zeros((rows, TILE), f32)
    return lax.fori_loop(0, count // 8, lambda i, t: t + jnp.sum(in_ref[pl.ds(i * 8, 8)].astype(f32), axis=0), total)


def pair_sum_kernel(early_ref, early_in_ref, late_ref, late_in_ref, out_ref):
    zero = jnp.zeros((16, TILE), bf16)
    late = late_ref.shape[0] - 1
    series, core = lax.axis_index("series"), lax.axis_index("tm") % 2
    out_ref[:, 32:40, :] = jnp.zeros((64, 8, TILE), bf16)

    def both(ref, in_ref, t):
        return ref[t].astype(f32) + in_ref[t].astype(f32)

    for t in range(128):
        value = zero
        if t < EARLY:
            value = both(early_ref, early_in_ref, t).astype(bf16)
        elif t < EARLY + late:
            value = both(late_ref, late_in_ref, t - EARLY).astype(bf16)
        out_ref[jnp.where(core == 0, t // 2, 63 - t // 2), t % 2 * 16 : t % 2 * 16 + 16, :] = value
    raw = both(late_ref, late_in_ref, late)
    for c in range(16):
        line = jnp.where(iota((8, 1), 0) == 0, raw[c : c + 1], 0.0)
        chip = series * 16 + c
        out_ref[jnp.where(core == 0, chip, 63 - chip), 32:40, :] = line.astype(bf16)


def sum_kernel(in_ref, out_ref, raw_ref):
    total = summed(in_ref)
    out_ref[...] = jnp.broadcast_to(total[:32].astype(bf16)[None], out_ref.shape)
    raw_ref[...] = total[32:33]


def unpack_kernel(own_ref, other_ref, act_in_ref, act_ref, lag_ref, qkv_ref, out_ref, gate_up_ref, down_ref, gains_ref, scale_ref):
    core = lax.axis_index("tm") % 2
    act_ref[...] = act_in_ref[...]

    def tile(t):
        rows = slice(t // 2 % 2 * 16, t // 2 % 2 * 16 + 16)
        first, second = jnp.where(core == 0, t // 4, 63 - t // 4), jnp.where(core == 0, 63 - t // 4, t // 4)
        return jnp.where(core == t % 2, own_ref[first, rows].astype(f32), other_ref[second, rows].astype(f32))

    def columns(first, count):
        return [jnp.concatenate([tile(first + 9 * c + r) for r in range(9)], axis=0) for c in range(count)]

    layers = ((207, 234, 117), (90, 243, 0))
    tails = []
    for layer, (at_qkv, at_tail, at_rest) in enumerate(layers):
        for c, part in enumerate(columns(at_qkv, 3)):
            qkv_ref[layer, :, c * TILE : (c + 1) * TILE] = part
        tail = columns(at_tail, 1)[0]
        tails.append(tail)
        qkv_ref[layer, :, MAXLAG:] = tail[:, :48]
        for c, part in enumerate(columns(at_rest, 3)):
            down_ref[layer, :, c * TILE : (c + 1) * TILE] = part
        for c, part in enumerate(columns(at_rest + 27, 6)):
            gate_up_ref[layer, :, c * TILE : (c + 1) * TILE] = part
        out_ref[layer, :, :TILE] = columns(at_rest + 81, 1)[0]
        out_ref[layer, :, TILE:] = tail[:, 48:64]
    lag = jnp.where(iota((1, TILE), 1) < 64, pltpu.roll(tails[0], 64, 1), tails[1])
    lag_ref[...] = lag[:, :FEATS]
    pick = (iota((8, TILE), 1) == iota((8, TILE), 0) + 96).astype(bf16)
    rest = nt(pick, tails[1].astype(bf16))
    gains_ref[0] = rest[0:2]
    gains_ref[1] = rest[2:4]
    scale_ref[...] = ((rest[4:5] + rest[5:6]) / rest[6:7])[:, :DATASETS]


def weights_kernel(
    traffic, lag_ref, w_lag_ref, w_qkv_ref, w_out_ref, w_gate_up_ref, cot_ref,
    dense_ref, qkv0_ref, out0_ref, gate_up0_ref, qkv1_ref, out1_ref, gate_up1_ref, chosen_ref, low_cot_ref,
):
    traffic.ready()
    rows = iota((FEATS, 1), 0)
    diagonal = iota((FEATS, LAGS), 0) == iota((FEATS, LAGS), 1)
    offsets = jnp.sum(jnp.where(diagonal, lag_ref[...].astype(f32), 0.0), axis=1, keepdims=True)
    offsets = jnp.where(rows < LAGS, offsets - 1.0, (rows - LAGS + MAXLAG + 1).astype(f32))
    chosen = (iota((FEATS, LAGCOLS), 1).astype(f32) == offsets).astype(bf16)
    chosen_ref[0:FEATS, :] = chosen
    chosen_ref[FEATS:, :] = jnp.zeros((96 - FEATS, LAGCOLS), bf16)
    dense_ref[...] = nn(w_lag_ref[...], chosen).astype(bf16)
    qkv0_ref[...] = turned(w_qkv_ref[0])
    out0_ref[...] = turned(w_out_ref[0])
    gate_up0_ref[...] = turned(w_gate_up_ref[0])
    qkv1_ref[...] = turned(w_qkv_ref[1])
    out1_ref[...] = turned(w_out_ref[1])
    gate_up1_ref[...] = turned(w_gate_up_ref[1])
    low_cot_ref[...] = cot_ref[...].astype(bf16)


def first_values_kernel(traffic, len_ref, scale_ref, raw_ref, hours_ref, out_ref):
    traffic.ready()
    places = lax.axis_index("tm") * TILE + iota((1, TILE), 1)
    own = doc_scale_at(places, len_ref, scale_ref)
    angle = hours_ref[...].astype(f32) * (2.0 * math.pi / 24.0)
    rows = [raw_ref[...] / own, jnp.sin(angle), jnp.cos(angle), jnp.log(own), jnp.zeros((4, TILE), f32)]
    out_ref[...] = jnp.broadcast_to(jnp.concatenate(rows, axis=0)[None], out_ref.shape)


def shape(*dims, dtype=f32):
    return jax.ShapeDtypeStruct(dims, dtype)


class Traffic:
    def __init__(self, loads, stores):
        self.loads, self.stores, self.waited, self.sent = loads, stores, 0, set()
        for copy in loads:
            copy.start()

    def ready(self, count=None):
        count = len(self.loads) if count is None else count
        for copy in self.loads[self.waited : count]:
            copy.wait()
        self.waited = max(self.waited, count)

    def send(self, *refs):
        for ref, copy in self.stores:
            if any(ref is r for r in refs):
                copy.start()
                self.sent.add(id(copy))

    def finish(self):
        self.ready()
        for _, copy in self.stores:
            if id(copy) not in self.sent:
                copy.start()
        for _, copy in self.stores:
            copy.wait()


def call(kernel, operands, outs, scratch=(), tables=(), weights=(), cost=None):
    several = isinstance(outs, list)
    outs = outs if several else [outs]
    layers = [None] * len(tables) + [x[1] if isinstance(x, tuple) else None for x in weights]
    fetched = (*tables, *(x[0] if isinstance(x, tuple) else x for x in weights))
    shapes = [x.shape if layer is None else x.shape[1:] for x, layer in zip(fetched, layers)]
    buffers = [(pltpu.SMEM if n < len(tables) else pltpu.VMEM)(shapes[n], x.dtype) for n, x in enumerate(fetched)]
    is_far = [not isinstance(out, jax.ShapeDtypeStruct) for out in outs]
    buffers += [pltpu.VMEM(out.shape, out.dtype) for out, far in zip(outs, is_far) if far]
    count, extra, copies = len(operands), len(buffers), len(buffers)

    def wrapped(*refs):
        refs = list(refs)
        ins, sources = refs[:count], refs[count : count + len(fetched)]
        results = refs[count + len(fetched) : count + len(fetched) + len(outs)]
        rest = refs[count + len(fetched) + len(outs) :]
        if not copies:
            kernel(*ins, *results, *rest)
            return
        own, held, sems = rest[: len(scratch)], rest[len(scratch) : -1], rest[-1]
        sources = [a if layer is None else a.at[layer] for a, layer in zip(sources, layers)]
        loads = [pltpu.make_async_copy(a, b, sems.at[n]) for n, (a, b) in enumerate(zip(sources, held))]
        stores, at = [], len(fetched)
        for n, far in enumerate(is_far):
            if far:
                stores.append((held[at], pltpu.make_async_copy(held[at], results[n], sems.at[at])))
                results[n] = held[at]
                at += 1
        traffic = Traffic(loads, stores)
        kernel(traffic, *ins, *held[: len(fetched)], *results, *own)
        traffic.finish()

    vmem, hbm = pl.BlockSpec(memory_space=pltpu.VMEM), pl.BlockSpec(memory_space=pltpu.HBM)
    results = pl.pallas_call(
        wrapped,
        out_shape=outs,
        in_specs=[vmem] * count + [hbm] * len(fetched),
        out_specs=[hbm if far else vmem for far in is_far],
        scratch_shapes=[*scratch, *buffers, pltpu.SemaphoreType.DMA((copies,))] if copies else list(scratch),
        compiler_params=pltpu.CompilerParams(vmem_limit_bytes=VMEM),
        cost_estimate=cost and pl.CostEstimate(flops=cost * 10**9, bytes_accessed=10**6, transcendentals=0),
    )(*operands, *(pltpu.with_memory_space_constraint(x, pltpu.HBM) for x in fetched))
    return results if several else results[0]


def pair_permute(x, bit):
    return lax.ppermute(x, "tm", [(i, i ^ bit) for i in range(32)])


def gather(copies, beside):
    groups = [[2 * chip for chip in range(16)], [31 - 2 * chip for chip in range(16)]]
    own = lax.all_to_all(copies, "tm", 0, 0, axis_index_groups=groups)
    own, beside = lax.optimization_barrier((own, beside))
    return own, pair_permute(own, 1), beside


def swap(block):
    return lax.ppermute(block, "tm", [(n, n if n % 2 == 0 else 32 - n) for n in range(32)])


def tile_halves(own, other):
    lane = iota((1, TILE), 1) < HALF
    return jnp.where(lane == (lax.axis_index("tm") < 16), own, other)


def rope_table():
    freqs = 10000.0 ** (-np.arange(8, dtype=np.float64) / 8)
    angle = np.arange(LEN, dtype=np.float64)[None, :] * freqs[:, None]
    return np.concatenate([np.cos(angle), np.sin(angle)], axis=0).astype(np.float32)


def body(
    raw_values, hours, doc_lengths, doc_scale, dataset_ids, lag_offsets, w_lag, w_qkv, w_out, w_gate_up, w_down, gains, cotangent
):
    lengths, scales, ids = doc_lengths.reshape(DOCS), doc_scale.reshape(DOCS), dataset_ids.reshape(DOCS)
    def low(*dims):
        return shape(*dims, dtype=bf16)

    def far(*dims, dtype=f32):
        return pltpu.HBM(dims, dtype)

    def far_low(*dims):
        return far(*dims, dtype=bf16)

    w_lag, w_down, lags = w_lag.T, w_down.transpose(0, 2, 1), lag_offsets.reshape(1, LAGS)
    rope = jnp.asarray(rope_table())
    values = lax.all_to_all(call(first_values_kernel, (), shape(32, 8, TILE), tables=(lengths, scales), weights=(raw_values, hours)), "tm", 0, 0)
    turned_shapes = [far_low(3 * D, D), far_low(D, D), far_low(2 * FF, D)]
    w_dense, *turned_weights, chosen, low_cot = call(
        weights_kernel, (), [far_low(D, LAGCOLS), *turned_shapes, *turned_shapes, far_low(96, LAGCOLS), far_low(D, TILE)],
        weights=(lags, w_lag, w_qkv, w_out, w_gate_up, cotangent[0].T), cost=3,
    )
    turned0, turned1 = turned_weights[:3], turned_weights[3:]
    values, w_dense = lax.optimization_barrier((values, w_dense))
    all_d = far_low(BLOCKS, D, BLOCK)
    mine, mine_low, ff_low, column_shape = far(D, TILE), far_low(D, TILE), far_low(FF, TILE), far(D, 1)
    payload_shapes = [far_low(16, AUG, TILE), far_low(AUG, TILE)]
    low_grads = [mine_low, far_low(2 * FF, TILE), mine_low, ff_low, mine_low]
    bd, wide_bd = pltpu.VMEM((2, ROWS, AUG), bf16), pltpu.VMEM((2, ROWS, WIDE), bf16)
    acc, acc_d = pltpu.VMEM((2, ROWS, AUG), f32), pltpu.VMEM((2, ROWS, D), f32)
    top = pltpu.VMEM((2, ROWS, 1), f32)
    back_scratch = [pltpu.VMEM((BLOCKS, AUG, BLOCK), bf16), wide_bd, bd, acc_d, acc]

    (copies, next1, resid1, keys0, values0, normal_all0, feats, resid0, normal_a0, q0, att0, stat0, mid0, gate_up0, own_rope) = call(
        first_kernel,
        (values,),
        [far_low(16, D, TILE), mine_low, mine, all_d, all_d, all_d, far_low(96, TILE), mine, mine_low, far_low(TILE, D), mine_low,
         far_low(STAT, TILE), mine, far(2 * FF, TILE), far(16, TILE)],
        [pltpu.VMEM((8 + TILES, TILE), f32), pltpu.VMEM((TILE, MAXLAG + LEN), bf16),
         pltpu.VMEM((LAGCOLS, TILE), bf16), wide_bd, top, acc],
        tables=(lengths,), weights=(w_dense, gains, turned0[0], rope, chosen, *turned0[1:], (w_down, 0)),
    )

    own, other, cot = gather(copies, swap(low_cot))
    copies, payload, act, keys1, values1, normal_all1, q1, grad, att1, d_gain_b1, *low1 = call(
        second_kernel,
        (own, other, cot, pair_permute(cot, 1)),
        [*payload_shapes, mine, all_d, all_d, all_d, far_low(TILE, D), mine, mine_low, column_shape, *low_grads],
        [wide_bd, top, acc],
        tables=(lengths,),
        weights=(turned1[0], rope, next1, own_rope, resid1, *turned1[1:], (w_out, 1), (w_gate_up, 1), (w_down, 1), gains),
    )

    rows_low = far_low(TILE, D)
    side_shapes = [mine, all_d, rows_low, rows_low]
    d_out, d_gate_up, d_branch, hidden, normal_b = low1
    pack, tail, dq, qall, k_rows, v_rows = call(
        second_window_kernel, (), [far_low(90, 16, TILE), mine, *side_shapes], [wide_bd, bd, acc_d],
        tables=(lengths,),
        weights=(hidden, d_out, normal_b, d_gate_up, att1, d_branch, d_gain_b1, payload, q1, own_rope, rope, keys1, values1, normal_all1,
                 turned1[0]), cost=8,
    )
    own, other, dq = gather(copies, dq)
    copies, payload, grad, d_mixed, d_gain_a1, d_gain_b0, *low0 = call(
        third_kernel,
        (own, other),
        [*payload_shapes, mine, far_low(3 * D, TILE), column_shape, column_shape, *low_grads],
        back_scratch,
        tables=(lengths,),
        weights=(qall, k_rows, v_rows, dq, grad, resid1, att0, stat0, mid0, gate_up0, own_rope, (w_qkv, 1), (w_out, 0), (w_gate_up, 0),
                 (w_down, 0), gains),
    )
    d_out, d_gate_up, d_branch, hidden, normal_b = low0
    early, early_out, rest, tail0, tail1, dq, qall, k_rows, v_rows = call(
        third_window_kernel, (),
        [far_low(EARLY, 16, TILE), far_low(EARLY, 16, TILE), far_low(1, 16, TILE), mine, mine, *side_shapes], [wide_bd, bd, acc_d],
        tables=(lengths,),
        weights=(pack, tail, next1, d_mixed, d_gain_a1, hidden, d_out, normal_b, d_gate_up, att0, d_branch, d_gain_b0, payload, q0,
                 own_rope, rope, keys0, values0, normal_all0, turned0[0]), cost=8,
    )
    own, other, (dq, early_out) = gather(copies, (dq, early_out))
    early_in = pair_permute(early_out, 1)
    late, late_out = call(
        last_kernel,
        (own, other),
        [low(LATE, 16, TILE)] * 2,
        [*back_scratch, pltpu.VMEM((2, 24, TILE), f32)],
        tables=(lengths, scales, ids),
        weights=(qall, k_rows, v_rows, dq, grad, resid0, normal_a0, tail0, tail1, rest, w_dense, feats, own_rope, (w_qkv, 0), gains),
    )
    packed = call(pair_sum_kernel, (early, early_in, late, pair_permute(late_out, 1)), low(64, 40, TILE))
    same_core = [[2 * chip for chip in range(64)], [127 - 2 * chip for chip in range(64)]]
    parts = lax.all_to_all(packed, ("series", "tm"), 0, 0, axis_index_groups=same_core)
    share, raw_grad = call(sum_kernel, (parts,), [low(64, 32, TILE), shape(1, TILE)])
    share, act = lax.optimization_barrier((share, act))
    own = lax.all_to_all(share, ("series", "tm"), 0, 0, axis_index_groups=same_core)
    own, act = lax.optimization_barrier((own, swap(tile_halves(act, pair_permute(act, 1)))))
    act, g_lag, g_qkv, g_out, g_gate_up, g_down, g_gains, scale = call(
        unpack_kernel,
        (own, pair_permute(own, 1), act),
        [shape(D, TILE), shape(D, FEATS), shape(LAYERS, D, 3 * D), shape(LAYERS, D, D), shape(LAYERS, D, 2 * FF), shape(LAYERS, D, FF),
         shape(LAYERS, 2, D), shape(1, DATASETS)],
    )
    return (
        act.T[None], raw_grad, scale.reshape(DATASETS), g_lag.T, g_qkv, g_out, g_gate_up, g_down.transpose(0, 2, 1), g_gains,
    )


def solution(mesh):
    placed = (
        P("series", "tm"),
        P("series", "tm"),
        P("series", None),
        P("series", None),
        P("series", None, None),
        P(),
        P(),
        P(),
        P(),
        P(),
        P(),
        P(),
        P("series", "tm", None),
    )
    return jax.shard_map(
        body,
        mesh=mesh,
        in_specs=placed,
        out_specs=(P("series", "tm", None), P("series", "tm"), P(), P(), P(), P(), P(), P(), P()),
        check_vma=False,
    )
```
